32 devices in a mesh: section: 2 (over x), rows: 16 (over z, y, core).
Axes of the slice: x: 2, y: 2, z: 4, core: 2. Of those that a mesh axis runs over, the one named last changes fastest.
Arguments:
- section_input: bfloat16 [2, 32, 512, 768], P('section', 'rows'), may hold values from -6 to 6
- enc_lengths: int32 [32, 4], P('rows'), may hold values from 1 to 256, 512 in all within a row
- dec_lengths: int32 [32, 4], P('rows'), may hold values from 1 to 128, 256 in all within a row
- attn_in: bfloat16 [2, 768, 2304], P('section'), may hold values from -0.21875 to 0.21875
- attn_out: bfloat16 [2, 768, 768], P('section'), may hold values from -1.25 to 1.25
- ffn_in: bfloat16 [2, 768, 4096], P('section'), may hold values from -0.21875 to 0.21875
- ffn_out: bfloat16 [2, 2048, 768], P('section'), may hold values from -0.125 to 0.125
- cross_weight: bfloat16 [2, 768, 1536], P('section'), may hold values from -8 to 8
- gains: float32 [2, 3, 768], P('section'), may hold values from 0.5 to 1.5
Outputs:
- results: float32 [2, 32, 512, 768], P('section', 'rows')
- grad_attn_in: float32 [2, 768, 2304], P('section', 'rows')
- grad_attn_out: float32 [2, 768, 768], P('section', 'rows')
- grad_ffn_in: float32 [2, 768, 4096], P('section', 'rows')
- grad_ffn_out: float32 [2, 2048, 768], P('section', 'rows')
- grad_cross: float32 [2, 768, 1536], P('section', 'rows')
- grad_gains: float32 [2, 3, 768], P('section', None, 'rows')
The draws below stay inside these ranges and needn't reach their ends.
Inputs may be any that keep to these rules, and one draw needn't show every extreme that they name: `enc_lengths`: the 4 lengths of a row sum to 512; the largest in each row is half of 512. Decoder document j belongs to encoder document j. `dec_lengths`: the 4 lengths of a row sum to 256; the largest in each row is half of 256.
All inputs are finite; a program needn't handle non-finite values.
Results may differ from the reference program's by a relative error of at most 0.02.
Values may be sent and summed in bfloat16 or wider, within the bound.
A program may use at most 320 MiB of HBM per device.

```python
import math
import jax
import jax.numpy as jnp
import numpy as np
from jax import lax

D = 768
HEADS = 12
HEAD = 64
FF = 2048
HD = 768
LE = 512
LD = 256
NSEG = 4
ROWS = 32


def draw_cross_weight(key, part):
    key = jax.random.fold_in(key, 7)
    base = jax.random.normal(key, (2, D, 2 * HD), jnp.float32)
    column_scale = jnp.concatenate([jnp.full((HD,), D ** (-0.5), jnp.float32), jnp.full((HD,), (HD // 8) ** (-0.5), jnp.float32)])
    return (base * column_scale).astype(jnp.bfloat16)


def level_of(rng, extent, shards, smallest, largest):
    loudness = 1.0
    for dim, shards_of in shards:
        steps = jax.random.uniform(jax.random.fold_in(jax.random.fold_in(rng, 6), dim), (shards_of,), jnp.float32, smallest / len(shards), largest / len(shards))
        loudness = loudness * jnp.repeat(jnp.exp(steps), extent[dim] // shards_of).reshape((-1,) + (1,) * (len(extent) - 1 - dim))
    return loudness


def profile(number_of, total, reach, slope):
    portions = [(1 << 20) // math.isqrt(grade ** slope) + 1 for grade in range(2, number_of + 1)]
    surplus, counts = total - reach - (number_of - 1), [1] * (number_of - 1)
    while surplus > 0:
        candidates = [i for i in range(number_of - 1) if counts[i] < reach]
        pool, left = sum([portions[i] for i in candidates]), surplus
        for i in candidates:
            more = min(reach - counts[i], max(1, left * portions[i] // pool), surplus)
            counts[i] = counts[i] + more
            surplus = surplus - more
    return np.array([reach] + counts)


def uneven(key, number_of, total, most, lean):
    if number_of == 2:
        one = jax.random.randint(key, (), max(1, total - most), min(most, total - 1) + 1)
        return jnp.stack([one, total - one])
    sizes = jnp.asarray(profile(number_of, total, most, lean), jnp.int32)
    pairs = (number_of - 1) // 2
    donor, taker = sizes[1:1 + 2 * pairs:2], sizes[2:2 + 2 * pairs:2]
    slack = jnp.minimum(donor - 1, most - taker)
    shifted = jax.random.randint(jax.random.fold_in(key, 1), (pairs,), 0, 1 << 20) % (slack + 1)
    sizes = sizes.at[1:1 + 2 * pairs:2].set(donor - shifted).at[2:2 + 2 * pairs:2].set(taker + shifted)
    return sizes[jax.random.permutation(jax.random.fold_in(key, 2), number_of)]


def gaussian(rng, extent, deviation, reach, split=(), held_as=jnp.bfloat16):
    drawn = deviation * jax.random.normal(rng, extent, jnp.float32)
    if split:
        drawn = drawn * level_of(rng, extent, split, -0.22, 0.18)
    return jnp.clip(drawn, -reach, reach).astype(held_as)


def setup_inputs(seed: int = 0) -> dict:
    splits = jax.random.split(jax.random.key(seed), 10)
    section_input = gaussian(splits[0], (2, ROWS, LE, D), 1.0, 6.0, ((0, 2), (1, 16)))
    enc_lengths = jax.vmap(lambda own: uneven(own, NSEG, LE, LE // 2, 2))(jax.random.split(splits[1], ROWS)).reshape((ROWS, NSEG)).astype(jnp.int32)
    dec_lengths = jax.vmap(lambda own: uneven(own, NSEG, LD, LD // 2, 2))(jax.random.split(splits[2], ROWS)).reshape((ROWS, NSEG)).astype(jnp.int32)
    attn_in = gaussian(splits[3], (2, D, 3 * HD), D ** -0.5, 0.21875, ((0, 2),))
    attn_out = gaussian(splits[4], (2, HD, D), (HD // 32) ** -0.5, 1.25, ((0, 2),))
    ffn_in = gaussian(splits[5], (2, D, 2 * FF), D ** -0.5, 0.21875, ((0, 2),))
    ffn_out = gaussian(splits[6], (2, FF, D), FF ** -0.5, 0.125, ((0, 2),))
    cross_weight = draw_cross_weight(jax.random.fold_in(splits[9], 71), 0)
    gains = jnp.clip(1.0 + 0.1 * jax.random.normal(splits[8], (2, 3, D), jnp.float32), 0.5, 1.5)
    return dict(section_input=section_input, enc_lengths=enc_lengths, dec_lengths=dec_lengths, attn_in=attn_in, attn_out=attn_out, ffn_in=ffn_in, ffn_out=ffn_out, cross_weight=cross_weight, gains=gains)


EPSILON = 1e-06
SCALE = 0.125
NEGATIVE = -1e+30
HIGHEST = lax.Precision.HIGHEST

@jax.custom_vjp
def low(v):
    return lax.optimization_barrier(v.astype(jnp.bfloat16)).astype(jnp.float32)

@jax.custom_vjp
def low_back(v):
    return v

def low_keep(v):
    return (low(v), None)

def low_pass(kept, grad):
    return (grad,)

def back_keep(v):
    return (v, None)

def back_low(kept, grad):
    return (low(grad),)
low.defvjp(low_keep, low_pass)
low_back.defvjp(back_keep, back_low)

def rounded(value_in):
    return low_back(low(value_in))

def rms_norm(value_in, gain_in):
    return value_in * lax.rsqrt(lax.optimization_barrier(jnp.mean(value_in * value_in, -1, keepdims=True)) + EPSILON) * gain_in

def matmul(left_op, right_op):
    return jnp.dot(left_op, right_op, precision=HIGHEST)

def segment_ids(lengths, span_len):
    seg_ends = jnp.cumsum(lengths, -1, dtype=jnp.int32)
    positions = jnp.arange(span_len, dtype=jnp.int32)
    return lax.optimization_barrier(jnp.sum((positions[None, :, None] >= seg_ends[:, None, :]).astype(jnp.int32), -1, dtype=jnp.int32))

def attend(queries, keys_in, values_in, allowed):
    count_q = queries.shape[0]
    count_k = keys_in.shape[0]
    query_heads = queries.reshape(count_q, HEADS, HEAD)
    key_heads = keys_in.reshape(count_k, HEADS, HEAD)
    value_heads = values_in.reshape(count_k, HEADS, HEAD)
    scores = low_back(jnp.einsum('qhd,khd->hqk', query_heads, key_heads, precision=HIGHEST) * SCALE)
    scores = jnp.where(allowed[None], scores, NEGATIVE)
    shifted_exp = jnp.exp(scores - lax.optimization_barrier(jnp.max(scores, -1, keepdims=True)))
    attn_probs = low(shifted_exp / lax.optimization_barrier(jnp.sum(shifted_exp, -1, keepdims=True)))
    attn_mixed = jnp.einsum('hqk,khd->qhd', attn_probs, value_heads, precision=HIGHEST)
    return rounded(attn_mixed.reshape(count_q, HEADS * HEAD))

def self_attention(hidden, gain_in, w_in, w_out, allowed):
    normed = low(rms_norm(hidden, gain_in))
    packed = rounded(matmul(normed, w_in))
    attn_mixed = attend(packed[:, :HD], packed[:, HD:2 * HD], packed[:, 2 * HD:], allowed)
    return hidden + low_back(matmul(attn_mixed, w_out))

def feed_forward(hidden, gain_in, w_in, w_out):
    normed = low(rms_norm(hidden, gain_in))
    gate_up = low_back(matmul(normed, w_in))
    activated = low(jax.nn.gelu(gate_up[:, :FF], approximate=True) * gate_up[:, FF:])
    return low_back(matmul(activated, w_out))

def encoder_row(hidden, seg_row, attn_in, attn_out, ffn_in, ffn_out, cross_weight, gains):
    allowed = seg_row[:, None] == seg_row[None, :]
    hidden = self_attention(hidden, gains[0], attn_in, attn_out, allowed)
    hidden = hidden + feed_forward(hidden, gains[2], ffn_in, ffn_out)
    memory = low(rms_norm(hidden, gains[1]))
    return rounded(matmul(memory, cross_weight))

def decoder_row(hidden, sent_kv, seg_row, seg_other, attn_in, attn_out, ffn_in, ffn_out, cross_weight, gains):
    positions = jnp.arange(LD, dtype=jnp.int32)
    allowed = (seg_row[:, None] == seg_row[None, :]) & (positions[None, :] <= positions[:, None])
    hidden = self_attention(hidden, gains[0], attn_in, attn_out, allowed)
    normed = low(rms_norm(hidden, gains[1]))
    queries = rounded(matmul(normed, cross_weight[:, :HD]))
    attn_mixed = attend(queries, sent_kv[:, :HD], sent_kv[:, HD:], seg_row[:, None] == seg_other[None, :])
    hidden = hidden + low_back(matmul(attn_mixed, cross_weight[:, HD:].T))
    return hidden + feed_forward(hidden, gains[2], ffn_in, ffn_out)

def reference(section_input, enc_lengths, dec_lengths, attn_in, attn_out, ffn_in, ffn_out, cross_weight, gains):
    seg_enc = segment_ids(enc_lengths, LE)
    seg_dec = segment_ids(dec_lengths, LD)
    enc_in = section_input[0].astype(jnp.float32)
    dec_in = section_input[1, :, :LD].astype(jnp.float32)
    cotangent = section_input[1, :, LD:].astype(jnp.float32)

    def forward(enc_in, dec_in, attn_in, attn_out, ffn_in, ffn_out, cross_weight, gains):

        def one_row(packed_row):
            enc_row, dec_row, row_enc, row_dec = packed_row
            sent_kv = encoder_row(enc_row, row_enc, attn_in[0], attn_out[0], ffn_in[0], ffn_out[0], cross_weight[0], gains[0])
            return decoder_row(dec_row, sent_kv, row_dec, row_enc, attn_in[1], attn_out[1], ffn_in[1], ffn_out[1], cross_weight[1], gains[1])
        return lax.map(jax.checkpoint(one_row), (enc_in, dec_in, seg_enc, seg_dec))
    output, pullback = jax.vjp(forward, enc_in, dec_in, attn_in.astype(jnp.float32), attn_out.astype(jnp.float32), ffn_in.astype(jnp.float32), ffn_out.astype(jnp.float32), cross_weight.astype(jnp.float32), gains.astype(jnp.float32))
    gradients = pullback(cotangent)
    results = jnp.stack([gradients[0], jnp.concatenate([output, gradients[1]], 1)])
    return (results, gradients[2], gradients[3], gradients[4], gradients[5], gradients[6], gradients[7])
```

```python
import functools

import jax
import jax.numpy as jnp
from jax import lax
from jax.experimental import pallas as pl
from jax.experimental.pallas import tpu as pltpu
from jax.sharding import PartitionSpec as P

HEADS = 12
HEAD = 64
PAIR = 128
EPSILON = 1e-06
SCALE = 0.125
LOG2E = 1.4426950408889634
NEGATIVE = -1e30
GELU_C = 0.7978845608028654
GELU_A = 0.044715

BF = jnp.bfloat16
F32 = jnp.float32
NT = (((1,), (1,)), ((), ()))
NN = (((1,), (0,)), ((), ()))
TN = (((0,), (0,)), ((), ()))


def mm(a, b, dims=NN):
    return lax.dot_general(a, b, dims, preferred_element_type=F32)


MESH = pl.DeviceIdType.MESH
LANES = 256
VMEM_LIMIT = 56 * 1024 * 1024

NZ, NY, NC = 4, 2, 2
Y_LAG = 2


def sum_scatter_kernel(counts, units, *refs):
    arrays = len(counts)
    ins, outs = refs[:arrays], refs[arrays : 2 * arrays]
    (own, got_core, got_y, got_r, got_l, s_local, s_core, r_core, s_y, r_y, s_r, r_r, s_l, r_l) = refs[
        2 * arrays :
    ]
    chunks = own.shape[0]
    sec, me = lax.axis_index("section"), lax.axis_index("rows")
    core, y, z = lax.rem(me, 2), lax.rem(me // 2, 2), me // 4
    by_core, by_y = me + 1 - 2 * core, me + 2 - 4 * y
    other, away = 1 - core, 1 - y

    barrier = pltpu.get_barrier_semaphore()

    def greet(peer):
        pl.semaphore_signal(barrier, inc=1, device_id=(sec, peer), device_id_type=MESH)

    greet(by_core)
    greet(by_y)

    @pl.when(z > 0)
    def _():
        greet(me - 4)

    @pl.when(z < NZ - 1)
    def _():
        greet(me + 4)

    @pl.when((z > 0) & (z < NZ - 1))
    def _():
        pl.semaphore_wait(barrier, 4)

    @pl.when((z == 0) | (z == NZ - 1))
    def _():
        pl.semaphore_wait(barrier, 3)

    def feed(src, dst_rows, chunk):
        pltpu.make_async_remote_copy(
            src_ref=src(other),
            dst_ref=got_core.at[chunk, :, :, dst_rows],
            send_sem=s_core.at[chunk],
            recv_sem=r_core.at[chunk],
            device_id=(sec, by_core),
            device_id_type=MESH,
        ).start()
        pltpu.make_async_copy(src(core), own.at[chunk, :, :, dst_rows], s_local.at[chunk]).start()

    base = 0
    for a in range(arrays):
        if units[a] is None:

            def panel(i, carry, a=a, base=base):
                at = pl.ds(pl.multiple_of(i * LANES, LANES), LANES)
                feed(lambda c: ins[a].at[:, :, c, :, at], pl.ds(0, own.shape[3]), base + i)
                return carry

            lax.fori_loop(0, counts[a], panel, 0)
        else:
            per = own.shape[3] // 16
            blocks = units[a]

            def unit(u, carry, a=a, base=base, blocks=blocks):
                at = pl.ds(pl.multiple_of((u // blocks) * LANES, LANES), LANES)
                rows_from = pl.ds(pl.multiple_of(lax.rem(u, blocks) * 16, 16), 16)
                rows_to = pl.ds(pl.multiple_of(lax.rem(u, per) * 16, 16), 16)
                feed(lambda c: ins[a].at[:, :, c, rows_from, at], rows_to, base + u // per)
                return carry

            lax.fori_loop(0, counts[a] * per, unit, 0)
        base += counts[a]

    def to_core(j):
        return pltpu.make_async_remote_copy(
            src_ref=got_core.at[j],
            dst_ref=got_core.at[j],
            send_sem=s_core.at[j],
            recv_sem=r_core.at[j],
            device_id=(sec, by_core),
            device_id_type=MESH,
        )

    def to_y(j):
        return pltpu.make_async_remote_copy(
            src_ref=own.at[j, :, away],
            dst_ref=got_y.at[j],
            send_sem=s_y.at[j],
            recv_sem=r_y.at[j],
            device_id=(sec, by_y),
            device_id_type=MESH,
        )

    def to_right(j, at):
        return pltpu.make_async_remote_copy(
            src_ref=own.at[j, pl.ds(at + 1, NZ - 1 - at), y],
            dst_ref=got_r.at[j, pl.ds(at + 1, NZ - 1 - at)],
            send_sem=s_r.at[j],
            recv_sem=r_r.at[j],
            device_id=(sec, me + 4),
            device_id_type=MESH,
        )

    def to_left(j, at):
        return pltpu.make_async_remote_copy(
            src_ref=own.at[j, pl.ds(0, at), y],
            dst_ref=got_l.at[j, pl.ds(0, at)],
            send_sem=s_l.at[j],
            recv_sem=r_l.at[j],
            device_id=(sec, me - 4),
            device_id_type=MESH,
        )

    def add_into(dst, src):
        dst[...] = (dst[...].astype(F32) + src[...].astype(F32)).astype(BF)

    def step(s, carry):
        @pl.when(s < chunks)
        def _():
            pltpu.make_async_copy(got_core.at[s], own.at[s], s_local.at[s]).wait()
            to_core(s).wait_recv()
            add_into(own.at[s], got_core.at[s])
            to_y(s).start()

        j_y = s - Y_LAG

        @pl.when((j_y >= 0) & (j_y < chunks))
        def _():
            to_y(j_y).wait_recv()
            for t in range(NZ):
                add_into(own.at[j_y, t, y], got_y.at[j_y, t])

        for at in range(NZ - 1):
            j_r = s - Y_LAG - at

            @pl.when((z == at) & (j_r >= 0) & (j_r < chunks))
            def _(at=at, j_r=j_r):
                if at > 0:
                    to_right(j_r, at - 1).wait_recv()
                    for t in range(at + 1, NZ):
                        add_into(own.at[j_r, t, y], got_r.at[j_r, t])
                to_right(j_r, at).start()

        for at in range(1, NZ):
            j_l = s - Y_LAG - (NZ - 1 - at)

            @pl.when((z == at) & (j_l >= 0) & (j_l < chunks))
            def _(at=at, j_l=j_l):
                if at < NZ - 1:
                    to_left(j_l, at + 1).wait_recv()
                    for t in range(at):
                        add_into(own.at[j_l, t, y], got_l.at[j_l, t])
                to_left(j_l, at).start()

        return carry

    lax.fori_loop(0, chunks + Y_LAG + NZ - 1, step, 0)

    def finish(j):
        for at in range(NZ):

            @pl.when(z == at)
            def _(at=at):
                if at == NZ - 1:
                    to_right(j, at - 1).wait_recv()
                if at == 0:
                    to_left(j, 1).wait_recv()
                to_y(j).wait_send()
                to_core(j).wait_send()
                if at < NZ - 1:
                    to_right(j, at).wait_send()
                if at > 0:
                    to_left(j, at).wait_send()

    def total(j, rows):
        mine = own[j, z, y, rows].astype(F32)
        right = got_r[j, z, rows].astype(F32)
        left = got_l[j, z, rows].astype(F32)
        return mine + jnp.where(z > 0, right, 0.0) + jnp.where(z < NZ - 1, left, 0.0)

    base = 0
    for a in range(arrays):
        if units[a] is None:

            def panel_out(i, carry, a=a, base=base):
                finish(base + i)
                at = pl.ds(pl.multiple_of(i * LANES, LANES), LANES)
                outs[a][:, at] = total(base + i, pl.ds(0, own.shape[3]))
                return carry

            lax.fori_loop(0, counts[a], panel_out, 0)
        else:
            per = own.shape[3] // 16
            blocks = units[a]

            def chunk_out(i, carry, base=base):
                finish(base + i)
                return carry

            lax.fori_loop(0, counts[a], chunk_out, 0)

            def unit_out(u, carry, a=a, base=base, blocks=blocks):
                at = pl.ds(pl.multiple_of((u // blocks) * LANES, LANES), LANES)
                rows_to = pl.ds(pl.multiple_of(lax.rem(u, blocks) * 16, 16), 16)
                rows_from = pl.ds(pl.multiple_of(lax.rem(u, per) * 16, 16), 16)
                outs[a][rows_to, at] = total(base + u // per, rows_from)
                return carry

            lax.fori_loop(0, counts[a] * per, unit_out, 0)
        base += counts[a]


def sum_scatter(pieces):
    peers = NZ * NY * NC
    height = min(p.shape[0] for p in pieces) // peers
    counts, units = [], []
    for p in pieces:
        rows = p.shape[0] // peers
        counts.append(rows * p.shape[1] // (height * LANES))
        units.append(None if rows == height else rows // 16)
    chunks = sum(counts)
    split = [p.reshape(NZ, NY, NC, p.shape[0] // peers, p.shape[1]) for p in pieces]
    half = (chunks, NZ, NY, height, LANES)
    fourth = (chunks, NZ, height, LANES)
    return pl.pallas_call(
        functools.partial(sum_scatter_kernel, tuple(counts), tuple(units)),
        in_specs=[pl.BlockSpec(memory_space=pl.ANY)] * len(pieces),
        out_specs=[pl.BlockSpec(memory_space=pltpu.VMEM)] * len(pieces),
        out_shape=[jax.ShapeDtypeStruct((p.shape[0] // peers, p.shape[1]), F32) for p in pieces],
        scratch_shapes=[
            pltpu.VMEM(half, BF),
            pltpu.VMEM(half, BF),
            pltpu.VMEM(fourth, BF),
            pltpu.VMEM(fourth, BF),
            pltpu.VMEM(fourth, BF),
        ]
        + [pltpu.SemaphoreType.DMA((chunks,))] * 9,
        compiler_params=pltpu.CompilerParams(
            collective_id=1, has_side_effects=True, vmem_limit_bytes=VMEM_LIMIT
        ),
    )(*split)


def low_half(rows):
    return lax.broadcasted_iota(jnp.int32, (rows, PAIR), 1) < HEAD


def masked_scores(q, k, qx, kx, head, causal):
    lo_q, lo_k = low_half(q.shape[0]), low_half(k.shape[0])
    if head == 0:
        qh, kh = jnp.where(lo_q, q, qx), jnp.where(lo_k, k, kx)
    else:
        qh, kh = jnp.where(lo_q, qx, q), jnp.where(lo_k, kx, k)
    s = mm(kh, qh, NT)
    if causal:
        key_at = lax.broadcasted_iota(jnp.int32, s.shape, 0)
        query_at = lax.broadcasted_iota(jnp.int32, s.shape, 1)
        s = jnp.where(key_at <= query_at, s, NEGATIVE)
    return s


def attn_fwd_kernel(q_ref, k_ref, v_ref, qx_ref, kx_ref, o_ref, lse_ref, *, causal):
    q, k, qx, kx = q_ref[0], k_ref[0], qx_ref[0], kx_ref[0]
    vt = v_ref[0].astype(F32).T.astype(BF)
    outs = []
    for head in range(2):
        s = masked_scores(q, k, qx, kx, head, causal)
        top = jnp.max(s, axis=0, keepdims=True)
        p = jnp.exp2((s - top) * (SCALE * LOG2E))
        total = jnp.sum(p, axis=0, keepdims=True)
        o = mm(vt[head * HEAD : (head + 1) * HEAD], p.astype(BF))
        outs.append(o / total)
        lse_ref[0, 0, head : head + 1, :] = top * (SCALE * LOG2E) + jnp.log2(total)
    o_ref[0] = jnp.concatenate(outs, axis=0).T.astype(BF)


def attn_bwd_kernel(
    q_ref, k_ref, v_ref, qx_ref, kx_ref, o_ref, do_ref, lse_ref, dq_ref, dk_ref, dv_ref, *, causal
):
    q, k, v, qx, kx = q_ref[0], k_ref[0], v_ref[0], qx_ref[0], kx_ref[0]
    do = do_ref[0]
    kt = k.astype(F32).T.astype(BF)
    spread = (do.astype(F32) * o_ref[0].astype(F32)).T
    lo_q, lo_k = low_half(q.shape[0]), low_half(k.shape[0])
    zero_q, zero_k = jnp.zeros_like(q), jnp.zeros_like(k)
    dqs, dk, dv = [], None, None
    for head in range(2):
        s = masked_scores(q, k, qx, kx, head, causal)
        p = jnp.exp2(s * (SCALE * LOG2E) - lse_ref[0, 0, head : head + 1, :])
        if head == 0:
            vh, doh, qh = (
                jnp.where(lo_k, v, zero_k),
                jnp.where(lo_q, do, zero_q),
                jnp.where(lo_q, q, zero_q),
            )
        else:
            vh, doh, qh = (
                jnp.where(lo_k, zero_k, v),
                jnp.where(lo_q, zero_q, do),
                jnp.where(lo_q, zero_q, q),
            )
        dp = mm(vh, do, NT)
        delta = jnp.sum(spread[head * HEAD : (head + 1) * HEAD], axis=0, keepdims=True)
        ds = (p * (dp - delta)).astype(BF)
        dv_part = mm(p.astype(BF), doh)
        dk_part = mm(ds, qh)
        dv = dv_part if dv is None else dv + dv_part
        dk = dk_part if dk is None else dk + dk_part
        dqs.append(mm(kt[head * HEAD : (head + 1) * HEAD], ds))
    dq_ref[0] = (jnp.concatenate(dqs, axis=0).T * SCALE).astype(BF)
    dk_ref[0] = (dk * SCALE).astype(BF)
    dv_ref[0] = dv.astype(BF)


def column_block(length, first):
    return pl.BlockSpec((1, length, PAIR), lambda r, p: (r, 0, first + p))


def whole_row(length):
    return pl.BlockSpec((1, length, PAIR), lambda r, p: (r, 0, 0))


def attention_forward(q_in, k_in, v_in, qx, kx, firsts, causal):
    rows, count_q, _ = q_in.shape
    count_k = k_in.shape[1]
    pairs = HEADS // 2
    return pl.pallas_call(
        functools.partial(attn_fwd_kernel, causal=causal),
        grid=(rows, pairs),
        in_specs=[
            column_block(count_q, firsts[0]),
            column_block(count_k, firsts[1]),
            column_block(count_k, firsts[2]),
            whole_row(count_q),
            whole_row(count_k),
        ],
        out_specs=[
            column_block(count_q, 0),
            pl.BlockSpec((1, 1, 2, count_q), lambda r, p: (r, p, 0, 0)),
        ],
        out_shape=[
            jax.ShapeDtypeStruct((rows, count_q, HEADS * HEAD), BF),
            jax.ShapeDtypeStruct((rows, pairs, 2, count_q), F32),
        ],
        compiler_params=pltpu.CompilerParams(vmem_limit_bytes=VMEM_LIMIT),
    )(q_in, k_in, v_in, qx, kx)


def attention_backward(q_in, k_in, v_in, qx, kx, firsts, mixed, grad_mixed, lse, causal):
    rows, count_q, _ = q_in.shape
    count_k = k_in.shape[1]
    pairs = HEADS // 2
    width = HEADS * HEAD
    return pl.pallas_call(
        functools.partial(attn_bwd_kernel, causal=causal),
        grid=(rows, pairs),
        in_specs=[
            column_block(count_q, firsts[0]),
            column_block(count_k, firsts[1]),
            column_block(count_k, firsts[2]),
            whole_row(count_q),
            whole_row(count_k),
            column_block(count_q, 0),
            column_block(count_q, 0),
            pl.BlockSpec((1, 1, 2, count_q), lambda r, p: (r, p, 0, 0)),
        ],
        out_specs=[
            column_block(count_q, 0),
            column_block(count_k, 0),
            column_block(count_k, 0),
        ],
        out_shape=[
            jax.ShapeDtypeStruct((rows, count_q, width), BF),
            jax.ShapeDtypeStruct((rows, count_k, width), BF),
            jax.ShapeDtypeStruct((rows, count_k, width), BF),
        ],
        compiler_params=pltpu.CompilerParams(vmem_limit_bytes=VMEM_LIMIT),
    )(q_in, k_in, v_in, qx, kx, mixed, grad_mixed, lse)


def segment_ids(lengths, span_len):
    seg_ends = jnp.cumsum(lengths, -1, dtype=jnp.int32)
    positions = jnp.arange(span_len, dtype=jnp.int32)
    return jnp.sum(
        (positions[None, :, None] >= seg_ends[:, None, :]).astype(jnp.int32), -1, dtype=jnp.int32
    )


def mask_lanes(seg, count):
    hit = seg[:, :, None] == jnp.arange(HEAD, dtype=jnp.int32)[None, None, :]
    member = hit.astype(BF)
    other = jnp.where(
        jnp.arange(HEAD, dtype=jnp.int32)[None, None, :] < count,
        jnp.where(hit, 0.0, NEGATIVE),
        0.0,
    ).astype(BF)
    return (
        jnp.concatenate([member, member], -1),
        jnp.concatenate([other, other], -1),
    )


def inverse_rms(v):
    return lax.rsqrt(jnp.mean(v * v, -1, keepdims=True) + EPSILON)


def norm(v, gain):
    return (v * inverse_rms(v) * gain).astype(BF)


def norm_back(v, gain, grad):
    inv = inverse_rms(v)
    scaled = grad * gain
    along = jnp.mean(scaled * v, -1, keepdims=True)
    return inv * scaled - v * (inv * inv * inv * along), jnp.sum(grad * v * inv, 0)


def gelu_parts(x):
    inner = GELU_C * (x + GELU_A * x * x * x)
    t = jnp.tanh(inner)
    value = 0.5 * x * (1.0 + t)
    slope = 0.5 * (1.0 + t) + 0.5 * x * (1.0 - t * t) * GELU_C * (1.0 + 3.0 * GELU_A * x * x)
    return value, slope


def ffn_forward(h, gain, w_in, w_out):
    m = norm(h, gain)
    u = mm(m, w_in)
    half = w_out.shape[0]
    value, _ = gelu_parts(u[:, :half])
    act = (value * u[:, half:]).astype(BF)
    return h + mm(act, w_out), (m, u.astype(BF), act)


def ffn_backward(h, gain, w_in, w_out, kept, grad):
    m, u, act = kept
    half = w_out.shape[0]
    branch = grad.astype(BF)
    d_act = mm(branch, w_out, NT)
    gate, up = u[:, :half].astype(F32), u[:, half:].astype(F32)
    value, slope = gelu_parts(gate)
    du = jnp.concatenate([d_act * up * slope, d_act * value], -1).astype(BF)
    dm = mm(du, w_in, NT)
    dh, dg = norm_back(h, gain, dm)
    return grad + dh, branch, du, dg


def shift(x, by):
    pairs = [(0, 1)] if by > 0 else [(1, 0)]
    return lax.ppermute(x, "section", pairs)


def body(
    section_input, enc_lengths, dec_lengths, attn_in, attn_out, ffn_in, ffn_out, cross_weight, gains
):
    wa, wo, wf, wd, wc = attn_in[0], attn_out[0], ffn_in[0], ffn_out[0], cross_weight[0]
    g0, g1, g2 = gains[0, 0], gains[0, 1], gains[0, 2]
    x_in = section_input[0]
    rows, le, dim = x_in.shape
    ld = le // 2
    width = wo.shape[0]
    docs = enc_lengths.shape[1]
    seg_enc = segment_ids(enc_lengths, le)
    seg_dec = segment_ids(dec_lengths, ld)
    enc_qx, enc_kx = mask_lanes(seg_enc, docs)
    dec_qx, dec_kx = mask_lanes(seg_dec, docs)
    on_decoder = lax.axis_index("section") == 1
    te, td = rows * le, rows * ld
    columns = width // PAIR
    own = (0, columns, 2 * columns)

    def self_forward(h, count, qx, kx, causal):
        n = norm(h, g0)
        packed = mm(n, wa).astype(BF)
        p3 = packed.reshape(rows, count, 3 * width)
        o, lse = attention_forward(p3, p3, p3, qx, kx, own, causal)
        o2 = o.reshape(rows * count, width)
        return h + mm(o2, wo), (n, packed, o, lse)

    def self_backward(h, count, qx, kx, causal, kept, grad):
        n, packed, o, lse = kept
        p3 = packed.reshape(rows, count, 3 * width)
        branch = grad.astype(BF)
        do = mm(branch, wo, NT).astype(BF).reshape(rows, count, width)
        dq, dk, dv = attention_backward(p3, p3, p3, qx, kx, own, o, do, lse, causal)
        dpacked = jnp.concatenate([dq, dk, dv], -1).reshape(rows * count, 3 * width)
        dn = mm(dpacked, wa, NT)
        dh, dg = norm_back(h, g0, dn)
        return grad + dh, branch, dpacked, dg

    def zeros(shape, dtype):
        return jnp.zeros(shape, dtype)

    def enc_first():
        h = x_in.reshape(te, dim).astype(F32)
        e1, (n, packed, o, lse) = self_forward(h, le, enc_qx, enc_kx, False)
        e2, (m, u, act) = ffn_forward(e1, g2, wf, wd)
        mem = norm(e2, g1)
        sent = mm(mem, wc).astype(BF)
        return (n, packed, o, lse, e1, m, u, act, e2, mem, sent, zeros((td, dim), BF))

    def dec_first():
        h = x_in[:, :ld].reshape(td, dim).astype(F32)
        d1, (n, packed, o, lse) = self_forward(h, ld, dec_qx, dec_kx, True)
        c = norm(d1, g1)
        cq = mm(c, wc[:, :width]).astype(BF)
        blank = jax.eval_shape(enc_first)

        def put(full, part):
            return lax.dynamic_update_slice(
                jnp.zeros(full.shape, full.dtype), part, (0,) * part.ndim
            )

        return (
            put(blank[0], n),
            put(blank[1], packed),
            put(blank[2], o),
            put(blank[3], lse),
            put(blank[4], d1),
            put(blank[5], c),
        ) + tuple(jnp.zeros(b.shape, b.dtype) for b in blank[6:11]) + (cq,)

    n, packed, o, lse, h1, m, u, act, e2, mem, sent, cq_out = lax.cond(
        on_decoder, dec_first, enc_first
    )
    cq = shift(cq_out, -1)

    def enc_cross():
        q3, s3 = cq.reshape(rows, ld, width), sent.reshape(rows, le, 2 * width)
        return tuple(
            attention_forward(q3, s3, s3, dec_qx, enc_kx, (0, 0, columns), False)
        )

    def dec_cross():
        return zeros((rows, ld, width), BF), zeros((rows, HEADS // 2, 2, ld), F32)

    oc_out, cross_lse = lax.cond(on_decoder, dec_cross, enc_cross)
    oc = shift(oc_out.reshape(td, width), 1)

    def enc_ffn():
        return (
            zeros((td, width), BF),
            zeros((td, dim), F32),
            zeros((td, dim), F32),
            zeros((td, dim), BF),
            zeros((td, wd.shape[0]), BF),
            zeros((td, dim), BF),
            zeros((td, wf.shape[1]), BF),
            zeros((td, dim), BF),
            zeros((dim,), F32),
        )

    def dec_ffn():
        d1 = h1[:td]
        d2 = d1 + mm(oc, wc[:, width:], NT)
        out, kept = ffn_forward(d2, g2, wf, wd)
        cot = x_in[:, ld:].reshape(td, dim).astype(F32)
        dd2, branch, du, dg = ffn_backward(d2, g2, wf, wd, kept, cot)
        cross_branch = dd2.astype(BF)
        doc = mm(cross_branch, wc[:, width:]).astype(BF)
        return doc, out, dd2, kept[0], kept[2], branch, du, cross_branch, dg

    doc_out, out, dd2, dec_m, dec_act, dec_branch, dec_du, cross_branch, dec_dg2 = lax.cond(
        on_decoder, dec_ffn, enc_ffn
    )
    doc = shift(doc_out, -1)

    def enc_cross_back():
        q3, s3 = cq.reshape(rows, ld, width), sent.reshape(rows, le, 2 * width)
        dq, dk, dv = attention_backward(
            q3, s3, s3, dec_qx, enc_kx, (0, 0, columns), oc_out,
            doc.reshape(rows, ld, width), cross_lse, False,
        )
        return dq, jnp.concatenate([dk, dv], -1).reshape(te, 2 * width)

    def dec_cross_back():
        return zeros((rows, ld, width), BF), zeros((te, 2 * width), BF)

    dcq_out, dsent = lax.cond(on_decoder, dec_cross_back, enc_cross_back)
    dcq = shift(dcq_out.reshape(td, width), 1)

    def enc_last():
        h = x_in.reshape(te, dim).astype(F32)
        dmem = mm(dsent, wc, NT)
        de2, dg1 = norm_back(e2, g1, dmem)
        de1, fbranch, du, dg2 = ffn_backward(h1, g2, wf, wd, (m, u, act), de2)
        dh, abranch, dpacked, dg0 = self_backward(
            h, le, enc_qx, enc_kx, False, (n, packed, o, lse), de1
        )
        return (
            dh.reshape(rows, le, dim),
            mm(n, dpacked, TN).astype(BF),
            mm(o.reshape(te, width), abranch, TN).astype(BF),
            mm(m, du, TN).astype(BF),
            mm(act, fbranch, TN).astype(BF),
            mm(mem, dsent, TN).astype(BF),
            jnp.stack([dg0, dg1, dg2]),
        )

    def dec_last():
        h = x_in[:, :ld].reshape(td, dim).astype(F32)
        d1, c = h1[:td], m[:td]
        dc = mm(dcq, wc[:, :width], NT)
        dd1_norm, dg1 = norm_back(d1, g1, dc)
        dd1 = dd2 + dd1_norm
        dn, dp, dox = n[:td], packed[:td], o[:, :ld]
        dlse = lse[..., :ld]
        dh, abranch, dpacked, dg0 = self_backward(
            h, ld, dec_qx, dec_kx, True, (dn, dp, dox, dlse), dd1
        )
        grad_cross = jnp.concatenate([mm(c, dcq, TN), mm(cross_branch, oc, TN)], -1)
        return (
            jnp.concatenate([out.reshape(rows, ld, dim), dh.reshape(rows, ld, dim)], 1),
            mm(dn, dpacked, TN).astype(BF),
            mm(dox.reshape(td, width), abranch, TN).astype(BF),
            mm(dec_m, dec_du, TN).astype(BF),
            mm(dec_act, dec_branch, TN).astype(BF),
            grad_cross.astype(BF),
            jnp.stack([dg0, dg1, dec_dg2]),
        )

    last = lax.cond(on_decoder, dec_last, enc_last)
    gain_terms = jnp.pad(last[6].T, ((0, 0), (0, LANES - last[6].shape[0]))).astype(BF)
    pieces = [last[1], last[2], last[3], last[5], gain_terms, last[4]]
    if lax.axis_size("rows") == NZ * NY * NC:
        sums = sum_scatter(pieces)
    else:
        sums = [
            lax.psum_scatter(piece, "rows", scatter_dimension=0, tiled=True).astype(F32)
            for piece in pieces
        ]
    s_in, s_out, s_fi, s_cross, s_gain, s_fo = sums
    return (
        last[0][None],
        s_in[None],
        s_out[None],
        s_fi[None],
        s_fo[None],
        s_cross[None],
        s_gain[:, : last[6].shape[0]].T[None],
    )


def solution(mesh):
    placed = (
        P("section", "rows", None, None),
        P("rows", None),
        P("rows", None),
    ) + (P("section", None, None),) * 6
    return jax.shard_map(
        body,
        mesh=mesh,
        in_specs=placed,
        out_specs=(
            P("section", "rows", None, None),
            P("section", "rows", None),
            P("section", "rows", None),
            P("section", "rows", None),
            P("section", "rows", None),
            P("section", "rows", None),
            P("section", None, "rows"),
        ),
        check_vma=False,
    )
```

```python
import functools

import jax
import jax.numpy as jnp
from jax import lax
from jax.experimental import pallas as pl
from jax.experimental.pallas import tpu as pltpu
from jax.sharding import PartitionSpec as P

HEADS = 12
HEAD = 64
PAIR = 128
EPSILON = 1e-06
SCALE = 0.125
LOG2E = 1.4426950408889634
NEGATIVE = -1e30
GELU_C = 0.7978845608028654
GELU_A = 0.044715

BF = jnp.bfloat16
F32 = jnp.float32
NT = (((1,), (1,)), ((), ()))
NN = (((1,), (0,)), ((), ()))
TN = (((0,), (0,)), ((), ()))


def mm(a, b, dims=NN):
    return lax.dot_general(a, b, dims, preferred_element_type=F32)


MESH = pl.DeviceIdType.MESH
LANES = 256
VMEM_LIMIT = 56 * 1024 * 1024

NZ, NY, NC = 4, 2, 2
Y_LAG = 2


def sum_scatter_kernel(counts, units, *refs):
    arrays = len(counts)
    ins, outs = refs[:arrays], refs[arrays : 2 * arrays]
    (own, got_core, got_y, got_r, got_l, s_local, s_core, r_core, s_y, r_y, s_r, r_r, s_l, r_l) = refs[
        2 * arrays :
    ]
    chunks = own.shape[0]
    sec, me = lax.axis_index("section"), lax.axis_index("rows")
    core, y, z = lax.rem(me, 2), lax.rem(me // 2, 2), me // 4
    by_core, by_y = me + 1 - 2 * core, me + 2 - 4 * y
    other, away = 1 - core, 1 - y

    barrier = pltpu.get_barrier_semaphore()

    def greet(peer):
        pl.semaphore_signal(barrier, inc=1, device_id=(sec, peer), device_id_type=MESH)

    greet(by_core)
    greet(by_y)

    @pl.when(z > 0)
    def _():
        greet(me - 4)

    @pl.when(z < NZ - 1)
    def _():
        greet(me + 4)

    @pl.when((z > 0) & (z < NZ - 1))
    def _():
        pl.semaphore_wait(barrier, 4)

    @pl.when((z == 0) | (z == NZ - 1))
    def _():
        pl.semaphore_wait(barrier, 3)

    def feed(src, dst_rows, chunk):
        pltpu.make_async_remote_copy(
            src_ref=src(other),
            dst_ref=got_core.at[chunk, :, :, dst_rows],
            send_sem=s_core.at[chunk],
            recv_sem=r_core.at[chunk],
            device_id=(sec, by_core),
            device_id_type=MESH,
        ).start()
        pltpu.make_async_copy(src(core), own.at[chunk, :, :, dst_rows], s_local.at[chunk]).start()

    base = 0
    for a in range(arrays):
        if units[a] is None:

            def panel(i, carry, a=a, base=base):
                at = pl.ds(pl.multiple_of(i * LANES, LANES), LANES)
                feed(lambda c: ins[a].at[:, :, c, :, at], pl.ds(0, own.shape[3]), base + i)
                return carry

            lax.fori_loop(0, counts[a], panel, 0)
        else:
            per = own.shape[3] // 16
            blocks = units[a]

            def unit(u, carry, a=a, base=base, blocks=blocks):
                at = pl.ds(pl.multiple_of((u // blocks) * LANES, LANES), LANES)
                rows_from = pl.ds(pl.multiple_of(lax.rem(u, blocks) * 16, 16), 16)
                rows_to = pl.ds(pl.multiple_of(lax.rem(u, per) * 16, 16), 16)
                feed(lambda c: ins[a].at[:, :, c, rows_from, at], rows_to, base + u // per)
                return carry

            lax.fori_loop(0, counts[a] * per, unit, 0)
        base += counts[a]

    def to_core(j):
        return pltpu.make_async_remote_copy(
            src_ref=got_core.at[j],
            dst_ref=got_core.at[j],
            send_sem=s_core.at[j],
            recv_sem=r_core.at[j],
            device_id=(sec, by_core),
            device_id_type=MESH,
        )

    def to_y(j):
        return pltpu.make_async_remote_copy(
            src_ref=own.at[j, :, away],
            dst_ref=got_y.at[j],
            send_sem=s_y.at[j],
            recv_sem=r_y.at[j],
            device_id=(sec, by_y),
            device_id_type=MESH,
        )

    def to_right(j, at):
        return pltpu.make_async_remote_copy(
            src_ref=own.at[j, pl.ds(at + 1, NZ - 1 - at), y],
            dst_ref=got_r.at[j, pl.ds(at + 1, NZ - 1 - at)],
            send_sem=s_r.at[j],
            recv_sem=r_r.at[j],
            device_id=(sec, me + 4),
            device_id_type=MESH,
        )

    def to_left(j, at):
        return pltpu.make_async_remote_copy(
            src_ref=own.at[j, pl.ds(0, at), y],
            dst_ref=got_l.at[j, pl.ds(0, at)],
            send_sem=s_l.at[j],
            recv_sem=r_l.at[j],
            device_id=(sec, me - 4),
            device_id_type=MESH,
        )

    def add_into(dst, src):
        dst[...] = (dst[...].astype(F32) + src[...].astype(F32)).astype(BF)

    def step(s, carry):
        @pl.when(s < chunks)
        def _():
            pltpu.make_async_copy(got_core.at[s], own.at[s], s_local.at[s]).wait()
            to_core(s).wait_recv()
            add_into(own.at[s], got_core.at[s])
            to_y(s).start()

        j_y = s - Y_LAG

        @pl.when((j_y >= 0) & (j_y < chunks))
        def _():
            to_y(j_y).wait_recv()
            for t in range(NZ):
                add_into(own.at[j_y, t, y], got_y.at[j_y, t])

        for at in range(NZ - 1):
            j_r = s - Y_LAG - at

            @pl.when((z == at) & (j_r >= 0) & (j_r < chunks))
            def _(at=at, j_r=j_r):
                if at > 0:
                    to_right(j_r, at - 1).wait_recv()
                    for t in range(at + 1, NZ):
                        add_into(own.at[j_r, t, y], got_r.at[j_r, t])
                to_right(j_r, at).start()

        for at in range(1, NZ):
            j_l = s - Y_LAG - (NZ - 1 - at)

            @pl.when((z == at) & (j_l >= 0) & (j_l < chunks))
            def _(at=at, j_l=j_l):
                if at < NZ - 1:
                    to_left(j_l, at + 1).wait_recv()
                    for t in range(at):
                        add_into(own.at[j_l, t, y], got_l.at[j_l, t])
                to_left(j_l, at).start()

        return carry

    lax.fori_loop(0, chunks + Y_LAG + NZ - 1, step, 0)

    def finish(j):
        for at in range(NZ):

            @pl.when(z == at)
            def _(at=at):
                if at == NZ - 1:
                    to_right(j, at - 1).wait_recv()
                if at == 0:
                    to_left(j, 1).wait_recv()
                to_y(j).wait_send()
                to_core(j).wait_send()
                if at < NZ - 1:
                    to_right(j, at).wait_send()
                if at > 0:
                    to_left(j, at).wait_send()

    def total(j, rows):
        mine = own[j, z, y, rows].astype(F32)
        right = got_r[j, z, rows].astype(F32)
        left = got_l[j, z, rows].astype(F32)
        return mine + jnp.where(z > 0, right, 0.0) + jnp.where(z < NZ - 1, left, 0.0)

    base = 0
    for a in range(arrays):
        if units[a] is None:

            def panel_out(i, carry, a=a, base=base):
                finish(base + i)
                at = pl.ds(pl.multiple_of(i * LANES, LANES), LANES)
                outs[a][:, at] = total(base + i, pl.ds(0, own.shape[3]))
                return carry

            lax.fori_loop(0, counts[a], panel_out, 0)
        else:
            per = own.shape[3] // 16
            blocks = units[a]

            def chunk_out(i, carry, base=base):
                finish(base + i)
                return carry

            lax.fori_loop(0, counts[a], chunk_out, 0)

            def unit_out(u, carry, a=a, base=base, blocks=blocks):
                at = pl.ds(pl.multiple_of((u // blocks) * LANES, LANES), LANES)
                rows_to = pl.ds(pl.multiple_of(lax.rem(u, blocks) * 16, 16), 16)
                rows_from = pl.ds(pl.multiple_of(lax.rem(u, per) * 16, 16), 16)
                outs[a][rows_to, at] = total(base + u // per, rows_from)
                return carry

            lax.fori_loop(0, counts[a] * per, unit_out, 0)
        base += counts[a]


def sum_scatter(pieces):
    peers = NZ * NY * NC
    height = min(p.shape[0] for p in pieces) // peers
    counts, units = [], []
    for p in pieces:
        rows = p.shape[0] // peers
        counts.append(rows * p.shape[1] // (height * LANES))
        units.append(None if rows == height else rows // 16)
    chunks = sum(counts)
    split = [p.reshape(NZ, NY, NC, p.shape[0] // peers, p.shape[1]) for p in pieces]
    half = (chunks, NZ, NY, height, LANES)
    fourth = (chunks, NZ, height, LANES)
    return pl.pallas_call(
        functools.partial(sum_scatter_kernel, tuple(counts), tuple(units)),
        in_specs=[pl.BlockSpec(memory_space=pl.ANY)] * len(pieces),
        out_specs=[pl.BlockSpec(memory_space=pltpu.VMEM)] * len(pieces),
        out_shape=[jax.ShapeDtypeStruct((p.shape[0] // peers, p.shape[1]), F32) for p in pieces],
        scratch_shapes=[
            pltpu.VMEM(half, BF),
            pltpu.VMEM(half, BF),
            pltpu.VMEM(fourth, BF),
            pltpu.VMEM(fourth, BF),
            pltpu.VMEM(fourth, BF),
        ]
        + [pltpu.SemaphoreType.DMA((chunks,))] * 9,
        compiler_params=pltpu.CompilerParams(
            collective_id=1, has_side_effects=True, vmem_limit_bytes=VMEM_LIMIT
        ),
    )(*split)


def low_half(rows):
    return lax.broadcasted_iota(jnp.int32, (rows, PAIR), 1) < HEAD


def masked_scores(q, k, qx, kx, head, causal):
    lo_q, lo_k = low_half(q.shape[0]), low_half(k.shape[0])
    if head == 0:
        qh, kh = jnp.where(lo_q, q, qx), jnp.where(lo_k, k, kx)
    else:
        qh, kh = jnp.where(lo_q, qx, q), jnp.where(lo_k, kx, k)
    s = mm(kh, qh, NT)
    if causal:
        key_at = lax.broadcasted_iota(jnp.int32, s.shape, 0)
        query_at = lax.broadcasted_iota(jnp.int32, s.shape, 1)
        s = jnp.where(key_at <= query_at, s, NEGATIVE)
    return s


def attn_fwd_kernel(q_ref, k_ref, v_ref, qx_ref, kx_ref, o_ref, lse_ref, *, causal):
    q, k, qx, kx = q_ref[...], k_ref[...], qx_ref[0], kx_ref[0]
    vt = v_ref[...].astype(F32).T.astype(BF)
    outs = []
    for head in range(2):
        s = masked_scores(q, k, qx, kx, head, causal)
        top = jnp.max(s, axis=0, keepdims=True)
        p = jnp.exp2((s - top) * (SCALE * LOG2E))
        total = jnp.sum(p, axis=0, keepdims=True)
        o = mm(vt[head * HEAD : (head + 1) * HEAD], p.astype(BF))
        outs.append(o / total)
        lse_ref[0, head : head + 1, :] = top * (SCALE * LOG2E) + jnp.log2(total)
    o_ref[...] = jnp.concatenate(outs, axis=0).T.astype(BF)


def attn_bwd_kernel(
    q_ref, k_ref, v_ref, qx_ref, kx_ref, o_ref, do_ref, lse_ref, dq_ref, dk_ref, dv_ref, *, causal
):
    q, k, v, qx, kx = q_ref[...], k_ref[...], v_ref[...], qx_ref[0], kx_ref[0]
    do = do_ref[...]
    kt = k.astype(F32).T.astype(BF)
    spread = (do.astype(F32) * o_ref[...].astype(F32)).T
    lo_q, lo_k = low_half(q.shape[0]), low_half(k.shape[0])
    zero_q, zero_k = jnp.zeros_like(q), jnp.zeros_like(k)
    dqs, dk, dv = [], None, None
    for head in range(2):
        s = masked_scores(q, k, qx, kx, head, causal)
        p = jnp.exp2(s * (SCALE * LOG2E) - lse_ref[0, head : head + 1, :])
        if head == 0:
            vh, doh, qh = (
                jnp.where(lo_k, v, zero_k),
                jnp.where(lo_q, do, zero_q),
                jnp.where(lo_q, q, zero_q),
            )
        else:
            vh, doh, qh = (
                jnp.where(lo_k, zero_k, v),
                jnp.where(lo_q, zero_q, do),
                jnp.where(lo_q, zero_q, q),
            )
        dp = mm(vh, do, NT)
        delta = jnp.sum(spread[head * HEAD : (head + 1) * HEAD], axis=0, keepdims=True)
        ds = (p * (dp - delta)).astype(BF)
        dv_part = mm(p.astype(BF), doh)
        dk_part = mm(ds, qh)
        dv = dv_part if dv is None else dv + dv_part
        dk = dk_part if dk is None else dk + dk_part
        dqs.append(mm(kt[head * HEAD : (head + 1) * HEAD], ds))
    dq_ref[...] = (jnp.concatenate(dqs, axis=0).T * SCALE).astype(BF)
    dk_ref[...] = (dk * SCALE).astype(BF)
    dv_ref[...] = dv.astype(BF)


def column_block(length, first):
    return pl.BlockSpec((length, PAIR), lambda p: (0, first + p))


def mask_block(length, row):
    return pl.BlockSpec((1, length, PAIR), lambda p: (row, 0, 0))


def pair_block(count_q):
    return pl.BlockSpec((1, 2, count_q), lambda p: (p, 0, 0))


def params(**more):
    return pltpu.CompilerParams(vmem_limit_bytes=VMEM_LIMIT, **more)


def attention_forward(q_in, k_in, v_in, qx, kx, row, firsts, causal):
    count_q, count_k, pairs = q_in.shape[0], k_in.shape[0], HEADS // 2
    return pl.pallas_call(
        functools.partial(attn_fwd_kernel, causal=causal),
        grid=(pairs,),
        in_specs=[
            column_block(count_q, firsts[0]),
            column_block(count_k, firsts[1]),
            column_block(count_k, firsts[2]),
            mask_block(count_q, row),
            mask_block(count_k, row),
        ],
        out_specs=[column_block(count_q, 0), pair_block(count_q)],
        out_shape=[
            jax.ShapeDtypeStruct((count_q, HEADS * HEAD), BF),
            jax.ShapeDtypeStruct((pairs, 2, count_q), F32),
        ],
        compiler_params=params(),
    )(q_in, k_in, v_in, qx, kx)


def attention_backward(q_in, k_in, v_in, qx, kx, row, firsts, mixed, grad_mixed, lse, causal):
    count_q, count_k, pairs = q_in.shape[0], k_in.shape[0], HEADS // 2
    width = HEADS * HEAD
    return pl.pallas_call(
        functools.partial(attn_bwd_kernel, causal=causal),
        grid=(pairs,),
        in_specs=[
            column_block(count_q, firsts[0]),
            column_block(count_k, firsts[1]),
            column_block(count_k, firsts[2]),
            mask_block(count_q, row),
            mask_block(count_k, row),
            column_block(count_q, 0),
            column_block(count_q, 0),
            pair_block(count_q),
        ],
        out_specs=[
            column_block(count_q, 0),
            column_block(count_k, 0),
            column_block(count_k, 0),
        ],
        out_shape=[
            jax.ShapeDtypeStruct((count_q, width), BF),
            jax.ShapeDtypeStruct((count_k, width), BF),
            jax.ShapeDtypeStruct((count_k, width), BF),
        ],
        compiler_params=params(),
    )(q_in, k_in, v_in, qx, kx, mixed, grad_mixed, lse)


BLOCK = 256
SLICE = 512


def inverse_rms(v):
    return lax.rsqrt(jnp.mean(v * v, -1, keepdims=True) + EPSILON)


def norm(v, gain):
    return (v * inverse_rms(v) * gain).astype(BF)


def norm_back(v, gain, grad):
    inv = inverse_rms(v)
    scaled = grad * gain
    along = jnp.mean(scaled * v, -1, keepdims=True)
    return (
        inv * scaled - v * (inv * inv * inv * along),
        jnp.sum(grad * v * inv, 0, keepdims=True),
    )


def gelu(x):
    return 0.5 * x * (1.0 + jnp.tanh(GELU_C * (x + GELU_A * x * x * x)))


def gelu_parts(x):
    square = x * x
    t = jnp.tanh(GELU_C * x * (1.0 + GELU_A * square))
    half = 0.5 * (1.0 + t)
    slope = half + 0.5 * x * (1.0 - t * t) * (GELU_C * (1.0 + 3.0 * GELU_A * square))
    return x * half, slope


class Fetch:
    def __init__(self, sources, held, sems):
        self.copies = [
            pltpu.make_async_copy(src, dst, sems.at[i])
            for i, (src, dst) in enumerate(zip(sources, held))
        ]
        self.held = held
        self.first = pl.program_id(0) == 0

        @pl.when(self.first)
        def _():
            for copy in self.copies:
                copy.start()

    def __getitem__(self, i):
        @pl.when(self.first)
        def _():
            self.copies[i].wait()

        return self.held[i]


def add_gain(ref, part):
    @pl.when(pl.program_id(0) == 0)
    def _():
        ref[...] = part

    @pl.when(pl.program_id(0) > 0)
    def _():
        ref[...] += part


def block_call(kernel, steps, ins, weights, outs, gain_outs=0):
    specs, arrays = [], []
    for array, row, first in ins:
        columns = array.shape[-1]
        if row is None:
            specs.append(pl.BlockSpec((BLOCK, columns), lambda i, f=first: (f + i, 0)))
        else:
            specs.append(
                pl.BlockSpec((None, BLOCK, columns), lambda i, r=row, f=first: (r, f + i, 0))
            )
        arrays.append(array)
    gains = [w for w in weights if w.dtype == F32]
    mats = [w for w in weights if w.dtype != F32]
    specs += [pl.BlockSpec((1, g.shape[1]), lambda i: (0, 0)) for g in gains]
    specs += [pl.BlockSpec(memory_space=pl.ANY)] * len(mats)
    dim = gains[0].shape[1]
    count = len(mats)

    def run(*refs):
        held, sems = refs[-1 - count : -1], refs[-1]
        at = len(arrays) + len(gains)
        fetch = Fetch(refs[at : at + count], held, sems)
        kernel(refs[: len(arrays)], [g[...] for g in refs[len(arrays) : at]], fetch, refs[at + count : -1 - count])

    return pl.pallas_call(
        run,
        grid=(steps,),
        in_specs=specs,
        out_specs=[pl.BlockSpec((BLOCK, c), lambda i: (i, 0)) for c, _ in outs]
        + [pl.BlockSpec((1, dim), lambda i: (0, 0))] * gain_outs,
        out_shape=[jax.ShapeDtypeStruct((steps * BLOCK, c), t) for c, t in outs]
        + [jax.ShapeDtypeStruct((1, dim), F32)] * gain_outs,
        scratch_shapes=[pltpu.VMEM(m.shape, m.dtype) for m in mats]
        + [pltpu.SemaphoreType.DMA((count,))],
        compiler_params=params(),
    )(*arrays, *gains, *mats)


def project_kernel(ins, gains, w, outs):
    (x,), (g0,), (n_ref, packed_ref) = ins, gains, outs
    n = norm(x[...].astype(F32), g0)
    n_ref[...] = n
    wa = w[0]
    dim = x.shape[1]
    for at in range(0, wa.shape[1], dim):
        packed_ref[:, at : at + dim] = mm(n, wa[:, at : at + dim]).astype(BF)


def ffn_up(m, wf, wd, acc, u_ref, act_ref):
    half = wd.shape[0]
    for at in range(0, half, SLICE):
        gate = mm(m, wf[:, at : at + SLICE])
        up = mm(m, wf[:, half + at : half + at + SLICE])
        u_ref[:, at : at + SLICE] = gate.astype(BF)
        u_ref[:, half + at : half + at + SLICE] = up.astype(BF)
        act = (gelu(gate) * up).astype(BF)
        if act_ref is not None:
            act_ref[:, at : at + SLICE] = act
        acc = acc + mm(act, wd[at : at + SLICE, :])
    return acc


def ffn_down(branch, wf, wd, u_ref, du_ref, act_ref):
    half = wd.shape[0]
    dm = None
    for at in range(0, half, SLICE):
        d_act = mm(branch, wd[at : at + SLICE, :], NT)
        gate = u_ref[:, at : at + SLICE].astype(F32)
        up = u_ref[:, half + at : half + at + SLICE].astype(F32)
        value, slope = gelu_parts(gate)
        if act_ref is not None:
            act_ref[:, at : at + SLICE] = (value * up).astype(BF)
        d_gate = (d_act * up * slope).astype(BF)
        d_up = (d_act * value).astype(BF)
        du_ref[:, at : at + SLICE] = d_gate
        du_ref[:, half + at : half + at + SLICE] = d_up
        part = mm(d_gate, wf[:, at : at + SLICE], NT) + mm(
            d_up, wf[:, half + at : half + at + SLICE], NT
        )
        dm = part if dm is None else dm + part
    return dm


def enc_rest_kernel(ins, gains, w, outs):
    (o, x), (g1, g2) = ins, gains
    e1_ref, u_ref, e2_ref, sent_ref = outs
    e1 = x[...].astype(F32) + mm(o[...], w[0][...])
    e1_ref[...] = e1
    e2 = ffn_up(norm(e1, g2), w[1], w[2], e1, u_ref, None)
    e2_ref[...] = e2
    sent_ref[...] = mm(norm(e2, g1), w[3][...]).astype(BF)


def dec_query_kernel(ins, gains, w, outs):
    (o, x), (g1,), (d1_ref, c_ref, cq_ref) = ins, gains, outs
    d1 = x[...].astype(F32) + mm(o[...], w[0][...])
    d1_ref[...] = d1
    c = norm(d1, g1)
    c_ref[...] = c
    cq_ref[...] = mm(c, w[1][:, : c.shape[1]]).astype(BF)


def dec_ffn_kernel(ins, gains, w, outs):
    (oc, d1, cot), (g2,) = ins, gains
    doc_ref, out_ref, dd2_ref, m_ref, act_ref, du_ref, branch_ref, u_ref, dg2_ref = outs
    width = oc.shape[1]
    out_proj = w[0]
    d2 = d1[...] + mm(oc[...], out_proj[:, width:], NT)
    m = norm(d2, g2)
    m_ref[...] = m
    wf, wd = w[1], w[2]
    out_ref[...] = ffn_up(m, wf, wd, d2, u_ref, act_ref)
    dm = ffn_down(cot[...], wf, wd, u_ref, du_ref, None)
    back, dg2 = norm_back(d2, g2, dm)
    dd2 = cot[...].astype(F32) + back
    dd2_ref[...] = dd2
    branch = dd2.astype(BF)
    branch_ref[...] = branch
    doc_ref[...] = mm(branch, out_proj[:, width:]).astype(BF)
    add_gain(dg2_ref, dg2)


def enc_back_kernel(ins, gains, w, outs):
    (dk, dv, e1_in, e2_in, u), (g1, g2) = ins, gains
    mem_ref, fb_ref, m_ref, act_ref, du_ref, de1_ref, ab_ref, do_ref, dg1_ref, dg2_ref = outs
    wc = w[0]
    width = dk.shape[1]
    e1, e2 = e1_in[...], e2_in[...]
    dmem = mm(dk[...], wc[:, :width], NT) + mm(dv[...], wc[:, width:], NT)
    mem_ref[...] = norm(e2, g1)
    de2, dg1 = norm_back(e2, g1, dmem)
    fb = de2.astype(BF)
    fb_ref[...] = fb
    m_ref[...] = norm(e1, g2)
    wd, wf = w[1], w[2]
    dm = ffn_down(fb, wf, wd, u, du_ref, act_ref)
    back, dg2 = norm_back(e1, g2, dm)
    de1 = de2 + back
    de1_ref[...] = de1
    ab = de1.astype(BF)
    ab_ref[...] = ab
    do_ref[...] = mm(ab, w[3][...], NT).astype(BF)
    add_gain(dg1_ref, dg1)
    add_gain(dg2_ref, dg2)


def dec_back_kernel(ins, gains, w, outs):
    (dcq, d1_in, dd2), (g1,), (dd1_ref, ab_ref, do_ref, dg1_ref) = ins, gains, outs
    d1 = d1_in[...]
    dc = mm(dcq[...], w[0][:, : dcq.shape[1]], NT)
    back, dg1 = norm_back(d1, g1, dc)
    dd1 = dd2[...] + back
    dd1_ref[...] = dd1
    ab = dd1.astype(BF)
    ab_ref[...] = ab
    do_ref[...] = mm(ab, w[1][...], NT).astype(BF)
    add_gain(dg1_ref, dg1)


def input_grad_kernel(ins, gains, w, outs):
    (dq, dk, dv, x, grad), (g0,), (dx_ref, dg0_ref) = ins, gains, outs
    wa = w[0]
    width = dq.shape[1]
    dn = (
        mm(dq[...], wa[:, :width], NT)
        + mm(dk[...], wa[:, width : 2 * width], NT)
        + mm(dv[...], wa[:, 2 * width :], NT)
    )
    back, dg0 = norm_back(x[...].astype(F32), g0, dn)
    dx_ref[...] = grad[...] + back
    add_gain(dg0_ref, dg0)


def nothing_kernel(*refs):
    pass


def unwritten(shapes):
    return pl.pallas_call(
        nothing_kernel,
        out_specs=[pl.BlockSpec(memory_space=pl.ANY)] * len(shapes),
        out_shape=[jax.ShapeDtypeStruct(s.shape, s.dtype) for s in shapes],
    )()


def by_section(on_decoder, encoder, decoder):
    enc_shapes = jax.eval_shape(encoder) if encoder else []
    dec_shapes = jax.eval_shape(decoder) if decoder else []
    none = lambda: []
    encoder, decoder = encoder or none, decoder or none
    pool = lambda shapes: list(unwritten(shapes)) if shapes else []
    both = lax.cond(
        on_decoder,
        lambda: pool(enc_shapes) + list(decoder()),
        lambda: list(encoder()) + pool(dec_shapes),
    )
    return both[: len(enc_shapes)], both[len(enc_shapes) :]


def segment_ids(lengths, span_len):
    seg_ends = jnp.cumsum(lengths, -1, dtype=jnp.int32)
    positions = jnp.arange(span_len, dtype=jnp.int32)
    return jnp.sum(
        (positions[None, :, None] >= seg_ends[:, None, :]).astype(jnp.int32), -1, dtype=jnp.int32
    )


def mask_lanes(seg, count):
    hit = seg[:, :, None] == jnp.arange(HEAD, dtype=jnp.int32)[None, None, :]
    member = hit.astype(BF)
    other = jnp.where(
        jnp.arange(HEAD, dtype=jnp.int32)[None, None, :] < count,
        jnp.where(hit, 0.0, NEGATIVE),
        0.0,
    ).astype(BF)
    return (
        jnp.concatenate([member, member], -1),
        jnp.concatenate([other, other], -1),
    )


def shift(x, by):
    pairs = [(0, 1)] if by > 0 else [(1, 0)]
    return lax.ppermute(x, "section", pairs)


def body(
    section_input, enc_lengths, dec_lengths, attn_in, attn_out, ffn_in, ffn_out, cross_weight, gains
):
    wa, wo, wf, wd, wc = attn_in[0], attn_out[0], ffn_in[0], ffn_out[0], cross_weight[0]
    g0, g1, g2 = gains[0, 0:1], gains[0, 1:2], gains[0, 2:3]
    x_in = section_input[0]
    rows, le, dim = x_in.shape
    ld = le // 2
    width = wo.shape[0]
    docs = enc_lengths.shape[1]
    enc_qx, enc_kx = mask_lanes(segment_ids(enc_lengths, le), docs)
    dec_qx, dec_kx = mask_lanes(segment_ids(dec_lengths, ld), docs)
    on_decoder = lax.axis_index("section") == 1
    steps_e, steps_d = le // BLOCK, ld // BLOCK
    columns = width // PAIR
    own = (0, columns, 2 * columns)
    across = (0, 0, columns)
    inner = wf.shape[1]

    def project(r, steps):
        return list(
            block_call(project_kernel, steps, [(x_in, r, 0)], [g0, wa], [(dim, BF), (3 * width, BF)])
        )

    def enc_first(r):
        n, packed = project(r, steps_e)
        o, lse = attention_forward(packed, packed, packed, enc_qx, enc_kx, r, own, False)
        return [n, packed, o, lse]

    def enc_rest(r, o):
        return list(
            block_call(
                enc_rest_kernel,
                steps_e,
                [(o, None, 0), (x_in, r, 0)],
                [g1, g2, wo, wf, wd, wc],
                [(dim, F32), (inner, BF), (dim, F32), (2 * width, BF)],
            )
        )

    def dec_first(r):
        n, packed = project(r, steps_d)
        o, lse = attention_forward(packed, packed, packed, dec_qx, dec_kx, r, own, True)
        d1, c, cq = block_call(
            dec_query_kernel,
            steps_d,
            [(o, None, 0), (x_in, r, 0)],
            [g1, wo, wc],
            [(dim, F32), (dim, BF), (width, BF)],
        )
        return [n, packed, o, lse, d1, c, cq]

    def cross(r, cq, sent):
        return list(attention_forward(cq, sent, sent, dec_qx, enc_kx, r, across, False))

    def dec_ffn(r, oc, d1):
        return list(
            block_call(
                dec_ffn_kernel,
                steps_d,
                [(oc, None, 0), (d1, None, 0), (x_in, r, ld // BLOCK)],
                [g2, wc, wf, wd],
                [
                    (width, BF),
                    (dim, F32),
                    (dim, F32),
                    (dim, BF),
                    (wd.shape[0], BF),
                    (inner, BF),
                    (dim, BF),
                    (inner, BF),
                ],
                1,
            )
        )

    def cross_back(r, cq, sent, oc, doc, lse):
        return list(
            attention_backward(cq, sent, sent, dec_qx, enc_kx, r, across, oc, doc, lse, False)
        )

    def enc_back(dk, dv, e1, e2, u):
        return list(
            block_call(
                enc_back_kernel,
                steps_e,
                [(dk, None, 0), (dv, None, 0), (e1, None, 0), (e2, None, 0), (u, None, 0)],
                [g1, g2, wc, wd, wf, wo],
                [
                    (dim, BF),
                    (dim, BF),
                    (dim, BF),
                    (wd.shape[0], BF),
                    (inner, BF),
                    (dim, F32),
                    (dim, BF),
                    (width, BF),
                ],
                2,
            )
        )

    def self_back(r, steps, masks, causal, packed, o, lse, do, grad):
        dq, dk, dv = attention_backward(
            packed, packed, packed, *masks, r, own, o, do, lse, causal
        )
        dx, dg0 = block_call(
            input_grad_kernel,
            steps,
            [(dq, None, 0), (dk, None, 0), (dv, None, 0), (x_in, r, 0), (grad, None, 0)],
            [g0, wa],
            [(dim, F32)],
            1,
        )
        return [dq, dk, dv, dx, dg0]

    def dec_back(dcq, d1, dd2):
        return list(
            block_call(
                dec_back_kernel,
                steps_d,
                [(dcq, None, 0), (d1, None, 0), (dd2, None, 0)],
                [g1, wc, wo],
                [(dim, F32), (dim, BF), (width, BF)],
                1,
            )
        )

    def run(encoder, decoder):
        return by_section(on_decoder, encoder, decoder)

    def after(value, *others):
        return lax.optimization_barrier((value,) + others)[0]

    every = range(rows)
    first, rest, dfirst, cqs = [None] * rows, [None] * rows, [None] * rows, [None] * rows
    crossed, ocs, mids, docs_in = [None] * rows, [None] * rows, [None] * rows, [None] * rows
    cross_b, dcqs, back, last = [None] * rows, [None] * rows, [None] * rows, [None] * rows
    dback, dlast = [None] * rows, [None] * rows

    first[0], dfirst[0] = run(lambda: enc_first(0), lambda: dec_first(0))
    cqs[0] = shift(dfirst[0][6], -1)
    rest[0], more = run(
        lambda: enc_rest(0, first[0][2]),
        lambda: [v for r in every[1:] for v in dec_first(r)],
    )
    for r in every[1:]:
        dfirst[r] = more[7 * (r - 1) : 7 * r]
        cqs[r] = shift(dfirst[r][6], -1)
    for r in every:
        if r > 0:
            first[r], _ = run(lambda: enc_first(r), None)
            rest[r], _ = run(lambda: enc_rest(r, first[r][2]), None)
        crossed[r], mid = run(
            lambda: cross(r, cqs[r], rest[r][3]),
            (lambda: dec_ffn(r - 1, ocs[r - 1], dfirst[r - 1][4])) if r > 0 else None,
        )
        if r > 0:
            mids[r - 1] = mid
            docs_in[r - 1] = shift(mid[0], -1)
        ocs[r] = shift(crossed[r][0], 1)
    for r in every:
        cross_b[r], _ = run(
            lambda: cross_back(r, cqs[r], rest[r][3], crossed[r][0], docs_in[r], crossed[r][1]),
            None,
        )
        dcqs[r] = shift(cross_b[r][0], 1)
        back[r], mid = run(
            lambda: enc_back(cross_b[r][1], cross_b[r][2], rest[r][0], rest[r][2], rest[r][1]),
            (lambda: dec_ffn(rows - 1, ocs[rows - 1], dfirst[rows - 1][4])) if r == 0 else None,
        )
        if r == 0:
            mids[rows - 1] = mid
            docs_in[rows - 1] = shift(mid[0], -1)

        def dec_last(r):
            p = dback[r] = dec_back(dcqs[r], dfirst[r][4], mids[r][2])
            n, packed, o, lse = dfirst[r][:4]
            return p + self_back(r, steps_d, (dec_qx, dec_kx), True, packed, o, lse, p[2], p[0])

        last[r], dlast[r] = run(
            lambda: self_back(
                r, steps_e, (enc_qx, enc_kx), False, *first[r][1:4], back[r][7], back[r][5]
            ),
            lambda: dec_last(r),
        )

    def weight_grads(pairs):
        total = None
        for left, right in pairs:
            part = mm(left, right, TN)
            total = part if total is None else total + part
        return total.astype(BF)

    def side(values):
        return jnp.concatenate(values, 1)

    def enc_weights():
        cols = lambda v: v
        return [
            jnp.stack([last[r][3] for r in every]),
            weight_grads([(first[r][0], side(last[r][0:3])) for r in every]),
            weight_grads([(first[r][2], back[r][6]) for r in every]),
            weight_grads([(back[r][2], back[r][4]) for r in every]),
            weight_grads([(back[r][3], back[r][1]) for r in every]),
            weight_grads([(back[r][0], side(cross_b[r][1:3])) for r in every]),
            jnp.concatenate(
                [sum(last[r][4] for r in every), sum(back[r][8] for r in every), sum(back[r][9] for r in every)], 0
            ),
        ]

    def dec_weights():
        return [
            jnp.stack([jnp.concatenate([mids[r][1], dlast[r][7]], 0) for r in every]),
            weight_grads([(dfirst[r][0], side(dlast[r][4:7])) for r in every]),
            weight_grads([(dfirst[r][2], dlast[r][1]) for r in every]),
            weight_grads([(mids[r][3], mids[r][5]) for r in every]),
            weight_grads([(mids[r][4], x_in[r, ld:]) for r in every]),
            side(
                [
                    weight_grads([(dfirst[r][5], dcqs[r]) for r in every]),
                    weight_grads([(mids[r][6], ocs[r]) for r in every]),
                ]
            ),
            jnp.concatenate(
                [sum(dlast[r][8] for r in every), sum(dlast[r][3] for r in every), sum(mids[r][8] for r in every)], 0
            ),
        ]

    last_all = lax.cond(on_decoder, dec_weights, enc_weights)
    gain_terms = jnp.pad(last_all[6].T, ((0, 0), (0, LANES - last_all[6].shape[0]))).astype(BF)
    pieces = [last_all[1], last_all[2], last_all[3], last_all[5], gain_terms, last_all[4]]
    if lax.axis_size("rows") == NZ * NY * NC:
        sums = sum_scatter(pieces)
    else:
        sums = [
            lax.psum_scatter(piece, "rows", scatter_dimension=0, tiled=True).astype(F32)
            for piece in pieces
        ]
    s_in, s_out, s_fi, s_cross, s_gain, s_fo = sums
    return (
        last_all[0][None],
        s_in[None],
        s_out[None],
        s_fi[None],
        s_fo[None],
        s_cross[None],
        s_gain[:, : last_all[6].shape[0]].T[None],
    )


def solution(mesh):
    placed = (
        P("section", "rows", None, None),
        P("rows", None),
        P("rows", None),
    ) + (P("section", None, None),) * 6
    return jax.shard_map(
        body,
        mesh=mesh,
        in_specs=placed,
        out_specs=(
            P("section", "rows", None, None),
            P("section", "rows", None),
            P("section", "rows", None),
            P("section", "rows", None),
            P("section", "rows", None),
            P("section", "rows", None),
            P("section", None, "rows"),
        ),
        check_vma=False,
    )
```

```python
import functools

import jax
import jax.numpy as jnp
from jax import lax
from jax.experimental import pallas as pl
from jax.experimental.pallas import tpu as pltpu
from jax.sharding import PartitionSpec as P

HEADS = 12
HEAD = 64
PAIR = 128
EPSILON = 1e-06
SCALE = 0.125
LOG2E = 1.4426950408889634
NEGATIVE = -1e30
GELU_C = 0.7978845608028654
GELU_A = 0.044715

BF = jnp.bfloat16
F32 = jnp.float32
NT = (((1,), (1,)), ((), ()))
NN = (((1,), (0,)), ((), ()))
TN = (((0,), (0,)), ((), ()))


def mm(a, b, dims=NN):
    return lax.dot_general(a, b, dims, preferred_element_type=F32)


MESH = pl.DeviceIdType.MESH
LANES = 256
VMEM_LIMIT = 56 * 1024 * 1024

NZ, NY, NC = 4, 2, 2
PEERS = NZ * NY * NC
C_LAG = 2
Y_LAG = C_LAG + 2
RING = 6
AHEAD = 3
PANELS = 4

TALL = 1
LEFT_ORDER = (0, 2, 3, 4, 5)
PRODUCTS = ((0, 0), (1, 1), (2, 2), (3, 3), (4, 4), (5, 5), (5, 6), (5, 7))


def grad_sum_kernel(rows, token_counts, chunk_counts, *refs):
    lefts_of, rights_of, at = [], [], 0
    for _ in range(2):
        lefts_of.append([refs[at + rows * i : at + rows * (i + 1)] for i in range(6)])
        at += 6 * rows
        rights_of.append([refs[at + rows * i : at + rows * (i + 1)] for i in range(8)])
        at += 8 * rows
    gain_ref = refs[at]
    o_in, o_out, o_fi, o_cross, o_gain, o_fo = refs[at + 1 : at + 7]
    (
        xt, xt_tall, left_stage, tall_stage, tall_right, panels, ring,
        own, got_core, got_y, got_r, got_l,
        s_left, s_tall, s_right, s_panel,
        s_core, r_core, s_y, r_y, s_r, r_r, s_l, r_l,
    ) = refs[at + 7 :]
    chunks, height = own.shape[0], own.shape[3]
    sec, me = lax.axis_index("section"), lax.axis_index("rows")
    core, y, z = lax.rem(me, 2), lax.rem(me // 2, 2), me // 4
    by_core, by_y = me + 1 - 2 * core, me + 2 - 4 * y
    other, away = 1 - core, 1 - y
    bases = [sum(chunk_counts[:i]) for i in range(len(chunk_counts))]

    barrier = pltpu.get_barrier_semaphore()

    def greet(peer):
        pl.semaphore_signal(barrier, inc=1, device_id=(sec, peer), device_id_type=MESH)

    greet(by_core)
    greet(by_y)

    @pl.when(z > 0)
    def _():
        greet(me - 4)

    @pl.when(z < NZ - 1)
    def _():
        greet(me + 4)

    @pl.when((z > 0) & (z < NZ - 1))
    def _():
        pl.semaphore_wait(barrier, 4)

    @pl.when((z == 0) | (z == NZ - 1))
    def _():
        pl.semaphore_wait(barrier, 3)


    def each(act):
        for side in range(2):

            @pl.when(sec == side)
            def _(side=side):
                act(side)

    def row_copies(sources, columns, dst, sems, side):
        tokens = token_counts[side]
        return [
            pltpu.make_async_copy(
                src if columns is None else src.at[:, columns],
                dst.at[pl.ds(r * tokens, tokens)],
                sems.at[r],
            )
            for r, src in enumerate(sources)
        ]

    def start_all(copies):
        for copy in copies:
            copy.start()

    def wait_all(copies):
        for copy in copies:
            copy.wait()

    def left_copies(q, side):
        source = lefts_of[side][LEFT_ORDER[q]]
        return row_copies(source, None, left_stage.at[q % 2], s_left.at[q % 2], side)

    def tall_copies(side):
        return row_copies(lefts_of[side][1], None, tall_stage, s_tall, side)

    def tall_right_copies(side):
        return row_copies(rights_of[side][1], None, tall_right, s_right, side)

    def panel_copies(p, i, slot, side):
        columns = pl.ds(pl.multiple_of(i * LANES, LANES), LANES)
        return row_copies(
            rights_of[side][PRODUCTS[p][1]], columns, panels.at[slot], s_panel.at[slot], side
        )

    def for_panel(t, act):
        slot = lax.rem(t, PANELS)
        for p in range(len(PRODUCTS)):
            if p != TALL:

                @pl.when((t >= bases[p]) & (t < bases[p] + chunk_counts[p]))
                def _(p=p):
                    each(lambda side: act(p, t - bases[p], slot, side))

    def flip(side, stage, columns, put):
        for at in range(0, rows * token_counts[side], LANES):
            tokens = slice(at, at + LANES)
            put(tokens, stage[tokens, columns].astype(F32).T.astype(BF))

    def build_left(q):
        def act(side):
            wait_all(left_copies(q, side))
            for at in range(0, xt.shape[0], LANES):

                def put(tokens, block, at=at):
                    xt[at : at + LANES, tokens] = block

                flip(side, left_stage.at[q % 2], slice(at, at + LANES), put)
            if q + 2 < len(LEFT_ORDER):
                start_all(left_copies(q + 2, side))

        each(act)

    groups = xt_tall.shape[0] // LANES
    tall_rows = xt_tall.shape[0] // PEERS

    def build_tall(part):
        columns = pl.ds(pl.multiple_of(part * LANES, LANES), LANES)
        targets = LANES // tall_rows

        def act(side):
            def put(tokens, block):
                for k in range(targets):
                    for j in range(tall_rows // 16):
                        to = j * LANES + (part * targets + k) * 16
                        xt_tall[pl.ds(pl.multiple_of(to, 16), 16), tokens] = block[
                            k * tall_rows + j * 16 : k * tall_rows + (j + 1) * 16
                        ]

            flip(side, tall_stage, columns, put)

        each(act)

    def send_core(j):
        slot = lax.rem(j, RING)
        return pltpu.make_async_remote_copy(
            src_ref=ring.at[slot, :, :, other],
            dst_ref=got_core.at[j],
            send_sem=s_core.at[j],
            recv_sem=r_core.at[j],
            device_id=(sec, by_core),
            device_id_type=MESH,
        )

    def send_y(j):
        return pltpu.make_async_remote_copy(
            src_ref=own.at[j, :, away],
            dst_ref=got_y.at[j],
            send_sem=s_y.at[j],
            recv_sem=r_y.at[j],
            device_id=(sec, by_y),
            device_id_type=MESH,
        )

    def send_right(j, at):
        return pltpu.make_async_remote_copy(
            src_ref=own.at[j, pl.ds(at + 1, NZ - 1 - at), y],
            dst_ref=got_r.at[j, pl.ds(at + 1, NZ - 1 - at)],
            send_sem=s_r.at[j],
            recv_sem=r_r.at[j],
            device_id=(sec, me + 4),
            device_id_type=MESH,
        )

    def send_left(j, at):
        return pltpu.make_async_remote_copy(
            src_ref=own.at[j, pl.ds(0, at), y],
            dst_ref=got_l.at[j, pl.ds(0, at)],
            send_sem=s_l.at[j],
            recv_sem=r_l.at[j],
            device_id=(sec, me - 4),
            device_id_type=MESH,
        )

    def add_into(dst, src):
        dst[...] = (dst[...].astype(F32) + src[...].astype(F32)).astype(BF)


    def compute(s):
        slot = lax.rem(s, RING)

        def put_panel(value):
            for t in range(PEERS):
                ring[slot, t // 4, t // 2 % 2, t % 2] = value[t * height : (t + 1) * height]

        for p in range(len(PRODUCTS)):
            left = PRODUCTS[p][0]

            @pl.when((s >= bases[p]) & (s < bases[p] + chunk_counts[p]))
            def _(p=p, left=left):
                if p != TALL:
                    if p == 0 or PRODUCTS[p - 1][0] != left:

                        @pl.when(s == bases[p])
                        def _():
                            build_left(LEFT_ORDER.index(left))

                    where = lax.rem(s, PANELS)

                    def act(side):
                        wait_all(panel_copies(p, s - bases[p], where, side))
                        tokens = rows * token_counts[side]
                        put_panel(mm(xt[:, :tokens], panels[where, :tokens, :]).astype(BF))

                    each(act)
                else:
                    rows_at = pl.ds(pl.multiple_of((s - bases[p]) * LANES, LANES), LANES)

                    @pl.when(s == bases[p])
                    def _():
                        each(lambda side: wait_all(tall_right_copies(side)))

                    def act(side):
                        tokens = rows * token_counts[side]
                        for k in range(tall_right.shape[1] // LANES):
                            value = mm(
                                xt_tall[rows_at, :tokens],
                                tall_right[:tokens, k * LANES : (k + 1) * LANES],
                            ).astype(BF)
                            for t in range(PEERS):
                                ring[slot, t // 4, t // 2 % 2, t % 2, k * 16 : (k + 1) * 16] = value[
                                    t * 16 : (t + 1) * 16
                                ]

                    each(act)

        @pl.when(s == chunks - 1)
        def _():
            put_panel(gain_ref[...])


    def open_first(side):
        start_all(left_copies(0, side))
        for t in range(AHEAD):
            start_all(panel_copies(0, t, t % PANELS, side))
        start_all(tall_copies(side))
        start_all(tall_right_copies(side))
        start_all(left_copies(1, side))

    each(open_first)

    def step(s, carry):
        @pl.when(s + AHEAD < chunks - 1)
        def _():
            for_panel(
                s + AHEAD,
                lambda p, i, slot, side: start_all(panel_copies(p, i, slot, side)),
            )

        @pl.when((s >= RING) & (s < chunks))
        def _():
            send_core(s - RING).wait_send()

        @pl.when(s < chunks)
        def _():
            compute(s)
            send_core(s).start()

        @pl.when(s == 0)
        def _():
            each(lambda side: wait_all(tall_copies(side)))

        @pl.when(s < groups)
        def _():
            build_tall(s)

        j_c = s - C_LAG

        @pl.when((j_c >= 0) & (j_c < chunks))
        def _():
            send_core(j_c).wait_recv()
            slot = lax.rem(j_c, RING)
            for a in range(NZ):
                for b in range(NY):
                    own[j_c, a, b] = (
                        ring[slot, a, b, core].astype(F32) + got_core[j_c, a, b].astype(F32)
                    ).astype(BF)
            send_y(j_c).start()

        j_y = s - Y_LAG

        @pl.when((j_y >= 0) & (j_y < chunks))
        def _():
            send_y(j_y).wait_recv()
            for t in range(NZ):
                add_into(own.at[j_y, t, y], got_y.at[j_y, t])

        for at in range(NZ - 1):
            j_r = s - Y_LAG - at

            @pl.when((z == at) & (j_r >= 0) & (j_r < chunks))
            def _(at=at, j_r=j_r):
                if at > 0:
                    send_right(j_r, at - 1).wait_recv()
                    for t in range(at + 1, NZ):
                        add_into(own.at[j_r, t, y], got_r.at[j_r, t])
                send_right(j_r, at).start()

        for at in range(1, NZ):
            j_l = s - Y_LAG - (NZ - 1 - at)

            @pl.when((z == at) & (j_l >= 0) & (j_l < chunks))
            def _(at=at, j_l=j_l):
                if at < NZ - 1:
                    send_left(j_l, at + 1).wait_recv()
                    for t in range(at):
                        add_into(own.at[j_l, t, y], got_l.at[j_l, t])
                send_left(j_l, at).start()

        return carry

    lax.fori_loop(0, chunks + Y_LAG + NZ - 1, step, 0)


    def finish(j):
        @pl.when(z == NZ - 1)
        def _():
            send_right(j, NZ - 2).wait_recv()

        @pl.when(z == 0)
        def _():
            send_left(j, 1).wait_recv()

        send_y(j).wait_send()

        @pl.when(j >= chunks - RING)
        def _():
            send_core(j).wait_send()

        for at in range(NZ):

            @pl.when(z == at)
            def _(at=at):
                if at < NZ - 1:
                    send_right(j, at).wait_send()
                if at > 0:
                    send_left(j, at).wait_send()

    def total(j, part):
        mine = own[j, z, y, part].astype(F32)
        right = got_r[j, z, part].astype(F32)
        left = got_l[j, z, part].astype(F32)
        return mine + jnp.where(z > 0, right, 0.0) + jnp.where(z < NZ - 1, left, 0.0)

    def close(out, base, count, column):
        def panel(i, carry):
            finish(base + i)
            at = pl.ds(pl.multiple_of(column + i * LANES, LANES), LANES)
            out[:, at] = total(base + i, pl.ds(0, height))
            return carry

        lax.fori_loop(0, count, panel, 0)

    dim = xt.shape[0]
    close(o_fi, bases[0], chunk_counts[0], 0)

    def tall_out(i, carry):
        finish(bases[TALL] + i)
        at = pl.ds(pl.multiple_of(i * 16, 16), 16)
        for k in range(tall_right.shape[1] // LANES):
            o_fo[at, k * LANES : (k + 1) * LANES] = total(bases[TALL] + i, pl.ds(k * 16, 16))
        return carry

    lax.fori_loop(0, chunk_counts[TALL], tall_out, 0)
    close(o_cross, bases[2], chunk_counts[2], 0)
    close(o_cross, bases[3], chunk_counts[3], dim)
    close(o_out, bases[4], chunk_counts[4], 0)
    for k in range(3):
        close(o_in, bases[5 + k], chunk_counts[5 + k], k * dim)
    close(o_gain, chunks - 1, 1, 0)


def grad_sum(sides, gain_terms):
    rows = len(sides[0][0][0])
    token_counts = tuple(lefts[0][0].shape[0] for lefts, _ in sides)
    tokens = rows * max(token_counts)
    lefts, rights = sides[0]
    dim, tall = lefts[0][0].shape[1], lefts[TALL][0].shape[1]
    height = dim // PEERS
    chunk_counts = tuple(
        lefts[a][0].shape[1] * rights[b][0].shape[1] // (dim * LANES) for a, b in PRODUCTS
    )
    chunks = sum(chunk_counts) + 1
    flat = [v for lefts, rights in sides for group in lefts + rights for v in group]
    half = (chunks, NZ, NY, height, LANES)
    fourth = (chunks, NZ, height, LANES)
    width = lambda *which: sum(rights[i][0].shape[1] for i in which)
    out_shape = [
        jax.ShapeDtypeStruct(s, F32)
        for s in (
            (height, width(5, 6, 7)),
            (height, width(4)),
            (height, width(0)),
            (height, width(2, 3)),
            (height, LANES),
            (tall // PEERS, width(1)),
        )
    ]
    return pl.pallas_call(
        functools.partial(grad_sum_kernel, rows, token_counts, chunk_counts),
        in_specs=[pl.BlockSpec(memory_space=pl.ANY)] * len(flat)
        + [pl.BlockSpec(memory_space=pltpu.VMEM)],
        out_specs=[pl.BlockSpec(memory_space=pltpu.VMEM)] * len(out_shape),
        out_shape=out_shape,
        scratch_shapes=[
            pltpu.VMEM((dim, tokens), BF),
            pltpu.VMEM((tall, tokens), BF),
            pltpu.VMEM((2, tokens, dim), BF),
            pltpu.VMEM((tokens, tall), BF),
            pltpu.VMEM((tokens, width(1)), BF),
            pltpu.VMEM((PANELS, tokens, LANES), BF),
            pltpu.VMEM((RING, NZ, NY, NC, height, LANES), BF),
            pltpu.VMEM(half, BF),
            pltpu.VMEM(half, BF),
            pltpu.VMEM(fourth, BF),
            pltpu.VMEM(fourth, BF),
            pltpu.VMEM(fourth, BF),
            pltpu.SemaphoreType.DMA((2, rows)),
            pltpu.SemaphoreType.DMA((rows,)),
            pltpu.SemaphoreType.DMA((rows,)),
            pltpu.SemaphoreType.DMA((PANELS, rows)),
        ]
        + [pltpu.SemaphoreType.DMA((chunks,))] * 8,
        compiler_params=pltpu.CompilerParams(
            collective_id=1, has_side_effects=True, vmem_limit_bytes=VMEM_LIMIT
        ),
    )(*flat, gain_terms)


def plain_sum(on_decoder, sides, gain_terms):
    def terms(lefts, rights):
        parts = [
            sum(mm(a, b, TN) for a, b in zip(lefts[i], rights[j])).astype(BF) for i, j in PRODUCTS
        ]
        return [
            jnp.concatenate(parts[5:8], 1),
            parts[4],
            parts[0],
            jnp.concatenate(parts[2:4], 1),
            parts[1],
        ]

    pieces = lax.cond(on_decoder, lambda: terms(*sides[1]), lambda: terms(*sides[0]))
    pieces.insert(4, gain_terms)
    return [
        lax.psum_scatter(piece, "rows", scatter_dimension=0, tiled=True).astype(F32)
        for piece in pieces
    ]


def low_half(rows):
    return lax.broadcasted_iota(jnp.int32, (rows, PAIR), 1) < HEAD


def masked_scores(q, k, qx, kx, head, causal):
    lo_q, lo_k = low_half(q.shape[0]), low_half(k.shape[0])
    if head == 0:
        qh, kh = jnp.where(lo_q, q, qx), jnp.where(lo_k, k, kx)
    else:
        qh, kh = jnp.where(lo_q, qx, q), jnp.where(lo_k, kx, k)
    s = mm(kh, qh, NT)
    if causal:
        key_at = lax.broadcasted_iota(jnp.int32, s.shape, 0)
        query_at = lax.broadcasted_iota(jnp.int32, s.shape, 1)
        s = jnp.where(key_at <= query_at, s, NEGATIVE)
    return s


def attn_fwd_kernel(q_ref, k_ref, v_ref, qx_ref, kx_ref, o_ref, lse_ref, *, causal):
    q, k, qx, kx = q_ref[...], k_ref[...], qx_ref[0], kx_ref[0]
    vt = v_ref[...].astype(F32).T.astype(BF)
    outs = []
    for head in range(2):
        s = masked_scores(q, k, qx, kx, head, causal)
        top = jnp.max(s, axis=0, keepdims=True)
        p = jnp.exp2((s - top) * (SCALE * LOG2E))
        total = jnp.sum(p, axis=0, keepdims=True)
        o = mm(vt[head * HEAD : (head + 1) * HEAD], p.astype(BF))
        outs.append(o / total)
        lse_ref[0, head : head + 1, :] = top * (SCALE * LOG2E) + jnp.log2(total)
    o_ref[...] = jnp.concatenate(outs, axis=0).T.astype(BF)


def attn_bwd_kernel(
    q_ref, k_ref, v_ref, qx_ref, kx_ref, o_ref, do_ref, lse_ref, dq_ref, dk_ref, dv_ref, *, causal
):
    q, k, v, qx, kx = q_ref[...], k_ref[...], v_ref[...], qx_ref[0], kx_ref[0]
    do = do_ref[...]
    kt = k.astype(F32).T.astype(BF)
    spread = (do.astype(F32) * o_ref[...].astype(F32)).T
    lo_q, lo_k = low_half(q.shape[0]), low_half(k.shape[0])
    zero_q, zero_k = jnp.zeros_like(q), jnp.zeros_like(k)
    dqs, dk, dv = [], None, None
    for head in range(2):
        s = masked_scores(q, k, qx, kx, head, causal)
        p = jnp.exp2(s * (SCALE * LOG2E) - lse_ref[0, head : head + 1, :])
        if head == 0:
            vh, doh, qh = (
                jnp.where(lo_k, v, zero_k),
                jnp.where(lo_q, do, zero_q),
                jnp.where(lo_q, q, zero_q),
            )
        else:
            vh, doh, qh = (
                jnp.where(lo_k, zero_k, v),
                jnp.where(lo_q, zero_q, do),
                jnp.where(lo_q, zero_q, q),
            )
        dp = mm(vh, do, NT)
        delta = jnp.sum(spread[head * HEAD : (head + 1) * HEAD], axis=0, keepdims=True)
        ds = (p * (dp - delta)).astype(BF)
        dv_part = mm(p.astype(BF), doh)
        dk_part = mm(ds, qh)
        dv = dv_part if dv is None else dv + dv_part
        dk = dk_part if dk is None else dk + dk_part
        dqs.append(mm(kt[head * HEAD : (head + 1) * HEAD], ds))
    dq_ref[...] = (jnp.concatenate(dqs, axis=0).T * SCALE).astype(BF)
    dk_ref[...] = (dk * SCALE).astype(BF)
    dv_ref[...] = dv.astype(BF)


def column_block(length, first):
    return pl.BlockSpec((length, PAIR), lambda p: (0, first + p))


def mask_block(length, row):
    return pl.BlockSpec((1, length, PAIR), lambda p: (row, 0, 0))


def pair_block(count_q):
    return pl.BlockSpec((1, 2, count_q), lambda p: (p, 0, 0))


def params(**more):
    return pltpu.CompilerParams(vmem_limit_bytes=VMEM_LIMIT, **more)


def attention_forward(q_in, k_in, v_in, qx, kx, row, firsts, causal):
    count_q, count_k, pairs = q_in.shape[0], k_in.shape[0], HEADS // 2
    return pl.pallas_call(
        functools.partial(attn_fwd_kernel, causal=causal),
        grid=(pairs,),
        in_specs=[
            column_block(count_q, firsts[0]),
            column_block(count_k, firsts[1]),
            column_block(count_k, firsts[2]),
            mask_block(count_q, row),
            mask_block(count_k, row),
        ],
        out_specs=[column_block(count_q, 0), pair_block(count_q)],
        out_shape=[
            jax.ShapeDtypeStruct((count_q, HEADS * HEAD), BF),
            jax.ShapeDtypeStruct((pairs, 2, count_q), F32),
        ],
        compiler_params=params(),
    )(q_in, k_in, v_in, qx, kx)


def attention_backward(q_in, k_in, v_in, qx, kx, row, firsts, mixed, grad_mixed, lse, causal):
    count_q, count_k, pairs = q_in.shape[0], k_in.shape[0], HEADS // 2
    width = HEADS * HEAD
    return pl.pallas_call(
        functools.partial(attn_bwd_kernel, causal=causal),
        grid=(pairs,),
        in_specs=[
            column_block(count_q, firsts[0]),
            column_block(count_k, firsts[1]),
            column_block(count_k, firsts[2]),
            mask_block(count_q, row),
            mask_block(count_k, row),
            column_block(count_q, 0),
            column_block(count_q, 0),
            pair_block(count_q),
        ],
        out_specs=[
            column_block(count_q, 0),
            column_block(count_k, 0),
            column_block(count_k, 0),
        ],
        out_shape=[
            jax.ShapeDtypeStruct((count_q, width), BF),
            jax.ShapeDtypeStruct((count_k, width), BF),
            jax.ShapeDtypeStruct((count_k, width), BF),
        ],
        compiler_params=params(),
    )(q_in, k_in, v_in, qx, kx, mixed, grad_mixed, lse)


BLOCK = 256
SLICE = 512


def inverse_rms(v):
    return lax.rsqrt(jnp.mean(v * v, -1, keepdims=True) + EPSILON)


def norm(v, gain):
    return (v * inverse_rms(v) * gain).astype(BF)


def norm_back(v, gain, grad):
    inv = inverse_rms(v)
    scaled = grad * gain
    along = jnp.mean(scaled * v, -1, keepdims=True)
    return (
        inv * scaled - v * (inv * inv * inv * along),
        jnp.sum(grad * v * inv, 0, keepdims=True),
    )


def gelu(x):
    return 0.5 * x * (1.0 + jnp.tanh(GELU_C * (x + GELU_A * x * x * x)))


def gelu_parts(x):
    square = x * x
    t = jnp.tanh(GELU_C * x * (1.0 + GELU_A * square))
    half = 0.5 * (1.0 + t)
    slope = half + 0.5 * x * (1.0 - t * t) * (GELU_C * (1.0 + 3.0 * GELU_A * square))
    return x * half, slope


class Fetch:
    def __init__(self, sources, held, sems):
        self.copies = [
            pltpu.make_async_copy(src, dst, sems.at[i])
            for i, (src, dst) in enumerate(zip(sources, held))
        ]
        self.held = held
        self.first = pl.program_id(0) == 0

        @pl.when(self.first)
        def _():
            for copy in self.copies:
                copy.start()

    def __getitem__(self, i):
        @pl.when(self.first)
        def _():
            self.copies[i].wait()

        return self.held[i]


def add_gain(ref, part):
    @pl.when(pl.program_id(0) == 0)
    def _():
        ref[...] = part

    @pl.when(pl.program_id(0) > 0)
    def _():
        ref[...] += part


def block_call(kernel, steps, ins, weights, outs, gain_outs=0):
    specs, arrays = [], []
    for array, row, first in ins:
        columns = array.shape[-1]
        if row is None:
            specs.append(pl.BlockSpec((BLOCK, columns), lambda i, f=first: (f + i, 0)))
        else:
            specs.append(
                pl.BlockSpec((None, BLOCK, columns), lambda i, r=row, f=first: (r, f + i, 0))
            )
        arrays.append(array)
    gains = [w for w in weights if w.dtype == F32]
    mats = [w for w in weights if w.dtype != F32]
    specs += [pl.BlockSpec((1, g.shape[1]), lambda i: (0, 0)) for g in gains]
    specs += [pl.BlockSpec(memory_space=pl.ANY)] * len(mats)
    dim = gains[0].shape[1]
    count = len(mats)

    def run(*refs):
        held, sems = refs[-1 - count : -1], refs[-1]
        at = len(arrays) + len(gains)
        fetch = Fetch(refs[at : at + count], held, sems)
        kernel(refs[: len(arrays)], [g[...] for g in refs[len(arrays) : at]], fetch, refs[at + count : -1 - count])

    return pl.pallas_call(
        run,
        grid=(steps,),
        in_specs=specs,
        out_specs=[pl.BlockSpec((BLOCK, c), lambda i: (i, 0)) for c, _ in outs]
        + [pl.BlockSpec((1, dim), lambda i: (0, 0))] * gain_outs,
        out_shape=[jax.ShapeDtypeStruct((steps * BLOCK, c), t) for c, t in outs]
        + [jax.ShapeDtypeStruct((1, dim), F32)] * gain_outs,
        scratch_shapes=[pltpu.VMEM(m.shape, m.dtype) for m in mats]
        + [pltpu.SemaphoreType.DMA((count,))],
        compiler_params=params(),
    )(*arrays, *gains, *mats)


def project_kernel(ins, gains, w, outs):
    (x,), (g0,), (n_ref, packed_ref) = ins, gains, outs
    n = norm(x[...].astype(F32), g0)
    n_ref[...] = n
    wa = w[0]
    dim = x.shape[1]
    for at in range(0, wa.shape[1], dim):
        packed_ref[:, at : at + dim] = mm(n, wa[:, at : at + dim]).astype(BF)


def ffn_up(m, wf, wd, acc, u_ref, act_ref):
    half = wd.shape[0]
    for at in range(0, half, SLICE):
        gate = mm(m, wf[:, at : at + SLICE])
        up = mm(m, wf[:, half + at : half + at + SLICE])
        u_ref[:, at : at + SLICE] = gate.astype(BF)
        u_ref[:, half + at : half + at + SLICE] = up.astype(BF)
        act = (gelu(gate) * up).astype(BF)
        if act_ref is not None:
            act_ref[:, at : at + SLICE] = act
        acc = acc + mm(act, wd[at : at + SLICE, :])
    return acc


def ffn_down(branch, wf, wd, u_ref, du_ref, act_ref):
    half = wd.shape[0]
    dm = None
    for at in range(0, half, SLICE):
        d_act = mm(branch, wd[at : at + SLICE, :], NT)
        gate = u_ref[:, at : at + SLICE].astype(F32)
        up = u_ref[:, half + at : half + at + SLICE].astype(F32)
        value, slope = gelu_parts(gate)
        if act_ref is not None:
            act_ref[:, at : at + SLICE] = (value * up).astype(BF)
        d_gate = (d_act * up * slope).astype(BF)
        d_up = (d_act * value).astype(BF)
        du_ref[:, at : at + SLICE] = d_gate
        du_ref[:, half + at : half + at + SLICE] = d_up
        part = mm(d_gate, wf[:, at : at + SLICE], NT) + mm(
            d_up, wf[:, half + at : half + at + SLICE], NT
        )
        dm = part if dm is None else dm + part
    return dm


def enc_rest_kernel(ins, gains, w, outs):
    (o, x), (g1, g2) = ins, gains
    e1_ref, u_ref, e2_ref, sent_ref = outs
    e1 = x[...].astype(F32) + mm(o[...], w[0][...])
    e1_ref[...] = e1
    e2 = ffn_up(norm(e1, g2), w[1], w[2], e1, u_ref, None)
    e2_ref[...] = e2
    sent_ref[...] = mm(norm(e2, g1), w[3][...]).astype(BF)


def dec_query_kernel(ins, gains, w, outs):
    (o, x), (g1,), (d1_ref, c_ref, cq_ref) = ins, gains, outs
    d1 = x[...].astype(F32) + mm(o[...], w[0][...])
    d1_ref[...] = d1
    c = norm(d1, g1)
    c_ref[...] = c
    cq_ref[...] = mm(c, w[1][:, : c.shape[1]]).astype(BF)


def dec_ffn_kernel(ins, gains, w, outs):
    (oc, d1, cot), (g2,) = ins, gains
    doc_ref, out_ref, dd2_ref, m_ref, act_ref, du_ref, branch_ref, u_ref, dg2_ref = outs
    width = oc.shape[1]
    out_proj = w[0]
    d2 = d1[...] + mm(oc[...], out_proj[:, width:], NT)
    m = norm(d2, g2)
    m_ref[...] = m
    wf, wd = w[1], w[2]
    out_ref[...] = ffn_up(m, wf, wd, d2, u_ref, act_ref)
    dm = ffn_down(cot[...], wf, wd, u_ref, du_ref, None)
    back, dg2 = norm_back(d2, g2, dm)
    dd2 = cot[...].astype(F32) + back
    dd2_ref[...] = dd2
    branch = dd2.astype(BF)
    branch_ref[...] = branch
    doc_ref[...] = mm(branch, out_proj[:, width:]).astype(BF)
    add_gain(dg2_ref, dg2)


def enc_back_kernel(ins, gains, w, outs):
    (dk, dv, e1_in, e2_in, u), (g1, g2) = ins, gains
    mem_ref, fb_ref, m_ref, act_ref, du_ref, de1_ref, ab_ref, do_ref, dg1_ref, dg2_ref = outs
    wc = w[0]
    width = dk.shape[1]
    e1, e2 = e1_in[...], e2_in[...]
    dmem = mm(dk[...], wc[:, :width], NT) + mm(dv[...], wc[:, width:], NT)
    mem_ref[...] = norm(e2, g1)
    de2, dg1 = norm_back(e2, g1, dmem)
    fb = de2.astype(BF)
    fb_ref[...] = fb
    m_ref[...] = norm(e1, g2)
    wd, wf = w[1], w[2]
    dm = ffn_down(fb, wf, wd, u, du_ref, act_ref)
    back, dg2 = norm_back(e1, g2, dm)
    de1 = de2 + back
    de1_ref[...] = de1
    ab = de1.astype(BF)
    ab_ref[...] = ab
    do_ref[...] = mm(ab, w[3][...], NT).astype(BF)
    add_gain(dg1_ref, dg1)
    add_gain(dg2_ref, dg2)


def dec_back_kernel(ins, gains, w, outs):
    (dcq, d1_in, dd2), (g1,), (dd1_ref, ab_ref, do_ref, dg1_ref) = ins, gains, outs
    d1 = d1_in[...]
    dc = mm(dcq[...], w[0][:, : dcq.shape[1]], NT)
    back, dg1 = norm_back(d1, g1, dc)
    dd1 = dd2[...] + back
    dd1_ref[...] = dd1
    ab = dd1.astype(BF)
    ab_ref[...] = ab
    do_ref[...] = mm(ab, w[1][...], NT).astype(BF)
    add_gain(dg1_ref, dg1)


def input_grad_kernel(ins, gains, w, outs):
    (dq, dk, dv, x, grad), (g0,), (dx_ref, dg0_ref) = ins, gains, outs
    wa = w[0]
    width = dq.shape[1]
    dn = (
        mm(dq[...], wa[:, :width], NT)
        + mm(dk[...], wa[:, width : 2 * width], NT)
        + mm(dv[...], wa[:, 2 * width :], NT)
    )
    back, dg0 = norm_back(x[...].astype(F32), g0, dn)
    dx_ref[...] = grad[...] + back
    add_gain(dg0_ref, dg0)


def nothing_kernel(*refs):
    pass


def unwritten(shapes):
    return pl.pallas_call(
        nothing_kernel,
        out_specs=[pl.BlockSpec(memory_space=pl.ANY)] * len(shapes),
        out_shape=[jax.ShapeDtypeStruct(s.shape, s.dtype) for s in shapes],
    )()


def by_section(on_decoder, encoder, decoder):
    enc_shapes = jax.eval_shape(encoder) if encoder else []
    dec_shapes = jax.eval_shape(decoder) if decoder else []
    none = lambda: []
    encoder, decoder = encoder or none, decoder or none
    pool = lambda shapes: list(unwritten(shapes)) if shapes else []
    both = lax.cond(
        on_decoder,
        lambda: pool(enc_shapes) + list(decoder()),
        lambda: list(encoder()) + pool(dec_shapes),
    )
    return both[: len(enc_shapes)], both[len(enc_shapes) :]


def segment_ids(lengths, span_len):
    positions = jnp.arange(span_len, dtype=jnp.int32)[None, :]
    seg, end = jnp.zeros((lengths.shape[0], span_len), jnp.int32), 0
    for j in range(lengths.shape[1]):
        end = end + lengths[:, j : j + 1]
        seg = seg + (positions >= end).astype(jnp.int32)
    return seg


def mask_lanes(seg, count):
    hit = seg[:, :, None] == jnp.arange(HEAD, dtype=jnp.int32)[None, None, :]
    member = hit.astype(BF)
    other = jnp.where(
        jnp.arange(HEAD, dtype=jnp.int32)[None, None, :] < count,
        jnp.where(hit, 0.0, NEGATIVE),
        0.0,
    ).astype(BF)
    return (
        jnp.concatenate([member, member], -1),
        jnp.concatenate([other, other], -1),
    )


def shift(x, by):
    pairs = [(0, 1)] if by > 0 else [(1, 0)]
    return lax.ppermute(x, "section", pairs)


def body(
    section_input, enc_lengths, dec_lengths, attn_in, attn_out, ffn_in, ffn_out, cross_weight, gains
):
    wa, wo, wf, wd, wc = attn_in[0], attn_out[0], ffn_in[0], ffn_out[0], cross_weight[0]
    g0, g1, g2 = gains[0, 0:1], gains[0, 1:2], gains[0, 2:3]
    x_in = section_input[0]
    rows, le, dim = x_in.shape
    ld = le // 2
    width = wo.shape[0]
    docs = enc_lengths.shape[1]
    enc_qx, enc_kx = mask_lanes(segment_ids(enc_lengths, le), docs)
    dec_qx, dec_kx = mask_lanes(segment_ids(dec_lengths, ld), docs)
    on_decoder = lax.axis_index("section") == 1
    steps_e, steps_d = le // BLOCK, ld // BLOCK
    columns = width // PAIR
    own = (0, columns, 2 * columns)
    across = (0, 0, columns)
    inner = wf.shape[1]

    def project(r, steps):
        return list(
            block_call(project_kernel, steps, [(x_in, r, 0)], [g0, wa], [(dim, BF), (3 * width, BF)])
        )

    def enc_first(r):
        n, packed = project(r, steps_e)
        o, lse = attention_forward(packed, packed, packed, enc_qx, enc_kx, r, own, False)
        return [n, packed, o, lse]

    def enc_rest(r, o):
        return list(
            block_call(
                enc_rest_kernel,
                steps_e,
                [(o, None, 0), (x_in, r, 0)],
                [g1, g2, wo, wf, wd, wc],
                [(dim, F32), (inner, BF), (dim, F32), (2 * width, BF)],
            )
        )

    def dec_first(r):
        n, packed = project(r, steps_d)
        o, lse = attention_forward(packed, packed, packed, dec_qx, dec_kx, r, own, True)
        d1, c, cq = block_call(
            dec_query_kernel,
            steps_d,
            [(o, None, 0), (x_in, r, 0)],
            [g1, wo, wc],
            [(dim, F32), (dim, BF), (width, BF)],
        )
        return [n, packed, o, lse, d1, c, cq]

    def cross(r, cq, sent):
        return list(attention_forward(cq, sent, sent, dec_qx, enc_kx, r, across, False))

    def dec_ffn(r, oc, d1):
        return list(
            block_call(
                dec_ffn_kernel,
                steps_d,
                [(oc, None, 0), (d1, None, 0), (x_in, r, ld // BLOCK)],
                [g2, wc, wf, wd],
                [
                    (width, BF),
                    (dim, F32),
                    (dim, F32),
                    (dim, BF),
                    (wd.shape[0], BF),
                    (inner, BF),
                    (dim, BF),
                    (inner, BF),
                ],
                1,
            )
        )

    def cross_back(r, cq, sent, oc, doc, lse):
        return list(
            attention_backward(cq, sent, sent, dec_qx, enc_kx, r, across, oc, doc, lse, False)
        )

    def enc_back(dk, dv, e1, e2, u):
        return list(
            block_call(
                enc_back_kernel,
                steps_e,
                [(dk, None, 0), (dv, None, 0), (e1, None, 0), (e2, None, 0), (u, None, 0)],
                [g1, g2, wc, wd, wf, wo],
                [
                    (dim, BF),
                    (dim, BF),
                    (dim, BF),
                    (wd.shape[0], BF),
                    (inner, BF),
                    (dim, F32),
                    (dim, BF),
                    (width, BF),
                ],
                2,
            )
        )

    def self_back(r, steps, masks, causal, packed, o, lse, do, grad):
        dq, dk, dv = attention_backward(
            packed, packed, packed, *masks, r, own, o, do, lse, causal
        )
        dx, dg0 = block_call(
            input_grad_kernel,
            steps,
            [(dq, None, 0), (dk, None, 0), (dv, None, 0), (x_in, r, 0), (grad, None, 0)],
            [g0, wa],
            [(dim, F32)],
            1,
        )
        return [dq, dk, dv, dx, dg0]

    def dec_back(dcq, d1, dd2):
        return list(
            block_call(
                dec_back_kernel,
                steps_d,
                [(dcq, None, 0), (d1, None, 0), (dd2, None, 0)],
                [g1, wc, wo],
                [(dim, F32), (dim, BF), (width, BF)],
                1,
            )
        )

    every = range(rows)
    state = [on_decoder]

    def run(encoder, decoder, *ready):
        held = lax.optimization_barrier(tuple(state) + ready)[0]
        out = by_section(held, encoder, decoder)
        state[1:] = [(out[0] or out[1])[0]]
        return out

    def slots():
        return [None] * rows

    first, rest, dfirst, cqs, crossed, ocs = slots(), slots(), slots(), slots(), slots(), slots()
    mids, docs_in, cross_b, dcqs, back, last, dlast = (slots() for _ in range(7))

    def begin_cross(r, beside=None):
        crossed[r], out = run(lambda: cross(r, cqs[r], rest[r][3]), beside)
        ocs[r] = shift(crossed[r][0], 1)
        return out

    def dec_mid(r):
        return lambda: dec_ffn(r, ocs[r], dfirst[r][4])

    def keep_mid(r, out):
        mids[r] = out
        docs_in[r] = shift(out[0], -1)

    def dec_last(r):
        p = dec_back(dcqs[r], dfirst[r][4], mids[r][2])
        n, packed, o, lse = dfirst[r][:4]
        return p + self_back(r, steps_d, (dec_qx, dec_kx), True, packed, o, lse, p[2], p[0])

    def enc_last(r):
        return self_back(
            r, steps_e, (enc_qx, enc_kx), False, *first[r][1:4], back[r][7], back[r][5]
        )

    first[0], dfirst[0] = run(lambda: enc_first(0), lambda: dec_first(0))
    cqs[0] = shift(dfirst[0][6], -1)
    rest[0], more = run(
        lambda: enc_rest(0, first[0][2]),
        lambda: [v for r in every[1:] for v in dec_first(r)],
    )
    for r in every[1:]:
        dfirst[r] = more[7 * (r - 1) : 7 * r]
        cqs[r] = shift(dfirst[r][6], -1)
    begin_cross(0)
    for r in every[1:]:
        first[r], _ = run(lambda: enc_first(r), None)
        rest[r], out = run(lambda: enc_rest(r, first[r][2]), dec_mid(r - 1), ocs[r - 1])
        keep_mid(r - 1, out)
        begin_cross(r)
    for r in every:
        cross_b[r], _ = run(
            lambda: cross_back(r, cqs[r], rest[r][3], crossed[r][0], docs_in[r], crossed[r][1]),
            None,
        )
        dcqs[r] = shift(cross_b[r][0], 1)
        back[r], out = run(
            lambda: enc_back(cross_b[r][1], cross_b[r][2], rest[r][0], rest[r][2], rest[r][1]),
            dec_mid(rows - 1) if r == 0 else None,
        )
        if r == 0:
            keep_mid(rows - 1, out)
        last[r], dlast[r] = run(lambda: enc_last(r), lambda: dec_last(r))

    def enc_parts():
        gain_rows = [sum(v) for v in zip(*[[last[r][4], back[r][8], back[r][9]] for r in every])]
        return [jnp.concatenate(gain_rows, 0), jnp.stack([last[r][3] for r in every])]

    def dec_parts():
        gain_rows = [sum(v) for v in zip(*[[dlast[r][8], dlast[r][3], mids[r][8]] for r in every])]
        both = [jnp.concatenate([mids[r][1], dlast[r][7]], 0) for r in every]
        return [jnp.concatenate(gain_rows, 0), jnp.stack(both)]

    gain_grads, results = lax.cond(on_decoder, dec_parts, enc_parts)
    gain_terms = jnp.pad(gain_grads.T, ((0, 0), (0, LANES - gain_grads.shape[0]))).astype(BF)

    def over_rows(lists):
        return [list(group) for group in zip(*lists)]

    enc_side = (
        over_rows([back[r][2], back[r][3], back[r][0], back[r][0], first[r][2], first[r][0]] for r in every),
        over_rows(
            [back[r][4], back[r][1], cross_b[r][1], cross_b[r][2], back[r][6]] + last[r][0:3]
            for r in every
        ),
    )
    dec_side = (
        over_rows(
            [mids[r][3], mids[r][4], dfirst[r][5], mids[r][6], dfirst[r][2], dfirst[r][0]]
            for r in every
        ),
        over_rows(
            [mids[r][5], x_in[r, ld:], dcqs[r], ocs[r], dlast[r][1]] + dlast[r][4:7] for r in every
        ),
    )
    if lax.axis_size("rows") == PEERS:
        sums = grad_sum((enc_side, dec_side), gain_terms)
    else:
        sums = plain_sum(on_decoder, (enc_side, dec_side), gain_terms)
    s_in, s_out, s_fi, s_cross, s_gain, s_fo = sums
    return (
        results[None],
        s_in[None],
        s_out[None],
        s_fi[None],
        s_fo[None],
        s_cross[None],
        s_gain[:, : gain_grads.shape[0]].T[None],
    )


def solution(mesh):
    placed = (
        P("section", "rows", None, None),
        P("rows", None),
        P("rows", None),
    ) + (P("section", None, None),) * 6
    return jax.shard_map(
        body,
        mesh=mesh,
        in_specs=placed,
        out_specs=(
            P("section", "rows", None, None),
            P("section", "rows", None),
            P("section", "rows", None),
            P("section", "rows", None),
            P("section", "rows", None),
            P("section", "rows", None),
            P("section", None, "rows"),
        ),
        check_vma=False,
    )
```

```python
import functools

import jax
import jax.numpy as jnp
from jax import lax
from jax.experimental import pallas as pl
from jax.experimental.pallas import tpu as pltpu
from jax.sharding import PartitionSpec as P

HEADS = 12
HEAD = 64
PAIR = 128
EPSILON = 1e-06
SCALE = 0.125
LOG2E = 1.4426950408889634
NEGATIVE = -1e30
GELU_C = 0.7978845608028654
GELU_A = 0.044715

BF = jnp.bfloat16
F32 = jnp.float32
NT = (((1,), (1,)), ((), ()))
NN = (((1,), (0,)), ((), ()))
TN = (((0,), (0,)), ((), ()))


def mm(a, b, dims=NN):
    return lax.dot_general(a, b, dims, preferred_element_type=F32)


MESH = pl.DeviceIdType.MESH
LANES = 256
VMEM_LIMIT = 56 * 1024 * 1024

NZ, NY, NC = 4, 2, 2
PEERS = NZ * NY * NC
C_LAG = 2
Y_LAG = C_LAG + 2
HOP = 2
RING = 6
AHEAD = 3
PANELS = 4

TALL = 1
LEFT_ORDER = (0, 2, 3, 4, 5)
PRODUCTS = ((0, 0), (1, 1), (2, 2), (3, 3), (4, 4), (5, 5), (5, 6), (5, 7))


def grad_sum_kernel(rows, token_counts, chunk_counts, *refs):
    lefts_of, rights_of, at = [], [], 0
    for _ in range(2):
        lefts_of.append([refs[at + rows * i : at + rows * (i + 1)] for i in range(6)])
        at += 6 * rows
        rights_of.append([refs[at + rows * i : at + rows * (i + 1)] for i in range(8)])
        at += 8 * rows
    gain_ref = refs[at]
    o_in, o_out, o_fi, o_cross, o_gain, o_fo = refs[at + 1 : at + 7]
    (
        xt, xt_tall, left_stage, tall_stage, tall_right, panels, ring,
        own, got_y, got_r, got_l,
        s_left, s_tall, s_right, s_panel,
        s_core, r_core, s_y, r_y, s_r, r_r, s_l, r_l,
    ) = refs[at + 7 :]
    chunks, height = own.shape[0], own.shape[3]
    sec, me = lax.axis_index("section"), lax.axis_index("rows")
    core, y, z = lax.rem(me, 2), lax.rem(me // 2, 2), me // 4
    by_core, by_y = me + 1 - 2 * core, me + 2 - 4 * y
    other, away = 1 - core, 1 - y
    bases = [sum(chunk_counts[:i]) for i in range(len(chunk_counts))]

    barrier = pltpu.get_barrier_semaphore()

    def greet(peer):
        pl.semaphore_signal(barrier, inc=1, device_id=(sec, peer), device_id_type=MESH)

    greet(by_core)
    greet(by_y)

    @pl.when(z > 0)
    def _():
        greet(me - 4)

    @pl.when(z < NZ - 1)
    def _():
        greet(me + 4)

    @pl.when((z > 0) & (z < NZ - 1))
    def _():
        pl.semaphore_wait(barrier, 4)

    @pl.when((z == 0) | (z == NZ - 1))
    def _():
        pl.semaphore_wait(barrier, 3)


    def each(act):
        for side in range(2):

            @pl.when(sec == side)
            def _(side=side):
                act(side)

    def row_copies(sources, columns, dst, sems, side):
        tokens = token_counts[side]
        return [
            pltpu.make_async_copy(
                src if columns is None else src.at[:, columns],
                dst.at[pl.ds(r * tokens, tokens)],
                sems.at[r],
            )
            for r, src in enumerate(sources)
        ]

    def start_all(copies):
        for copy in copies:
            copy.start()

    def wait_all(copies):
        for copy in copies:
            copy.wait()

    def left_copies(q, side):
        source = lefts_of[side][LEFT_ORDER[q]]
        return row_copies(source, None, left_stage.at[q % 2], s_left.at[q % 2], side)

    def tall_copies(side):
        return row_copies(lefts_of[side][1], None, tall_stage, s_tall, side)

    def tall_right_copies(side):
        return row_copies(rights_of[side][1], None, tall_right, s_right, side)

    def panel_copies(p, i, slot, side):
        columns = pl.ds(pl.multiple_of(i * LANES, LANES), LANES)
        return row_copies(
            rights_of[side][PRODUCTS[p][1]], columns, panels.at[slot], s_panel.at[slot], side
        )

    def for_panel(t, act):
        slot = lax.rem(t, PANELS)
        for p in range(len(PRODUCTS)):
            if p != TALL:

                @pl.when((t >= bases[p]) & (t < bases[p] + chunk_counts[p]))
                def _(p=p):
                    each(lambda side: act(p, t - bases[p], slot, side))

    def flip(side, stage, columns, put):
        for at in range(0, rows * token_counts[side], LANES):
            tokens = slice(at, at + LANES)
            put(tokens, stage[tokens, columns].astype(F32).T.astype(BF))

    def build_left(q):
        def act(side):
            wait_all(left_copies(q, side))
            for at in range(0, xt.shape[0], LANES):

                def put(tokens, block, at=at):
                    xt[at : at + LANES, tokens] = block

                flip(side, left_stage.at[q % 2], slice(at, at + LANES), put)
            if q + 2 < len(LEFT_ORDER):
                start_all(left_copies(q + 2, side))

        each(act)

    groups = xt_tall.shape[0] // LANES
    tall_rows = xt_tall.shape[0] // PEERS

    def build_tall(part):
        columns = pl.ds(pl.multiple_of(part * LANES, LANES), LANES)
        targets = LANES // tall_rows

        def act(side):
            def put(tokens, block):
                for k in range(targets):
                    for j in range(tall_rows // 16):
                        to = j * LANES + (part * targets + k) * 16
                        xt_tall[pl.ds(pl.multiple_of(to, 16), 16), tokens] = block[
                            k * tall_rows + j * 16 : k * tall_rows + (j + 1) * 16
                        ]

            flip(side, tall_stage, columns, put)

        each(act)

    def send_core(j):
        slot = lax.rem(j, RING)
        return pltpu.make_async_remote_copy(
            src_ref=ring.at[slot, :, :, other],
            dst_ref=own.at[j],
            send_sem=s_core.at[j],
            recv_sem=r_core.at[j],
            device_id=(sec, by_core),
            device_id_type=MESH,
        )

    def send_y(j):
        return pltpu.make_async_remote_copy(
            src_ref=own.at[j, :, away],
            dst_ref=got_y.at[j],
            send_sem=s_y.at[j],
            recv_sem=r_y.at[j],
            device_id=(sec, by_y),
            device_id_type=MESH,
        )

    def send_right(j, at):
        return pltpu.make_async_remote_copy(
            src_ref=own.at[j, pl.ds(at + 1, NZ - 1 - at), y],
            dst_ref=got_r.at[j, pl.ds(at + 1, NZ - 1 - at)],
            send_sem=s_r.at[j],
            recv_sem=r_r.at[j],
            device_id=(sec, me + 4),
            device_id_type=MESH,
        )

    def send_left(j, at):
        return pltpu.make_async_remote_copy(
            src_ref=own.at[j, pl.ds(0, at), y],
            dst_ref=got_l.at[j, pl.ds(0, at)],
            send_sem=s_l.at[j],
            recv_sem=r_l.at[j],
            device_id=(sec, me - 4),
            device_id_type=MESH,
        )

    def add_into(dst, src):
        dst[...] = (dst[...].astype(F32) + src[...].astype(F32)).astype(BF)


    def compute(s):
        slot = lax.rem(s, RING)

        def put_panel(value):
            for t in range(PEERS):
                ring[slot, t // 4, t // 2 % 2, t % 2] = value[t * height : (t + 1) * height]

        for p in range(len(PRODUCTS)):
            left = PRODUCTS[p][0]

            @pl.when((s >= bases[p]) & (s < bases[p] + chunk_counts[p]))
            def _(p=p, left=left):
                if p != TALL:
                    if p == 0 or PRODUCTS[p - 1][0] != left:

                        @pl.when(s == bases[p])
                        def _():
                            build_left(LEFT_ORDER.index(left))

                    where = lax.rem(s, PANELS)

                    def act(side):
                        wait_all(panel_copies(p, s - bases[p], where, side))
                        tokens = rows * token_counts[side]
                        put_panel(mm(xt[:, :tokens], panels[where, :tokens, :]).astype(BF))

                    each(act)
                else:
                    rows_at = pl.ds(pl.multiple_of((s - bases[p]) * LANES, LANES), LANES)

                    @pl.when(s == bases[p])
                    def _():
                        each(lambda side: wait_all(tall_right_copies(side)))

                    def act(side):
                        tokens = rows * token_counts[side]
                        for k in range(tall_right.shape[1] // LANES):
                            value = mm(
                                xt_tall[rows_at, :tokens],
                                tall_right[:tokens, k * LANES : (k + 1) * LANES],
                            ).astype(BF)
                            for t in range(PEERS):
                                ring[slot, t // 4, t // 2 % 2, t % 2, k * 16 : (k + 1) * 16] = value[
                                    t * 16 : (t + 1) * 16
                                ]

                    each(act)

        @pl.when(s == chunks - 1)
        def _():
            put_panel(gain_ref[...])


    def open_first(side):
        start_all(left_copies(0, side))
        for t in range(AHEAD):
            start_all(panel_copies(0, t, t % PANELS, side))

    each(open_first)

    def step(s, carry):
        @pl.when(s + AHEAD < chunks - 1)
        def _():
            for_panel(
                s + AHEAD,
                lambda p, i, slot, side: start_all(panel_copies(p, i, slot, side)),
            )

        @pl.when((s >= RING) & (s < chunks))
        def _():
            send_core(s - RING).wait_send()

        @pl.when(s < chunks)
        def _():
            compute(s)
            send_core(s).start()

        @pl.when(s == 1)
        def _():
            each(lambda side: start_all(tall_copies(side)))

        @pl.when(s == 4)
        def _():
            each(lambda side: wait_all(tall_copies(side)))
            each(lambda side: start_all(left_copies(1, side)))
            each(lambda side: start_all(tall_right_copies(side)))

        @pl.when((s >= 4) & (s < 4 + groups))
        def _():
            build_tall(s - 4)

        j_c = s - C_LAG

        @pl.when((j_c >= 0) & (j_c < chunks))
        def _():
            send_core(j_c).wait_recv()
            slot = lax.rem(j_c, RING)
            for a in range(NZ):
                for b in range(NY):
                    add_into(own.at[j_c, a, b], ring.at[slot, a, b, core])
            send_y(j_c).start()

        j_y = s - Y_LAG

        @pl.when((j_y >= 0) & (j_y < chunks))
        def _():
            send_y(j_y).wait_recv()
            for t in range(NZ):
                add_into(own.at[j_y, t, y], got_y.at[j_y, t])

        for at in range(NZ - 1):
            j_r = s - Y_LAG - HOP * at

            @pl.when((z == at) & (j_r >= 0) & (j_r < chunks))
            def _(at=at, j_r=j_r):
                if at > 0:
                    send_right(j_r, at - 1).wait_recv()
                    for t in range(at + 1, NZ):
                        add_into(own.at[j_r, t, y], got_r.at[j_r, t])
                send_right(j_r, at).start()

        for at in range(1, NZ):
            j_l = s - Y_LAG - HOP * (NZ - 1 - at)

            @pl.when((z == at) & (j_l >= 0) & (j_l < chunks))
            def _(at=at, j_l=j_l):
                if at < NZ - 1:
                    send_left(j_l, at + 1).wait_recv()
                    for t in range(at):
                        add_into(own.at[j_l, t, y], got_l.at[j_l, t])
                send_left(j_l, at).start()

        return carry

    lax.fori_loop(0, chunks + Y_LAG + HOP * (NZ - 1), step, 0)


    def finish(j):
        @pl.when(z == NZ - 1)
        def _():
            send_right(j, NZ - 2).wait_recv()

        @pl.when(z == 0)
        def _():
            send_left(j, 1).wait_recv()

        send_y(j).wait_send()

        @pl.when(j >= chunks - RING)
        def _():
            send_core(j).wait_send()

        for at in range(NZ):

            @pl.when(z == at)
            def _(at=at):
                if at < NZ - 1:
                    send_right(j, at).wait_send()
                if at > 0:
                    send_left(j, at).wait_send()

    def total(j, part):
        mine = own[j, z, y, part].astype(F32)
        right = got_r[j, z, part].astype(F32)
        left = got_l[j, z, part].astype(F32)
        return mine + jnp.where(z > 0, right, 0.0) + jnp.where(z < NZ - 1, left, 0.0)

    def close(out, base, count, column):
        def panel(i, carry):
            finish(base + i)
            at = pl.ds(pl.multiple_of(column + i * LANES, LANES), LANES)
            out[:, at] = total(base + i, pl.ds(0, height))
            return carry

        lax.fori_loop(0, count, panel, 0)

    dim = xt.shape[0]
    close(o_fi, bases[0], chunk_counts[0], 0)

    def tall_out(i, carry):
        finish(bases[TALL] + i)
        at = pl.ds(pl.multiple_of(i * 16, 16), 16)
        for k in range(tall_right.shape[1] // LANES):
            o_fo[at, k * LANES : (k + 1) * LANES] = total(bases[TALL] + i, pl.ds(k * 16, 16))
        return carry

    lax.fori_loop(0, chunk_counts[TALL], tall_out, 0)
    close(o_cross, bases[2], chunk_counts[2], 0)
    close(o_cross, bases[3], chunk_counts[3], dim)
    close(o_out, bases[4], chunk_counts[4], 0)
    for k in range(3):
        close(o_in, bases[5 + k], chunk_counts[5 + k], k * dim)
    close(o_gain, chunks - 1, 1, 0)


def grad_sum(sides, gain_terms):
    rows = len(sides[0][0][0])
    token_counts = tuple(lefts[0][0].shape[0] for lefts, _ in sides)
    tokens = rows * max(token_counts)
    lefts, rights = sides[0]
    dim, tall = lefts[0][0].shape[1], lefts[TALL][0].shape[1]
    height = dim // PEERS
    chunk_counts = tuple(
        lefts[a][0].shape[1] * rights[b][0].shape[1] // (dim * LANES) for a, b in PRODUCTS
    )
    chunks = sum(chunk_counts) + 1
    flat = [v for lefts, rights in sides for group in lefts + rights for v in group]
    half = (chunks, NZ, NY, height, LANES)
    fourth = (chunks, NZ, height, LANES)
    width = lambda *which: sum(rights[i][0].shape[1] for i in which)
    out_shape = [
        jax.ShapeDtypeStruct(s, F32)
        for s in (
            (height, width(5, 6, 7)),
            (height, width(4)),
            (height, width(0)),
            (height, width(2, 3)),
            (height, LANES),
            (tall // PEERS, width(1)),
        )
    ]
    return pl.pallas_call(
        functools.partial(grad_sum_kernel, rows, token_counts, chunk_counts),
        in_specs=[pl.BlockSpec(memory_space=pl.ANY)] * len(flat)
        + [pl.BlockSpec(memory_space=pltpu.VMEM)],
        out_specs=[pl.BlockSpec(memory_space=pltpu.VMEM)] * len(out_shape),
        out_shape=out_shape,
        scratch_shapes=[
            pltpu.VMEM((dim, tokens), BF),
            pltpu.VMEM((tall, tokens), BF),
            pltpu.VMEM((2, tokens, dim), BF),
            pltpu.VMEM((tokens, tall), BF),
            pltpu.VMEM((tokens, width(1)), BF),
            pltpu.VMEM((PANELS, tokens, LANES), BF),
            pltpu.VMEM((RING, NZ, NY, NC, height, LANES), BF),
            pltpu.VMEM(half, BF),
            pltpu.VMEM(fourth, BF),
            pltpu.VMEM(fourth, BF),
            pltpu.VMEM(fourth, BF),
            pltpu.SemaphoreType.DMA((2, rows)),
            pltpu.SemaphoreType.DMA((rows,)),
            pltpu.SemaphoreType.DMA((rows,)),
            pltpu.SemaphoreType.DMA((PANELS, rows)),
        ]
        + [pltpu.SemaphoreType.DMA((chunks,))] * 8,
        compiler_params=pltpu.CompilerParams(
            collective_id=1, has_side_effects=True, vmem_limit_bytes=VMEM_LIMIT
        ),
    )(*flat, gain_terms)


def plain_sum(on_decoder, sides, gain_terms):
    def terms(lefts, rights):
        parts = [
            sum(mm(a, b, TN) for a, b in zip(lefts[i], rights[j])).astype(BF) for i, j in PRODUCTS
        ]
        return [
            jnp.concatenate(parts[5:8], 1),
            parts[4],
            parts[0],
            jnp.concatenate(parts[2:4], 1),
            parts[1],
        ]

    pieces = lax.cond(on_decoder, lambda: terms(*sides[1]), lambda: terms(*sides[0]))
    pieces.insert(4, gain_terms)
    return [
        lax.psum_scatter(piece, "rows", scatter_dimension=0, tiled=True).astype(F32)
        for piece in pieces
    ]


def low_half(rows):
    return lax.broadcasted_iota(jnp.int32, (rows, PAIR), 1) < HEAD


def masked_scores(q, k, qx, kx, head, causal):
    lo_q, lo_k = low_half(q.shape[0]), low_half(k.shape[0])
    if head == 0:
        qh, kh = jnp.where(lo_q, q, qx), jnp.where(lo_k, k, kx)
    else:
        qh, kh = jnp.where(lo_q, qx, q), jnp.where(lo_k, kx, k)
    s = mm(kh, qh, NT)
    if causal:
        key_at = lax.broadcasted_iota(jnp.int32, s.shape, 0)
        query_at = lax.broadcasted_iota(jnp.int32, s.shape, 1)
        s = jnp.where(key_at <= query_at, s, NEGATIVE)
    return s


def pair_backward(q, k, v, qx, kx, o, do, lse, causal):
    kt = k.astype(F32).T.astype(BF)
    spread = (do.astype(F32) * o.astype(F32)).T
    low_q, low_k = low_half(q.shape[0]), low_half(k.shape[0])
    zero_q, zero_k = jnp.zeros_like(q), jnp.zeros_like(k)
    dqs, grads = [], []

    def begin(head):
        s = mm(pick(head, low_k, k, kx), pick(head, low_q, q, qx), NT)
        return causal_only(s) if causal else s, mm(pick(head, low_k, v, zero_k), do, NT)

    def end(head, values):
        s, dp = values
        half = slice(head * HEAD, (head + 1) * HEAD)
        p = jnp.exp2(s * (SCALE * LOG2E) - lse[head : head + 1])
        ds = (p * (dp - jnp.sum(spread[half], axis=0, keepdims=True))).astype(BF)
        dqs.append(mm(kt[half], ds))
        grads.append(
            (mm(ds, pick(head, low_q, q, zero_q)), mm(p.astype(BF), pick(head, low_q, do, zero_q)))
        )

    in_order(range(2), begin, end)
    (dk0, dv0), (dk1, dv1) = grads
    return jnp.concatenate(dqs, axis=0).T * SCALE, (dk0 + dk1) * SCALE, dv0 + dv1


def attn_bwd_kernel(
    q_ref, k_ref, v_ref, qx_ref, kx_ref, o_ref, do_ref, lse_ref, dq_ref, dk_ref, dv_ref, *, causal
):
    dq, dk, dv = pair_backward(
        q_ref[...], k_ref[...], v_ref[...], qx_ref[0], kx_ref[0], o_ref[...], do_ref[...],
        lse_ref[0], causal,
    )
    dq_ref[...] = dq.astype(BF)
    dk_ref[...] = dk.astype(BF)
    dv_ref[...] = dv.astype(BF)


def column_block(length, first):
    return pl.BlockSpec((length, PAIR), lambda p: (0, first + p))


def mask_block(length, row):
    return pl.BlockSpec((1, length, PAIR), lambda p: (row, 0, 0))


def pair_block(count_q):
    return pl.BlockSpec((1, 2, count_q), lambda p: (p, 0, 0))


def params(**more):
    return pltpu.CompilerParams(vmem_limit_bytes=VMEM_LIMIT, **more)


def attention_backward(q_in, k_in, v_in, qx, kx, row, firsts, mixed, grad_mixed, lse, causal):
    count_q, count_k, pairs = q_in.shape[0], k_in.shape[0], HEADS // 2
    width = HEADS * HEAD
    return pl.pallas_call(
        functools.partial(attn_bwd_kernel, causal=causal),
        grid=(pairs,),
        in_specs=[
            column_block(count_q, firsts[0]),
            column_block(count_k, firsts[1]),
            column_block(count_k, firsts[2]),
            mask_block(count_q, row),
            mask_block(count_k, row),
            column_block(count_q, 0),
            column_block(count_q, 0),
            pair_block(count_q),
        ],
        out_specs=[
            column_block(count_q, 0),
            column_block(count_k, 0),
            column_block(count_k, 0),
        ],
        out_shape=[
            jax.ShapeDtypeStruct((count_q, width), BF),
            jax.ShapeDtypeStruct((count_k, width), BF),
            jax.ShapeDtypeStruct((count_k, width), BF),
        ],
        compiler_params=params(),
    )(q_in, k_in, v_in, qx, kx, mixed, grad_mixed, lse)


BLOCK = 256
SLICE = 512


def inverse_rms(v):
    return lax.rsqrt(jnp.mean(v * v, -1, keepdims=True) + EPSILON)


def norm(v, gain):
    return (v * inverse_rms(v) * gain).astype(BF)


def norm_back(v, gain, grad):
    inv = inverse_rms(v)
    scaled = grad * gain
    along = jnp.mean(scaled * v, -1, keepdims=True)
    return (
        inv * scaled - v * (inv * inv * inv * along),
        jnp.sum(grad * v * inv, 0, keepdims=True),
    )


def gelu(x):
    return 0.5 * x * (1.0 + jnp.tanh(GELU_C * (x + GELU_A * x * x * x)))


def gelu_parts(x):
    square = x * x
    t = jnp.tanh(GELU_C * x * (1.0 + GELU_A * square))
    half = 0.5 * (1.0 + t)
    slope = half + 0.5 * x * (1.0 - t * t) * (GELU_C * (1.0 + 3.0 * GELU_A * square))
    return x * half, slope


class Fetch:
    def __init__(self, sources, held, sems):
        self.copies = [
            pltpu.make_async_copy(src, dst, sems.at[i])
            for i, (src, dst) in enumerate(zip(sources, held))
        ]
        self.held = held
        self.first = pl.program_id(0) == 0

        @pl.when(self.first)
        def _():
            for copy in self.copies:
                copy.start()

    def __getitem__(self, i):
        @pl.when(self.first)
        def _():
            self.copies[i].wait()

        return self.held[i]


def add_gain(ref, part):
    @pl.when(pl.program_id(0) == 0)
    def _():
        ref[...] = part

    @pl.when(pl.program_id(0) > 0)
    def _():
        ref[...] += part


def block_call(kernel, steps, ins, weights, outs, gain_outs=0):
    specs, arrays = [], []
    for array, row, first in ins:
        columns = array.shape[-1]
        if row is None:
            specs.append(pl.BlockSpec((BLOCK, columns), lambda i, f=first: (f + i, 0)))
        else:
            specs.append(
                pl.BlockSpec((None, BLOCK, columns), lambda i, r=row, f=first: (r, f + i, 0))
            )
        arrays.append(array)
    gains = [w for w in weights if w.dtype == F32]
    mats = [w for w in weights if w.dtype != F32]
    specs += [pl.BlockSpec((1, g.shape[1]), lambda i: (0, 0)) for g in gains]
    specs += [pl.BlockSpec(memory_space=pl.ANY)] * len(mats)
    dim = gains[0].shape[1]
    count = len(mats)

    def run(*refs):
        held, sems = refs[-1 - count : -1], refs[-1]
        at = len(arrays) + len(gains)
        fetch = Fetch(refs[at : at + count], held, sems)
        kernel(refs[: len(arrays)], [g[...] for g in refs[len(arrays) : at]], fetch, refs[at + count : -1 - count])

    return pl.pallas_call(
        run,
        grid=(steps,),
        in_specs=specs,
        out_specs=[pl.BlockSpec((BLOCK, c), lambda i: (i, 0)) for c, _ in outs]
        + [pl.BlockSpec((1, dim), lambda i: (0, 0))] * gain_outs,
        out_shape=[jax.ShapeDtypeStruct((steps * BLOCK, c), t) for c, t in outs]
        + [jax.ShapeDtypeStruct((1, dim), F32)] * gain_outs,
        scratch_shapes=[pltpu.VMEM(m.shape, m.dtype) for m in mats]
        + [pltpu.SemaphoreType.DMA((count,))],
        compiler_params=params(),
    )(*arrays, *gains, *mats)


def project_kernel(ins, gains, w, outs):
    (x,), (g0,), (n_ref, packed_ref) = ins, gains, outs
    n = norm(x[...].astype(F32), g0)
    n_ref[...] = n
    wa = w[0]
    dim = x.shape[1]
    for at in range(0, wa.shape[1], dim):
        packed_ref[:, at : at + dim] = mm(n, wa[:, at : at + dim]).astype(BF)


def ffn_up(m, wf, wd, acc, u_ref, act_ref):
    half = wd.shape[0]
    for at in range(0, half, SLICE):
        gate = mm(m, wf[:, at : at + SLICE])
        up = mm(m, wf[:, half + at : half + at + SLICE])
        u_ref[:, at : at + SLICE] = gate.astype(BF)
        u_ref[:, half + at : half + at + SLICE] = up.astype(BF)
        act = (gelu(gate) * up).astype(BF)
        if act_ref is not None:
            act_ref[:, at : at + SLICE] = act
        acc = acc + mm(act, wd[at : at + SLICE, :])
    return acc


def ffn_down(branch, wf, wd, u_ref, du_ref, act_ref):
    half = wd.shape[0]
    dm = None
    for at in range(0, half, SLICE):
        d_act = mm(branch, wd[at : at + SLICE, :], NT)
        gate = u_ref[:, at : at + SLICE].astype(F32)
        up = u_ref[:, half + at : half + at + SLICE].astype(F32)
        value, slope = gelu_parts(gate)
        if act_ref is not None:
            act_ref[:, at : at + SLICE] = (value * up).astype(BF)
        d_gate = (d_act * up * slope).astype(BF)
        d_up = (d_act * value).astype(BF)
        du_ref[:, at : at + SLICE] = d_gate
        du_ref[:, half + at : half + at + SLICE] = d_up
        part = mm(d_gate, wf[:, at : at + SLICE], NT) + mm(
            d_up, wf[:, half + at : half + at + SLICE], NT
        )
        dm = part if dm is None else dm + part
    return dm


def dec_query_kernel(ins, gains, w, outs):
    (o, x), (g1,), (d1_ref, c_ref, cq_ref) = ins, gains, outs
    d1 = x[...].astype(F32) + mm(o[...], w[0][...])
    d1_ref[...] = d1
    c = norm(d1, g1)
    c_ref[...] = c
    cq_ref[...] = mm(c, w[1][:, : c.shape[1]]).astype(BF)


def dec_ffn_kernel(ins, gains, w, outs):
    (oc, d1, cot), (g2,) = ins, gains
    doc_ref, out_ref, dd2_ref, m_ref, act_ref, du_ref, branch_ref, u_ref, dg2_ref = outs
    width = oc.shape[1]
    out_proj = w[0]
    d2 = d1[...] + mm(oc[...], out_proj[:, width:], NT)
    m = norm(d2, g2)
    m_ref[...] = m
    wf, wd = w[1], w[2]
    out_ref[...] = ffn_up(m, wf, wd, d2, u_ref, act_ref)
    dm = ffn_down(cot[...], wf, wd, u_ref, du_ref, None)
    back, dg2 = norm_back(d2, g2, dm)
    dd2 = cot[...].astype(F32) + back
    dd2_ref[...] = dd2
    branch = dd2.astype(BF)
    branch_ref[...] = branch
    doc_ref[...] = mm(branch, out_proj[:, width:]).astype(BF)
    add_gain(dg2_ref, dg2)


def enc_back_kernel(ins, gains, w, outs):
    (dk, dv, e1_in, e2_in, u), (g1, g2) = ins, gains
    mem_ref, fb_ref, m_ref, act_ref, du_ref, de1_ref, ab_ref, do_ref, dg1_ref, dg2_ref = outs
    wc = w[0]
    width = dk.shape[1]
    e1, e2 = e1_in[...], e2_in[...]
    dmem = mm(dk[...], wc[:, :width], NT) + mm(dv[...], wc[:, width:], NT)
    mem_ref[...] = norm(e2, g1)
    de2, dg1 = norm_back(e2, g1, dmem)
    fb = de2.astype(BF)
    fb_ref[...] = fb
    m_ref[...] = norm(e1, g2)
    wd, wf = w[1], w[2]
    dm = ffn_down(fb, wf, wd, u, du_ref, act_ref)
    back, dg2 = norm_back(e1, g2, dm)
    de1 = de2 + back
    de1_ref[...] = de1
    ab = de1.astype(BF)
    ab_ref[...] = ab
    do_ref[...] = mm(ab, w[3][...], NT).astype(BF)
    add_gain(dg1_ref, dg1)
    add_gain(dg2_ref, dg2)


def dec_back_kernel(ins, gains, w, outs):
    (dcq, d1_in, dd2), (g1,), (dd1_ref, ab_ref, do_ref, dg1_ref) = ins, gains, outs
    d1 = d1_in[...]
    dc = mm(dcq[...], w[0][:, : dcq.shape[1]], NT)
    back, dg1 = norm_back(d1, g1, dc)
    dd1 = dd2[...] + back
    dd1_ref[...] = dd1
    ab = dd1.astype(BF)
    ab_ref[...] = ab
    do_ref[...] = mm(ab, w[1][...], NT).astype(BF)
    add_gain(dg1_ref, dg1)


def input_grad_kernel(ins, gains, w, outs):
    (dq, dk, dv, x, grad), (g0,), (dx_ref, dg0_ref) = ins, gains, outs
    wa = w[0]
    width = dq.shape[1]
    dn = (
        mm(dq[...], wa[:, :width], NT)
        + mm(dk[...], wa[:, width : 2 * width], NT)
        + mm(dv[...], wa[:, 2 * width :], NT)
    )
    back, dg0 = norm_back(x[...].astype(F32), g0, dn)
    dx_ref[...] = grad[...] + back
    add_gain(dg0_ref, dg0)


class Mover:
    def __init__(self, sems):
        self.sems, self.used, self.stores = sems, 0, []

    def copy(self, src, dst):
        made = pltpu.make_async_copy(src, dst, self.sems.at[self.used])
        self.used += 1
        made.start()
        return made

    def store(self, src, dst):
        self.stores.append(self.copy(src, dst))

    def drain(self):
        for made in self.stores:
            made.wait()


def pair_columns(first, p):
    return slice(first + p * PAIR, first + (p + 1) * PAIR)


def pick(head, low, a, b):
    return jnp.where(low, a, b) if head % 2 == 0 else jnp.where(low, b, a)


def in_order(items, begin, end, lead=1):
    waiting = []
    for item in items:
        waiting.append((item, begin(item)))
        if len(waiting) > lead:
            end(*waiting.pop(0))
    while waiting:
        end(*waiting.pop(0))


def attend(q_ref, kv_ref, firsts, qx, kx, o_ref, lse_ref, causal):
    count_q, count_k = qx.shape[0], kx.shape[0]
    low_q, low_k = low_half(count_q), low_half(count_k)
    ones = jnp.ones((8, count_k), BF)
    values, outs = {}, {}

    def begin(head):
        q = q_ref[:, pair_columns(firsts[0], head // 2)]
        k = kv_ref[:, pair_columns(firsts[1], head // 2)]
        s = mm(pick(head, low_k, k, kx), pick(head, low_q, q, qx), NT)
        return causal_only(s) if causal else s

    def end(head, s):
        p = head // 2
        if head % 2 == 0:
            values[p] = kv_ref[:, pair_columns(firsts[2], p)].astype(F32).T.astype(BF)
        vt = values[p][(head % 2) * HEAD : (head % 2 + 1) * HEAD]
        top = jnp.max(s, axis=0, keepdims=True)
        e = jnp.exp2((s - top) * (SCALE * LOG2E)).astype(BF)
        mixed = mm(jnp.concatenate([vt, ones], axis=0), e)
        total = mixed[HEAD : HEAD + 1]
        outs[head] = mixed[:HEAD] * (1.0 / total)
        lse_ref[p, head % 2 : head % 2 + 1, :] = top * (SCALE * LOG2E) + jnp.log2(total)
        if head % 2 == 1:
            both = jnp.concatenate([outs.pop(head - 1), outs.pop(head)], axis=0)
            o_ref[:, pair_columns(0, p)] = both.T.astype(BF)

    in_order(range(HEADS), begin, end)


def causal_only(s):
    key_at = lax.broadcasted_iota(jnp.int32, s.shape, 0)
    query_at = lax.broadcasted_iota(jnp.int32, s.shape, 1)
    return jnp.where(key_at <= query_at, s, NEGATIVE)


def attend_kernel(firsts, row, causal, same, *refs):
    if same:
        q_ref, (qx_ref, kx_ref, o_ref, lse_ref) = refs[0], refs[1:]
        kv_ref = q_ref
    else:
        q_ref, kv_ref, qx_ref, kx_ref, o_ref, lse_ref = refs
    attend(q_ref, kv_ref, firsts, qx_ref[row], kx_ref[row], o_ref, lse_ref, causal)


def attention_forward(q_in, kv_in, qx, kx, row, firsts, causal):
    count_q = q_in.shape[0]
    ins = [q_in] if kv_in is None else [q_in, kv_in]
    vmem = pl.BlockSpec(memory_space=pltpu.VMEM)
    return pl.pallas_call(
        functools.partial(attend_kernel, firsts, row, causal, kv_in is None),
        in_specs=[vmem] * (len(ins) + 2),
        out_specs=[vmem] * 2,
        out_shape=[
            jax.ShapeDtypeStruct((count_q, HEADS * HEAD), BF),
            jax.ShapeDtypeStruct((HEADS // 2, 2, count_q), F32),
        ],
        compiler_params=params(),
    )(*ins, qx, kx)


def enc_attend_kernel(row, x_hbm, qx_hbm, kx_hbm, g0, wa_hbm, *refs):
    outs, (n_v, packed_v, o_v, lse_v, x, qx, kx, wa, sems) = refs[:4], refs[4:]
    move = Mover(sems)
    got_x = move.copy(x_hbm.at[row], x)
    got_wa = move.copy(wa_hbm, wa)
    got_masks = move.copy(qx_hbm.at[row], qx), move.copy(kx_hbm.at[row], kx)
    tokens, dim = x.shape
    got_x.wait()
    blocks = [slice(at, at + BLOCK) for at in range(0, tokens, BLOCK)]
    for b in blocks:
        n_v[b] = norm(x[b].astype(F32), g0[...])
    move.store(n_v, outs[0])
    got_wa.wait()
    for b in blocks:
        for at in range(0, wa.shape[1], dim):
            packed_v[b, at : at + dim] = mm(n_v[b], wa[:, at : at + dim]).astype(BF)
    move.store(packed_v, outs[1])
    for made in got_masks:
        made.wait()
    attend(packed_v, packed_v, (0, dim, 2 * dim), qx[...], kx[...], o_v, lse_v, False)
    move.store(o_v, outs[2])
    move.store(lse_v, outs[3])
    move.drain()


def enc_rest_kernel(row, x_hbm, o_hbm, g1, g2, wo_hbm, wf_hbm, wd_hbm, wc_hbm, *refs):
    outs, (e1_v, u_v, e2_v, sent_v, x, o, wo, wf, wd, wc, sems) = refs[:4], refs[4:]
    move = Mover(sems)
    got = [
        move.copy(a, b)
        for a, b in (
            (x_hbm.at[row], x), (o_hbm, o), (wo_hbm, wo), (wf_hbm, wf), (wd_hbm, wd), (wc_hbm, wc)
        )
    ]
    for made in got[:3]:
        made.wait()
    blocks = [slice(at, at + BLOCK) for at in range(0, x.shape[0], BLOCK)]
    for b in blocks:
        e1_v[b] = x[b].astype(F32) + mm(o[b], wo[...])
        move.store(e1_v.at[b], outs[0].at[b])
    for made in got[3:]:
        made.wait()
    for b in blocks:
        e1 = e1_v[b]
        e2 = ffn_up(norm(e1, g2[...]), wf, wd, e1, u_v.at[b], None)
        e2_v[b] = e2
        sent_v[b] = mm(norm(e2, g1[...]), wc[...]).astype(BF)
        for src, dst in ((u_v, outs[1]), (e2_v, outs[2]), (sent_v, outs[3])):
            move.store(src.at[b], dst.at[b])
    move.drain()


HBM = pl.BlockSpec(memory_space=pl.ANY)
VMEM = pl.BlockSpec(memory_space=pltpu.VMEM)


def moved_call(kernel, ins, specs, outs, held, copies):
    return list(
        pl.pallas_call(
            kernel,
            in_specs=specs,
            out_specs=[HBM] * len(outs),
            out_shape=[jax.ShapeDtypeStruct(s, t) for s, t in outs],
            scratch_shapes=[pltpu.VMEM(s, t) for s, t in outs + held]
            + [pltpu.SemaphoreType.DMA((copies,))],
            compiler_params=params(),
        )(*ins)
    )


def enc_attend(row, x_in, qx, kx, g0, wa):
    tokens, dim = x_in.shape[1:]
    width = wa.shape[1] // 3
    kept = [
        ((tokens, dim), BF),
        ((tokens, wa.shape[1]), BF),
        ((tokens, width), BF),
        ((HEADS // 2, 2, tokens), F32),
    ]
    held = [(x_in.shape[1:], BF), (qx.shape[1:], BF), (kx.shape[1:], BF), (wa.shape, BF)]
    return moved_call(
        functools.partial(enc_attend_kernel, row),
        (x_in, qx, kx, g0, wa),
        [HBM] * 3 + [VMEM] + [HBM],
        kept,
        held,
        8,
    )


def enc_rest(row, x_in, o, g1, g2, wo, wf, wd, wc):
    tokens, dim = x_in.shape[1:]
    kept = [
        ((tokens, dim), F32),
        ((tokens, wf.shape[1]), BF),
        ((tokens, dim), F32),
        ((tokens, wc.shape[1]), BF),
    ]
    held = [(x_in.shape[1:], BF), (o.shape, BF)] + [(w.shape, BF) for w in (wo, wf, wd, wc)]
    return moved_call(
        functools.partial(enc_rest_kernel, row),
        (x_in, o, g1, g2, wo, wf, wd, wc),
        [HBM] * 2 + [VMEM] * 2 + [HBM] * 4,
        kept,
        held,
        6 + 4 * (tokens // BLOCK),
    )


def nothing_kernel(*refs):
    pass


def unwritten(shapes):
    return pl.pallas_call(
        nothing_kernel,
        out_specs=[pl.BlockSpec(memory_space=pl.ANY)] * len(shapes),
        out_shape=[jax.ShapeDtypeStruct(s.shape, s.dtype) for s in shapes],
    )()


def by_section(on_decoder, encoder, decoder):
    enc_shapes = jax.eval_shape(encoder) if encoder else []
    dec_shapes = jax.eval_shape(decoder) if decoder else []
    none = lambda: []
    encoder, decoder = encoder or none, decoder or none
    pool = lambda shapes: list(unwritten(shapes)) if shapes else []
    both = lax.cond(
        on_decoder,
        lambda: pool(enc_shapes) + list(decoder()),
        lambda: list(encoder()) + pool(dec_shapes),
    )
    return both[: len(enc_shapes)], both[len(enc_shapes) :]


def segment_ids(lengths, span_len):
    positions = jnp.arange(span_len, dtype=jnp.int32)[None, :]
    seg, end = jnp.zeros((lengths.shape[0], span_len), jnp.int32), 0
    for j in range(lengths.shape[1]):
        end = end + lengths[:, j : j + 1]
        seg = seg + (positions >= end).astype(jnp.int32)
    return seg


def mask_lanes(seg, count):
    hit = seg[:, :, None] == jnp.arange(HEAD, dtype=jnp.int32)[None, None, :]
    member = hit.astype(BF)
    other = jnp.where(
        jnp.arange(HEAD, dtype=jnp.int32)[None, None, :] < count,
        jnp.where(hit, 0.0, NEGATIVE),
        0.0,
    ).astype(BF)
    return (
        jnp.concatenate([member, member], -1),
        jnp.concatenate([other, other], -1),
    )


def shift(x, by):
    pairs = [(0, 1)] if by > 0 else [(1, 0)]
    return lax.ppermute(x, "section", pairs)


def body(
    section_input, enc_lengths, dec_lengths, attn_in, attn_out, ffn_in, ffn_out, cross_weight, gains
):
    wa, wo, wf, wd, wc = attn_in[0], attn_out[0], ffn_in[0], ffn_out[0], cross_weight[0]
    g0, g1, g2 = gains[0, 0:1], gains[0, 1:2], gains[0, 2:3]
    x_in = section_input[0]
    rows, le, dim = x_in.shape
    ld = le // 2
    width = wo.shape[0]
    docs = enc_lengths.shape[1]
    enc_qx, enc_kx = mask_lanes(segment_ids(enc_lengths, le), docs)
    dec_qx, dec_kx = mask_lanes(segment_ids(dec_lengths, ld), docs)
    on_decoder = lax.axis_index("section") == 1
    steps_e, steps_d = le // BLOCK, ld // BLOCK
    columns = width // PAIR
    own = (0, columns, 2 * columns)
    across = (0, 0, columns)
    inner = wf.shape[1]

    def project(r, steps):
        return list(
            block_call(project_kernel, steps, [(x_in, r, 0)], [g0, wa], [(dim, BF), (3 * width, BF)])
        )

    def dec_first(r):
        n, packed = project(r, steps_d)
        o, lse = attention_forward(packed, None, dec_qx, dec_kx, r, (0, width, 2 * width), True)
        d1, c, cq = block_call(
            dec_query_kernel,
            steps_d,
            [(o, None, 0), (x_in, r, 0)],
            [g1, wo, wc],
            [(dim, F32), (dim, BF), (width, BF)],
        )
        return [n, packed, o, lse, d1, c, cq]

    def cross(r, cq, sent):
        return list(attention_forward(cq, sent, dec_qx, enc_kx, r, (0, 0, width), False))

    def dec_ffn(r, oc, d1):
        return list(
            block_call(
                dec_ffn_kernel,
                steps_d,
                [(oc, None, 0), (d1, None, 0), (x_in, r, ld // BLOCK)],
                [g2, wc, wf, wd],
                [
                    (width, BF),
                    (dim, F32),
                    (dim, F32),
                    (dim, BF),
                    (wd.shape[0], BF),
                    (inner, BF),
                    (dim, BF),
                    (inner, BF),
                ],
                1,
            )
        )

    def cross_back(r, cq, sent, oc, doc, lse):
        return list(
            attention_backward(cq, sent, sent, dec_qx, enc_kx, r, across, oc, doc, lse, False)
        )

    def enc_back(dk, dv, e1, e2, u):
        return list(
            block_call(
                enc_back_kernel,
                steps_e,
                [(dk, None, 0), (dv, None, 0), (e1, None, 0), (e2, None, 0), (u, None, 0)],
                [g1, g2, wc, wd, wf, wo],
                [
                    (dim, BF),
                    (dim, BF),
                    (dim, BF),
                    (wd.shape[0], BF),
                    (inner, BF),
                    (dim, F32),
                    (dim, BF),
                    (width, BF),
                ],
                2,
            )
        )

    def self_back(r, steps, masks, causal, packed, o, lse, do, grad):
        dq, dk, dv = attention_backward(
            packed, packed, packed, *masks, r, own, o, do, lse, causal
        )
        dx, dg0 = block_call(
            input_grad_kernel,
            steps,
            [(dq, None, 0), (dk, None, 0), (dv, None, 0), (x_in, r, 0), (grad, None, 0)],
            [g0, wa],
            [(dim, F32)],
            1,
        )
        return [dq, dk, dv, dx, dg0]

    def dec_back(dcq, d1, dd2):
        return list(
            block_call(
                dec_back_kernel,
                steps_d,
                [(dcq, None, 0), (d1, None, 0), (dd2, None, 0)],
                [g1, wc, wo],
                [(dim, F32), (dim, BF), (width, BF)],
                1,
            )
        )

    every = range(rows)
    state = [on_decoder]

    def run(encoder, decoder, *ready):
        held = lax.optimization_barrier(tuple(state) + ready)[0]
        out = by_section(held, encoder, decoder)
        state[1:] = [(out[0] or out[1])[0]]
        return out

    def slots():
        return [None] * rows

    first, rest, dfirst, cqs, crossed, ocs = slots(), slots(), slots(), slots(), slots(), slots()
    mids, docs_in, cross_b, dcqs, back, last, dlast = (slots() for _ in range(7))

    def begin_cross(r, beside=None):
        crossed[r], out = run(lambda: cross(r, cqs[r], rest[r][3]), beside)
        ocs[r] = shift(crossed[r][0], 1)
        return out

    def dec_mid(r):
        return lambda: dec_ffn(r, ocs[r], dfirst[r][4])

    def keep_mid(r, out):
        mids[r] = out
        docs_in[r] = shift(out[0], -1)

    def dec_last(r):
        p = dec_back(dcqs[r], dfirst[r][4], mids[r][2])
        n, packed, o, lse = dfirst[r][:4]
        return p + self_back(r, steps_d, (dec_qx, dec_kx), True, packed, o, lse, p[2], p[0])

    def enc_last(r):
        return self_back(
            r, steps_e, (enc_qx, enc_kx), False, *first[r][1:4], back[r][7], back[r][5]
        )

    def enc_first(r):
        return lambda: enc_attend(r, x_in, enc_qx, enc_kx, g0, wa)

    def enc_then(r):
        return lambda: enc_rest(r, x_in, first[r][2], g1, g2, wo, wf, wd, wc)

    first[0], dfirst[0] = run(enc_first(0), lambda: dec_first(0))
    cqs[0] = shift(dfirst[0][6], -1)
    rest[0], more = run(enc_then(0), lambda: [v for r in every[1:] for v in dec_first(r)])
    begin_cross(0)
    for r in every[1:]:
        dfirst[r] = more[7 * (r - 1) : 7 * r]
        cqs[r] = shift(dfirst[r][6], -1)
    for r in every[1:]:
        first[r], _ = run(enc_first(r), None)
        rest[r], out = run(enc_then(r), dec_mid(r - 1), ocs[r - 1])
        keep_mid(r - 1, out)
        begin_cross(r)
    for r in every:
        cross_b[r], _ = run(
            lambda: cross_back(r, cqs[r], rest[r][3], crossed[r][0], docs_in[r], crossed[r][1]),
            None,
        )
        dcqs[r] = shift(cross_b[r][0], 1)
        back[r], out = run(
            lambda: enc_back(cross_b[r][1], cross_b[r][2], rest[r][0], rest[r][2], rest[r][1]),
            dec_mid(rows - 1) if r == 0 else None,
        )
        if r == 0:
            keep_mid(rows - 1, out)
        last[r], dlast[r] = run(lambda: enc_last(r), lambda: dec_last(r))

    def enc_parts():
        gain_rows = [sum(v) for v in zip(*[[last[r][4], back[r][8], back[r][9]] for r in every])]
        return [jnp.concatenate(gain_rows, 0), jnp.stack([last[r][3] for r in every])]

    def dec_parts():
        gain_rows = [sum(v) for v in zip(*[[dlast[r][8], dlast[r][3], mids[r][8]] for r in every])]
        both = [jnp.concatenate([mids[r][1], dlast[r][7]], 0) for r in every]
        return [jnp.concatenate(gain_rows, 0), jnp.stack(both)]

    gain_grads, results = lax.cond(on_decoder, dec_parts, enc_parts)
    gain_terms = jnp.pad(gain_grads.T, ((0, 0), (0, LANES - gain_grads.shape[0]))).astype(BF)

    def over_rows(lists):
        return [list(group) for group in zip(*lists)]

    enc_side = (
        over_rows([back[r][2], back[r][3], back[r][0], back[r][0], first[r][2], first[r][0]] for r in every),
        over_rows(
            [back[r][4], back[r][1], cross_b[r][1], cross_b[r][2], back[r][6]] + last[r][0:3]
            for r in every
        ),
    )
    dec_side = (
        over_rows(
            [mids[r][3], mids[r][4], dfirst[r][5], mids[r][6], dfirst[r][2], dfirst[r][0]]
            for r in every
        ),
        over_rows(
            [mids[r][5], x_in[r, ld:], dcqs[r], ocs[r], dlast[r][1]] + dlast[r][4:7] for r in every
        ),
    )
    if lax.axis_size("rows") == PEERS:
        sums = grad_sum((enc_side, dec_side), gain_terms)
    else:
        sums = plain_sum(on_decoder, (enc_side, dec_side), gain_terms)
    s_in, s_out, s_fi, s_cross, s_gain, s_fo = sums
    return (
        results[None],
        s_in[None],
        s_out[None],
        s_fi[None],
        s_fo[None],
        s_cross[None],
        s_gain[:, : gain_grads.shape[0]].T[None],
    )


def solution(mesh):
    placed = (
        P("section", "rows", None, None),
        P("rows", None),
        P("rows", None),
    ) + (P("section", None, None),) * 6
    return jax.shard_map(
        body,
        mesh=mesh,
        in_specs=placed,
        out_specs=(
            P("section", "rows", None, None),
            P("section", "rows", None),
            P("section", "rows", None),
            P("section", "rows", None),
            P("section", "rows", None),
            P("section", "rows", None),
            P("section", None, "rows"),
        ),
        check_vma=False,
    )
```

```python
import functools

import jax
import jax.numpy as jnp
from jax import lax
from jax.experimental import pallas as pl
from jax.experimental.pallas import tpu as pltpu
from jax.sharding import PartitionSpec as P

HEADS = 12
HEAD = 64
PAIR = 128
EPSILON = 1e-06
SCALE = 0.125
LOG2E = 1.4426950408889634
NEGATIVE = -1e30
GELU_C = 0.7978845608028654
GELU_A = 0.044715

BF = jnp.bfloat16
F32 = jnp.float32
NT = (((1,), (1,)), ((), ()))
NN = (((1,), (0,)), ((), ()))
TN = (((0,), (0,)), ((), ()))


def mm(a, b, dims=NN):
    return lax.dot_general(a, b, dims, preferred_element_type=F32)


MESH = pl.DeviceIdType.MESH
LANES = 256
VMEM_LIMIT = 56 * 1024 * 1024
SUM_VMEM = 60 * 1024 * 1024

NZ, NY, NC = 4, 2, 2
PEERS = NZ * NY * NC
C_LAG = 2
Y_LAG = C_LAG + 2
HOP = 2
RING = 6
AHEAD = 3
PANELS = 4

TALL = 1
LEFT_ORDER = (0, 2, 3, 4, 5)
PRODUCTS = ((0, 0), (1, 1), (2, 2), (3, 3), (4, 4), (5, 5), (5, 6), (5, 7))


def grad_sum_kernel(rows, token_counts, chunk_counts, unit_steps, *refs):
    remaining = list(refs)

    def take(groups):
        out = [remaining[rows * i : rows * (i + 1)] for i in range(groups)]
        del remaining[: rows * groups]
        return out

    def take_one():
        return remaining.pop(0)

    lefts_of, rights_of = [], []
    for side in range(2):
        lefts_of.append(take(6))
        rights_of.append(take(5 if side == 0 else 8))
    packed_of, o_of, do_of, lse_of, de1_of = take(5)
    out_of, dx_of = take(2)
    gain_rows = [[None] + take(2), take(3)]
    x_ref, qx_ref, kx_ref, wa_ref, g0_ref = [take_one() for _ in range(5)]
    o_in, o_out, o_fi, o_cross, o_gain, o_fo, o_results = [take_one() for _ in range(7)]
    (
        xt, xt_tall, left_stage, tall_stage, tall_right, panels, ring,
        own, got_y, got_r, got_l,
        s_left, s_tall, s_right, s_panel,
        s_core, r_core, s_y, r_y, s_r, r_r, s_l, r_l,
        d_packed, wa, att, qx, kx, lse, x_stage, grad_stage, dx_stage, dg0,
        s_att, s_const, s_lse, s_block, s_out, s_dec,
    ) = remaining
    chunks, height, dim = own.shape[0], own.shape[3], xt.shape[0]
    sec, me = lax.axis_index("section"), lax.axis_index("rows")
    core, y, z = lax.rem(me, 2), lax.rem(me // 2, 2), me // 4
    by_core, by_y = me + 1 - 2 * core, me + 2 - 4 * y
    other, away = 1 - core, 1 - y
    bases = [sum(chunk_counts[:i]) for i in range(len(chunk_counts))]

    barrier = pltpu.get_barrier_semaphore()

    def greet(peer):
        pl.semaphore_signal(barrier, inc=1, device_id=(sec, peer), device_id_type=MESH)

    greet(by_core)
    greet(by_y)

    @pl.when(z > 0)
    def _():
        greet(me - 4)

    @pl.when(z < NZ - 1)
    def _():
        greet(me + 4)

    @pl.when((z > 0) & (z < NZ - 1))
    def _():
        pl.semaphore_wait(barrier, 4)

    @pl.when((z == 0) | (z == NZ - 1))
    def _():
        pl.semaphore_wait(barrier, 3)


    def each(act):
        for side in range(2):

            @pl.when(sec == side)
            def _(side=side):
                act(side)

    def row_copies(sources, columns, dst, sems, side):
        tokens = token_counts[side]
        return [
            pltpu.make_async_copy(
                src if columns is None else src.at[:, columns],
                dst.at[pl.ds(r * tokens, tokens)],
                sems.at[r],
            )
            for r, src in enumerate(sources)
        ]

    def start_all(copies):
        for copy in copies:
            copy.start()

    def wait_all(copies):
        for copy in copies:
            copy.wait()

    def left_copies(q, side):
        source = lefts_of[side][LEFT_ORDER[q]]
        return row_copies(source, None, left_stage.at[q % 2], s_left.at[q % 2], side)

    def tall_copies(side):
        return row_copies(lefts_of[side][1], None, tall_stage, s_tall, side)

    def tall_right_copies(side):
        return row_copies(rights_of[side][1], None, tall_right, s_right, side)

    def panel_copies(p, i, slot, side):
        if PRODUCTS[p][1] >= len(rights_of[side]):
            return []
        columns = pl.ds(pl.multiple_of(i * LANES, LANES), LANES)
        return row_copies(
            rights_of[side][PRODUCTS[p][1]], columns, panels.at[slot], s_panel.at[slot], side
        )

    def for_panel(t, act):
        slot = lax.rem(t, PANELS)
        for p in range(len(PRODUCTS)):
            if p != TALL:

                @pl.when((t >= bases[p]) & (t < bases[p] + chunk_counts[p]))
                def _(p=p):
                    each(lambda side: act(p, t - bases[p], slot, side))

    def flip(side, stage, columns, put):
        for at in range(0, rows * token_counts[side], LANES):
            tokens = slice(at, at + LANES)
            put(tokens, stage[tokens, columns].astype(F32).T.astype(BF))

    def build_left(q):
        def act(side):
            wait_all(left_copies(q, side))
            for at in range(0, xt.shape[0], LANES):

                def put(tokens, block, at=at):
                    xt[at : at + LANES, tokens] = block

                flip(side, left_stage.at[q % 2], slice(at, at + LANES), put)
            if q + 2 < len(LEFT_ORDER):
                start_all(left_copies(q + 2, side))

        each(act)

    groups = xt_tall.shape[0] // LANES
    tall_rows = xt_tall.shape[0] // PEERS

    def build_tall(part):
        columns = pl.ds(pl.multiple_of(part * LANES, LANES), LANES)
        targets = LANES // tall_rows

        def act(side):
            def put(tokens, block):
                for k in range(targets):
                    for j in range(tall_rows // 16):
                        to = j * LANES + (part * targets + k) * 16
                        xt_tall[pl.ds(pl.multiple_of(to, 16), 16), tokens] = block[
                            k * tall_rows + j * 16 : k * tall_rows + (j + 1) * 16
                        ]

            flip(side, tall_stage, columns, put)

        each(act)

    def send_core(j):
        slot = lax.rem(j, RING)
        return pltpu.make_async_remote_copy(
            src_ref=ring.at[slot, :, :, other],
            dst_ref=own.at[j],
            send_sem=s_core.at[j],
            recv_sem=r_core.at[j],
            device_id=(sec, by_core),
            device_id_type=MESH,
        )

    def send_y(j):
        return pltpu.make_async_remote_copy(
            src_ref=own.at[j, :, away],
            dst_ref=got_y.at[j],
            send_sem=s_y.at[j],
            recv_sem=r_y.at[j],
            device_id=(sec, by_y),
            device_id_type=MESH,
        )

    def send_right(j, at):
        return pltpu.make_async_remote_copy(
            src_ref=own.at[j, pl.ds(at + 1, NZ - 1 - at), y],
            dst_ref=got_r.at[j, pl.ds(at + 1, NZ - 1 - at)],
            send_sem=s_r.at[j],
            recv_sem=r_r.at[j],
            device_id=(sec, me + 4),
            device_id_type=MESH,
        )

    def send_left(j, at):
        return pltpu.make_async_remote_copy(
            src_ref=own.at[j, pl.ds(0, at), y],
            dst_ref=got_l.at[j, pl.ds(0, at)],
            send_sem=s_l.at[j],
            recv_sem=r_l.at[j],
            device_id=(sec, me - 4),
            device_id_type=MESH,
        )

    def add_into(dst, src):
        dst[...] = (dst[...].astype(F32) + src[...].astype(F32)).astype(BF)


    def compute(s):
        slot = lax.rem(s, RING)

        def put_panel(value):
            for t in range(PEERS):
                ring[slot, t // 4, t // 2 % 2, t % 2] = value[t * height : (t + 1) * height]

        for p in range(len(PRODUCTS)):
            left = PRODUCTS[p][0]

            @pl.when((s >= bases[p]) & (s < bases[p] + chunk_counts[p]))
            def _(p=p, left=left):
                if p != TALL:
                    if p == 0 or PRODUCTS[p - 1][0] != left:

                        @pl.when(s == bases[p])
                        def _():
                            build_left(LEFT_ORDER.index(left))

                    where = lax.rem(s, PANELS)

                    def act(side):
                        wait_all(panel_copies(p, s - bases[p], where, side))
                        tokens = rows * token_counts[side]
                        if PRODUCTS[p][1] < len(rights_of[side]):
                            right = panels[where, :tokens, :]
                        else:
                            first = (PRODUCTS[p][1] - 5) * dim + (s - bases[p]) * LANES
                            right = d_packed[:, pl.ds(pl.multiple_of(first, LANES), LANES)]
                        put_panel(mm(xt[:, :tokens], right).astype(BF))

                    each(act)
                else:
                    rows_at = pl.ds(pl.multiple_of((s - bases[p]) * LANES, LANES), LANES)

                    @pl.when(s == bases[p])
                    def _():
                        each(lambda side: wait_all(tall_right_copies(side)))

                    def act(side):
                        tokens = rows * token_counts[side]
                        for k in range(tall_right.shape[1] // LANES):
                            value = mm(
                                xt_tall[rows_at, :tokens],
                                tall_right[:tokens, k * LANES : (k + 1) * LANES],
                            ).astype(BF)
                            for t in range(PEERS):
                                ring[slot, t // 4, t // 2 % 2, t % 2, k * 16 : (k + 1) * 16] = value[
                                    t * 16 : (t + 1) * 16
                                ]

                    each(act)

        @pl.when(s == chunks - 1)
        def _():
            def act(side):
                parts = []
                for group in gain_rows[side]:
                    total_row = dg0[...]
                    if group is not None:
                        total_row = group[0][...]
                        for ref in group[1:]:
                            total_row = total_row + ref[...]
                    parts.append(total_row)
                parts.append(jnp.zeros((LANES - len(parts), dim), F32))
                put_panel(jnp.concatenate(parts, axis=0).T.astype(BF))

            each(act)


    attn_units, block_units, first_block = unit_steps
    tokens_e = token_counts[0]
    per_row = tokens_e // BLOCK
    const_copies = [
        pltpu.make_async_copy(src, dst, s_const.at[i])
        for i, (src, dst) in enumerate(((qx_ref, qx), (kx_ref, kx), (wa_ref, wa)))
    ]
    lse_copies = [
        pltpu.make_async_copy(ref, lse.at[r], s_lse.at[r]) for r, ref in enumerate(lse_of)
    ]

    def attn_loads(u, act):
        slot, p = lax.rem(u, 2), lax.rem(u, HEADS // 2)
        for r in range(rows):

            @pl.when(u // (HEADS // 2) == r)
            def _(r=r):
                at = lambda first: pl.ds(pl.multiple_of(first + p * PAIR, PAIR), PAIR)
                sources = [packed_of[r].at[:, at(k * dim)] for k in range(3)]
                sources += [o_of[r].at[:, at(0)], do_of[r].at[:, at(0)]]
                act(
                    [
                        pltpu.make_async_copy(src, att.at[slot, k], s_att.at[slot, k])
                        for k, src in enumerate(sources)
                    ]
                )

    def attn_unit(u):
        slot, p, r = lax.rem(u, 2), lax.rem(u, HEADS // 2), u // (HEADS // 2)
        attn_loads(u, wait_all)
        q, k, v, o, do = [att[slot, i] for i in range(5)]
        grads = pair_backward(q, k, v, qx[r], kx[r], o, do, lse[r, p], False)
        where = pl.ds(pl.multiple_of(r * tokens_e, tokens_e), tokens_e)
        for i, value in enumerate(grads):
            at = pl.ds(pl.multiple_of(i * dim + p * PAIR, PAIR), PAIR)
            d_packed[where, at] = value.astype(BF)

    def block_loads(v, act):
        slot = lax.rem(v, 2)
        where = pl.ds(pl.multiple_of(lax.rem(v, per_row) * BLOCK, BLOCK), BLOCK)
        for r in range(rows):

            @pl.when(v // per_row == r)
            def _(r=r):
                act(
                    [
                        pltpu.make_async_copy(x_ref.at[r, where], x_stage.at[slot], s_block.at[slot, 0]),
                        pltpu.make_async_copy(
                            de1_of[r].at[where], grad_stage.at[slot], s_block.at[slot, 1]
                        ),
                    ]
                )

    def block_store(v):
        slot = lax.rem(v, 2)
        where = pl.ds(pl.multiple_of(lax.rem(v, per_row) * BLOCK, BLOCK), BLOCK)
        return pltpu.make_async_copy(
            dx_stage.at[slot], o_results.at[v // per_row, where], s_out.at[slot]
        )

    def block_unit(v):
        slot = lax.rem(v, 2)
        block_loads(v, wait_all)

        @pl.when(v == 0)
        def _():
            const_copies[2].wait()
            dg0[...] = jnp.zeros_like(dg0)

        @pl.when(v >= 2)
        def _():
            block_store(v - 2).wait()

        where = pl.ds(pl.multiple_of(v * BLOCK, BLOCK), BLOCK)
        dn = None
        for i in range(3):
            part = mm(d_packed[where, i * dim : (i + 1) * dim], wa[:, i * dim : (i + 1) * dim], NT)
            dn = part if dn is None else dn + part
        back, gain_part = norm_back(x_stage[slot].astype(F32), g0_ref[...], dn)
        dg0[...] += gain_part
        dx_stage[slot] = grad_stage[slot] + back
        block_store(v).start()

    def dec_results(store):
        half = token_counts[1]
        parts = [
            (ref, stage.at[r], o_results.at[r, k * half : (k + 1) * half], s_dec.at[k, r])
            for k, (group, stage) in enumerate(((out_of, grad_stage), (dx_of, dx_stage)))
            for r, ref in enumerate(group)
        ]
        return [
            pltpu.make_async_copy(held, dst, sem) if store else pltpu.make_async_copy(src, held, sem)
            for src, held, dst, sem in parts
        ]

    def side_work(s):
        @pl.when(s == 0)
        def _():
            start_all(lse_copies)
            start_all(const_copies)
            for v in range(2):
                block_loads(jnp.int32(v), start_all)

        u = s // 2

        @pl.when((lax.rem(s, 2) == 0) & (u < attn_units))
        def _():
            attn_loads(u, start_all)

        @pl.when((lax.rem(s, 2) == 0) & (u >= 1) & (u <= attn_units))
        def _():
            @pl.when(u == 1)
            def _():
                wait_all(lse_copies)
                wait_all(const_copies[:2])

            attn_unit(u - 1)

        v = (s - first_block) // 2

        @pl.when((lax.rem(s, 2) == 0) & (s >= first_block) & (v < block_units))
        def _():
            block_unit(v)

            @pl.when(v + 2 < block_units)
            def _():
                block_loads(v + 2, start_all)


    def open_first(side):
        start_all(left_copies(0, side))
        for t in range(AHEAD):
            start_all(panel_copies(0, t, t % PANELS, side))

    each(open_first)

    @pl.when(sec == 1)
    def _():
        start_all(dec_results(False))

    def step(s, carry):
        @pl.when(s + AHEAD < chunks - 1)
        def _():
            for_panel(
                s + AHEAD,
                lambda p, i, slot, side: start_all(panel_copies(p, i, slot, side)),
            )

        @pl.when((s >= RING) & (s < chunks))
        def _():
            send_core(s - RING).wait_send()

        @pl.when(s < chunks)
        def _():
            compute(s)
            send_core(s).start()

        @pl.when(sec == 0)
        def _():
            side_work(s)

        @pl.when((sec == 1) & (s == RING))
        def _():
            wait_all(dec_results(False))
            start_all(dec_results(True))

        @pl.when(s == 1)
        def _():
            each(lambda side: start_all(tall_copies(side)))

        @pl.when(s == 4)
        def _():
            each(lambda side: wait_all(tall_copies(side)))
            each(lambda side: start_all(left_copies(1, side)))
            each(lambda side: start_all(tall_right_copies(side)))

        @pl.when((s >= 4) & (s < 4 + groups))
        def _():
            build_tall(s - 4)

        j_c = s - C_LAG

        @pl.when((j_c >= 0) & (j_c < chunks))
        def _():
            send_core(j_c).wait_recv()
            slot = lax.rem(j_c, RING)
            for a in range(NZ):
                for b in range(NY):
                    add_into(own.at[j_c, a, b], ring.at[slot, a, b, core])
            send_y(j_c).start()

        j_y = s - Y_LAG

        @pl.when((j_y >= 0) & (j_y < chunks))
        def _():
            send_y(j_y).wait_recv()
            for t in range(NZ):
                add_into(own.at[j_y, t, y], got_y.at[j_y, t])

        for at in range(NZ - 1):
            j_r = s - Y_LAG - HOP * at

            @pl.when((z == at) & (j_r >= 0) & (j_r < chunks))
            def _(at=at, j_r=j_r):
                if at > 0:
                    send_right(j_r, at - 1).wait_recv()
                    for t in range(at + 1, NZ):
                        add_into(own.at[j_r, t, y], got_r.at[j_r, t])
                send_right(j_r, at).start()

        for at in range(1, NZ):
            j_l = s - Y_LAG - HOP * (NZ - 1 - at)

            @pl.when((z == at) & (j_l >= 0) & (j_l < chunks))
            def _(at=at, j_l=j_l):
                if at < NZ - 1:
                    send_left(j_l, at + 1).wait_recv()
                    for t in range(at):
                        add_into(own.at[j_l, t, y], got_l.at[j_l, t])
                send_left(j_l, at).start()

        return carry

    lax.fori_loop(0, chunks + Y_LAG + HOP * (NZ - 1), step, 0)


    def finish(j):
        @pl.when(z == NZ - 1)
        def _():
            send_right(j, NZ - 2).wait_recv()

        @pl.when(z == 0)
        def _():
            send_left(j, 1).wait_recv()

        send_y(j).wait_send()

        @pl.when(j >= chunks - RING)
        def _():
            send_core(j).wait_send()

        for at in range(NZ):

            @pl.when(z == at)
            def _(at=at):
                if at < NZ - 1:
                    send_right(j, at).wait_send()
                if at > 0:
                    send_left(j, at).wait_send()

    def total(j, part):
        mine = own[j, z, y, part].astype(F32)
        right = got_r[j, z, part].astype(F32)
        left = got_l[j, z, part].astype(F32)
        return mine + jnp.where(z > 0, right, 0.0) + jnp.where(z < NZ - 1, left, 0.0)

    def close(out, base, count, column):
        def panel(i, carry):
            finish(base + i)
            at = pl.ds(pl.multiple_of(column + i * LANES, LANES), LANES)
            out[:, at] = total(base + i, pl.ds(0, height))
            return carry

        lax.fori_loop(0, count, panel, 0)

    close(o_fi, bases[0], chunk_counts[0], 0)

    def tall_out(i, carry):
        finish(bases[TALL] + i)
        at = pl.ds(pl.multiple_of(i * 16, 16), 16)
        for k in range(tall_right.shape[1] // LANES):
            o_fo[at, k * LANES : (k + 1) * LANES] = total(bases[TALL] + i, pl.ds(k * 16, 16))
        return carry

    lax.fori_loop(0, chunk_counts[TALL], tall_out, 0)
    close(o_cross, bases[2], chunk_counts[2], 0)
    close(o_cross, bases[3], chunk_counts[3], dim)
    close(o_out, bases[4], chunk_counts[4], 0)
    for k in range(3):
        close(o_in, bases[5 + k], chunk_counts[5 + k], k * dim)
    close(o_gain, chunks - 1, 1, 0)

    @pl.when(sec == 0)
    def _():
        for v in range(max(0, block_units - 2), block_units):
            block_store(jnp.int32(v)).wait()

    @pl.when(sec == 1)
    def _():
        wait_all(dec_results(True))


def grad_sum(sides, kept, decoded, gain_rows, shared):
    (enc_lefts, enc_rights), (dec_lefts, dec_rights) = sides
    x_in, qx, kx, wa, g0 = shared
    rows = len(enc_lefts[0])
    token_counts = (enc_lefts[0][0].shape[0], dec_lefts[0][0].shape[0])
    tokens = rows * max(token_counts)
    dim, tall = dec_lefts[0][0].shape[1], dec_lefts[TALL][0].shape[1]
    height = dim // PEERS
    chunk_counts = tuple(
        dec_lefts[a][0].shape[1] * dec_rights[b][0].shape[1] // (dim * LANES) for a, b in PRODUCTS
    )
    chunks = sum(chunk_counts) + 1
    attn_units, block_units = rows * HEADS // 2, rows * token_counts[0] // BLOCK
    unit_steps = (attn_units, block_units, 2 * attn_units + 2)
    flat = lambda groups: [v for group in groups for v in group]
    moved = flat(enc_lefts + enc_rights + dec_lefts + dec_rights + kept + decoded)
    gains = flat(gain_rows[0] + gain_rows[1])
    half = (chunks, NZ, NY, height, LANES)
    fourth = (chunks, NZ, height, LANES)
    width = lambda *which: sum(dec_rights[i][0].shape[1] for i in which)
    out_shape = [
        jax.ShapeDtypeStruct(s, F32)
        for s in (
            (height, width(5, 6, 7)),
            (height, width(4)),
            (height, width(0)),
            (height, width(2, 3)),
            (height, LANES),
            (tall // PEERS, width(1)),
            x_in.shape,
        )
    ]
    hbm, vmem = pl.BlockSpec(memory_space=pl.ANY), pl.BlockSpec(memory_space=pltpu.VMEM)
    dma = pltpu.SemaphoreType.DMA
    return pl.pallas_call(
        functools.partial(grad_sum_kernel, rows, token_counts, chunk_counts, unit_steps),
        in_specs=[hbm] * len(moved) + [vmem] * len(gains) + [hbm] * 4 + [vmem],
        out_specs=[vmem] * 6 + [hbm],
        out_shape=out_shape,
        scratch_shapes=[
            pltpu.VMEM((dim, tokens), BF),
            pltpu.VMEM((tall, tokens), BF),
            pltpu.VMEM((2, tokens, dim), BF),
            pltpu.VMEM((tokens, tall), BF),
            pltpu.VMEM((tokens, width(1)), BF),
            pltpu.VMEM((PANELS, tokens, LANES), BF),
            pltpu.VMEM((RING, NZ, NY, NC, height, LANES), BF),
            pltpu.VMEM(half, BF),
            pltpu.VMEM(fourth, BF),
            pltpu.VMEM(fourth, BF),
            pltpu.VMEM(fourth, BF),
            dma((2, rows)),
            dma((rows,)),
            dma((rows,)),
            dma((PANELS, rows)),
        ]
        + [dma((chunks,))] * 8
        + [
            pltpu.VMEM((rows * token_counts[0], 3 * dim), BF),
            pltpu.VMEM(wa.shape, BF),
            pltpu.VMEM((2, 5, token_counts[0], PAIR), BF),
            pltpu.VMEM(qx.shape, BF),
            pltpu.VMEM(kx.shape, BF),
            pltpu.VMEM((rows,) + kept[3][0].shape, F32),
            pltpu.VMEM((2, BLOCK, dim), BF),
            pltpu.VMEM((max(2, rows), BLOCK, dim), F32),
            pltpu.VMEM((max(2, rows), BLOCK, dim), F32),
            pltpu.VMEM((1, dim), F32),
            dma((2, 5)),
            dma((3,)),
            dma((rows,)),
            dma((2, 2)),
            dma((2,)),
            dma((2, rows)),
        ],
        compiler_params=pltpu.CompilerParams(
            collective_id=1, has_side_effects=True, vmem_limit_bytes=SUM_VMEM
        ),
    )(*moved, *gains, x_in, qx, kx, wa, g0)


def hand_over_kernel(rows, *refs):
    count = (len(refs) - 3) // 3
    gain_ref, sources, gain_out = refs[0], refs[1 : 1 + count], refs[1 + count]
    targets, held = refs[2 + count : 2 + 2 * count], refs[2 + 2 * count : 2 + 3 * count]
    gain, sems = refs[2 + 3 * count], refs[3 + 3 * count]
    moves = []
    for src, keep, dst in zip(sources, held, targets):
        for part in range(rows) if len(src.shape) == 3 else [slice(None)]:
            i = len(moves)
            load = pltpu.make_async_copy(src.at[part], keep.at[part], sems.at[0, i])
            load.start()
            moves.append((load, keep.at[part], dst.at[0].at[part], sems.at[1, i]))
    load_gain = pltpu.make_async_copy(gain_ref, gain, sems.at[0, len(moves)])
    load_gain.start()
    stores = []
    for load, keep, dst, sem in moves:
        load.wait()
        stores.append(pltpu.make_async_copy(keep, dst, sem))
        stores[-1].start()
    load_gain.wait()
    gain_out[0] = gain[...].T[: gain_out.shape[1]]
    for store in stores:
        store.wait()


def hand_over(gain, gain_rows, arrays):
    hbm, vmem = pl.BlockSpec(memory_space=pl.ANY), pl.BlockSpec(memory_space=pltpu.VMEM)
    rows = max(a.shape[0] for a in arrays if a.ndim == 3)
    return pl.pallas_call(
        functools.partial(hand_over_kernel, rows),
        in_specs=[hbm] * (1 + len(arrays)),
        out_specs=[vmem] + [hbm] * len(arrays),
        out_shape=[jax.ShapeDtypeStruct((1, gain_rows, gain.shape[0]), F32)]
        + [jax.ShapeDtypeStruct((1,) + a.shape, F32) for a in arrays],
        scratch_shapes=[pltpu.VMEM(a.shape, F32) for a in arrays]
        + [
            pltpu.VMEM(gain.shape, F32),
            pltpu.SemaphoreType.DMA((2, len(arrays) + rows)),
        ],
        compiler_params=pltpu.CompilerParams(vmem_limit_bytes=SUM_VMEM),
    )(gain, *arrays)


def plain_sum(on_decoder, sides, gain_terms):
    def terms(lefts, rights):
        parts = [
            sum(mm(a, b, TN) for a, b in zip(lefts[i], rights[j])).astype(BF) for i, j in PRODUCTS
        ]
        return [
            jnp.concatenate(parts[5:8], 1),
            parts[4],
            parts[0],
            jnp.concatenate(parts[2:4], 1),
            parts[1],
        ]

    pieces = lax.cond(on_decoder, lambda: terms(*sides[1]), lambda: terms(*sides[0]))
    pieces.insert(4, gain_terms)
    return [
        lax.psum_scatter(piece, "rows", scatter_dimension=0, tiled=True).astype(F32)
        for piece in pieces
    ]


def low_half(rows):
    return lax.broadcasted_iota(jnp.int32, (rows, PAIR), 1) < HEAD


def masked_scores(q, k, qx, kx, head, causal):
    lo_q, lo_k = low_half(q.shape[0]), low_half(k.shape[0])
    if head == 0:
        qh, kh = jnp.where(lo_q, q, qx), jnp.where(lo_k, k, kx)
    else:
        qh, kh = jnp.where(lo_q, qx, q), jnp.where(lo_k, kx, k)
    s = mm(kh, qh, NT)
    if causal:
        key_at = lax.broadcasted_iota(jnp.int32, s.shape, 0)
        query_at = lax.broadcasted_iota(jnp.int32, s.shape, 1)
        s = jnp.where(key_at <= query_at, s, NEGATIVE)
    return s


def pair_backward(q, k, v, qx, kx, o, do, lse, causal):
    kt = k.astype(F32).T.astype(BF)
    spread = (do.astype(F32) * o.astype(F32)).T
    low_q, low_k = low_half(q.shape[0]), low_half(k.shape[0])
    zero_q, zero_k = jnp.zeros_like(q), jnp.zeros_like(k)
    dqs, grads = [], []

    def begin(head):
        s = mm(pick(head, low_k, k, kx), pick(head, low_q, q, qx), NT)
        return causal_only(s) if causal else s, mm(pick(head, low_k, v, zero_k), do, NT)

    def end(head, values):
        s, dp = values
        half = slice(head * HEAD, (head + 1) * HEAD)
        p = jnp.exp2(s * (SCALE * LOG2E) - lse[head : head + 1])
        ds = (p * (dp - jnp.sum(spread[half], axis=0, keepdims=True))).astype(BF)
        dqs.append(mm(kt[half], ds))
        grads.append(
            (mm(ds, pick(head, low_q, q, zero_q)), mm(p.astype(BF), pick(head, low_q, do, zero_q)))
        )

    in_order(range(2), begin, end)
    (dk0, dv0), (dk1, dv1) = grads
    return jnp.concatenate(dqs, axis=0).T * SCALE, (dk0 + dk1) * SCALE, dv0 + dv1


def attn_bwd_kernel(
    q_ref, k_ref, v_ref, qx_ref, kx_ref, o_ref, do_ref, lse_ref, dq_ref, dk_ref, dv_ref, *, causal
):
    dq, dk, dv = pair_backward(
        q_ref[...], k_ref[...], v_ref[...], qx_ref[0], kx_ref[0], o_ref[...], do_ref[...],
        lse_ref[0], causal,
    )
    dq_ref[...] = dq.astype(BF)
    dk_ref[...] = dk.astype(BF)
    dv_ref[...] = dv.astype(BF)


def column_block(length, first):
    return pl.BlockSpec((length, PAIR), lambda p: (0, first + p))


def mask_block(length, row):
    return pl.BlockSpec((1, length, PAIR), lambda p: (row, 0, 0))


def pair_block(count_q):
    return pl.BlockSpec((1, 2, count_q), lambda p: (p, 0, 0))


def params(**more):
    return pltpu.CompilerParams(vmem_limit_bytes=VMEM_LIMIT, **more)


def attention_backward(q_in, k_in, v_in, qx, kx, row, firsts, mixed, grad_mixed, lse, causal):
    count_q, count_k, pairs = q_in.shape[0], k_in.shape[0], HEADS // 2
    width = HEADS * HEAD
    return pl.pallas_call(
        functools.partial(attn_bwd_kernel, causal=causal),
        grid=(pairs,),
        in_specs=[
            column_block(count_q, firsts[0]),
            column_block(count_k, firsts[1]),
            column_block(count_k, firsts[2]),
            mask_block(count_q, row),
            mask_block(count_k, row),
            column_block(count_q, 0),
            column_block(count_q, 0),
            pair_block(count_q),
        ],
        out_specs=[
            column_block(count_q, 0),
            column_block(count_k, 0),
            column_block(count_k, 0),
        ],
        out_shape=[
            jax.ShapeDtypeStruct((count_q, width), BF),
            jax.ShapeDtypeStruct((count_k, width), BF),
            jax.ShapeDtypeStruct((count_k, width), BF),
        ],
        compiler_params=params(),
    )(q_in, k_in, v_in, qx, kx, mixed, grad_mixed, lse)


BLOCK = 256
SLICE = 512


def inverse_rms(v):
    return lax.rsqrt(jnp.mean(v * v, -1, keepdims=True) + EPSILON)


def norm(v, gain):
    return (v * inverse_rms(v) * gain).astype(BF)


def norm_back(v, gain, grad):
    inv = inverse_rms(v)
    scaled = grad * gain
    along = jnp.mean(scaled * v, -1, keepdims=True)
    return (
        inv * scaled - v * (inv * inv * inv * along),
        jnp.sum(grad * v * inv, 0, keepdims=True),
    )


def gelu(x):
    return 0.5 * x * (1.0 + jnp.tanh(GELU_C * (x + GELU_A * x * x * x)))


def gelu_parts(x):
    square = x * x
    t = jnp.tanh(GELU_C * x * (1.0 + GELU_A * square))
    half = 0.5 * (1.0 + t)
    slope = half + 0.5 * x * (1.0 - t * t) * (GELU_C * (1.0 + 3.0 * GELU_A * square))
    return x * half, slope


class Fetch:
    def __init__(self, sources, held, sems):
        self.copies = [
            pltpu.make_async_copy(src, dst, sems.at[i])
            for i, (src, dst) in enumerate(zip(sources, held))
        ]
        self.held = held
        self.first = pl.program_id(0) == 0

        @pl.when(self.first)
        def _():
            for copy in self.copies:
                copy.start()

    def __getitem__(self, i):
        @pl.when(self.first)
        def _():
            self.copies[i].wait()

        return self.held[i]


def add_gain(ref, part):
    @pl.when(pl.program_id(0) == 0)
    def _():
        ref[...] = part

    @pl.when(pl.program_id(0) > 0)
    def _():
        ref[...] += part


def block_call(kernel, steps, ins, weights, outs, gain_outs=0):
    specs, arrays = [], []
    for array, row, first in ins:
        columns = array.shape[-1]
        if row is None:
            specs.append(pl.BlockSpec((BLOCK, columns), lambda i, f=first: (f + i, 0)))
        else:
            specs.append(
                pl.BlockSpec((None, BLOCK, columns), lambda i, r=row, f=first: (r, f + i, 0))
            )
        arrays.append(array)
    gains = [w for w in weights if w.dtype == F32]
    mats = [w for w in weights if w.dtype != F32]
    specs += [pl.BlockSpec((1, g.shape[1]), lambda i: (0, 0)) for g in gains]
    specs += [pl.BlockSpec(memory_space=pl.ANY)] * len(mats)
    dim = gains[0].shape[1]
    count = len(mats)

    def run(*refs):
        held, sems = refs[-1 - count : -1], refs[-1]
        at = len(arrays) + len(gains)
        fetch = Fetch(refs[at : at + count], held, sems)
        kernel(refs[: len(arrays)], [g[...] for g in refs[len(arrays) : at]], fetch, refs[at + count : -1 - count])

    return pl.pallas_call(
        run,
        grid=(steps,),
        in_specs=specs,
        out_specs=[pl.BlockSpec((BLOCK, c), lambda i: (i, 0)) for c, _ in outs]
        + [pl.BlockSpec((1, dim), lambda i: (0, 0))] * gain_outs,
        out_shape=[jax.ShapeDtypeStruct((steps * BLOCK, c), t) for c, t in outs]
        + [jax.ShapeDtypeStruct((1, dim), F32)] * gain_outs,
        scratch_shapes=[pltpu.VMEM(m.shape, m.dtype) for m in mats]
        + [pltpu.SemaphoreType.DMA((count,))],
        compiler_params=params(),
    )(*arrays, *gains, *mats)


def project_kernel(ins, gains, w, outs):
    (x,), (g0,), (n_ref, packed_ref) = ins, gains, outs
    n = norm(x[...].astype(F32), g0)
    n_ref[...] = n
    wa = w[0]
    dim = x.shape[1]
    for at in range(0, wa.shape[1], dim):
        packed_ref[:, at : at + dim] = mm(n, wa[:, at : at + dim]).astype(BF)


def ffn_up(m, wf, wd, acc, u_ref, act_ref):
    half = wd.shape[0]
    for at in range(0, half, SLICE):
        gate = mm(m, wf[:, at : at + SLICE])
        up = mm(m, wf[:, half + at : half + at + SLICE])
        u_ref[:, at : at + SLICE] = gate.astype(BF)
        u_ref[:, half + at : half + at + SLICE] = up.astype(BF)
        act = (gelu(gate) * up).astype(BF)
        if act_ref is not None:
            act_ref[:, at : at + SLICE] = act
        acc = acc + mm(act, wd[at : at + SLICE, :])
    return acc


def ffn_down(branch, wf, wd, u_ref, du_ref, act_ref):
    half = wd.shape[0]
    dm = None
    for at in range(0, half, SLICE):
        d_act = mm(branch, wd[at : at + SLICE, :], NT)
        gate = u_ref[:, at : at + SLICE].astype(F32)
        up = u_ref[:, half + at : half + at + SLICE].astype(F32)
        value, slope = gelu_parts(gate)
        if act_ref is not None:
            act_ref[:, at : at + SLICE] = (value * up).astype(BF)
        d_gate = (d_act * up * slope).astype(BF)
        d_up = (d_act * value).astype(BF)
        du_ref[:, at : at + SLICE] = d_gate
        du_ref[:, half + at : half + at + SLICE] = d_up
        part = mm(d_gate, wf[:, at : at + SLICE], NT) + mm(
            d_up, wf[:, half + at : half + at + SLICE], NT
        )
        dm = part if dm is None else dm + part
    return dm


def dec_query_kernel(ins, gains, w, outs):
    (o, x), (g1,), (d1_ref, c_ref, cq_ref) = ins, gains, outs
    d1 = x[...].astype(F32) + mm(o[...], w[0][...])
    d1_ref[...] = d1
    c = norm(d1, g1)
    c_ref[...] = c
    cq_ref[...] = mm(c, w[1][:, : c.shape[1]]).astype(BF)


def dec_ffn_kernel(ins, gains, w, outs):
    (oc, d1, cot), (g2,) = ins, gains
    doc_ref, out_ref, dd2_ref, m_ref, act_ref, du_ref, branch_ref, u_ref, dg2_ref = outs
    width = oc.shape[1]
    out_proj = w[0]
    d2 = d1[...] + mm(oc[...], out_proj[:, width:], NT)
    m = norm(d2, g2)
    m_ref[...] = m
    wf, wd = w[1], w[2]
    out_ref[...] = ffn_up(m, wf, wd, d2, u_ref, act_ref)
    dm = ffn_down(cot[...], wf, wd, u_ref, du_ref, None)
    back, dg2 = norm_back(d2, g2, dm)
    dd2 = cot[...].astype(F32) + back
    dd2_ref[...] = dd2
    branch = dd2.astype(BF)
    branch_ref[...] = branch
    doc_ref[...] = mm(branch, out_proj[:, width:]).astype(BF)
    add_gain(dg2_ref, dg2)


def enc_back_kernel(ins, gains, w, outs):
    (dk, dv, e1_in, e2_in, u), (g1, g2) = ins, gains
    mem_ref, fb_ref, m_ref, act_ref, du_ref, de1_ref, ab_ref, do_ref, dg1_ref, dg2_ref = outs
    wc = w[0]
    width = dk.shape[1]
    e1, e2 = e1_in[...], e2_in[...]
    dmem = mm(dk[...], wc[:, :width], NT) + mm(dv[...], wc[:, width:], NT)
    mem_ref[...] = norm(e2, g1)
    de2, dg1 = norm_back(e2, g1, dmem)
    fb = de2.astype(BF)
    fb_ref[...] = fb
    m_ref[...] = norm(e1, g2)
    wd, wf = w[1], w[2]
    dm = ffn_down(fb, wf, wd, u, du_ref, act_ref)
    back, dg2 = norm_back(e1, g2, dm)
    de1 = de2 + back
    de1_ref[...] = de1
    ab = de1.astype(BF)
    ab_ref[...] = ab
    do_ref[...] = mm(ab, w[3][...], NT).astype(BF)
    add_gain(dg1_ref, dg1)
    add_gain(dg2_ref, dg2)


def dec_back_kernel(ins, gains, w, outs):
    (dcq, d1_in, dd2), (g1,), (dd1_ref, ab_ref, do_ref, dg1_ref) = ins, gains, outs
    d1 = d1_in[...]
    dc = mm(dcq[...], w[0][:, : dcq.shape[1]], NT)
    back, dg1 = norm_back(d1, g1, dc)
    dd1 = dd2[...] + back
    dd1_ref[...] = dd1
    ab = dd1.astype(BF)
    ab_ref[...] = ab
    do_ref[...] = mm(ab, w[1][...], NT).astype(BF)
    add_gain(dg1_ref, dg1)


def input_grad_kernel(ins, gains, w, outs):
    (dq, dk, dv, x, grad), (g0,), (dx_ref, dg0_ref) = ins, gains, outs
    wa = w[0]
    width = dq.shape[1]
    dn = (
        mm(dq[...], wa[:, :width], NT)
        + mm(dk[...], wa[:, width : 2 * width], NT)
        + mm(dv[...], wa[:, 2 * width :], NT)
    )
    back, dg0 = norm_back(x[...].astype(F32), g0, dn)
    dx_ref[...] = grad[...] + back
    add_gain(dg0_ref, dg0)


class Mover:
    def __init__(self, sems):
        self.sems, self.used, self.stores = sems, 0, []

    def copy(self, src, dst):
        made = pltpu.make_async_copy(src, dst, self.sems.at[self.used])
        self.used += 1
        made.start()
        return made

    def store(self, src, dst):
        self.stores.append(self.copy(src, dst))

    def drain(self):
        for made in self.stores:
            made.wait()


def pair_columns(first, p):
    return slice(first + p * PAIR, first + (p + 1) * PAIR)


def pick(head, low, a, b):
    return jnp.where(low, a, b) if head % 2 == 0 else jnp.where(low, b, a)


def in_order(items, begin, end, lead=1):
    waiting = []
    for item in items:
        waiting.append((item, begin(item)))
        if len(waiting) > lead:
            end(*waiting.pop(0))
    while waiting:
        end(*waiting.pop(0))


def attend(q_ref, kv_ref, firsts, qx, kx, o_ref, lse_ref, causal):
    count_q, count_k = qx.shape[0], kx.shape[0]
    low_q, low_k = low_half(count_q), low_half(count_k)
    ones = jnp.ones((8, count_k), BF)
    values, outs = {}, {}

    def begin(head):
        q = q_ref[:, pair_columns(firsts[0], head // 2)]
        k = kv_ref[:, pair_columns(firsts[1], head // 2)]
        s = mm(pick(head, low_k, k, kx), pick(head, low_q, q, qx), NT)
        return causal_only(s) if causal else s

    def end(head, s):
        p = head // 2
        if head % 2 == 0:
            values[p] = kv_ref[:, pair_columns(firsts[2], p)].astype(F32).T.astype(BF)
        vt = values[p][(head % 2) * HEAD : (head % 2 + 1) * HEAD]
        top = jnp.max(s, axis=0, keepdims=True)
        e = jnp.exp2((s - top) * (SCALE * LOG2E)).astype(BF)
        mixed = mm(jnp.concatenate([vt, ones], axis=0), e)
        total = mixed[HEAD : HEAD + 1]
        outs[head] = mixed[:HEAD] * (1.0 / total)
        lse_ref[p, head % 2 : head % 2 + 1, :] = top * (SCALE * LOG2E) + jnp.log2(total)
        if head % 2 == 1:
            both = jnp.concatenate([outs.pop(head - 1), outs.pop(head)], axis=0)
            o_ref[:, pair_columns(0, p)] = both.T.astype(BF)

    in_order(range(HEADS), begin, end)


def causal_only(s):
    key_at = lax.broadcasted_iota(jnp.int32, s.shape, 0)
    query_at = lax.broadcasted_iota(jnp.int32, s.shape, 1)
    return jnp.where(key_at <= query_at, s, NEGATIVE)


def attend_kernel(firsts, row, causal, same, *refs):
    if same:
        q_ref, (qx_ref, kx_ref, o_ref, lse_ref) = refs[0], refs[1:]
        kv_ref = q_ref
    else:
        q_ref, kv_ref, qx_ref, kx_ref, o_ref, lse_ref = refs
    attend(q_ref, kv_ref, firsts, qx_ref[row], kx_ref[row], o_ref, lse_ref, causal)


def attention_forward(q_in, kv_in, qx, kx, row, firsts, causal):
    count_q = q_in.shape[0]
    ins = [q_in] if kv_in is None else [q_in, kv_in]
    vmem = pl.BlockSpec(memory_space=pltpu.VMEM)
    return pl.pallas_call(
        functools.partial(attend_kernel, firsts, row, causal, kv_in is None),
        in_specs=[vmem] * (len(ins) + 2),
        out_specs=[vmem] * 2,
        out_shape=[
            jax.ShapeDtypeStruct((count_q, HEADS * HEAD), BF),
            jax.ShapeDtypeStruct((HEADS // 2, 2, count_q), F32),
        ],
        compiler_params=params(),
    )(*ins, qx, kx)


def enc_attend_kernel(row, x_hbm, qx_hbm, kx_hbm, g0, wa_hbm, *refs):
    outs, (n_v, packed_v, o_v, lse_v, x, qx, kx, wa, sems) = refs[:4], refs[4:]
    move = Mover(sems)
    got_x = move.copy(x_hbm.at[row], x)
    got_wa = move.copy(wa_hbm, wa)
    got_masks = move.copy(qx_hbm.at[row], qx), move.copy(kx_hbm.at[row], kx)
    tokens, dim = x.shape
    got_x.wait()
    blocks = [slice(at, at + BLOCK) for at in range(0, tokens, BLOCK)]
    for b in blocks:
        n_v[b] = norm(x[b].astype(F32), g0[...])
    move.store(n_v, outs[0])
    got_wa.wait()
    for b in blocks:
        for at in range(0, wa.shape[1], dim):
            packed_v[b, at : at + dim] = mm(n_v[b], wa[:, at : at + dim]).astype(BF)
    move.store(packed_v, outs[1])
    for made in got_masks:
        made.wait()
    attend(packed_v, packed_v, (0, dim, 2 * dim), qx[...], kx[...], o_v, lse_v, False)
    move.store(o_v, outs[2])
    move.store(lse_v, outs[3])
    move.drain()


def enc_rest_kernel(row, x_hbm, o_hbm, g1, g2, wo_hbm, wf_hbm, wd_hbm, wc_hbm, *refs):
    outs, (e1_v, u_v, e2_v, sent_v, x, o, wo, wf, wd, wc, sems) = refs[:4], refs[4:]
    move = Mover(sems)
    got = [
        move.copy(a, b)
        for a, b in (
            (x_hbm.at[row], x), (o_hbm, o), (wo_hbm, wo), (wf_hbm, wf), (wd_hbm, wd), (wc_hbm, wc)
        )
    ]
    for made in got[:3]:
        made.wait()
    blocks = [slice(at, at + BLOCK) for at in range(0, x.shape[0], BLOCK)]
    for b in blocks:
        e1_v[b] = x[b].astype(F32) + mm(o[b], wo[...])
        move.store(e1_v.at[b], outs[0].at[b])
    for made in got[3:]:
        made.wait()
    for b in blocks:
        e1 = e1_v[b]
        e2 = ffn_up(norm(e1, g2[...]), wf, wd, e1, u_v.at[b], None)
        e2_v[b] = e2
        sent_v[b] = mm(norm(e2, g1[...]), wc[...]).astype(BF)
        for src, dst in ((u_v, outs[1]), (e2_v, outs[2]), (sent_v, outs[3])):
            move.store(src.at[b], dst.at[b])
    move.drain()


HBM = pl.BlockSpec(memory_space=pl.ANY)
VMEM = pl.BlockSpec(memory_space=pltpu.VMEM)


def moved_call(kernel, ins, specs, outs, held, copies):
    return list(
        pl.pallas_call(
            kernel,
            in_specs=specs,
            out_specs=[HBM] * len(outs),
            out_shape=[jax.ShapeDtypeStruct(s, t) for s, t in outs],
            scratch_shapes=[pltpu.VMEM(s, t) for s, t in outs + held]
            + [pltpu.SemaphoreType.DMA((copies,))],
            compiler_params=params(),
        )(*ins)
    )


def enc_attend(row, x_in, qx, kx, g0, wa):
    tokens, dim = x_in.shape[1:]
    width = wa.shape[1] // 3
    kept = [
        ((tokens, dim), BF),
        ((tokens, wa.shape[1]), BF),
        ((tokens, width), BF),
        ((HEADS // 2, 2, tokens), F32),
    ]
    held = [(x_in.shape[1:], BF), (qx.shape[1:], BF), (kx.shape[1:], BF), (wa.shape, BF)]
    return moved_call(
        functools.partial(enc_attend_kernel, row),
        (x_in, qx, kx, g0, wa),
        [HBM] * 3 + [VMEM] + [HBM],
        kept,
        held,
        8,
    )


def enc_rest(row, x_in, o, g1, g2, wo, wf, wd, wc):
    tokens, dim = x_in.shape[1:]
    kept = [
        ((tokens, dim), F32),
        ((tokens, wf.shape[1]), BF),
        ((tokens, dim), F32),
        ((tokens, wc.shape[1]), BF),
    ]
    held = [(x_in.shape[1:], BF), (o.shape, BF)] + [(w.shape, BF) for w in (wo, wf, wd, wc)]
    return moved_call(
        functools.partial(enc_rest_kernel, row),
        (x_in, o, g1, g2, wo, wf, wd, wc),
        [HBM] * 2 + [VMEM] * 2 + [HBM] * 4,
        kept,
        held,
        6 + 4 * (tokens // BLOCK),
    )


def nothing_kernel(*refs):
    pass


def unwritten(shapes):
    return pl.pallas_call(
        nothing_kernel,
        out_specs=[pl.BlockSpec(memory_space=pl.ANY)] * len(shapes),
        out_shape=[jax.ShapeDtypeStruct(s.shape, s.dtype) for s in shapes],
    )()


def by_section(on_decoder, encoder, decoder):
    enc_shapes = jax.eval_shape(encoder) if encoder else []
    dec_shapes = jax.eval_shape(decoder) if decoder else []
    none = lambda: []
    encoder, decoder = encoder or none, decoder or none
    pool = lambda shapes: list(unwritten(shapes)) if shapes else []
    both = lax.cond(
        on_decoder,
        lambda: pool(enc_shapes) + list(decoder()),
        lambda: list(encoder()) + pool(dec_shapes),
    )
    return both[: len(enc_shapes)], both[len(enc_shapes) :]


def segment_ids(lengths, span_len):
    positions = jnp.arange(span_len, dtype=jnp.int32)[None, :]
    seg, end = jnp.zeros((lengths.shape[0], span_len), jnp.int32), 0
    for j in range(lengths.shape[1]):
        end = end + lengths[:, j : j + 1]
        seg = seg + (positions >= end).astype(jnp.int32)
    return seg


def mask_lanes(seg, count):
    hit = seg[:, :, None] == jnp.arange(HEAD, dtype=jnp.int32)[None, None, :]
    member = hit.astype(BF)
    other = jnp.where(
        jnp.arange(HEAD, dtype=jnp.int32)[None, None, :] < count,
        jnp.where(hit, 0.0, NEGATIVE),
        0.0,
    ).astype(BF)
    return (
        jnp.concatenate([member, member], -1),
        jnp.concatenate([other, other], -1),
    )


def shift(x, by):
    pairs = [(0, 1)] if by > 0 else [(1, 0)]
    return lax.ppermute(x, "section", pairs)


def body(
    section_input, enc_lengths, dec_lengths, attn_in, attn_out, ffn_in, ffn_out, cross_weight, gains
):
    wa, wo, wf, wd, wc = attn_in[0], attn_out[0], ffn_in[0], ffn_out[0], cross_weight[0]
    g0, g1, g2 = gains[0, 0:1], gains[0, 1:2], gains[0, 2:3]
    x_in = section_input[0]
    rows, le, dim = x_in.shape
    ld = le // 2
    width = wo.shape[0]
    docs = enc_lengths.shape[1]
    enc_qx, enc_kx = mask_lanes(segment_ids(enc_lengths, le), docs)
    dec_qx, dec_kx = mask_lanes(segment_ids(dec_lengths, ld), docs)
    on_decoder = lax.axis_index("section") == 1
    steps_e, steps_d = le // BLOCK, ld // BLOCK
    columns = width // PAIR
    own = (0, columns, 2 * columns)
    across = (0, 0, columns)
    inner = wf.shape[1]

    def project(r, steps):
        return list(
            block_call(project_kernel, steps, [(x_in, r, 0)], [g0, wa], [(dim, BF), (3 * width, BF)])
        )

    def dec_first(r):
        n, packed = project(r, steps_d)
        o, lse = attention_forward(packed, None, dec_qx, dec_kx, r, (0, width, 2 * width), True)
        d1, c, cq = block_call(
            dec_query_kernel,
            steps_d,
            [(o, None, 0), (x_in, r, 0)],
            [g1, wo, wc],
            [(dim, F32), (dim, BF), (width, BF)],
        )
        return [n, packed, o, lse, d1, c, cq]

    def cross(r, cq, sent):
        return list(attention_forward(cq, sent, dec_qx, enc_kx, r, (0, 0, width), False))

    def dec_ffn(r, oc, d1):
        return list(
            block_call(
                dec_ffn_kernel,
                steps_d,
                [(oc, None, 0), (d1, None, 0), (x_in, r, ld // BLOCK)],
                [g2, wc, wf, wd],
                [
                    (width, BF),
                    (dim, F32),
                    (dim, F32),
                    (dim, BF),
                    (wd.shape[0], BF),
                    (inner, BF),
                    (dim, BF),
                    (inner, BF),
                ],
                1,
            )
        )

    def cross_back(r, cq, sent, oc, doc, lse):
        return list(
            attention_backward(cq, sent, sent, dec_qx, enc_kx, r, across, oc, doc, lse, False)
        )

    def enc_back(dk, dv, e1, e2, u):
        return list(
            block_call(
                enc_back_kernel,
                steps_e,
                [(dk, None, 0), (dv, None, 0), (e1, None, 0), (e2, None, 0), (u, None, 0)],
                [g1, g2, wc, wd, wf, wo],
                [
                    (dim, BF),
                    (dim, BF),
                    (dim, BF),
                    (wd.shape[0], BF),
                    (inner, BF),
                    (dim, F32),
                    (dim, BF),
                    (width, BF),
                ],
                2,
            )
        )

    def self_back(r, steps, masks, causal, packed, o, lse, do, grad):
        dq, dk, dv = attention_backward(
            packed, packed, packed, *masks, r, own, o, do, lse, causal
        )
        dx, dg0 = block_call(
            input_grad_kernel,
            steps,
            [(dq, None, 0), (dk, None, 0), (dv, None, 0), (x_in, r, 0), (grad, None, 0)],
            [g0, wa],
            [(dim, F32)],
            1,
        )
        return [dq, dk, dv, dx, dg0]

    def dec_back(dcq, d1, dd2):
        return list(
            block_call(
                dec_back_kernel,
                steps_d,
                [(dcq, None, 0), (d1, None, 0), (dd2, None, 0)],
                [g1, wc, wo],
                [(dim, F32), (dim, BF), (width, BF)],
                1,
            )
        )

    every = range(rows)
    plain = lax.axis_size("rows") != PEERS
    state = [on_decoder]

    def run(encoder, decoder, *ready):
        held = lax.optimization_barrier(tuple(state) + ready)[0]
        out = by_section(held, encoder, decoder)
        state[1:] = [(out[0] or out[1])[0]]
        return out

    def slots():
        return [None] * rows

    first, rest, dfirst, cqs, crossed, ocs = slots(), slots(), slots(), slots(), slots(), slots()
    mids, docs_in, cross_b, dcqs, back, last, dlast = (slots() for _ in range(7))

    def begin_cross(r, beside=None):
        crossed[r], out = run(lambda: cross(r, cqs[r], rest[r][3]), beside)
        ocs[r] = shift(crossed[r][0], 1)
        return out

    def dec_mid(r):
        return lambda: dec_ffn(r, ocs[r], dfirst[r][4])

    def keep_mid(r, out):
        mids[r] = out
        docs_in[r] = shift(out[0], -1)

    def dec_last(r):
        p = dec_back(dcqs[r], dfirst[r][4], mids[r][2])
        n, packed, o, lse = dfirst[r][:4]
        return p + self_back(r, steps_d, (dec_qx, dec_kx), True, packed, o, lse, p[2], p[0])

    def enc_last(r):
        return self_back(
            r, steps_e, (enc_qx, enc_kx), False, *first[r][1:4], back[r][7], back[r][5]
        )

    def enc_first(r):
        return lambda: enc_attend(r, x_in, enc_qx, enc_kx, g0, wa)

    def enc_then(r):
        return lambda: enc_rest(r, x_in, first[r][2], g1, g2, wo, wf, wd, wc)

    first[0], dfirst[0] = run(enc_first(0), lambda: dec_first(0))
    cqs[0] = shift(dfirst[0][6], -1)
    rest[0], more = run(enc_then(0), lambda: [v for r in every[1:] for v in dec_first(r)])
    begin_cross(0)
    for r in every[1:]:
        dfirst[r] = more[7 * (r - 1) : 7 * r]
        cqs[r] = shift(dfirst[r][6], -1)
    for r in every[1:]:
        first[r], _ = run(enc_first(r), None)
        rest[r], out = run(enc_then(r), dec_mid(r - 1), ocs[r - 1])
        keep_mid(r - 1, out)
        begin_cross(r)
    for r in every:
        cross_b[r], _ = run(
            lambda: cross_back(r, cqs[r], rest[r][3], crossed[r][0], docs_in[r], crossed[r][1]),
            None,
        )
        dcqs[r] = shift(cross_b[r][0], 1)
        back[r], out = run(
            lambda: enc_back(cross_b[r][1], cross_b[r][2], rest[r][0], rest[r][2], rest[r][1]),
            dec_mid(rows - 1) if r == 0 else None,
        )
        if r == 0:
            keep_mid(rows - 1, out)
        last[r], dlast[r] = run((lambda: enc_last(r)) if plain else None, lambda: dec_last(r))

    def over_rows(lists):
        return [list(group) for group in zip(*lists)]

    enc_side = (
        over_rows([back[r][2], back[r][3], back[r][0], back[r][0], first[r][2], first[r][0]] for r in every),
        over_rows(
            [back[r][4], back[r][1], cross_b[r][1], cross_b[r][2], back[r][6]] + last[r][0:3]
            for r in every
        ),
    )
    dec_side = (
        over_rows(
            [mids[r][3], mids[r][4], dfirst[r][5], mids[r][6], dfirst[r][2], dfirst[r][0]]
            for r in every
        ),
        over_rows(
            [mids[r][5], x_in[r, ld:], dcqs[r], ocs[r], dlast[r][1]] + dlast[r][4:7] for r in every
        ),
    )
    if not plain:
        kept = over_rows(
            [first[r][1], first[r][2], back[r][7], first[r][3], back[r][5]] for r in every
        )
        decoded = over_rows([mids[r][1], dlast[r][7]] for r in every)
        gain_rows = (
            over_rows([back[r][8], back[r][9]] for r in every),
            over_rows([dlast[r][8], dlast[r][3], mids[r][8]] for r in every),
        )
        s_in, s_out, s_fi, s_cross, s_gain, s_fo, results = grad_sum(
            (enc_side, dec_side), kept, decoded, gain_rows, (x_in, enc_qx, enc_kx, wa, g0)
        )
        o_gain, *outs = hand_over(
            s_gain, gains.shape[1], [results, s_in, s_out, s_fi, s_fo, s_cross]
        )
        return tuple(outs) + (o_gain,)

    def enc_parts():
        gain_rows = [sum(v) for v in zip(*[[last[r][4], back[r][8], back[r][9]] for r in every])]
        return [jnp.concatenate(gain_rows, 0), jnp.stack([last[r][3] for r in every])]

    def dec_parts():
        gain_rows = [sum(v) for v in zip(*[[dlast[r][8], dlast[r][3], mids[r][8]] for r in every])]
        both = [jnp.concatenate([mids[r][1], dlast[r][7]], 0) for r in every]
        return [jnp.concatenate(gain_rows, 0), jnp.stack(both)]

    gain_grads, results = lax.cond(on_decoder, dec_parts, enc_parts)
    gain_terms = jnp.pad(gain_grads.T, ((0, 0), (0, LANES - gain_grads.shape[0]))).astype(BF)

    s_in, s_out, s_fi, s_cross, s_gain, s_fo = plain_sum(on_decoder, (enc_side, dec_side), gain_terms)
    return (
        results[None],
        s_in[None],
        s_out[None],
        s_fi[None],
        s_fo[None],
        s_cross[None],
        s_gain[:, : gain_grads.shape[0]].T[None],
    )


def solution(mesh):
    placed = (
        P("section", "rows", None, None),
        P("rows", None),
        P("rows", None),
    ) + (P("section", None, None),) * 6
    return jax.shard_map(
        body,
        mesh=mesh,
        in_specs=placed,
        out_specs=(
            P("section", "rows", None, None),
            P("section", "rows", None),
            P("section", "rows", None),
            P("section", "rows", None),
            P("section", "rows", None),
            P("section", "rows", None),
            P("section", None, "rows"),
        ),
        check_vma=False,
    )
```

```python
import functools

import jax
import jax.numpy as jnp
from jax import lax
from jax.experimental import pallas as pl
from jax.experimental.pallas import tpu as pltpu
from jax.sharding import PartitionSpec as P

HEADS = 12
HEAD = 64
PAIR = 128
EPSILON = 1e-06
SCALE = 0.125
LOG2E = 1.4426950408889634
NEGATIVE = -1e30
GELU_C = 0.7978845608028654
GELU_A = 0.044715

BF = jnp.bfloat16
F32 = jnp.float32
NT = (((1,), (1,)), ((), ()))
NN = (((1,), (0,)), ((), ()))
TN = (((0,), (0,)), ((), ()))


def mm(a, b, dims=NN):
    return lax.dot_general(a, b, dims, preferred_element_type=F32)


MESH = pl.DeviceIdType.MESH
LANES = 256
VMEM_LIMIT = 56 * 1024 * 1024
SUM_VMEM = 60 * 1024 * 1024

NZ, NY, NC = 4, 2, 2
PEERS = NZ * NY * NC
C_LAG = 2
Y_LAG = C_LAG + 2
HOP = 2
RING = 6
AHEAD = 3
PANELS = 4

TALL = 1
LEFT_ORDER = (0, 2, 3, 4, 5)
PRODUCTS = ((0, 0), (1, 1), (2, 2), (3, 3), (4, 4), (5, 5), (5, 6), (5, 7))


def grad_sum_kernel(rows, group_sizes, token_counts, chunk_counts, unit_steps, *refs):
    remaining = list(refs)
    sizes = list(group_sizes)

    def take(groups):
        return [[remaining.pop(0) for _ in range(sizes.pop(0))] for _ in range(groups)]

    def take_one():
        return remaining.pop(0)

    lefts_of, rights_of = [], []
    for side in range(2):
        lefts_of.append(take(6))
        rights_of.append(take(5 if side == 0 else 8))
    packed_of, o_of, do_of, lse_of, de1_of = take(5)
    out_of, dx_of = take(2)
    gain_rows = [[None] + take(2), take(3)]
    x_ref, qx_ref, kx_ref, wa_ref, g0_ref = [take_one() for _ in range(5)]
    o_in, o_out, o_fi, o_cross, o_gain, o_fo, o_results = [take_one() for _ in range(7)]
    (
        xt, xt_tall, left_stage, tall_stage, tall_right, panels, ring,
        own, got_y, got_r, got_l,
        s_left, s_tall, s_right, s_panel,
        s_core, r_core, s_y, r_y, s_r, r_r, s_l, r_l,
        d_packed, wa, att, qx, kx, lse, x_stage, grad_stage, dx_stage, dg0,
        s_att, s_const, s_lse, s_block, s_out, s_dec,
    ) = remaining
    chunks, height, dim = own.shape[0], own.shape[3], xt.shape[0]
    sec, me = lax.axis_index("section"), lax.axis_index("rows")
    core, y, z = lax.rem(me, 2), lax.rem(me // 2, 2), me // 4
    by_core, by_y = me + 1 - 2 * core, me + 2 - 4 * y
    other, away = 1 - core, 1 - y
    bases = [sum(chunk_counts[:i]) for i in range(len(chunk_counts))]


    def each(act):
        for side in range(2):

            @pl.when(sec == side)
            def _(side=side):
                act(side)

    def row_copies(sources, columns, dst, sems, side):
        del side
        copies, at = [], 0
        for i, src in enumerate(sources):
            copies.append(
                pltpu.make_async_copy(
                    src if columns is None else src.at[:, columns],
                    dst.at[at : at + src.shape[0]],
                    sems.at[i],
                )
            )
            at += src.shape[0]
        return copies

    def start_all(copies):
        for copy in copies:
            copy.start()

    def wait_all(copies):
        for copy in copies:
            copy.wait()

    def left_copies(q, side):
        source = lefts_of[side][LEFT_ORDER[q]]
        return row_copies(source, None, left_stage.at[q % 2], s_left.at[q % 2], side)

    def tall_copies(side):
        return row_copies(lefts_of[side][1], None, tall_stage, s_tall, side)

    def tall_right_copies(side):
        return row_copies(rights_of[side][1], None, tall_right, s_right, side)

    def panel_copies(p, i, slot, side):
        if PRODUCTS[p][1] >= len(rights_of[side]):
            return []
        columns = pl.ds(pl.multiple_of(i * LANES, LANES), LANES)
        return row_copies(
            rights_of[side][PRODUCTS[p][1]], columns, panels.at[slot], s_panel.at[slot], side
        )

    def for_panel(t, act):
        slot = lax.rem(t, PANELS)
        for p in range(len(PRODUCTS)):
            if p != TALL:

                @pl.when((t >= bases[p]) & (t < bases[p] + chunk_counts[p]))
                def _(p=p):
                    each(lambda side: act(p, t - bases[p], slot, side))

    def flip(side, stage, columns, put):
        for at in range(0, rows * token_counts[side], LANES):
            tokens = slice(at, at + LANES)
            put(tokens, stage[tokens, columns].astype(F32).T.astype(BF))

    def build_left(q):
        def act(side):
            wait_all(left_copies(q, side))
            for at in range(0, xt.shape[0], LANES):

                def put(tokens, block, at=at):
                    xt[at : at + LANES, tokens] = block

                flip(side, left_stage.at[q % 2], slice(at, at + LANES), put)
            if q + 2 < len(LEFT_ORDER):
                start_all(left_copies(q + 2, side))

        each(act)

    groups = xt_tall.shape[0] // LANES
    tall_rows = xt_tall.shape[0] // PEERS

    def build_tall(part):
        columns = pl.ds(pl.multiple_of(part * LANES, LANES), LANES)
        targets = LANES // tall_rows

        def act(side):
            def put(tokens, block):
                for k in range(targets):
                    for j in range(tall_rows // 16):
                        to = j * LANES + (part * targets + k) * 16
                        xt_tall[pl.ds(pl.multiple_of(to, 16), 16), tokens] = block[
                            k * tall_rows + j * 16 : k * tall_rows + (j + 1) * 16
                        ]

            flip(side, tall_stage, columns, put)

        each(act)

    def send_core(j):
        slot = lax.rem(j, RING)
        return pltpu.make_async_remote_copy(
            src_ref=ring.at[slot, :, :, other],
            dst_ref=own.at[j],
            send_sem=s_core.at[j],
            recv_sem=r_core.at[j],
            device_id=(sec, by_core),
            device_id_type=MESH,
        )

    def send_y(j):
        return pltpu.make_async_remote_copy(
            src_ref=own.at[j, :, away],
            dst_ref=got_y.at[j],
            send_sem=s_y.at[j],
            recv_sem=r_y.at[j],
            device_id=(sec, by_y),
            device_id_type=MESH,
        )

    def send_right(j, at):
        return pltpu.make_async_remote_copy(
            src_ref=own.at[j, pl.ds(at + 1, NZ - 1 - at), y],
            dst_ref=got_r.at[j, pl.ds(at + 1, NZ - 1 - at)],
            send_sem=s_r.at[j],
            recv_sem=r_r.at[j],
            device_id=(sec, me + 4),
            device_id_type=MESH,
        )

    def send_left(j, at):
        return pltpu.make_async_remote_copy(
            src_ref=own.at[j, pl.ds(0, at), y],
            dst_ref=got_l.at[j, pl.ds(0, at)],
            send_sem=s_l.at[j],
            recv_sem=r_l.at[j],
            device_id=(sec, me - 4),
            device_id_type=MESH,
        )

    def add_into(dst, src):
        dst[...] = (dst[...].astype(F32) + src[...].astype(F32)).astype(BF)


    def compute(s):
        slot = lax.rem(s, RING)

        def put_panel(value):
            for t in range(PEERS):
                ring[slot, t // 4, t // 2 % 2, t % 2] = value[t * height : (t + 1) * height]

        for p in range(len(PRODUCTS)):
            left = PRODUCTS[p][0]

            @pl.when((s >= bases[p]) & (s < bases[p] + chunk_counts[p]))
            def _(p=p, left=left):
                if p != TALL:
                    if p == 0 or PRODUCTS[p - 1][0] != left:

                        @pl.when(s == bases[p])
                        def _():
                            build_left(LEFT_ORDER.index(left))

                    where = lax.rem(s, PANELS)

                    def act(side):
                        wait_all(panel_copies(p, s - bases[p], where, side))
                        tokens = rows * token_counts[side]
                        if PRODUCTS[p][1] < len(rights_of[side]):
                            right = panels[where, :tokens, :]
                        else:
                            first = (PRODUCTS[p][1] - 5) * dim + (s - bases[p]) * LANES
                            right = d_packed[:, pl.ds(pl.multiple_of(first, LANES), LANES)]
                        put_panel(mm(xt[:, :tokens], right).astype(BF))

                    each(act)
                else:
                    rows_at = pl.ds(pl.multiple_of((s - bases[p]) * LANES, LANES), LANES)

                    @pl.when(s == bases[p])
                    def _():
                        each(lambda side: wait_all(tall_right_copies(side)))

                    def act(side):
                        tokens = rows * token_counts[side]
                        for k in range(tall_right.shape[1] // LANES):
                            value = mm(
                                xt_tall[rows_at, :tokens],
                                tall_right[:tokens, k * LANES : (k + 1) * LANES],
                            ).astype(BF)
                            for t in range(PEERS):
                                ring[slot, t // 4, t // 2 % 2, t % 2, k * 16 : (k + 1) * 16] = value[
                                    t * 16 : (t + 1) * 16
                                ]

                    each(act)

        @pl.when(s == chunks - 1)
        def _():
            def act(side):
                parts = []
                for group in gain_rows[side]:
                    total_row = dg0[...]
                    if group is not None:
                        total_row = group[0][...]
                        for ref in group[1:]:
                            total_row = total_row + ref[...]
                    parts.append(total_row)
                parts.append(jnp.zeros((LANES - len(parts), dim), F32))
                put_panel(jnp.concatenate(parts, axis=0).T.astype(BF))

            each(act)


    attn_units, block_units, first_block = unit_steps
    tokens_e = token_counts[0]
    per_row = tokens_e // BLOCK
    const_copies = [
        pltpu.make_async_copy(src, dst, s_const.at[i])
        for i, (src, dst) in enumerate(((qx_ref, qx), (kx_ref, kx), (wa_ref, wa)))
    ]
    lse_copies = [
        pltpu.make_async_copy(ref, lse.at[r], s_lse.at[r]) for r, ref in enumerate(lse_of)
    ]

    def row_pieces(refs_of, r):
        found, at = [], 0
        for ref in refs_of:
            if r * tokens_e <= at < (r + 1) * tokens_e:
                found.append((ref, at - r * tokens_e))
            at += ref.shape[0]
        return found

    def attn_loads(u, act):
        slot, p = lax.rem(u, 2), lax.rem(u, HEADS // 2)
        for r in range(rows):

            @pl.when(u // (HEADS // 2) == r)
            def _(r=r):
                at = lambda first: pl.ds(pl.multiple_of(first + p * PAIR, PAIR), PAIR)
                sources = [packed_of[r].at[:, at(k * dim)] for k in range(3)]
                sources.append(o_of[r].at[:, at(0)])
                copies = [
                    pltpu.make_async_copy(src, att.at[slot, k], s_att.at[slot, k])
                    for k, src in enumerate(sources)
                ]
                for ref, begin in row_pieces(do_of, r):
                    copies.append(
                        pltpu.make_async_copy(
                            ref.at[:, at(0)],
                            att.at[slot, 4, begin : begin + ref.shape[0]],
                            s_att.at[slot, len(copies)],
                        )
                    )
                act(copies)

    def attn_unit(u):
        slot, p, r = lax.rem(u, 2), lax.rem(u, HEADS // 2), u // (HEADS // 2)
        attn_loads(u, wait_all)
        q, k, v, o, do = [att[slot, i] for i in range(5)]
        grads = pair_backward(q, k, v, qx[r], kx[r], o, do, lse[r, p], False)
        where = pl.ds(pl.multiple_of(r * tokens_e, tokens_e), tokens_e)
        for i, value in enumerate(grads):
            at = pl.ds(pl.multiple_of(i * dim + p * PAIR, PAIR), PAIR)
            d_packed[where, at] = value.astype(BF)

    def block_loads(v, act):
        slot = lax.rem(v, 2)
        where = pl.ds(pl.multiple_of(lax.rem(v, per_row) * BLOCK, BLOCK), BLOCK)
        for r in range(rows):

            @pl.when(v // per_row == r)
            def _(r=r):
                act([pltpu.make_async_copy(x_ref.at[r, where], x_stage.at[slot], s_block.at[slot, 0])])

            for ref, begin in row_pieces(de1_of, r):
                for at in range(0, ref.shape[0], BLOCK):

                    @pl.when(v == (r * tokens_e + begin + at) // BLOCK)
                    def _(ref=ref, at=at):
                        act(
                            [
                                pltpu.make_async_copy(
                                    ref.at[at : at + BLOCK], grad_stage.at[slot], s_block.at[slot, 1]
                                )
                            ]
                        )

    def block_store(v):
        slot = lax.rem(v, 2)
        where = pl.ds(pl.multiple_of(lax.rem(v, per_row) * BLOCK, BLOCK), BLOCK)
        return pltpu.make_async_copy(
            dx_stage.at[slot], o_results.at[v // per_row, where], s_out.at[slot]
        )

    def block_unit(v):
        slot = lax.rem(v, 2)
        block_loads(v, wait_all)

        @pl.when(v == 0)
        def _():
            const_copies[2].wait()
            dg0[...] = jnp.zeros_like(dg0)

        @pl.when(v >= 2)
        def _():
            block_store(v - 2).wait()

        where = pl.ds(pl.multiple_of(v * BLOCK, BLOCK), BLOCK)
        dn = None
        for i in range(3):
            part = mm(d_packed[where, i * dim : (i + 1) * dim], wa[:, i * dim : (i + 1) * dim], NT)
            dn = part if dn is None else dn + part
        back, gain_part = norm_back(x_stage[slot].astype(F32), g0_ref[...], dn)
        dg0[...] += gain_part
        dx_stage[slot] = grad_stage[slot] + back
        block_store(v).start()

    def dec_results(store):
        half = token_counts[1]
        parts = [
            (ref, stage.at[r], o_results.at[r, k * half : (k + 1) * half], s_dec.at[k, r])
            for k, (group, stage) in enumerate(((out_of, grad_stage), (dx_of, dx_stage)))
            for r, ref in enumerate(group)
        ]
        return [
            pltpu.make_async_copy(held, dst, sem) if store else pltpu.make_async_copy(src, held, sem)
            for src, held, dst, sem in parts
        ]

    def side_work(s):
        @pl.when(s == 0)
        def _():
            start_all(lse_copies)
            start_all(const_copies)
            for v in range(2):
                block_loads(jnp.int32(v), start_all)

        u = s // 2

        @pl.when((lax.rem(s, 2) == 0) & (u < attn_units))
        def _():
            attn_loads(u, start_all)

        @pl.when((lax.rem(s, 2) == 0) & (u >= 1) & (u <= attn_units))
        def _():
            @pl.when(u == 1)
            def _():
                wait_all(lse_copies)
                wait_all(const_copies[:2])

            attn_unit(u - 1)

        v = (s - first_block) // 2

        @pl.when((lax.rem(s, 2) == 0) & (s >= first_block) & (v < block_units))
        def _():
            block_unit(v)

            @pl.when(v + 2 < block_units)
            def _():
                block_loads(v + 2, start_all)


    def open_first(side):
        start_all(left_copies(0, side))
        for t in range(AHEAD):
            start_all(panel_copies(0, t, t % PANELS, side))

    each(open_first)

    barrier = pltpu.get_barrier_semaphore()

    def greet(peer):
        pl.semaphore_signal(barrier, inc=1, device_id=(sec, peer), device_id_type=MESH)

    greet(by_core)
    greet(by_y)

    @pl.when(z > 0)
    def _():
        greet(me - 4)

    @pl.when(z < NZ - 1)
    def _():
        greet(me + 4)

    @pl.when((z > 0) & (z < NZ - 1))
    def _():
        pl.semaphore_wait(barrier, 4)

    @pl.when((z == 0) | (z == NZ - 1))
    def _():
        pl.semaphore_wait(barrier, 3)


    @pl.when(sec == 1)
    def _():
        start_all(dec_results(False))

    def step(s, carry):
        @pl.when(s + AHEAD < chunks - 1)
        def _():
            for_panel(
                s + AHEAD,
                lambda p, i, slot, side: start_all(panel_copies(p, i, slot, side)),
            )

        @pl.when((s >= RING) & (s < chunks))
        def _():
            send_core(s - RING).wait_send()

        @pl.when(s < chunks)
        def _():
            compute(s)
            send_core(s).start()

        @pl.when(sec == 0)
        def _():
            side_work(s)

        @pl.when((sec == 1) & (s == RING))
        def _():
            wait_all(dec_results(False))
            start_all(dec_results(True))

        @pl.when(s == 1)
        def _():
            each(lambda side: start_all(tall_copies(side)))

        @pl.when(s == 4)
        def _():
            each(lambda side: wait_all(tall_copies(side)))
            each(lambda side: start_all(left_copies(1, side)))
            each(lambda side: start_all(tall_right_copies(side)))

        @pl.when((s >= 4) & (s < 4 + groups))
        def _():
            build_tall(s - 4)

        j_c = s - C_LAG

        @pl.when((j_c >= 0) & (j_c < chunks))
        def _():
            send_core(j_c).wait_recv()
            slot = lax.rem(j_c, RING)
            for a in range(NZ):
                for b in range(NY):
                    add_into(own.at[j_c, a, b], ring.at[slot, a, b, core])
            send_y(j_c).start()

        j_y = s - Y_LAG

        @pl.when((j_y >= 0) & (j_y < chunks))
        def _():
            send_y(j_y).wait_recv()
            for t in range(NZ):
                add_into(own.at[j_y, t, y], got_y.at[j_y, t])

        for at in range(NZ - 1):
            j_r = s - Y_LAG - HOP * at

            @pl.when((z == at) & (j_r >= 0) & (j_r < chunks))
            def _(at=at, j_r=j_r):
                if at > 0:
                    send_right(j_r, at - 1).wait_recv()
                    for t in range(at + 1, NZ):
                        add_into(own.at[j_r, t, y], got_r.at[j_r, t])
                send_right(j_r, at).start()

        for at in range(1, NZ):
            j_l = s - Y_LAG - HOP * (NZ - 1 - at)

            @pl.when((z == at) & (j_l >= 0) & (j_l < chunks))
            def _(at=at, j_l=j_l):
                if at < NZ - 1:
                    send_left(j_l, at + 1).wait_recv()
                    for t in range(at):
                        add_into(own.at[j_l, t, y], got_l.at[j_l, t])
                send_left(j_l, at).start()

        return carry

    lax.fori_loop(0, chunks + Y_LAG + HOP * (NZ - 1), step, 0)


    def finish(j):
        @pl.when(z == NZ - 1)
        def _():
            send_right(j, NZ - 2).wait_recv()

        @pl.when(z == 0)
        def _():
            send_left(j, 1).wait_recv()

        send_y(j).wait_send()

        @pl.when(j >= chunks - RING)
        def _():
            send_core(j).wait_send()

        for at in range(NZ):

            @pl.when(z == at)
            def _(at=at):
                if at < NZ - 1:
                    send_right(j, at).wait_send()
                if at > 0:
                    send_left(j, at).wait_send()

    def total(j, part):
        mine = own[j, z, y, part].astype(F32)
        right = got_r[j, z, part].astype(F32)
        left = got_l[j, z, part].astype(F32)
        return mine + jnp.where(z > 0, right, 0.0) + jnp.where(z < NZ - 1, left, 0.0)

    def close(out, base, count, column):
        def panel(i, carry):
            finish(base + i)
            at = pl.ds(pl.multiple_of(column + i * LANES, LANES), LANES)
            out[:, at] = total(base + i, pl.ds(0, height))
            return carry

        lax.fori_loop(0, count, panel, 0)

    close(o_fi, bases[0], chunk_counts[0], 0)

    def tall_out(i, carry):
        finish(bases[TALL] + i)
        at = pl.ds(pl.multiple_of(i * 16, 16), 16)
        for k in range(tall_right.shape[1] // LANES):
            o_fo[at, k * LANES : (k + 1) * LANES] = total(bases[TALL] + i, pl.ds(k * 16, 16))
        return carry

    lax.fori_loop(0, chunk_counts[TALL], tall_out, 0)
    close(o_cross, bases[2], chunk_counts[2], 0)
    close(o_cross, bases[3], chunk_counts[3], dim)
    close(o_out, bases[4], chunk_counts[4], 0)
    for k in range(3):
        close(o_in, bases[5 + k], chunk_counts[5 + k], k * dim)
    close(o_gain, chunks - 1, 1, 0)

    @pl.when(sec == 0)
    def _():
        for v in range(max(0, block_units - 2), block_units):
            block_store(jnp.int32(v)).wait()

    @pl.when(sec == 1)
    def _():
        wait_all(dec_results(True))


def grad_sum(sides, kept, decoded, gain_rows, shared):
    (enc_lefts, enc_rights), (dec_lefts, dec_rights) = sides
    x_in, qx, kx, wa, g0 = shared
    rows = x_in.shape[0]
    token_counts = (enc_lefts[5][0].shape[0], dec_lefts[5][0].shape[0])
    tokens = rows * max(token_counts)
    groups = enc_lefts + enc_rights + dec_lefts + dec_rights + kept + decoded
    group_sizes = tuple(len(g) for g in groups + gain_rows[0] + gain_rows[1])
    most = max(group_sizes)
    dim, tall = dec_lefts[0][0].shape[1], dec_lefts[TALL][0].shape[1]
    height = dim // PEERS
    chunk_counts = tuple(
        dec_lefts[a][0].shape[1] * dec_rights[b][0].shape[1] // (dim * LANES) for a, b in PRODUCTS
    )
    chunks = sum(chunk_counts) + 1
    attn_units, block_units = rows * HEADS // 2, rows * token_counts[0] // BLOCK
    unit_steps = (attn_units, block_units, 2 * attn_units + 2)
    flat = lambda groups: [v for group in groups for v in group]
    moved = flat(groups)
    gains = flat(gain_rows[0] + gain_rows[1])
    half = (chunks, NZ, NY, height, LANES)
    fourth = (chunks, NZ, height, LANES)
    width = lambda *which: sum(dec_rights[i][0].shape[1] for i in which)
    out_shape = [
        jax.ShapeDtypeStruct(s, F32)
        for s in (
            (height, width(5, 6, 7)),
            (height, width(4)),
            (height, width(0)),
            (height, width(2, 3)),
            (height, LANES),
            (tall // PEERS, width(1)),
            x_in.shape,
        )
    ]
    hbm, vmem = pl.BlockSpec(memory_space=pl.ANY), pl.BlockSpec(memory_space=pltpu.VMEM)
    dma = pltpu.SemaphoreType.DMA
    return pl.pallas_call(
        functools.partial(
            grad_sum_kernel, rows, group_sizes, token_counts, chunk_counts, unit_steps
        ),
        in_specs=[hbm] * len(moved) + [vmem] * len(gains) + [hbm] * 4 + [vmem],
        out_specs=[vmem] * 6 + [hbm],
        out_shape=out_shape,
        scratch_shapes=[
            pltpu.VMEM((dim, tokens), BF),
            pltpu.VMEM((tall, tokens), BF),
            pltpu.VMEM((2, tokens, dim), BF),
            pltpu.VMEM((tokens, tall), BF),
            pltpu.VMEM((tokens, width(1)), BF),
            pltpu.VMEM((PANELS, tokens, LANES), BF),
            pltpu.VMEM((RING, NZ, NY, NC, height, LANES), BF),
            pltpu.VMEM(half, BF),
            pltpu.VMEM(fourth, BF),
            pltpu.VMEM(fourth, BF),
            pltpu.VMEM(fourth, BF),
            dma((2, most)),
            dma((most,)),
            dma((most,)),
            dma((PANELS, most)),
        ]
        + [dma((chunks,))] * 8
        + [
            pltpu.VMEM((rows * token_counts[0], 3 * dim), BF),
            pltpu.VMEM(wa.shape, BF),
            pltpu.VMEM((2, 5, token_counts[0], PAIR), BF),
            pltpu.VMEM(qx.shape, BF),
            pltpu.VMEM(kx.shape, BF),
            pltpu.VMEM((rows,) + kept[3][0].shape, F32),
            pltpu.VMEM((2, BLOCK, dim), BF),
            pltpu.VMEM((max(2, rows), BLOCK, dim), F32),
            pltpu.VMEM((max(2, rows), BLOCK, dim), F32),
            pltpu.VMEM((1, dim), F32),
            dma((2, 4 + most)),
            dma((3,)),
            dma((rows,)),
            dma((2, 2)),
            dma((2,)),
            dma((2, rows)),
        ],
        compiler_params=pltpu.CompilerParams(
            collective_id=1, has_side_effects=True, vmem_limit_bytes=SUM_VMEM
        ),
    )(*moved, *gains, x_in, qx, kx, wa, g0)


def hand_over_kernel(rows, *refs):
    count = (len(refs) - 3) // 3
    gain_ref, sources, gain_out = refs[0], refs[1 : 1 + count], refs[1 + count]
    targets, held = refs[2 + count : 2 + 2 * count], refs[2 + 2 * count : 2 + 3 * count]
    gain, sems = refs[2 + 3 * count], refs[3 + 3 * count]
    moves = []
    for src, keep, dst in zip(sources, held, targets):
        for part in range(rows) if len(src.shape) == 3 else [slice(None)]:
            i = len(moves)
            load = pltpu.make_async_copy(src.at[part], keep.at[part], sems.at[0, i])
            load.start()
            moves.append((load, keep.at[part], dst.at[0].at[part], sems.at[1, i]))
    load_gain = pltpu.make_async_copy(gain_ref, gain, sems.at[0, len(moves)])
    load_gain.start()
    stores = []
    for load, keep, dst, sem in moves:
        load.wait()
        stores.append(pltpu.make_async_copy(keep, dst, sem))
        stores[-1].start()
    load_gain.wait()
    gain_out[0] = gain[...].T[: gain_out.shape[1]]
    for store in stores:
        store.wait()


def hand_over(gain, gain_rows, arrays):
    hbm, vmem = pl.BlockSpec(memory_space=pl.ANY), pl.BlockSpec(memory_space=pltpu.VMEM)
    rows = max(a.shape[0] for a in arrays if a.ndim == 3)
    return pl.pallas_call(
        functools.partial(hand_over_kernel, rows),
        in_specs=[hbm] * (1 + len(arrays)),
        out_specs=[vmem] + [hbm] * len(arrays),
        out_shape=[jax.ShapeDtypeStruct((1, gain_rows, gain.shape[0]), F32)]
        + [jax.ShapeDtypeStruct((1,) + a.shape, F32) for a in arrays],
        scratch_shapes=[pltpu.VMEM(a.shape, F32) for a in arrays]
        + [
            pltpu.VMEM(gain.shape, F32),
            pltpu.SemaphoreType.DMA((2, len(arrays) + rows)),
        ],
        compiler_params=pltpu.CompilerParams(vmem_limit_bytes=SUM_VMEM),
    )(gain, *arrays)


def plain_sum(on_decoder, sides, gain_terms):
    def terms(lefts, rights):
        parts = [
            mm(jnp.concatenate(lefts[i], 0), jnp.concatenate(rights[j], 0), TN).astype(BF)
            for i, j in PRODUCTS
        ]
        return [
            jnp.concatenate(parts[5:8], 1),
            parts[4],
            parts[0],
            jnp.concatenate(parts[2:4], 1),
            parts[1],
        ]

    pieces = lax.cond(on_decoder, lambda: terms(*sides[1]), lambda: terms(*sides[0]))
    pieces.insert(4, gain_terms)
    return [
        lax.psum_scatter(piece, "rows", scatter_dimension=0, tiled=True).astype(F32)
        for piece in pieces
    ]


def low_half(rows):
    return lax.broadcasted_iota(jnp.int32, (rows, PAIR), 1) < HEAD


def masked_scores(q, k, qx, kx, head, causal):
    lo_q, lo_k = low_half(q.shape[0]), low_half(k.shape[0])
    if head == 0:
        qh, kh = jnp.where(lo_q, q, qx), jnp.where(lo_k, k, kx)
    else:
        qh, kh = jnp.where(lo_q, qx, q), jnp.where(lo_k, kx, k)
    s = mm(kh, qh, NT)
    if causal:
        key_at = lax.broadcasted_iota(jnp.int32, s.shape, 0)
        query_at = lax.broadcasted_iota(jnp.int32, s.shape, 1)
        s = jnp.where(key_at <= query_at, s, NEGATIVE)
    return s


def pair_backward(q, k, v, qx, kx, o, do, lse, causal):
    kt = k.astype(F32).T.astype(BF)
    spread = (do.astype(F32) * o.astype(F32)).T
    low_q, low_k = low_half(q.shape[0]), low_half(k.shape[0])
    zero_q, zero_k = jnp.zeros_like(q), jnp.zeros_like(k)
    dqs, grads = [], []

    def begin(head):
        s = mm(pick(head, low_k, k, kx), pick(head, low_q, q, qx), NT)
        return causal_only(s) if causal else s, mm(pick(head, low_k, v, zero_k), do, NT)

    def end(head, values):
        s, dp = values
        half = slice(head * HEAD, (head + 1) * HEAD)
        p = jnp.exp2(s * (SCALE * LOG2E) - lse[head : head + 1])
        ds = (p * (dp - jnp.sum(spread[half], axis=0, keepdims=True))).astype(BF)
        dqs.append(mm(kt[half], ds))
        grads.append(
            (mm(ds, pick(head, low_q, q, zero_q)), mm(p.astype(BF), pick(head, low_q, do, zero_q)))
        )

    in_order(range(2), begin, end)
    (dk0, dv0), (dk1, dv1) = grads
    return jnp.concatenate(dqs, axis=0).T * SCALE, (dk0 + dk1) * SCALE, dv0 + dv1


def attn_bwd_kernel(
    q_ref, k_ref, v_ref, qx_ref, kx_ref, o_ref, do_ref, lse_ref, dq_ref, dk_ref, dv_ref, *, causal
):
    dq, dk, dv = pair_backward(
        q_ref[...], k_ref[...], v_ref[...], qx_ref[0], kx_ref[0], o_ref[...], do_ref[...],
        lse_ref[0], causal,
    )
    dq_ref[...] = dq.astype(BF)
    dk_ref[...] = dk.astype(BF)
    dv_ref[...] = dv.astype(BF)


def column_block(length, first):
    return pl.BlockSpec((length, PAIR), lambda p: (0, first + p))


def mask_block(length, row):
    return pl.BlockSpec((1, length, PAIR), lambda p: (row, 0, 0))


def pair_block(count_q):
    return pl.BlockSpec((1, 2, count_q), lambda p: (p, 0, 0))


def params(**more):
    return pltpu.CompilerParams(vmem_limit_bytes=VMEM_LIMIT, **more)


def attention_backward(q_in, k_in, v_in, qx, kx, row, firsts, mixed, grad_mixed, lse, causal):
    count_q, count_k, pairs = q_in.shape[0], k_in.shape[0], HEADS // 2
    width = HEADS * HEAD
    return pl.pallas_call(
        functools.partial(attn_bwd_kernel, causal=causal),
        grid=(pairs,),
        in_specs=[
            column_block(count_q, firsts[0]),
            column_block(count_k, firsts[1]),
            column_block(count_k, firsts[2]),
            mask_block(count_q, row),
            mask_block(count_k, row),
            column_block(count_q, 0),
            column_block(count_q, 0),
            pair_block(count_q),
        ],
        out_specs=[
            column_block(count_q, 0),
            column_block(count_k, 0),
            column_block(count_k, 0),
        ],
        out_shape=[
            jax.ShapeDtypeStruct((count_q, width), BF),
            jax.ShapeDtypeStruct((count_k, width), BF),
            jax.ShapeDtypeStruct((count_k, width), BF),
        ],
        compiler_params=params(),
    )(q_in, k_in, v_in, qx, kx, mixed, grad_mixed, lse)


BLOCK = 256
SLICE = 512


def inverse_rms(v):
    return lax.rsqrt(jnp.mean(v * v, -1, keepdims=True) + EPSILON)


def norm(v, gain):
    return (v * inverse_rms(v) * gain).astype(BF)


def norm_back(v, gain, grad):
    inv = inverse_rms(v)
    scaled = grad * gain
    along = jnp.mean(scaled * v, -1, keepdims=True)
    return (
        inv * scaled - v * (inv * inv * inv * along),
        jnp.sum(grad * v * inv, 0, keepdims=True),
    )


def gelu(x):
    return 0.5 * x * (1.0 + jnp.tanh(GELU_C * (x + GELU_A * x * x * x)))


def gelu_parts(x):
    square = x * x
    t = jnp.tanh(GELU_C * x * (1.0 + GELU_A * square))
    half = 0.5 * (1.0 + t)
    slope = half + 0.5 * x * (1.0 - t * t) * (GELU_C * (1.0 + 3.0 * GELU_A * square))
    return x * half, slope


class Fetch:
    def __init__(self, sources, held, sems):
        self.copies = [
            pltpu.make_async_copy(src, dst, sems.at[i])
            for i, (src, dst) in enumerate(zip(sources, held))
        ]
        self.held = held
        self.first = pl.program_id(0) == 0

        @pl.when(self.first)
        def _():
            for copy in self.copies:
                copy.start()

    def __getitem__(self, i):
        @pl.when(self.first)
        def _():
            self.copies[i].wait()

        return self.held[i]


def add_gain(ref, part):
    @pl.when(pl.program_id(0) == 0)
    def _():
        ref[...] = part

    @pl.when(pl.program_id(0) > 0)
    def _():
        ref[...] += part


def block_call(kernel, steps, ins, weights, outs, gain_outs=0):
    specs, arrays = [], []
    for array, row, first in ins:
        columns = array.shape[-1]
        if row is None:
            specs.append(pl.BlockSpec((BLOCK, columns), lambda i, f=first: (f + i, 0)))
        else:
            specs.append(
                pl.BlockSpec((None, BLOCK, columns), lambda i, r=row, f=first: (r, f + i, 0))
            )
        arrays.append(array)
    gains = [w for w in weights if w.dtype == F32]
    mats = [w for w in weights if w.dtype != F32]
    specs += [pl.BlockSpec((1, g.shape[1]), lambda i: (0, 0)) for g in gains]
    specs += [pl.BlockSpec(memory_space=pl.ANY)] * len(mats)
    dim = gains[0].shape[1]
    count = len(mats)

    def run(*refs):
        held, sems = refs[-1 - count : -1], refs[-1]
        at = len(arrays) + len(gains)
        fetch = Fetch(refs[at : at + count], held, sems)
        kernel(refs[: len(arrays)], [g[...] for g in refs[len(arrays) : at]], fetch, refs[at + count : -1 - count])

    return pl.pallas_call(
        run,
        grid=(steps,),
        in_specs=specs,
        out_specs=[pl.BlockSpec((BLOCK, c), lambda i: (i, 0)) for c, _ in outs]
        + [pl.BlockSpec((1, dim), lambda i: (0, 0))] * gain_outs,
        out_shape=[jax.ShapeDtypeStruct((steps * BLOCK, c), t) for c, t in outs]
        + [jax.ShapeDtypeStruct((1, dim), F32)] * gain_outs,
        scratch_shapes=[pltpu.VMEM(m.shape, m.dtype) for m in mats]
        + [pltpu.SemaphoreType.DMA((count,))],
        compiler_params=params(),
    )(*arrays, *gains, *mats)


def project_kernel(ins, gains, w, outs):
    (x,), (g0,), (n_ref, packed_ref) = ins, gains, outs
    n = norm(x[...].astype(F32), g0)
    n_ref[...] = n
    wa = w[0]
    dim = x.shape[1]
    for at in range(0, wa.shape[1], dim):
        packed_ref[:, at : at + dim] = mm(n, wa[:, at : at + dim]).astype(BF)


class FeedForward:
    def __init__(self, move, wf_hbm, wd_hbm, wf, wd):
        self.wf, self.wd, self.half = wf, wd, wd.shape[0]
        self.copies, self.move = {}, move
        self.sources = wf_hbm, wd_hbm

    def load(self):
        wf_hbm, wd_hbm = self.sources
        for at in range(0, self.half, SLICE):
            self.copies[at] = [
                self.move.copy(wd_hbm.at[at : at + SLICE], self.wd.at[at : at + SLICE])
            ] + [
                self.move.copy(wf_hbm.at[:, first : first + SLICE], self.wf.at[:, first : first + SLICE])
                for first in (at, self.half + at)
            ]

    def ready(self, at):
        for made in self.copies.pop(at, []):
            made.wait()

    def slices(self):
        return range(0, self.half, SLICE)

    def parts(self, at):
        self.ready(at)
        up = slice(self.half + at, self.half + at + SLICE)
        return self.wf[:, at : at + SLICE], self.wf[:, up], self.wd[at : at + SLICE, :]


def ffn_up(m, ffn, acc, u_ref, act_ref):
    half = ffn.half

    def begin(at):
        gate_w, up_w, _ = ffn.parts(at)
        return mm(m, gate_w), mm(m, up_w)

    total = [acc]

    def end(at, values):
        gate, up = values
        u_ref[:, at : at + SLICE] = gate.astype(BF)
        u_ref[:, half + at : half + at + SLICE] = up.astype(BF)
        act = (gelu(gate) * up).astype(BF)
        if act_ref is not None:
            act_ref[:, at : at + SLICE] = act
        total[0] = total[0] + mm(act, ffn.wd[at : at + SLICE, :])

    in_order(ffn.slices(), begin, end)
    return total[0]


def ffn_down(branch, ffn, u_ref, du_ref, act_ref):
    half = ffn.half
    total = []

    def begin(at):
        return mm(branch, ffn.parts(at)[2], NT)

    def end(at, d_act):
        gate_w, up_w, _ = ffn.parts(at)
        gate = u_ref[:, at : at + SLICE].astype(F32)
        up = u_ref[:, half + at : half + at + SLICE].astype(F32)
        value, slope = gelu_parts(gate)
        if act_ref is not None:
            act_ref[:, at : at + SLICE] = (value * up).astype(BF)
        d_gate = (d_act * up * slope).astype(BF)
        d_up = (d_act * value).astype(BF)
        du_ref[:, at : at + SLICE] = d_gate
        du_ref[:, half + at : half + at + SLICE] = d_up
        part = mm(d_gate, gate_w, NT) + mm(d_up, up_w, NT)
        total[:] = [part if not total else total[0] + part]

    in_order(ffn.slices(), begin, end)
    return total[0]


def dec_query_kernel(ins, gains, w, outs):
    (o, x), (g1,), (d1_ref, c_ref, cq_ref) = ins, gains, outs
    d1 = x[...].astype(F32) + mm(o[...], w[0][...])
    d1_ref[...] = d1
    c = norm(d1, g1)
    c_ref[...] = c
    cq_ref[...] = mm(c, w[1][:, : c.shape[1]]).astype(BF)


def dec_ffn_kernel(row, x_hbm, oc_hbm, d1_hbm, g2, wc_hbm, wf_hbm, wd_hbm, *refs):
    outs, results, held = refs[:8], refs[8:16], refs[16:]
    doc, out, dd2_v, m_v, act, du, branch, dg2 = results
    oc, d1, cot, u, proj, wf, wd, sems = held
    move = Mover(sems)
    tokens, width = oc.shape
    got = [
        move.copy(a, b)
        for a, b in ((oc_hbm, oc), (wc_hbm.at[:, width:], proj), (d1_hbm, d1))
    ]
    ffn = FeedForward(move, wf_hbm, wd_hbm, wf, wd)
    ffn.load()
    got_cot = move.copy(x_hbm.at[row, tokens:], cot)
    for made in got:
        made.wait()
    d2 = d1[...] + mm(oc[...], proj[...], NT)
    m = norm(d2, g2[...])
    m_v[...] = m
    out[...] = ffn_up(m, ffn, d2, u, act)
    for i in (3, 1, 4):
        move.store(results[i], outs[i])
    got_cot.wait()
    dm = ffn_down(cot[...], ffn, u, du, None)
    back, dg2[...] = norm_back(d2, g2[...], dm)
    dd2 = cot[...].astype(F32) + back
    branch[...] = dd2.astype(BF)
    doc[...] = mm(branch[...], proj[...]).astype(BF)
    dd2_v[...] = dd2
    for i in (0, 2, 5, 6, 7):
        move.store(results[i], outs[i])
    move.drain()


def enc_back_kernel(blocks, dk_hbm, dv_hbm, e1_hbm, e2_hbm, u_hbm, g1, g2, wc_hbm, wd_hbm, wf_hbm, wo_hbm, *refs):
    outs, results, held = refs[:10], refs[10:20], refs[20:]
    mem, fb_v, m_v, act, du, de1_v, ab_v, do, dg1, dg2 = results
    dk, dv, e1_in, e2_in, u, wc, wd, wf, wo, sems = held
    move = Mover(sems)
    width = dk.shape[1]
    here = [slice(i * BLOCK, (i + 1) * BLOCK) for i in range(len(blocks))]
    there = [slice(i * BLOCK, (i + 1) * BLOCK) for i in blocks]

    def load(i, pairs):
        return [move.copy(src.at[there[i]], dst.at[here[i]]) for src, dst in pairs]

    early = ((dk_hbm, dk), (dv_hbm, dv), (e2_hbm, e2_in))
    late = ((u_hbm, u), (e1_hbm, e1_in))
    got_early, got_late = [load(0, early)], []
    got_early[0].append(move.copy(wc_hbm, wc))
    ffn = FeedForward(move, wf_hbm, wd_hbm, wf, wd)
    got_late.append(load(0, late))
    ffn.load()
    got_late[0].append(move.copy(wo_hbm, wo))
    for i in range(1, len(blocks)):
        got_early.append(load(i, early))
        got_late.append(load(i, late))
    for i, b in enumerate(here):
        for made in got_early[i]:
            made.wait()
        dmem = mm(dk[b], wc[:, :width], NT) + mm(dv[b], wc[:, width:], NT)
        mem[b] = norm(e2_in[b], g1[...])
        de2, gain1 = norm_back(e2_in[b], g1[...], dmem)
        fb = de2.astype(BF)
        fb_v[b] = fb
        for made in got_late[i]:
            made.wait()
        m_v[b] = norm(e1_in[b], g2[...])
        dm = ffn_down(fb, ffn, u.at[b], du.at[b], act.at[b])
        back, gain2 = norm_back(e1_in[b], g2[...], dm)
        de1 = de2 + back
        de1_v[b] = de1
        ab = de1.astype(BF)
        ab_v[b] = ab
        do[b] = mm(ab, wo[...], NT).astype(BF)
        for k in range(8):
            move.store(results[k].at[b], outs[k].at[b])
        dg1[...] = gain1 if i == 0 else dg1[...] + gain1
        dg2[...] = gain2 if i == 0 else dg2[...] + gain2
    move.store(dg1, outs[8])
    move.store(dg2, outs[9])
    move.drain()


def dec_back_kernel(ins, gains, w, outs):
    (dcq, d1_in, dd2), (g1,), (dd1_ref, ab_ref, do_ref, dg1_ref) = ins, gains, outs
    d1 = d1_in[...]
    dc = mm(dcq[...], w[0][:, : dcq.shape[1]], NT)
    back, dg1 = norm_back(d1, g1, dc)
    dd1 = dd2[...] + back
    dd1_ref[...] = dd1
    ab = dd1.astype(BF)
    ab_ref[...] = ab
    do_ref[...] = mm(ab, w[1][...], NT).astype(BF)
    add_gain(dg1_ref, dg1)


def input_grad_kernel(ins, gains, w, outs):
    (dq, dk, dv, x, grad), (g0,), (dx_ref, dg0_ref) = ins, gains, outs
    wa = w[0]
    width = dq.shape[1]
    dn = (
        mm(dq[...], wa[:, :width], NT)
        + mm(dk[...], wa[:, width : 2 * width], NT)
        + mm(dv[...], wa[:, 2 * width :], NT)
    )
    back, dg0 = norm_back(x[...].astype(F32), g0, dn)
    dx_ref[...] = grad[...] + back
    add_gain(dg0_ref, dg0)


class Mover:
    def __init__(self, sems):
        self.sems, self.used, self.stores = sems, 0, []

    def copy(self, src, dst):
        made = pltpu.make_async_copy(src, dst, self.sems.at[self.used])
        self.used += 1
        made.start()
        return made

    def store(self, src, dst):
        self.stores.append(self.copy(src, dst))

    def drain(self):
        for made in self.stores:
            made.wait()


def pair_columns(first, p):
    return slice(first + p * PAIR, first + (p + 1) * PAIR)


def pick(head, low, a, b):
    return jnp.where(low, a, b) if head % 2 == 0 else jnp.where(low, b, a)


def in_order(items, begin, end, lead=1):
    waiting = []
    for item in items:
        waiting.append((item, begin(item)))
        if len(waiting) > lead:
            end(*waiting.pop(0))
    while waiting:
        end(*waiting.pop(0))


def attend(q_ref, kv_ref, firsts, qx, kx, o_ref, lse_ref, causal):
    count_q, count_k = qx.shape[0], kx.shape[0]
    low_q, low_k = low_half(count_q), low_half(count_k)
    ones = jnp.ones((8, count_k), BF)
    values, outs = {}, {}

    def begin(head):
        q = q_ref[:, pair_columns(firsts[0], head // 2)]
        k = kv_ref[:, pair_columns(firsts[1], head // 2)]
        s = mm(pick(head, low_k, k, kx), pick(head, low_q, q, qx), NT)
        return causal_only(s) if causal else s

    def end(head, s):
        p = head // 2
        if head % 2 == 0:
            values[p] = kv_ref[:, pair_columns(firsts[2], p)].astype(F32).T.astype(BF)
        vt = values[p][(head % 2) * HEAD : (head % 2 + 1) * HEAD]
        top = jnp.max(s, axis=0, keepdims=True)
        e = jnp.exp2((s - top) * (SCALE * LOG2E)).astype(BF)
        mixed = mm(jnp.concatenate([vt, ones], axis=0), e)
        total = mixed[HEAD : HEAD + 1]
        outs[head] = mixed[:HEAD] * (1.0 / total)
        lse_ref[p, head % 2 : head % 2 + 1, :] = top * (SCALE * LOG2E) + jnp.log2(total)
        if head % 2 == 1:
            both = jnp.concatenate([outs.pop(head - 1), outs.pop(head)], axis=0)
            o_ref[:, pair_columns(0, p)] = both.T.astype(BF)

    in_order(range(HEADS), begin, end)


def causal_only(s):
    key_at = lax.broadcasted_iota(jnp.int32, s.shape, 0)
    query_at = lax.broadcasted_iota(jnp.int32, s.shape, 1)
    return jnp.where(key_at <= query_at, s, NEGATIVE)


def attend_kernel(firsts, row, causal, same, *refs):
    if same:
        q_ref, (qx_ref, kx_ref, o_ref, lse_ref) = refs[0], refs[1:]
        kv_ref = q_ref
    else:
        q_ref, kv_ref, qx_ref, kx_ref, o_ref, lse_ref = refs
    attend(q_ref, kv_ref, firsts, qx_ref[row], kx_ref[row], o_ref, lse_ref, causal)


def attention_forward(q_in, kv_in, qx, kx, row, firsts, causal):
    count_q = q_in.shape[0]
    ins = [q_in] if kv_in is None else [q_in, kv_in]
    vmem = pl.BlockSpec(memory_space=pltpu.VMEM)
    return pl.pallas_call(
        functools.partial(attend_kernel, firsts, row, causal, kv_in is None),
        in_specs=[vmem] * (len(ins) + 2),
        out_specs=[vmem] * 2,
        out_shape=[
            jax.ShapeDtypeStruct((count_q, HEADS * HEAD), BF),
            jax.ShapeDtypeStruct((HEADS // 2, 2, count_q), F32),
        ],
        compiler_params=params(),
    )(*ins, qx, kx)


def enc_attend_kernel(row, x_hbm, qx_hbm, kx_hbm, g0, wa_hbm, *refs):
    outs, (n_v, packed_v, o_v, lse_v, x, qx, kx, wa, sems) = refs[:4], refs[4:]
    move = Mover(sems)
    got_x = move.copy(x_hbm.at[row], x)
    got_wa = move.copy(wa_hbm, wa)
    got_masks = move.copy(qx_hbm.at[row], qx), move.copy(kx_hbm.at[row], kx)
    tokens, dim = x.shape
    got_x.wait()
    blocks = [slice(at, at + BLOCK) for at in range(0, tokens, BLOCK)]
    for b in blocks:
        n_v[b] = norm(x[b].astype(F32), g0[...])
    move.store(n_v, outs[0])
    got_wa.wait()
    for b in blocks:
        for at in range(0, wa.shape[1], dim):
            packed_v[b, at : at + dim] = mm(n_v[b], wa[:, at : at + dim]).astype(BF)
    move.store(packed_v, outs[1])
    for made in got_masks:
        made.wait()
    attend(packed_v, packed_v, (0, dim, 2 * dim), qx[...], kx[...], o_v, lse_v, False)
    move.store(o_v, outs[2])
    move.store(lse_v, outs[3])
    move.drain()


def enc_rest_kernel(row, x_hbm, o_hbm, g1, g2, wo_hbm, wf_hbm, wd_hbm, wc_hbm, *refs):
    outs, (e1_v, u_v, e2_v, sent_v, x, o, wo, wf, wd, wc, sems) = refs[:4], refs[4:]
    move = Mover(sems)
    got = [move.copy(a, b) for a, b in ((x_hbm.at[row], x), (o_hbm, o), (wo_hbm, wo))]
    ffn = FeedForward(move, wf_hbm, wd_hbm, wf, wd)
    ffn.load()
    got_wc = [move.copy(wc_hbm, wc)]
    for made in got:
        made.wait()
    blocks = [slice(at, at + BLOCK) for at in range(0, x.shape[0], BLOCK)]
    for b in blocks:
        e1_v[b] = x[b].astype(F32) + mm(o[b], wo[...])
        move.store(e1_v.at[b], outs[0].at[b])
    for b in blocks:
        e1 = e1_v[b]
        e2 = ffn_up(norm(e1, g2[...]), ffn, e1, u_v.at[b], None)
        e2_v[b] = e2
        while got_wc:
            got_wc.pop().wait()
        sent_v[b] = mm(norm(e2, g1[...]), wc[...]).astype(BF)
        for src, dst in ((u_v, outs[1]), (e2_v, outs[2]), (sent_v, outs[3])):
            move.store(src.at[b], dst.at[b])
    move.drain()


HBM = pl.BlockSpec(memory_space=pl.ANY)
VMEM = pl.BlockSpec(memory_space=pltpu.VMEM)


def moved_call(kernel, ins, specs, outs, held, copies):
    return list(
        pl.pallas_call(
            kernel,
            in_specs=specs,
            out_specs=[HBM] * len(outs),
            out_shape=[jax.ShapeDtypeStruct(s, t) for s, t in outs],
            scratch_shapes=[pltpu.VMEM(s, t) for s, t in outs + held]
            + [pltpu.SemaphoreType.DMA((copies,))],
            compiler_params=params(),
        )(*ins)
    )


def enc_attend(row, x_in, qx, kx, g0, wa):
    tokens, dim = x_in.shape[1:]
    width = wa.shape[1] // 3
    kept = [
        ((tokens, dim), BF),
        ((tokens, wa.shape[1]), BF),
        ((tokens, width), BF),
        ((HEADS // 2, 2, tokens), F32),
    ]
    held = [(x_in.shape[1:], BF), (qx.shape[1:], BF), (kx.shape[1:], BF), (wa.shape, BF)]
    return moved_call(
        functools.partial(enc_attend_kernel, row),
        (x_in, qx, kx, g0, wa),
        [HBM] * 3 + [VMEM] + [HBM],
        kept,
        held,
        8,
    )


def enc_rest(row, x_in, o, g1, g2, wo, wf, wd, wc):
    tokens, dim = x_in.shape[1:]
    kept = [
        ((tokens, dim), F32),
        ((tokens, wf.shape[1]), BF),
        ((tokens, dim), F32),
        ((tokens, wc.shape[1]), BF),
    ]
    held = [(x_in.shape[1:], BF), (o.shape, BF)] + [(w.shape, BF) for w in (wo, wf, wd, wc)]
    return moved_call(
        functools.partial(enc_rest_kernel, row),
        (x_in, o, g1, g2, wo, wf, wd, wc),
        [HBM] * 2 + [VMEM] * 2 + [HBM] * 4,
        kept,
        held,
        4 + 3 * (wd.shape[0] // SLICE) + 4 * (tokens // BLOCK),
    )


def nothing_kernel(*refs):
    pass


def unwritten(shapes):
    return pl.pallas_call(
        nothing_kernel,
        out_specs=[pl.BlockSpec(memory_space=pl.ANY)] * len(shapes),
        out_shape=[jax.ShapeDtypeStruct(s.shape, s.dtype) for s in shapes],
    )()


def by_section(on_decoder, encoder, decoder):
    enc_shapes = jax.eval_shape(encoder) if encoder else []
    dec_shapes = jax.eval_shape(decoder) if decoder else []
    none = lambda: []
    encoder, decoder = encoder or none, decoder or none
    pool = lambda shapes: list(unwritten(shapes)) if shapes else []
    both = lax.cond(
        on_decoder,
        lambda: pool(enc_shapes) + list(decoder()),
        lambda: list(encoder()) + pool(dec_shapes),
    )
    return both[: len(enc_shapes)], both[len(enc_shapes) :]


def segment_ids(lengths, span_len):
    positions = jnp.arange(span_len, dtype=jnp.int32)[None, :]
    seg, end = jnp.zeros((lengths.shape[0], span_len), jnp.int32), 0
    for j in range(lengths.shape[1]):
        end = end + lengths[:, j : j + 1]
        seg = seg + (positions >= end).astype(jnp.int32)
    return seg


def mask_lanes(seg, count):
    hit = seg[:, :, None] == jnp.arange(HEAD, dtype=jnp.int32)[None, None, :]
    member = hit.astype(BF)
    other = jnp.where(
        jnp.arange(HEAD, dtype=jnp.int32)[None, None, :] < count,
        jnp.where(hit, 0.0, NEGATIVE),
        0.0,
    ).astype(BF)
    return (
        jnp.concatenate([member, member], -1),
        jnp.concatenate([other, other], -1),
    )


def shift(x, by):
    pairs = [(0, 1)] if by > 0 else [(1, 0)]
    return lax.ppermute(x, "section", pairs)


def body(
    section_input, enc_lengths, dec_lengths, attn_in, attn_out, ffn_in, ffn_out, cross_weight, gains
):
    wa, wo, wf, wd, wc = attn_in[0], attn_out[0], ffn_in[0], ffn_out[0], cross_weight[0]
    g0, g1, g2 = gains[0, 0:1], gains[0, 1:2], gains[0, 2:3]
    x_in = section_input[0]
    rows, le, dim = x_in.shape
    ld = le // 2
    width = wo.shape[0]
    docs = enc_lengths.shape[1]
    enc_qx, enc_kx = mask_lanes(segment_ids(enc_lengths, le), docs)
    dec_qx, dec_kx = mask_lanes(segment_ids(dec_lengths, ld), docs)
    on_decoder = lax.axis_index("section") == 1
    steps_e, steps_d = le // BLOCK, ld // BLOCK
    columns = width // PAIR
    own = (0, columns, 2 * columns)
    across = (0, 0, columns)
    inner = wf.shape[1]

    def project(r, steps):
        return list(
            block_call(project_kernel, steps, [(x_in, r, 0)], [g0, wa], [(dim, BF), (3 * width, BF)])
        )

    def dec_first(r):
        n, packed = project(r, steps_d)
        o, lse = attention_forward(packed, None, dec_qx, dec_kx, r, (0, width, 2 * width), True)
        d1, c, cq = block_call(
            dec_query_kernel,
            steps_d,
            [(o, None, 0), (x_in, r, 0)],
            [g1, wo, wc],
            [(dim, F32), (dim, BF), (width, BF)],
        )
        return [n, packed, o, lse, d1, c, cq]

    def cross(r, cq, sent):
        return list(attention_forward(cq, sent, dec_qx, enc_kx, r, (0, 0, width), False))

    feeds = 3 * (wd.shape[0] // SLICE)

    def dec_ffn(r, oc, d1):
        row = lambda columns, kind: ((ld, columns), kind)
        return moved_call(
            functools.partial(dec_ffn_kernel, r),
            (x_in, oc, d1, g2, wc, wf, wd),
            [HBM] * 3 + [VMEM] + [HBM] * 3,
            [row(width, BF), row(dim, F32), row(dim, F32), row(dim, BF), row(wd.shape[0], BF)]
            + [row(inner, BF), row(dim, BF), ((1, dim), F32)],
            [row(width, BF), row(dim, F32), row(dim, BF), row(inner, BF), ((dim, width), BF)]
            + [(wf.shape, BF), (wd.shape, BF)],
            feeds + 4 + 8,
        )

    def cross_back(r, cq, sent, oc, doc, lse):
        return list(
            attention_backward(cq, sent, sent, dec_qx, enc_kx, r, across, oc, doc, lse, False)
        )

    def enc_back(dk, dv, e1, e2, u, blocks):
        row = lambda columns, kind: ((len(blocks) * BLOCK, columns), kind)
        return moved_call(
            functools.partial(enc_back_kernel, blocks),
            (dk, dv, e1, e2, u, g1, g2, wc, wd, wf, wo),
            [HBM] * 5 + [VMEM] * 2 + [HBM] * 4,
            [row(dim, BF)] * 3
            + [row(wd.shape[0], BF), row(inner, BF), row(dim, F32), row(dim, BF), row(width, BF)]
            + [((1, dim), F32)] * 2,
            [row(width, BF)] * 2
            + [row(dim, F32)] * 2
            + [row(inner, BF)]
            + [(w.shape, BF) for w in (wc, wd, wf, wo)],
            feeds + 2 + 5 * len(blocks) + 8 * len(blocks) + 2,
        )

    def self_back(r, steps, masks, causal, packed, o, lse, do, grad):
        dq, dk, dv = attention_backward(
            packed, packed, packed, *masks, r, own, o, do, lse, causal
        )
        dx, dg0 = block_call(
            input_grad_kernel,
            steps,
            [(dq, None, 0), (dk, None, 0), (dv, None, 0), (x_in, r, 0), (grad, None, 0)],
            [g0, wa],
            [(dim, F32)],
            1,
        )
        return [dq, dk, dv, dx, dg0]

    def dec_back(dcq, d1, dd2):
        return list(
            block_call(
                dec_back_kernel,
                steps_d,
                [(dcq, None, 0), (d1, None, 0), (dd2, None, 0)],
                [g1, wc, wo],
                [(dim, F32), (dim, BF), (width, BF)],
                1,
            )
        )

    every = range(rows)
    plain = lax.axis_size("rows") != PEERS
    state = []

    def run(encoder, decoder, *ready):
        held = on_decoder
        if state:
            held, state[0][1], *_ = lax.optimization_barrier((on_decoder, state[0][1]) + ready)
        out = by_section(held, encoder, decoder)
        state[:] = [out[0] or out[1]]
        return out

    def slots():
        return [None] * rows

    first, rest, dfirst, cqs, crossed, ocs = slots(), slots(), slots(), slots(), slots(), slots()
    mids, docs_in, cross_b, dcqs, back, last, dlast = (slots() for _ in range(7))

    def begin_cross(r, beside=None):
        crossed[r], out = run(lambda: cross(r, cqs[r], rest[r][3]), beside)
        ocs[r] = shift(crossed[r][0], 1)
        return out

    def dec_mid(r):
        return lambda: dec_ffn(r, ocs[r], dfirst[r][4])

    def keep_mid(r, out):
        mids[r] = out
        docs_in[r] = shift(out[0], -1)

    def dec_last(r):
        p = dec_back(dcqs[r], dfirst[r][4], mids[r][2])
        n, packed, o, lse = dfirst[r][:4]
        return p + self_back(r, steps_d, (dec_qx, dec_kx), True, packed, o, lse, p[2], p[0])

    def enc_last(r):
        return self_back(
            r, steps_e, (enc_qx, enc_kx), False, *first[r][1:4],
            jnp.concatenate(backs(r, 7), 0), jnp.concatenate(backs(r, 5), 0),
        )

    def enc_first(r):
        return lambda: enc_attend(r, x_in, enc_qx, enc_kx, g0, wa)

    def enc_then(r):
        return lambda: enc_rest(r, x_in, first[r][2], g1, g2, wo, wf, wd, wc)

    first[0], dfirst[0] = run(enc_first(0), lambda: dec_first(0))
    cqs[0] = shift(dfirst[0][6], -1)
    rest[0], more = run(enc_then(0), lambda: [v for r in every[1:] for v in dec_first(r)])
    begin_cross(0)
    for r in every[1:]:
        dfirst[r] = more[7 * (r - 1) : 7 * r]
        cqs[r] = shift(dfirst[r][6], -1)
    for r in every[1:]:
        first[r], _ = run(enc_first(r), None)
        rest[r], out = run(enc_then(r), dec_mid(r - 1), ocs[r - 1])
        keep_mid(r - 1, out)
        begin_cross(r)
    def backs(r, i):
        return [part[i] for part in back[r]]

    def enc_backs(r, blocks):
        return lambda: enc_back(
            cross_b[r][1], cross_b[r][2], rest[r][0], rest[r][2], rest[r][1], blocks
        )

    for r in every:
        cross_b[r], _ = run(
            lambda: cross_back(r, cqs[r], rest[r][3], crossed[r][0], docs_in[r], crossed[r][1]),
            None,
        )
        if r == 0 and steps_e > 1:
            part, out = run(enc_backs(0, (0,)), dec_mid(rows - 1))
            keep_mid(rows - 1, out)
            dcqs[0] = shift(cross_b[0][0], 1)
            others, _ = run(enc_backs(0, tuple(range(1, steps_e))), None)
            back[0] = [part, others]
        else:
            dcqs[r] = shift(cross_b[r][0], 1)
            out = run(enc_backs(r, tuple(range(steps_e))), dec_mid(rows - 1) if r == 0 else None)
            back[r] = [out[0]]
            if r == 0:
                keep_mid(rows - 1, out[1])
        last[r], dlast[r] = run((lambda: enc_last(r)) if plain else None, lambda: dec_last(r))

    def over_rows(lists):
        pieces = lambda v: v if isinstance(v, list) else [v]
        return [[p for v in group for p in pieces(v)] for group in zip(*lists)]

    enc_side = (
        over_rows(
            [backs(r, 2), backs(r, 3), backs(r, 0), backs(r, 0), first[r][2], first[r][0]]
            for r in every
        ),
        over_rows(
            [backs(r, 4), backs(r, 1), cross_b[r][1], cross_b[r][2], backs(r, 6)] + last[r][0:3]
            for r in every
        ),
    )
    dec_side = (
        over_rows(
            [mids[r][3], mids[r][4], dfirst[r][5], mids[r][6], dfirst[r][2], dfirst[r][0]]
            for r in every
        ),
        over_rows(
            [mids[r][5], x_in[r, ld:], dcqs[r], ocs[r], dlast[r][1]] + dlast[r][4:7] for r in every
        ),
    )
    if not plain:
        kept = over_rows(
            [first[r][1], first[r][2], backs(r, 7), first[r][3], backs(r, 5)] for r in every
        )
        decoded = over_rows([mids[r][1], dlast[r][7]] for r in every)
        gain_rows = (
            over_rows([backs(r, 8), backs(r, 9)] for r in every),
            over_rows([dlast[r][8], dlast[r][3], mids[r][7]] for r in every),
        )
        s_in, s_out, s_fi, s_cross, s_gain, s_fo, results = grad_sum(
            (enc_side, dec_side), kept, decoded, gain_rows, (x_in, enc_qx, enc_kx, wa, g0)
        )
        o_gain, *outs = hand_over(
            s_gain, gains.shape[1], [results, s_in, s_out, s_fi, s_fo, s_cross]
        )
        return tuple(outs) + (o_gain,)

    def enc_parts():
        gain_rows = [sum(v) for v in zip(*[[last[r][4], sum(backs(r, 8)), sum(backs(r, 9))] for r in every])]
        return [jnp.concatenate(gain_rows, 0), jnp.stack([last[r][3] for r in every])]

    def dec_parts():
        gain_rows = [sum(v) for v in zip(*[[dlast[r][8], dlast[r][3], mids[r][7]] for r in every])]
        both = [jnp.concatenate([mids[r][1], dlast[r][7]], 0) for r in every]
        return [jnp.concatenate(gain_rows, 0), jnp.stack(both)]

    gain_grads, results = lax.cond(on_decoder, dec_parts, enc_parts)
    gain_terms = jnp.pad(gain_grads.T, ((0, 0), (0, LANES - gain_grads.shape[0]))).astype(BF)

    s_in, s_out, s_fi, s_cross, s_gain, s_fo = plain_sum(on_decoder, (enc_side, dec_side), gain_terms)
    return (
        results[None],
        s_in[None],
        s_out[None],
        s_fi[None],
        s_fo[None],
        s_cross[None],
        s_gain[:, : gain_grads.shape[0]].T[None],
    )


def solution(mesh):
    placed = (
        P("section", "rows", None, None),
        P("rows", None),
        P("rows", None),
    ) + (P("section", None, None),) * 6
    return jax.shard_map(
        body,
        mesh=mesh,
        in_specs=placed,
        out_specs=(
            P("section", "rows", None, None),
            P("section", "rows", None),
            P("section", "rows", None),
            P("section", "rows", None),
            P("section", "rows", None),
            P("section", "rows", None),
            P("section", None, "rows"),
        ),
        check_vma=False,
    )
```

```python
import functools

import jax
import jax.numpy as jnp
from jax import lax
from jax.experimental import pallas as pl
from jax.experimental.pallas import tpu as pltpu
from jax.sharding import PartitionSpec as P

HEADS = 12
HEAD = 64
PAIR = 128
EPSILON = 1e-06
SCALE = 0.125
LOG2E = 1.4426950408889634
NEGATIVE = -1e30
GELU_C = 0.7978845608028654
GELU_A = 0.044715

BF = jnp.bfloat16
F32 = jnp.float32
NT = (((1,), (1,)), ((), ()))
NN = (((1,), (0,)), ((), ()))
TN = (((0,), (0,)), ((), ()))


def mm(a, b, dims=NN):
    return lax.dot_general(a, b, dims, preferred_element_type=F32)


MESH = pl.DeviceIdType.MESH
LANES = 256
VMEM_LIMIT = 56 * 1024 * 1024
SUM_VMEM = 60 * 1024 * 1024

NZ, NY, NC = 4, 2, 2
PEERS = NZ * NY * NC
C_LAG = 2
Y_LAG = C_LAG + 4
HOP = 3
ZF_EVERY, ZF_AT = 6, 3
ZF_LAG = C_LAG + HOP * (NZ - 1)
RING = 6
AHEAD = 3
PANELS = 4

TALL = 1
LEFT_ORDER = (0, 2, 3, 4, 5)
PRODUCTS = ((0, 0), (1, 1), (2, 2), (3, 3), (4, 4), (5, 5), (5, 6), (5, 7))


def grad_sum_kernel(rows, group_sizes, token_counts, chunk_counts, unit_steps, *refs):
    remaining = list(refs)
    sizes = list(group_sizes)

    def take(groups):
        return [[remaining.pop(0) for _ in range(sizes.pop(0))] for _ in range(groups)]

    def take_one():
        return remaining.pop(0)

    lefts_of, rights_of = [], []
    for side in range(2):
        lefts_of.append(take(6))
        rights_of.append(take(5 if side == 0 else 8))
    packed_of, o_of, do_of, lse_of, de1_of = take(5)
    out_of, dx_of = take(2)
    gain_rows = [[None] + take(2), take(3)]
    x_ref, qx_ref, kx_ref, wa_ref, g0_ref = [take_one() for _ in range(5)]
    o_in, o_out, o_fi, o_cross, o_gain, o_fo, o_results = [take_one() for _ in range(7)]
    (
        xt, xt_tall, left_stage, tall_stage, tall_right, panels, ring,
        own, got_y, got_r, got_l, z_right, z_left,
        s_left, s_tall, s_right, s_panel,
        s_core, r_core, s_y, r_y, s_r, r_r, s_l, r_l,
        d_packed, wa, att, qx, kx, lse, x_stage, grad_stage, dx_stage, dg0,
        s_att, s_const, s_lse, s_block, s_out, s_dec,
    ) = remaining
    chunks, height, dim = own.shape[0], own.shape[3], xt.shape[0]
    sec, me = lax.axis_index("section"), lax.axis_index("rows")
    core, y, z = lax.rem(me, 2), lax.rem(me // 2, 2), me // 4
    by_core, by_y = me + 1 - 2 * core, me + 2 - 4 * y
    other, away = 1 - core, 1 - y
    bases = [sum(chunk_counts[:i]) for i in range(len(chunk_counts))]


    def each(act):
        for side in range(2):

            @pl.when(sec == side)
            def _(side=side):
                act(side)

    def row_copies(sources, columns, dst, sems, side):
        del side
        copies, at = [], 0
        for i, src in enumerate(sources):
            copies.append(
                pltpu.make_async_copy(
                    src if columns is None else src.at[:, columns],
                    dst.at[at : at + src.shape[0]],
                    sems.at[i],
                )
            )
            at += src.shape[0]
        return copies

    def start_all(copies):
        for copy in copies:
            copy.start()

    def wait_all(copies):
        for copy in copies:
            copy.wait()

    def left_copies(q, side):
        source = lefts_of[side][LEFT_ORDER[q]]
        return row_copies(source, None, left_stage.at[q % 2], s_left.at[q % 2], side)

    def tall_copies(side):
        return row_copies(lefts_of[side][1], None, tall_stage, s_tall, side)

    def tall_right_copies(side):
        return row_copies(rights_of[side][1], None, tall_right, s_right, side)

    def panel_copies(p, i, slot, side):
        if PRODUCTS[p][1] >= len(rights_of[side]):
            return []
        columns = pl.ds(pl.multiple_of(i * LANES, LANES), LANES)
        return row_copies(
            rights_of[side][PRODUCTS[p][1]], columns, panels.at[slot], s_panel.at[slot], side
        )

    def for_panel(t, act):
        slot = lax.rem(t, PANELS)
        for p in range(len(PRODUCTS)):
            if p != TALL:

                @pl.when((t >= bases[p]) & (t < bases[p] + chunk_counts[p]))
                def _(p=p):
                    each(lambda side: act(p, t - bases[p], slot, side))

    def flip(side, stage, columns, put):
        for at in range(0, rows * token_counts[side], LANES):
            tokens = slice(at, at + LANES)
            put(tokens, stage[tokens, columns].astype(F32).T.astype(BF))

    def build_left(q):
        def act(side):
            wait_all(left_copies(q, side))
            for at in range(0, xt.shape[0], LANES):

                def put(tokens, block, at=at):
                    xt[at : at + LANES, tokens] = block

                flip(side, left_stage.at[q % 2], slice(at, at + LANES), put)
            if q + 2 < len(LEFT_ORDER):
                start_all(left_copies(q + 2, side))

        each(act)

    groups = xt_tall.shape[0] // LANES
    tall_rows = xt_tall.shape[0] // PEERS

    def build_tall(part):
        columns = pl.ds(pl.multiple_of(part * LANES, LANES), LANES)
        targets = LANES // tall_rows

        def act(side):
            def put(tokens, block):
                for k in range(targets):
                    for j in range(tall_rows // 16):
                        to = j * LANES + (part * targets + k) * 16
                        xt_tall[pl.ds(pl.multiple_of(to, 16), 16), tokens] = block[
                            k * tall_rows + j * 16 : k * tall_rows + (j + 1) * 16
                        ]

            flip(side, tall_stage, columns, put)

        each(act)

    def send_core(j):
        slot = lax.rem(j, RING)
        return pltpu.make_async_remote_copy(
            src_ref=ring.at[slot, :, :, other],
            dst_ref=own.at[j],
            send_sem=s_core.at[j],
            recv_sem=r_core.at[j],
            device_id=(sec, by_core),
            device_id_type=MESH,
        )

    def send_y(j):
        return pltpu.make_async_remote_copy(
            src_ref=own.at[j, :, away],
            dst_ref=got_y.at[j],
            send_sem=s_y.at[j],
            recv_sem=r_y.at[j],
            device_id=(sec, by_y),
            device_id_type=MESH,
        )

    def send_right(j, at):
        return pltpu.make_async_remote_copy(
            src_ref=own.at[j, pl.ds(at + 1, NZ - 1 - at), y],
            dst_ref=got_r.at[j, pl.ds(at, NZ - 1 - at)],
            send_sem=s_r.at[j],
            recv_sem=r_r.at[j],
            device_id=(sec, me + 4),
            device_id_type=MESH,
        )

    def send_left(j, at):
        return pltpu.make_async_remote_copy(
            src_ref=own.at[j, pl.ds(0, at), y],
            dst_ref=got_l.at[j, pl.ds(0, at)],
            send_sem=s_l.at[j],
            recv_sem=r_l.at[j],
            device_id=(sec, me - 4),
            device_id_type=MESH,
        )

    def z_first(j):
        return lax.rem(j, ZF_EVERY) == ZF_AT

    def send_along(j, at, right):
        targets = pl.ds(at + 1, NZ - 1 - at) if right else pl.ds(0, at)
        buffer = z_right if right else z_left
        return pltpu.make_async_remote_copy(
            src_ref=own.at[j, targets],
            dst_ref=buffer.at[j // ZF_EVERY, pl.ds(at, NZ - 1 - at) if right else targets],
            send_sem=(s_r if right else s_l).at[j],
            recv_sem=(r_r if right else r_l).at[j],
            device_id=(sec, me + 4 if right else me - 4),
            device_id_type=MESH,
        )

    def send_y_last(j):
        return pltpu.make_async_remote_copy(
            src_ref=own.at[j, z, away],
            dst_ref=got_y.at[j, z],
            send_sem=s_y.at[j],
            recv_sem=r_y.at[j],
            device_id=(sec, by_y),
            device_id_type=MESH,
        )

    def forward_along(j, at, right):
        source = at - 1 if right else at + 1
        if 0 <= source < NZ:
            send_along(j, source, right).wait_recv()
            buffer = z_right if right else z_left
            for t in range(at + 1, NZ) if right else range(at):
                for b in range(NY):
                    add_into(own.at[j, t, b], buffer.at[j // ZF_EVERY, t - 1 if right else t, b])
        send_along(j, at, right).start()

    def turn_to_y(j):
        for at in range(NZ):

            @pl.when(z == at)
            def _(at=at):
                if at == NZ - 1:
                    send_along(j, at - 1, True).wait_recv()
                if at == 0:
                    send_along(j, at + 1, False).wait_recv()
                for b in range(NY):
                    if at > 0:
                        add_into(own.at[j, at, b], z_right.at[j // ZF_EVERY, at - 1, b])
                    if at < NZ - 1:
                        add_into(own.at[j, at, b], z_left.at[j // ZF_EVERY, at, b])

        send_y_last(j).start()

    def add_into(dst, src):
        dst[...] = (dst[...].astype(F32) + src[...].astype(F32)).astype(BF)


    def compute(s):
        slot = lax.rem(s, RING)

        def put_panel(value):
            for t in range(PEERS):
                ring[slot, t // 4, t // 2 % 2, t % 2] = value[t * height : (t + 1) * height]

        for p in range(len(PRODUCTS)):
            left = PRODUCTS[p][0]

            @pl.when((s >= bases[p]) & (s < bases[p] + chunk_counts[p]))
            def _(p=p, left=left):
                if p != TALL:
                    if p == 0 or PRODUCTS[p - 1][0] != left:

                        @pl.when(s == bases[p])
                        def _():
                            build_left(LEFT_ORDER.index(left))

                    where = lax.rem(s, PANELS)

                    def act(side):
                        wait_all(panel_copies(p, s - bases[p], where, side))
                        tokens = rows * token_counts[side]
                        if PRODUCTS[p][1] < len(rights_of[side]):
                            right = panels[where, :tokens, :]
                        else:
                            first = (PRODUCTS[p][1] - 5) * dim + (s - bases[p]) * LANES
                            right = d_packed[:, pl.ds(pl.multiple_of(first, LANES), LANES)]
                        put_panel(mm(xt[:, :tokens], right).astype(BF))

                    each(act)
                else:
                    rows_at = pl.ds(pl.multiple_of((s - bases[p]) * LANES, LANES), LANES)

                    @pl.when(s == bases[p])
                    def _():
                        each(lambda side: wait_all(tall_right_copies(side)))

                    def act(side):
                        tokens = rows * token_counts[side]
                        for k in range(tall_right.shape[1] // LANES):
                            value = mm(
                                xt_tall[rows_at, :tokens],
                                tall_right[:tokens, k * LANES : (k + 1) * LANES],
                            ).astype(BF)
                            for t in range(PEERS):
                                ring[slot, t // 4, t // 2 % 2, t % 2, k * 16 : (k + 1) * 16] = value[
                                    t * 16 : (t + 1) * 16
                                ]

                    each(act)

        @pl.when(s == chunks - 1)
        def _():
            def act(side):
                parts = []
                for group in gain_rows[side]:
                    total_row = dg0[...]
                    if group is not None:
                        total_row = group[0][...]
                        for ref in group[1:]:
                            total_row = total_row + ref[...]
                    parts.append(total_row)
                parts.append(jnp.zeros((LANES - len(parts), dim), F32))
                put_panel(jnp.concatenate(parts, axis=0).T.astype(BF))

            each(act)


    attn_units, block_units, first_block = unit_steps
    tokens_e = token_counts[0]
    per_row = tokens_e // BLOCK
    const_copies = [
        pltpu.make_async_copy(src, dst, s_const.at[i])
        for i, (src, dst) in enumerate(((qx_ref, qx), (kx_ref, kx), (wa_ref, wa)))
    ]
    lse_copies = [
        pltpu.make_async_copy(ref, lse.at[r], s_lse.at[r]) for r, ref in enumerate(lse_of)
    ]

    def row_pieces(refs_of, r):
        found, at = [], 0
        for ref in refs_of:
            if r * tokens_e <= at < (r + 1) * tokens_e:
                found.append((ref, at - r * tokens_e))
            at += ref.shape[0]
        return found

    def attn_loads(u, act):
        slot, p = lax.rem(u, 2), lax.rem(u, HEADS // 2)
        for r in range(rows):

            @pl.when(u // (HEADS // 2) == r)
            def _(r=r):
                at = lambda first: pl.ds(pl.multiple_of(first + p * PAIR, PAIR), PAIR)
                sources = [packed_of[r].at[:, at(k * dim)] for k in range(3)]
                sources.append(o_of[r].at[:, at(0)])
                copies = [
                    pltpu.make_async_copy(src, att.at[slot, k], s_att.at[slot, k])
                    for k, src in enumerate(sources)
                ]
                for ref, begin in row_pieces(do_of, r):
                    copies.append(
                        pltpu.make_async_copy(
                            ref.at[:, at(0)],
                            att.at[slot, 4, begin : begin + ref.shape[0]],
                            s_att.at[slot, len(copies)],
                        )
                    )
                act(copies)

    def attn_unit(u):
        slot, p, r = lax.rem(u, 2), lax.rem(u, HEADS // 2), u // (HEADS // 2)
        attn_loads(u, wait_all)
        q, k, v, o, do = [att[slot, i] for i in range(5)]
        grads = pair_backward(q, k, v, qx[r], kx[r], o, do, lse[r, p], False)
        where = pl.ds(pl.multiple_of(r * tokens_e, tokens_e), tokens_e)
        for i, value in enumerate(grads):
            at = pl.ds(pl.multiple_of(i * dim + p * PAIR, PAIR), PAIR)
            d_packed[where, at] = value.astype(BF)

    def block_loads(v, act):
        slot = lax.rem(v, 2)
        where = pl.ds(pl.multiple_of(lax.rem(v, per_row) * BLOCK, BLOCK), BLOCK)
        for r in range(rows):

            @pl.when(v // per_row == r)
            def _(r=r):
                act([pltpu.make_async_copy(x_ref.at[r, where], x_stage.at[slot], s_block.at[slot, 0])])

            for ref, begin in row_pieces(de1_of, r):
                for at in range(0, ref.shape[0], BLOCK):

                    @pl.when(v == (r * tokens_e + begin + at) // BLOCK)
                    def _(ref=ref, at=at):
                        act(
                            [
                                pltpu.make_async_copy(
                                    ref.at[at : at + BLOCK], grad_stage.at[slot], s_block.at[slot, 1]
                                )
                            ]
                        )

    def block_store(v):
        slot = lax.rem(v, 2)
        where = pl.ds(pl.multiple_of(lax.rem(v, per_row) * BLOCK, BLOCK), BLOCK)
        return pltpu.make_async_copy(
            dx_stage.at[slot], o_results.at[v // per_row, where], s_out.at[slot]
        )

    def block_unit(v):
        slot = lax.rem(v, 2)
        block_loads(v, wait_all)

        @pl.when(v == 0)
        def _():
            const_copies[2].wait()
            dg0[...] = jnp.zeros_like(dg0)

        @pl.when(v >= 2)
        def _():
            block_store(v - 2).wait()

        where = pl.ds(pl.multiple_of(v * BLOCK, BLOCK), BLOCK)
        dn = None
        for i in range(3):
            part = mm(d_packed[where, i * dim : (i + 1) * dim], wa[:, i * dim : (i + 1) * dim], NT)
            dn = part if dn is None else dn + part
        back, gain_part = norm_back(x_stage[slot].astype(F32), g0_ref[...], dn)
        dg0[...] += gain_part
        dx_stage[slot] = grad_stage[slot] + back
        block_store(v).start()

    def dec_results(store):
        half = token_counts[1]
        parts = [
            (ref, stage.at[r], o_results.at[r, k * half : (k + 1) * half], s_dec.at[k, r])
            for k, (group, stage) in enumerate(((out_of, grad_stage), (dx_of, dx_stage)))
            for r, ref in enumerate(group)
        ]
        return [
            pltpu.make_async_copy(held, dst, sem) if store else pltpu.make_async_copy(src, held, sem)
            for src, held, dst, sem in parts
        ]

    def side_work(s):
        @pl.when(s == 0)
        def _():
            start_all(lse_copies)
            start_all(const_copies)
            for v in range(2):
                block_loads(jnp.int32(v), start_all)

        u = s // 2

        @pl.when((lax.rem(s, 2) == 0) & (u < attn_units))
        def _():
            attn_loads(u, start_all)

        @pl.when((lax.rem(s, 2) == 0) & (u >= 1) & (u <= attn_units))
        def _():
            @pl.when(u == 1)
            def _():
                wait_all(lse_copies)
                wait_all(const_copies[:2])

            attn_unit(u - 1)

        v = (s - first_block) // 2

        @pl.when((lax.rem(s, 2) == 0) & (s >= first_block) & (v < block_units))
        def _():
            block_unit(v)

            @pl.when(v + 2 < block_units)
            def _():
                block_loads(v + 2, start_all)


    def open_first(side):
        start_all(left_copies(0, side))
        for t in range(AHEAD):
            start_all(panel_copies(0, t, t % PANELS, side))

    each(open_first)

    barrier = pltpu.get_barrier_semaphore()

    def greet(peer):
        pl.semaphore_signal(barrier, inc=1, device_id=(sec, peer), device_id_type=MESH)

    greet(by_core)
    greet(by_y)

    @pl.when(z > 0)
    def _():
        greet(me - 4)

    @pl.when(z < NZ - 1)
    def _():
        greet(me + 4)

    @pl.when((z > 0) & (z < NZ - 1))
    def _():
        pl.semaphore_wait(barrier, 4)

    @pl.when((z == 0) | (z == NZ - 1))
    def _():
        pl.semaphore_wait(barrier, 3)


    @pl.when(sec == 1)
    def _():
        start_all(dec_results(False))

    def step(s, carry):
        @pl.when(s + AHEAD < chunks - 1)
        def _():
            for_panel(
                s + AHEAD,
                lambda p, i, slot, side: start_all(panel_copies(p, i, slot, side)),
            )

        @pl.when((s >= RING) & (s < chunks))
        def _():
            send_core(s - RING).wait_send()

        @pl.when(s < chunks)
        def _():
            compute(s)
            send_core(s).start()

        @pl.when(sec == 0)
        def _():
            side_work(s)

        @pl.when((sec == 1) & (s == RING))
        def _():
            wait_all(dec_results(False))
            start_all(dec_results(True))

        @pl.when(s == 1)
        def _():
            each(lambda side: start_all(tall_copies(side)))

        @pl.when(s == 4)
        def _():
            each(lambda side: wait_all(tall_copies(side)))
            each(lambda side: start_all(left_copies(1, side)))
            each(lambda side: start_all(tall_right_copies(side)))

        @pl.when((s >= 4) & (s < 4 + groups))
        def _():
            build_tall(s - 4)

        j_c = s - C_LAG

        @pl.when((j_c >= 0) & (j_c < chunks))
        def _():
            send_core(j_c).wait_recv()
            slot = lax.rem(j_c, RING)
            for a in range(NZ):
                for b in range(NY):
                    add_into(own.at[j_c, a, b], ring.at[slot, a, b, core])

            @pl.when(jnp.logical_not(z_first(j_c)))
            def _():
                send_y(j_c).start()

        j_y = s - Y_LAG

        @pl.when((j_y >= 0) & (j_y < chunks) & jnp.logical_not(z_first(j_y)))
        def _():
            send_y(j_y).wait_recv()
            for t in range(NZ):
                add_into(own.at[j_y, t, y], got_y.at[j_y, t])

        for at in range(NZ - 1):
            j_r = s - Y_LAG - HOP * at

            @pl.when((z == at) & (j_r >= 0) & (j_r < chunks) & jnp.logical_not(z_first(j_r)))
            def _(at=at, j_r=j_r):
                if at > 0:
                    send_right(j_r, at - 1).wait_recv()
                    for t in range(at + 1, NZ):
                        add_into(own.at[j_r, t, y], got_r.at[j_r, t - 1])
                send_right(j_r, at).start()

        for at in range(1, NZ):
            j_l = s - Y_LAG - HOP * (NZ - 1 - at)

            @pl.when((z == at) & (j_l >= 0) & (j_l < chunks) & jnp.logical_not(z_first(j_l)))
            def _(at=at, j_l=j_l):
                if at < NZ - 1:
                    send_left(j_l, at + 1).wait_recv()
                    for t in range(at):
                        add_into(own.at[j_l, t, y], got_l.at[j_l, t])
                send_left(j_l, at).start()

        for at in range(NZ):
            for right, hop in ((True, at), (False, NZ - 1 - at)):
                if hop < NZ - 1:
                    j_z = s - C_LAG - HOP * hop

                    @pl.when((z == at) & (j_z >= 0) & (j_z < chunks) & z_first(j_z))
                    def _(at=at, j_z=j_z, right=right):
                        forward_along(j_z, at, right)

        j_t = s - ZF_LAG

        @pl.when((j_t >= 0) & (j_t < chunks) & z_first(j_t))
        def _():
            turn_to_y(j_t)

        return carry

    lax.fori_loop(0, chunks + Y_LAG + HOP * (NZ - 1), step, 0)


    def finish(j):
        @pl.when(j >= chunks - RING)
        def _():
            send_core(j).wait_send()

        @pl.when(z_first(j))
        def _():
            send_y_last(j).wait()
            for at in range(NZ):

                @pl.when(z == at)
                def _(at=at):
                    if at < NZ - 1:
                        send_along(j, at, True).wait_send()
                    if at > 0:
                        send_along(j, at, False).wait_send()

        @pl.when(jnp.logical_not(z_first(j)))
        def _():
            finish_y_first(j)

    def finish_y_first(j):
        @pl.when(z == NZ - 1)
        def _():
            send_right(j, NZ - 2).wait_recv()

        @pl.when(z == 0)
        def _():
            send_left(j, 1).wait_recv()

        send_y(j).wait_send()
        for at in range(NZ):

            @pl.when(z == at)
            def _(at=at):
                if at < NZ - 1:
                    send_right(j, at).wait_send()
                if at > 0:
                    send_left(j, at).wait_send()

    def total(j, part):
        mine = own[j, z, y, part].astype(F32)
        right = got_r[j, jnp.maximum(z - 1, 0), part].astype(F32)
        left = got_l[j, jnp.minimum(z, NZ - 2), part].astype(F32)
        across = got_y[j, z, part].astype(F32)
        along = jnp.where(z > 0, right, 0.0) + jnp.where(z < NZ - 1, left, 0.0)
        return mine + jnp.where(z_first(j), across, along)

    def close(out, base, count, column):
        def panel(i, carry):
            finish(base + i)
            at = pl.ds(pl.multiple_of(column + i * LANES, LANES), LANES)
            out[:, at] = total(base + i, pl.ds(0, height))
            return carry

        lax.fori_loop(0, count, panel, 0)

    close(o_fi, bases[0], chunk_counts[0], 0)

    def tall_out(i, carry):
        finish(bases[TALL] + i)
        at = pl.ds(pl.multiple_of(i * 16, 16), 16)
        for k in range(tall_right.shape[1] // LANES):
            o_fo[at, k * LANES : (k + 1) * LANES] = total(bases[TALL] + i, pl.ds(k * 16, 16))
        return carry

    lax.fori_loop(0, chunk_counts[TALL], tall_out, 0)
    close(o_cross, bases[2], chunk_counts[2], 0)
    close(o_cross, bases[3], chunk_counts[3], dim)
    close(o_out, bases[4], chunk_counts[4], 0)
    for k in range(3):
        close(o_in, bases[5 + k], chunk_counts[5 + k], k * dim)
    close(o_gain, chunks - 1, 1, 0)

    @pl.when(sec == 0)
    def _():
        for v in range(max(0, block_units - 2), block_units):
            block_store(jnp.int32(v)).wait()

    @pl.when(sec == 1)
    def _():
        wait_all(dec_results(True))


def grad_sum(sides, kept, decoded, gain_rows, shared):
    (enc_lefts, enc_rights), (dec_lefts, dec_rights) = sides
    x_in, qx, kx, wa, g0 = shared
    rows = x_in.shape[0]
    token_counts = (enc_lefts[5][0].shape[0], dec_lefts[5][0].shape[0])
    tokens = rows * max(token_counts)
    groups = enc_lefts + enc_rights + dec_lefts + dec_rights + kept + decoded
    group_sizes = tuple(len(g) for g in groups + gain_rows[0] + gain_rows[1])
    most = max(group_sizes)
    dim, tall = dec_lefts[0][0].shape[1], dec_lefts[TALL][0].shape[1]
    height = dim // PEERS
    chunk_counts = tuple(
        dec_lefts[a][0].shape[1] * dec_rights[b][0].shape[1] // (dim * LANES) for a, b in PRODUCTS
    )
    chunks = sum(chunk_counts) + 1
    attn_units, block_units = rows * HEADS // 2, rows * token_counts[0] // BLOCK
    unit_steps = (attn_units, block_units, 2 * attn_units + 2)
    flat = lambda groups: [v for group in groups for v in group]
    moved = flat(groups)
    gains = flat(gain_rows[0] + gain_rows[1])
    half = (chunks, NZ, NY, height, LANES)
    fourth = (chunks, NZ, height, LANES)
    width = lambda *which: sum(dec_rights[i][0].shape[1] for i in which)
    out_shape = [
        jax.ShapeDtypeStruct(s, F32)
        for s in (
            (height, width(5, 6, 7)),
            (height, width(4)),
            (height, width(0)),
            (height, width(2, 3)),
            (height, LANES),
            (tall // PEERS, width(1)),
            x_in.shape,
        )
    ]
    hbm, vmem = pl.BlockSpec(memory_space=pl.ANY), pl.BlockSpec(memory_space=pltpu.VMEM)
    dma = pltpu.SemaphoreType.DMA
    return pl.pallas_call(
        functools.partial(
            grad_sum_kernel, rows, group_sizes, token_counts, chunk_counts, unit_steps
        ),
        in_specs=[hbm] * len(moved) + [vmem] * len(gains) + [hbm] * 4 + [vmem],
        out_specs=[vmem] * 6 + [hbm],
        out_shape=out_shape,
        scratch_shapes=[
            pltpu.VMEM((dim, tokens), BF),
            pltpu.VMEM((tall, tokens), BF),
            pltpu.VMEM((2, tokens, dim), BF),
            pltpu.VMEM((tokens, tall), BF),
            pltpu.VMEM((tokens, width(1)), BF),
            pltpu.VMEM((PANELS, tokens, LANES), BF),
            pltpu.VMEM((RING, NZ, NY, NC, height, LANES), BF),
            pltpu.VMEM(half, BF),
            pltpu.VMEM(fourth, BF),
            pltpu.VMEM((chunks, NZ - 1) + fourth[2:], BF),
            pltpu.VMEM((chunks, NZ - 1) + fourth[2:], BF),
            pltpu.VMEM((-(-chunks // ZF_EVERY), NZ - 1) + half[2:], BF),
            pltpu.VMEM((-(-chunks // ZF_EVERY), NZ - 1) + half[2:], BF),
            dma((2, most)),
            dma((most,)),
            dma((most,)),
            dma((PANELS, most)),
        ]
        + [dma((chunks,))] * 8
        + [
            pltpu.VMEM((rows * token_counts[0], 3 * dim), BF),
            pltpu.VMEM(wa.shape, BF),
            pltpu.VMEM((2, 5, token_counts[0], PAIR), BF),
            pltpu.VMEM(qx.shape, BF),
            pltpu.VMEM(kx.shape, BF),
            pltpu.VMEM((rows,) + kept[3][0].shape, F32),
            pltpu.VMEM((2, BLOCK, dim), BF),
            pltpu.VMEM((max(2, rows), BLOCK, dim), F32),
            pltpu.VMEM((max(2, rows), BLOCK, dim), F32),
            pltpu.VMEM((1, dim), F32),
            dma((2, 4 + most)),
            dma((3,)),
            dma((rows,)),
            dma((2, 2)),
            dma((2,)),
            dma((2, rows)),
        ],
        compiler_params=pltpu.CompilerParams(
            collective_id=1, has_side_effects=True, vmem_limit_bytes=SUM_VMEM
        ),
    )(*moved, *gains, x_in, qx, kx, wa, g0)


def hand_over_kernel(rows, *refs):
    count = (len(refs) - 3) // 3
    gain_ref, sources, gain_out = refs[0], refs[1 : 1 + count], refs[1 + count]
    targets, held = refs[2 + count : 2 + 2 * count], refs[2 + 2 * count : 2 + 3 * count]
    gain, sems = refs[2 + 3 * count], refs[3 + 3 * count]
    moves = []
    for src, keep, dst in zip(sources, held, targets):
        for part in range(rows) if len(src.shape) == 3 else [slice(None)]:
            i = len(moves)
            load = pltpu.make_async_copy(src.at[part], keep.at[part], sems.at[0, i])
            load.start()
            moves.append((load, keep.at[part], dst.at[0].at[part], sems.at[1, i]))
    load_gain = pltpu.make_async_copy(gain_ref, gain, sems.at[0, len(moves)])
    load_gain.start()
    stores = []
    for load, keep, dst, sem in moves:
        load.wait()
        stores.append(pltpu.make_async_copy(keep, dst, sem))
        stores[-1].start()
    load_gain.wait()
    gain_out[0] = gain[...].T[: gain_out.shape[1]]
    for store in stores:
        store.wait()


def hand_over(gain, gain_rows, arrays):
    hbm, vmem = pl.BlockSpec(memory_space=pl.ANY), pl.BlockSpec(memory_space=pltpu.VMEM)
    rows = max(a.shape[0] for a in arrays if a.ndim == 3)
    return pl.pallas_call(
        functools.partial(hand_over_kernel, rows),
        in_specs=[hbm] * (1 + len(arrays)),
        out_specs=[vmem] + [hbm] * len(arrays),
        out_shape=[jax.ShapeDtypeStruct((1, gain_rows, gain.shape[0]), F32)]
        + [jax.ShapeDtypeStruct((1,) + a.shape, F32) for a in arrays],
        scratch_shapes=[pltpu.VMEM(a.shape, F32) for a in arrays]
        + [
            pltpu.VMEM(gain.shape, F32),
            pltpu.SemaphoreType.DMA((2, len(arrays) + rows)),
        ],
        compiler_params=pltpu.CompilerParams(vmem_limit_bytes=SUM_VMEM),
    )(gain, *arrays)


def plain_sum(on_decoder, sides, gain_terms):
    def terms(lefts, rights):
        parts = [
            mm(jnp.concatenate(lefts[i], 0), jnp.concatenate(rights[j], 0), TN).astype(BF)
            for i, j in PRODUCTS
        ]
        return [
            jnp.concatenate(parts[5:8], 1),
            parts[4],
            parts[0],
            jnp.concatenate(parts[2:4], 1),
            parts[1],
        ]

    pieces = lax.cond(on_decoder, lambda: terms(*sides[1]), lambda: terms(*sides[0]))
    pieces.insert(4, gain_terms)
    return [
        lax.psum_scatter(piece, "rows", scatter_dimension=0, tiled=True).astype(F32)
        for piece in pieces
    ]


def low_half(rows):
    return lax.broadcasted_iota(jnp.int32, (rows, PAIR), 1) < HEAD


def masked_scores(q, k, qx, kx, head, causal):
    lo_q, lo_k = low_half(q.shape[0]), low_half(k.shape[0])
    if head == 0:
        qh, kh = jnp.where(lo_q, q, qx), jnp.where(lo_k, k, kx)
    else:
        qh, kh = jnp.where(lo_q, qx, q), jnp.where(lo_k, kx, k)
    s = mm(kh, qh, NT)
    if causal:
        key_at = lax.broadcasted_iota(jnp.int32, s.shape, 0)
        query_at = lax.broadcasted_iota(jnp.int32, s.shape, 1)
        s = jnp.where(key_at <= query_at, s, NEGATIVE)
    return s


def pair_backward(q, k, v, qx, kx, o, do, lse, causal):
    kt = k.astype(F32).T.astype(BF)
    spread = (do.astype(F32) * o.astype(F32)).T
    low_q, low_k = low_half(q.shape[0]), low_half(k.shape[0])
    zero_q, zero_k = jnp.zeros_like(q), jnp.zeros_like(k)
    dqs, grads = [], []

    def begin(head):
        s = mm(pick(head, low_k, k, kx), pick(head, low_q, q, qx), NT)
        return causal_only(s) if causal else s, mm(pick(head, low_k, v, zero_k), do, NT)

    def end(head, values):
        s, dp = values
        half = slice(head * HEAD, (head + 1) * HEAD)
        p = jnp.exp2(s * (SCALE * LOG2E) - lse[head : head + 1])
        ds = (p * (dp - jnp.sum(spread[half], axis=0, keepdims=True))).astype(BF)
        dqs.append(mm(kt[half], ds))
        grads.append(
            (mm(ds, pick(head, low_q, q, zero_q)), mm(p.astype(BF), pick(head, low_q, do, zero_q)))
        )

    in_order(range(2), begin, end)
    (dk0, dv0), (dk1, dv1) = grads
    return jnp.concatenate(dqs, axis=0).T * SCALE, (dk0 + dk1) * SCALE, dv0 + dv1


def attn_bwd_kernel(
    q_ref, k_ref, v_ref, qx_ref, kx_ref, o_ref, do_ref, lse_ref, dq_ref, dk_ref, dv_ref, *, causal
):
    dq, dk, dv = pair_backward(
        q_ref[...], k_ref[...], v_ref[...], qx_ref[0], kx_ref[0], o_ref[...], do_ref[...],
        lse_ref[0], causal,
    )
    dq_ref[...] = dq.astype(BF)
    dk_ref[...] = dk.astype(BF)
    dv_ref[...] = dv.astype(BF)


def column_block(length, first):
    return pl.BlockSpec((length, PAIR), lambda p: (0, first + p))


def mask_block(length, row):
    return pl.BlockSpec((1, length, PAIR), lambda p: (row, 0, 0))


def pair_block(count_q):
    return pl.BlockSpec((1, 2, count_q), lambda p: (p, 0, 0))


def params(**more):
    return pltpu.CompilerParams(vmem_limit_bytes=VMEM_LIMIT, **more)


def attention_backward(q_in, k_in, v_in, qx, kx, row, firsts, mixed, grad_mixed, lse, causal):
    count_q, count_k, pairs = q_in.shape[0], k_in.shape[0], HEADS // 2
    width = HEADS * HEAD
    return pl.pallas_call(
        functools.partial(attn_bwd_kernel, causal=causal),
        grid=(pairs,),
        in_specs=[
            column_block(count_q, firsts[0]),
            column_block(count_k, firsts[1]),
            column_block(count_k, firsts[2]),
            mask_block(count_q, row),
            mask_block(count_k, row),
            column_block(count_q, 0),
            column_block(count_q, 0),
            pair_block(count_q),
        ],
        out_specs=[
            column_block(count_q, 0),
            column_block(count_k, 0),
            column_block(count_k, 0),
        ],
        out_shape=[
            jax.ShapeDtypeStruct((count_q, width), BF),
            jax.ShapeDtypeStruct((count_k, width), BF),
            jax.ShapeDtypeStruct((count_k, width), BF),
        ],
        compiler_params=params(),
    )(q_in, k_in, v_in, qx, kx, mixed, grad_mixed, lse)


BLOCK = 256
SLICE = 512


def inverse_rms(v):
    return lax.rsqrt(jnp.mean(v * v, -1, keepdims=True) + EPSILON)


def norm(v, gain):
    return (v * inverse_rms(v) * gain).astype(BF)


def norm_back(v, gain, grad):
    inv = inverse_rms(v)
    scaled = grad * gain
    along = jnp.mean(scaled * v, -1, keepdims=True)
    return (
        inv * scaled - v * (inv * inv * inv * along),
        jnp.sum(grad * v * inv, 0, keepdims=True),
    )


def gelu(x):
    return 0.5 * x * (1.0 + jnp.tanh(GELU_C * (x + GELU_A * x * x * x)))


def gelu_parts(x):
    square = x * x
    t = jnp.tanh(GELU_C * x * (1.0 + GELU_A * square))
    half = 0.5 * (1.0 + t)
    slope = half + 0.5 * x * (1.0 - t * t) * (GELU_C * (1.0 + 3.0 * GELU_A * square))
    return x * half, slope


class Fetch:
    def __init__(self, sources, held, sems):
        self.copies = [
            pltpu.make_async_copy(src, dst, sems.at[i])
            for i, (src, dst) in enumerate(zip(sources, held))
        ]
        self.held = held
        self.first = pl.program_id(0) == 0

        @pl.when(self.first)
        def _():
            for copy in self.copies:
                copy.start()

    def __getitem__(self, i):
        @pl.when(self.first)
        def _():
            self.copies[i].wait()

        return self.held[i]


def add_gain(ref, part):
    @pl.when(pl.program_id(0) == 0)
    def _():
        ref[...] = part

    @pl.when(pl.program_id(0) > 0)
    def _():
        ref[...] += part


def block_call(kernel, steps, ins, weights, outs, gain_outs=0):
    specs, arrays = [], []
    for array, row, first in ins:
        columns = array.shape[-1]
        if row is None:
            specs.append(pl.BlockSpec((BLOCK, columns), lambda i, f=first: (f + i, 0)))
        else:
            specs.append(
                pl.BlockSpec((None, BLOCK, columns), lambda i, r=row, f=first: (r, f + i, 0))
            )
        arrays.append(array)
    gains = [w for w in weights if w.dtype == F32]
    mats = [w for w in weights if w.dtype != F32]
    specs += [pl.BlockSpec((1, g.shape[1]), lambda i: (0, 0)) for g in gains]
    specs += [pl.BlockSpec(memory_space=pl.ANY)] * len(mats)
    dim = gains[0].shape[1]
    count = len(mats)

    def run(*refs):
        held, sems = refs[-1 - count : -1], refs[-1]
        at = len(arrays) + len(gains)
        fetch = Fetch(refs[at : at + count], held, sems)
        kernel(refs[: len(arrays)], [g[...] for g in refs[len(arrays) : at]], fetch, refs[at + count : -1 - count])

    return pl.pallas_call(
        run,
        grid=(steps,),
        in_specs=specs,
        out_specs=[pl.BlockSpec((BLOCK, c), lambda i: (i, 0)) for c, _ in outs]
        + [pl.BlockSpec((1, dim), lambda i: (0, 0))] * gain_outs,
        out_shape=[jax.ShapeDtypeStruct((steps * BLOCK, c), t) for c, t in outs]
        + [jax.ShapeDtypeStruct((1, dim), F32)] * gain_outs,
        scratch_shapes=[pltpu.VMEM(m.shape, m.dtype) for m in mats]
        + [pltpu.SemaphoreType.DMA((count,))],
        compiler_params=params(),
    )(*arrays, *gains, *mats)


def project_kernel(ins, gains, w, outs):
    (x,), (g0,), (n_ref, packed_ref) = ins, gains, outs
    n = norm(x[...].astype(F32), g0)
    n_ref[...] = n
    wa = w[0]
    dim = x.shape[1]
    for at in range(0, wa.shape[1], dim):
        packed_ref[:, at : at + dim] = mm(n, wa[:, at : at + dim]).astype(BF)


class FeedForward:
    def __init__(self, move, wf_hbm, wd_hbm, wf, wd):
        self.wf, self.wd, self.half = wf, wd, wd.shape[0]
        self.copies, self.move = {}, move
        self.sources = wf_hbm, wd_hbm

    def load(self):
        wf_hbm, wd_hbm = self.sources
        for at in range(0, self.half, SLICE):
            self.copies[at] = [
                self.move.copy(wd_hbm.at[at : at + SLICE], self.wd.at[at : at + SLICE])
            ] + [
                self.move.copy(wf_hbm.at[:, first : first + SLICE], self.wf.at[:, first : first + SLICE])
                for first in (at, self.half + at)
            ]

    def ready(self, at):
        for made in self.copies.pop(at, []):
            made.wait()

    def slices(self):
        return range(0, self.half, SLICE)

    def parts(self, at):
        self.ready(at)
        up = slice(self.half + at, self.half + at + SLICE)
        return self.wf[:, at : at + SLICE], self.wf[:, up], self.wd[at : at + SLICE, :]


def ffn_up(m, ffn, acc, u_ref, act_ref):
    half = ffn.half

    def begin(at):
        gate_w, up_w, _ = ffn.parts(at)
        return mm(m, gate_w), mm(m, up_w)

    total = [acc]

    def end(at, values):
        gate, up = values
        u_ref[:, at : at + SLICE] = gate.astype(BF)
        u_ref[:, half + at : half + at + SLICE] = up.astype(BF)
        act = (gelu(gate) * up).astype(BF)
        if act_ref is not None:
            act_ref[:, at : at + SLICE] = act
        total[0] = total[0] + mm(act, ffn.wd[at : at + SLICE, :])

    in_order(ffn.slices(), begin, end)
    return total[0]


def ffn_down(branch, ffn, u_ref, du_ref, act_ref):
    half = ffn.half
    total = []

    def begin(at):
        return mm(branch, ffn.parts(at)[2], NT)

    def end(at, d_act):
        gate_w, up_w, _ = ffn.parts(at)
        gate = u_ref[:, at : at + SLICE].astype(F32)
        up = u_ref[:, half + at : half + at + SLICE].astype(F32)
        value, slope = gelu_parts(gate)
        if act_ref is not None:
            act_ref[:, at : at + SLICE] = (value * up).astype(BF)
        d_gate = (d_act * up * slope).astype(BF)
        d_up = (d_act * value).astype(BF)
        du_ref[:, at : at + SLICE] = d_gate
        du_ref[:, half + at : half + at + SLICE] = d_up
        part = mm(d_gate, gate_w, NT) + mm(d_up, up_w, NT)
        total[:] = [part if not total else total[0] + part]

    in_order(ffn.slices(), begin, end)
    return total[0]


def dec_query_kernel(ins, gains, w, outs):
    (o, x), (g1,), (d1_ref, c_ref, cq_ref) = ins, gains, outs
    d1 = x[...].astype(F32) + mm(o[...], w[0][...])
    d1_ref[...] = d1
    c = norm(d1, g1)
    c_ref[...] = c
    cq_ref[...] = mm(c, w[1][:, : c.shape[1]]).astype(BF)


def dec_ffn_kernel(row, x_hbm, oc_hbm, d1_hbm, g2, wc_hbm, wf_hbm, wd_hbm, *refs):
    outs, results, held = refs[:8], refs[8:16], refs[16:]
    doc, out, dd2_v, m_v, act, du, branch, dg2 = results
    oc, d1, cot, u, proj, wf, wd, sems = held
    move = Mover(sems)
    tokens, width = oc.shape
    got = [
        move.copy(a, b)
        for a, b in ((oc_hbm, oc), (wc_hbm.at[:, width:], proj), (d1_hbm, d1))
    ]
    ffn = FeedForward(move, wf_hbm, wd_hbm, wf, wd)
    ffn.load()
    got_cot = move.copy(x_hbm.at[row, tokens:], cot)
    for made in got:
        made.wait()
    d2 = d1[...] + mm(oc[...], proj[...], NT)
    m = norm(d2, g2[...])
    m_v[...] = m
    out[...] = ffn_up(m, ffn, d2, u, act)
    for i in (3, 1, 4):
        move.store(results[i], outs[i])
    got_cot.wait()
    dm = ffn_down(cot[...], ffn, u, du, None)
    back, dg2[...] = norm_back(d2, g2[...], dm)
    dd2 = cot[...].astype(F32) + back
    branch[...] = dd2.astype(BF)
    doc[...] = mm(branch[...], proj[...]).astype(BF)
    dd2_v[...] = dd2
    for i in (0, 2, 5, 6, 7):
        move.store(results[i], outs[i])
    move.drain()


def enc_back_kernel(blocks, dk_hbm, dv_hbm, e1_hbm, e2_hbm, u_hbm, g1, g2, wc_hbm, wd_hbm, wf_hbm, wo_hbm, *refs):
    outs, results, held = refs[:10], refs[10:20], refs[20:]
    mem, fb_v, m_v, act, du, de1_v, ab_v, do, dg1, dg2 = results
    dk, dv, e1_in, e2_in, u, wc, wd, wf, wo, sems = held
    move = Mover(sems)
    width = dk.shape[1]
    here = [slice(i * BLOCK, (i + 1) * BLOCK) for i in range(len(blocks))]
    there = [slice(i * BLOCK, (i + 1) * BLOCK) for i in blocks]

    def load(i, pairs):
        return [move.copy(src.at[there[i]], dst.at[here[i]]) for src, dst in pairs]

    early = ((dk_hbm, dk), (dv_hbm, dv), (e2_hbm, e2_in))
    late = ((u_hbm, u), (e1_hbm, e1_in))
    got_early, got_late = [load(0, early)], []
    got_early[0].append(move.copy(wc_hbm, wc))
    ffn = FeedForward(move, wf_hbm, wd_hbm, wf, wd)
    got_late.append(load(0, late))
    ffn.load()
    got_late[0].append(move.copy(wo_hbm, wo))
    for i in range(1, len(blocks)):
        got_early.append(load(i, early))
        got_late.append(load(i, late))
    for i, b in enumerate(here):
        for made in got_early[i]:
            made.wait()
        dmem = mm(dk[b], wc[:, :width], NT) + mm(dv[b], wc[:, width:], NT)
        mem[b] = norm(e2_in[b], g1[...])
        de2, gain1 = norm_back(e2_in[b], g1[...], dmem)
        fb = de2.astype(BF)
        fb_v[b] = fb
        for made in got_late[i]:
            made.wait()
        m_v[b] = norm(e1_in[b], g2[...])
        dm = ffn_down(fb, ffn, u.at[b], du.at[b], act.at[b])
        back, gain2 = norm_back(e1_in[b], g2[...], dm)
        de1 = de2 + back
        de1_v[b] = de1
        ab = de1.astype(BF)
        ab_v[b] = ab
        do[b] = mm(ab, wo[...], NT).astype(BF)
        for k in range(8):
            move.store(results[k].at[b], outs[k].at[b])
        dg1[...] = gain1 if i == 0 else dg1[...] + gain1
        dg2[...] = gain2 if i == 0 else dg2[...] + gain2
    move.store(dg1, outs[8])
    move.store(dg2, outs[9])
    move.drain()


def dec_back_kernel(ins, gains, w, outs):
    (dcq, d1_in, dd2), (g1,), (dd1_ref, ab_ref, do_ref, dg1_ref) = ins, gains, outs
    d1 = d1_in[...]
    dc = mm(dcq[...], w[0][:, : dcq.shape[1]], NT)
    back, dg1 = norm_back(d1, g1, dc)
    dd1 = dd2[...] + back
    dd1_ref[...] = dd1
    ab = dd1.astype(BF)
    ab_ref[...] = ab
    do_ref[...] = mm(ab, w[1][...], NT).astype(BF)
    add_gain(dg1_ref, dg1)


def input_grad_kernel(ins, gains, w, outs):
    (dq, dk, dv, x, grad), (g0,), (dx_ref, dg0_ref) = ins, gains, outs
    wa = w[0]
    width = dq.shape[1]
    dn = (
        mm(dq[...], wa[:, :width], NT)
        + mm(dk[...], wa[:, width : 2 * width], NT)
        + mm(dv[...], wa[:, 2 * width :], NT)
    )
    back, dg0 = norm_back(x[...].astype(F32), g0, dn)
    dx_ref[...] = grad[...] + back
    add_gain(dg0_ref, dg0)


class Mover:
    def __init__(self, sems):
        self.sems, self.used, self.stores = sems, 0, []

    def copy(self, src, dst):
        made = pltpu.make_async_copy(src, dst, self.sems.at[self.used])
        self.used += 1
        made.start()
        return made

    def store(self, src, dst):
        self.stores.append(self.copy(src, dst))

    def drain(self):
        for made in self.stores:
            made.wait()


def pair_columns(first, p):
    return slice(first + p * PAIR, first + (p + 1) * PAIR)


def pick(head, low, a, b):
    return jnp.where(low, a, b) if head % 2 == 0 else jnp.where(low, b, a)


def in_order(items, begin, end, lead=1):
    waiting = []
    for item in items:
        waiting.append((item, begin(item)))
        if len(waiting) > lead:
            end(*waiting.pop(0))
    while waiting:
        end(*waiting.pop(0))


def attend(q_ref, kv_ref, firsts, qx, kx, o_ref, lse_ref, causal):
    count_q, count_k = qx.shape[0], kx.shape[0]
    low_q, low_k = low_half(count_q), low_half(count_k)
    ones = jnp.ones((8, count_k), BF)
    values, outs = {}, {}

    def begin(head):
        q = q_ref[:, pair_columns(firsts[0], head // 2)]
        k = kv_ref[:, pair_columns(firsts[1], head // 2)]
        s = mm(pick(head, low_k, k, kx), pick(head, low_q, q, qx), NT)
        return causal_only(s) if causal else s

    def end(head, s):
        p = head // 2
        if head % 2 == 0:
            values[p] = kv_ref[:, pair_columns(firsts[2], p)].astype(F32).T.astype(BF)
        vt = values[p][(head % 2) * HEAD : (head % 2 + 1) * HEAD]
        top = jnp.max(s, axis=0, keepdims=True)
        e = jnp.exp2((s - top) * (SCALE * LOG2E)).astype(BF)
        mixed = mm(jnp.concatenate([vt, ones], axis=0), e)
        total = mixed[HEAD : HEAD + 1]
        outs[head] = mixed[:HEAD] * (1.0 / total)
        lse_ref[p, head % 2 : head % 2 + 1, :] = top * (SCALE * LOG2E) + jnp.log2(total)
        if head % 2 == 1:
            both = jnp.concatenate([outs.pop(head - 1), outs.pop(head)], axis=0)
            o_ref[:, pair_columns(0, p)] = both.T.astype(BF)

    in_order(range(HEADS), begin, end)


def causal_only(s):
    key_at = lax.broadcasted_iota(jnp.int32, s.shape, 0)
    query_at = lax.broadcasted_iota(jnp.int32, s.shape, 1)
    return jnp.where(key_at <= query_at, s, NEGATIVE)


def attend_kernel(firsts, row, causal, same, *refs):
    if same:
        q_ref, (qx_ref, kx_ref, o_ref, lse_ref) = refs[0], refs[1:]
        kv_ref = q_ref
    else:
        q_ref, kv_ref, qx_ref, kx_ref, o_ref, lse_ref = refs
    attend(q_ref, kv_ref, firsts, qx_ref[row], kx_ref[row], o_ref, lse_ref, causal)


def attention_forward(q_in, kv_in, qx, kx, row, firsts, causal):
    count_q = q_in.shape[0]
    ins = [q_in] if kv_in is None else [q_in, kv_in]
    vmem = pl.BlockSpec(memory_space=pltpu.VMEM)
    return pl.pallas_call(
        functools.partial(attend_kernel, firsts, row, causal, kv_in is None),
        in_specs=[vmem] * (len(ins) + 2),
        out_specs=[vmem] * 2,
        out_shape=[
            jax.ShapeDtypeStruct((count_q, HEADS * HEAD), BF),
            jax.ShapeDtypeStruct((HEADS // 2, 2, count_q), F32),
        ],
        compiler_params=params(),
    )(*ins, qx, kx)


def enc_attend_kernel(row, x_hbm, qx_hbm, kx_hbm, g0, wa_hbm, *refs):
    outs, (n_v, packed_v, o_v, lse_v, x, qx, kx, wa, sems) = refs[:4], refs[4:]
    move = Mover(sems)
    got_x = move.copy(x_hbm.at[row], x)
    got_wa = move.copy(wa_hbm, wa)
    got_masks = move.copy(qx_hbm.at[row], qx), move.copy(kx_hbm.at[row], kx)
    tokens, dim = x.shape
    got_x.wait()
    blocks = [slice(at, at + BLOCK) for at in range(0, tokens, BLOCK)]
    for b in blocks:
        n_v[b] = norm(x[b].astype(F32), g0[...])
    move.store(n_v, outs[0])
    got_wa.wait()
    for b in blocks:
        for at in range(0, wa.shape[1], dim):
            packed_v[b, at : at + dim] = mm(n_v[b], wa[:, at : at + dim]).astype(BF)
    move.store(packed_v, outs[1])
    for made in got_masks:
        made.wait()
    attend(packed_v, packed_v, (0, dim, 2 * dim), qx[...], kx[...], o_v, lse_v, False)
    move.store(o_v, outs[2])
    move.store(lse_v, outs[3])
    move.drain()


def enc_rest_kernel(row, x_hbm, o_hbm, g1, g2, wo_hbm, wf_hbm, wd_hbm, wc_hbm, *refs):
    outs, (e1_v, u_v, e2_v, sent_v, x, o, wo, wf, wd, wc, sems) = refs[:4], refs[4:]
    move = Mover(sems)
    got = [move.copy(a, b) for a, b in ((x_hbm.at[row], x), (o_hbm, o), (wo_hbm, wo))]
    ffn = FeedForward(move, wf_hbm, wd_hbm, wf, wd)
    ffn.load()
    got_wc = [move.copy(wc_hbm, wc)]
    for made in got:
        made.wait()
    blocks = [slice(at, at + BLOCK) for at in range(0, x.shape[0], BLOCK)]
    for b in blocks:
        e1_v[b] = x[b].astype(F32) + mm(o[b], wo[...])
        move.store(e1_v.at[b], outs[0].at[b])
    for b in blocks:
        e1 = e1_v[b]
        e2 = ffn_up(norm(e1, g2[...]), ffn, e1, u_v.at[b], None)
        e2_v[b] = e2
        while got_wc:
            got_wc.pop().wait()
        sent_v[b] = mm(norm(e2, g1[...]), wc[...]).astype(BF)
        for src, dst in ((u_v, outs[1]), (e2_v, outs[2]), (sent_v, outs[3])):
            move.store(src.at[b], dst.at[b])
    move.drain()


HBM = pl.BlockSpec(memory_space=pl.ANY)
VMEM = pl.BlockSpec(memory_space=pltpu.VMEM)


def moved_call(kernel, ins, specs, outs, held, copies):
    return list(
        pl.pallas_call(
            kernel,
            in_specs=specs,
            out_specs=[HBM] * len(outs),
            out_shape=[jax.ShapeDtypeStruct(s, t) for s, t in outs],
            scratch_shapes=[pltpu.VMEM(s, t) for s, t in outs + held]
            + [pltpu.SemaphoreType.DMA((copies,))],
            compiler_params=params(),
        )(*ins)
    )


def enc_attend(row, x_in, qx, kx, g0, wa):
    tokens, dim = x_in.shape[1:]
    width = wa.shape[1] // 3
    kept = [
        ((tokens, dim), BF),
        ((tokens, wa.shape[1]), BF),
        ((tokens, width), BF),
        ((HEADS // 2, 2, tokens), F32),
    ]
    held = [(x_in.shape[1:], BF), (qx.shape[1:], BF), (kx.shape[1:], BF), (wa.shape, BF)]
    return moved_call(
        functools.partial(enc_attend_kernel, row),
        (x_in, qx, kx, g0, wa),
        [HBM] * 3 + [VMEM] + [HBM],
        kept,
        held,
        8,
    )


def enc_rest(row, x_in, o, g1, g2, wo, wf, wd, wc):
    tokens, dim = x_in.shape[1:]
    kept = [
        ((tokens, dim), F32),
        ((tokens, wf.shape[1]), BF),
        ((tokens, dim), F32),
        ((tokens, wc.shape[1]), BF),
    ]
    held = [(x_in.shape[1:], BF), (o.shape, BF)] + [(w.shape, BF) for w in (wo, wf, wd, wc)]
    return moved_call(
        functools.partial(enc_rest_kernel, row),
        (x_in, o, g1, g2, wo, wf, wd, wc),
        [HBM] * 2 + [VMEM] * 2 + [HBM] * 4,
        kept,
        held,
        4 + 3 * (wd.shape[0] // SLICE) + 4 * (tokens // BLOCK),
    )


def nothing_kernel(*refs):
    pass


def unwritten(shapes):
    return pl.pallas_call(
        nothing_kernel,
        out_specs=[pl.BlockSpec(memory_space=pl.ANY)] * len(shapes),
        out_shape=[jax.ShapeDtypeStruct(s.shape, s.dtype) for s in shapes],
    )()


def by_section(on_decoder, encoder, decoder):
    enc_shapes = jax.eval_shape(encoder) if encoder else []
    dec_shapes = jax.eval_shape(decoder) if decoder else []
    none = lambda: []
    encoder, decoder = encoder or none, decoder or none
    pool = lambda shapes: list(unwritten(shapes)) if shapes else []
    both = lax.cond(
        on_decoder,
        lambda: pool(enc_shapes) + list(decoder()),
        lambda: list(encoder()) + pool(dec_shapes),
    )
    return both[: len(enc_shapes)], both[len(enc_shapes) :]


def segment_ids(lengths, span_len):
    positions = jnp.arange(span_len, dtype=jnp.int32)[None, :]
    seg, end = jnp.zeros((lengths.shape[0], span_len), jnp.int32), 0
    for j in range(lengths.shape[1]):
        end = end + lengths[:, j : j + 1]
        seg = seg + (positions >= end).astype(jnp.int32)
    return seg


def mask_lanes(seg, count):
    hit = seg[:, :, None] == jnp.arange(HEAD, dtype=jnp.int32)[None, None, :]
    member = hit.astype(BF)
    other = jnp.where(
        jnp.arange(HEAD, dtype=jnp.int32)[None, None, :] < count,
        jnp.where(hit, 0.0, NEGATIVE),
        0.0,
    ).astype(BF)
    return (
        jnp.concatenate([member, member], -1),
        jnp.concatenate([other, other], -1),
    )


def shift(x, by):
    pairs = [(0, 1)] if by > 0 else [(1, 0)]
    return lax.ppermute(x, "section", pairs)


def body(
    section_input, enc_lengths, dec_lengths, attn_in, attn_out, ffn_in, ffn_out, cross_weight, gains
):
    wa, wo, wf, wd, wc = attn_in[0], attn_out[0], ffn_in[0], ffn_out[0], cross_weight[0]
    g0, g1, g2 = gains[0, 0:1], gains[0, 1:2], gains[0, 2:3]
    x_in = section_input[0]
    rows, le, dim = x_in.shape
    ld = le // 2
    width = wo.shape[0]
    docs = enc_lengths.shape[1]
    enc_qx, enc_kx = mask_lanes(segment_ids(enc_lengths, le), docs)
    dec_qx, dec_kx = mask_lanes(segment_ids(dec_lengths, ld), docs)
    on_decoder = lax.axis_index("section") == 1
    steps_e, steps_d = le // BLOCK, ld // BLOCK
    columns = width // PAIR
    own = (0, columns, 2 * columns)
    across = (0, 0, columns)
    inner = wf.shape[1]

    def project(r, steps):
        return list(
            block_call(project_kernel, steps, [(x_in, r, 0)], [g0, wa], [(dim, BF), (3 * width, BF)])
        )

    def dec_first(r):
        n, packed = project(r, steps_d)
        o, lse = attention_forward(packed, None, dec_qx, dec_kx, r, (0, width, 2 * width), True)
        d1, c, cq = block_call(
            dec_query_kernel,
            steps_d,
            [(o, None, 0), (x_in, r, 0)],
            [g1, wo, wc],
            [(dim, F32), (dim, BF), (width, BF)],
        )
        return [n, packed, o, lse, d1, c, cq]

    def cross(r, cq, sent):
        return list(attention_forward(cq, sent, dec_qx, enc_kx, r, (0, 0, width), False))

    feeds = 3 * (wd.shape[0] // SLICE)

    def dec_ffn(r, oc, d1):
        row = lambda columns, kind: ((ld, columns), kind)
        return moved_call(
            functools.partial(dec_ffn_kernel, r),
            (x_in, oc, d1, g2, wc, wf, wd),
            [HBM] * 3 + [VMEM] + [HBM] * 3,
            [row(width, BF), row(dim, F32), row(dim, F32), row(dim, BF), row(wd.shape[0], BF)]
            + [row(inner, BF), row(dim, BF), ((1, dim), F32)],
            [row(width, BF), row(dim, F32), row(dim, BF), row(inner, BF), ((dim, width), BF)]
            + [(wf.shape, BF), (wd.shape, BF)],
            feeds + 4 + 8,
        )

    def cross_back(r, cq, sent, oc, doc, lse):
        return list(
            attention_backward(cq, sent, sent, dec_qx, enc_kx, r, across, oc, doc, lse, False)
        )

    def enc_back(dk, dv, e1, e2, u, blocks):
        row = lambda columns, kind: ((len(blocks) * BLOCK, columns), kind)
        return moved_call(
            functools.partial(enc_back_kernel, blocks),
            (dk, dv, e1, e2, u, g1, g2, wc, wd, wf, wo),
            [HBM] * 5 + [VMEM] * 2 + [HBM] * 4,
            [row(dim, BF)] * 3
            + [row(wd.shape[0], BF), row(inner, BF), row(dim, F32), row(dim, BF), row(width, BF)]
            + [((1, dim), F32)] * 2,
            [row(width, BF)] * 2
            + [row(dim, F32)] * 2
            + [row(inner, BF)]
            + [(w.shape, BF) for w in (wc, wd, wf, wo)],
            feeds + 2 + 5 * len(blocks) + 8 * len(blocks) + 2,
        )

    def self_back(r, steps, masks, causal, packed, o, lse, do, grad):
        dq, dk, dv = attention_backward(
            packed, packed, packed, *masks, r, own, o, do, lse, causal
        )
        dx, dg0 = block_call(
            input_grad_kernel,
            steps,
            [(dq, None, 0), (dk, None, 0), (dv, None, 0), (x_in, r, 0), (grad, None, 0)],
            [g0, wa],
            [(dim, F32)],
            1,
        )
        return [dq, dk, dv, dx, dg0]

    def dec_back(dcq, d1, dd2):
        return list(
            block_call(
                dec_back_kernel,
                steps_d,
                [(dcq, None, 0), (d1, None, 0), (dd2, None, 0)],
                [g1, wc, wo],
                [(dim, F32), (dim, BF), (width, BF)],
                1,
            )
        )

    every = range(rows)
    plain = lax.axis_size("rows") != PEERS
    state = []

    def run(encoder, decoder, *ready):
        held = on_decoder
        if state:
            held, state[0][1], *_ = lax.optimization_barrier((on_decoder, state[0][1]) + ready)
        out = by_section(held, encoder, decoder)
        state[:] = [out[0] or out[1]]
        return out

    def slots():
        return [None] * rows

    first, rest, dfirst, cqs, crossed, ocs = slots(), slots(), slots(), slots(), slots(), slots()
    mids, docs_in, cross_b, dcqs, back, last, dlast = (slots() for _ in range(7))

    def begin_cross(r, beside=None):
        crossed[r], out = run(lambda: cross(r, cqs[r], rest[r][3]), beside)
        ocs[r] = shift(crossed[r][0], 1)
        return out

    def dec_mid(r):
        return lambda: dec_ffn(r, ocs[r], dfirst[r][4])

    def keep_mid(r, out):
        mids[r] = out
        docs_in[r] = shift(out[0], -1)

    def dec_last(r):
        p = dec_back(dcqs[r], dfirst[r][4], mids[r][2])
        n, packed, o, lse = dfirst[r][:4]
        return p + self_back(r, steps_d, (dec_qx, dec_kx), True, packed, o, lse, p[2], p[0])

    def enc_last(r):
        return self_back(
            r, steps_e, (enc_qx, enc_kx), False, *first[r][1:4],
            jnp.concatenate(backs(r, 7), 0), jnp.concatenate(backs(r, 5), 0),
        )

    def enc_first(r):
        return lambda: enc_attend(r, x_in, enc_qx, enc_kx, g0, wa)

    def enc_then(r):
        return lambda: enc_rest(r, x_in, first[r][2], g1, g2, wo, wf, wd, wc)

    first[0], dfirst[0] = run(enc_first(0), lambda: dec_first(0))
    cqs[0] = shift(dfirst[0][6], -1)
    rest[0], more = run(enc_then(0), lambda: [v for r in every[1:] for v in dec_first(r)])
    begin_cross(0)
    for r in every[1:]:
        dfirst[r] = more[7 * (r - 1) : 7 * r]
        cqs[r] = shift(dfirst[r][6], -1)
    for r in every[1:]:
        first[r], _ = run(enc_first(r), None)
        rest[r], out = run(enc_then(r), dec_mid(r - 1), ocs[r - 1])
        keep_mid(r - 1, out)
        begin_cross(r)
    def backs(r, i):
        return [part[i] for part in back[r]]

    def enc_backs(r, blocks):
        return lambda: enc_back(
            cross_b[r][1], cross_b[r][2], rest[r][0], rest[r][2], rest[r][1], blocks
        )

    for r in every:
        cross_b[r], _ = run(
            lambda: cross_back(r, cqs[r], rest[r][3], crossed[r][0], docs_in[r], crossed[r][1]),
            None,
        )
        if r == 0 and steps_e > 1:
            part, out = run(enc_backs(0, (0,)), dec_mid(rows - 1))
            keep_mid(rows - 1, out)
            dcqs[0] = shift(cross_b[0][0], 1)
            others, _ = run(enc_backs(0, tuple(range(1, steps_e))), None)
            back[0] = [part, others]
        else:
            dcqs[r] = shift(cross_b[r][0], 1)
            out = run(enc_backs(r, tuple(range(steps_e))), dec_mid(rows - 1) if r == 0 else None)
            back[r] = [out[0]]
            if r == 0:
                keep_mid(rows - 1, out[1])
        last[r], dlast[r] = run((lambda: enc_last(r)) if plain else None, lambda: dec_last(r))

    def over_rows(lists):
        pieces = lambda v: v if isinstance(v, list) else [v]
        return [[p for v in group for p in pieces(v)] for group in zip(*lists)]

    enc_side = (
        over_rows(
            [backs(r, 2), backs(r, 3), backs(r, 0), backs(r, 0), first[r][2], first[r][0]]
            for r in every
        ),
        over_rows(
            [backs(r, 4), backs(r, 1), cross_b[r][1], cross_b[r][2], backs(r, 6)] + last[r][0:3]
            for r in every
        ),
    )
    dec_side = (
        over_rows(
            [mids[r][3], mids[r][4], dfirst[r][5], mids[r][6], dfirst[r][2], dfirst[r][0]]
            for r in every
        ),
        over_rows(
            [mids[r][5], x_in[r, ld:], dcqs[r], ocs[r], dlast[r][1]] + dlast[r][4:7] for r in every
        ),
    )
    if not plain:
        kept = over_rows(
            [first[r][1], first[r][2], backs(r, 7), first[r][3], backs(r, 5)] for r in every
        )
        decoded = over_rows([mids[r][1], dlast[r][7]] for r in every)
        gain_rows = (
            over_rows([backs(r, 8), backs(r, 9)] for r in every),
            over_rows([dlast[r][8], dlast[r][3], mids[r][7]] for r in every),
        )
        s_in, s_out, s_fi, s_cross, s_gain, s_fo, results = grad_sum(
            (enc_side, dec_side), kept, decoded, gain_rows, (x_in, enc_qx, enc_kx, wa, g0)
        )
        o_gain, *outs = hand_over(
            s_gain, gains.shape[1], [results, s_in, s_out, s_fi, s_fo, s_cross]
        )
        return tuple(outs) + (o_gain,)

    def enc_parts():
        gain_rows = [sum(v) for v in zip(*[[last[r][4], sum(backs(r, 8)), sum(backs(r, 9))] for r in every])]
        return [jnp.concatenate(gain_rows, 0), jnp.stack([last[r][3] for r in every])]

    def dec_parts():
        gain_rows = [sum(v) for v in zip(*[[dlast[r][8], dlast[r][3], mids[r][7]] for r in every])]
        both = [jnp.concatenate([mids[r][1], dlast[r][7]], 0) for r in every]
        return [jnp.concatenate(gain_rows, 0), jnp.stack(both)]

    gain_grads, results = lax.cond(on_decoder, dec_parts, enc_parts)
    gain_terms = jnp.pad(gain_grads.T, ((0, 0), (0, LANES - gain_grads.shape[0]))).astype(BF)

    s_in, s_out, s_fi, s_cross, s_gain, s_fo = plain_sum(on_decoder, (enc_side, dec_side), gain_terms)
    return (
        results[None],
        s_in[None],
        s_out[None],
        s_fi[None],
        s_fo[None],
        s_cross[None],
        s_gain[:, : gain_grads.shape[0]].T[None],
    )


def solution(mesh):
    placed = (
        P("section", "rows", None, None),
        P("rows", None),
        P("rows", None),
    ) + (P("section", None, None),) * 6
    return jax.shard_map(
        body,
        mesh=mesh,
        in_specs=placed,
        out_specs=(
            P("section", "rows", None, None),
            P("section", "rows", None),
            P("section", "rows", None),
            P("section", "rows", None),
            P("section", "rows", None),
            P("section", "rows", None),
            P("section", None, "rows"),
        ),
        check_vma=False,
    )
```

```python
import functools

import jax
import jax.numpy as jnp
from jax import lax
from jax.experimental import pallas as pl
from jax.experimental.pallas import tpu as pltpu
from jax.sharding import PartitionSpec as P

HEADS = 12
HEAD = 64
PAIR = 128
EPSILON = 1e-06
SCALE = 0.125
LOG2E = 1.4426950408889634
NEGATIVE = -1e30
GELU_C = 0.7978845608028654
GELU_A = 0.044715

BF = jnp.bfloat16
F32 = jnp.float32
NT = (((1,), (1,)), ((), ()))
NN = (((1,), (0,)), ((), ()))
TN = (((0,), (0,)), ((), ()))


def mm(a, b, dims=NN):
    return lax.dot_general(a, b, dims, preferred_element_type=F32)


MESH = pl.DeviceIdType.MESH
LANES = 256
VMEM_LIMIT = 56 * 1024 * 1024
SUM_VMEM = 60 * 1024 * 1024

NZ, NY, NC = 4, 2, 2
PEERS = NZ * NY * NC
C_LAG = 2
Y_LAG = C_LAG + 4
HOP = 3
ZF_EVERY, ZF_AT = 6, 3
ZF_LAG = C_LAG + HOP * (NZ - 1)
RING = 6
AHEAD = 3
PANELS = 4

TALL = 1
LEFT_ORDER = (0, 2, 3, 4, 5)
PRODUCTS = ((0, 0), (1, 1), (2, 2), (3, 3), (4, 4), (5, 5), (5, 6), (5, 7))


def grad_sum_kernel(rows, group_sizes, token_counts, chunk_counts, unit_steps, *refs):
    remaining = list(refs)
    sizes = list(group_sizes)

    def take(groups):
        return [[remaining.pop(0) for _ in range(sizes.pop(0))] for _ in range(groups)]

    def take_one():
        return remaining.pop(0)

    lefts_of, rights_of = [], []
    for side in range(2):
        lefts_of.append(take(6))
        rights_of.append(take(5 if side == 0 else 8))
    packed_of, o_of, do_of, lse_of, de1_of = take(5)
    out_of, dx_of = take(2)
    gain_rows = [[None] + take(2), take(3)]
    x_ref, qx_ref, kx_ref, wa_ref, g0_ref = [take_one() for _ in range(5)]
    o_in, o_out, o_fi, o_cross, o_gain, o_fo, o_results = [take_one() for _ in range(7)]
    (
        xt, xt_tall, left_stage, tall_stage, tall_right, panels, ring,
        own, got_y, got_r, got_l, z_right, z_left,
        s_left, s_tall, s_right, s_panel,
        s_core, r_core, s_y, r_y, s_r, r_r, s_l, r_l,
        d_packed, wa, att, qx, kx, lse, x_stage, grad_stage, dx_stage, dg0,
        s_att, s_const, s_lse, s_block, s_out, s_dec,
    ) = remaining
    chunks, height, dim = own.shape[0], own.shape[3], xt.shape[0]
    sec, me = lax.axis_index("section"), lax.axis_index("rows")
    core, y, z = lax.rem(me, 2), lax.rem(me // 2, 2), me // 4
    by_core, by_y = me + 1 - 2 * core, me + 2 - 4 * y
    other, away = 1 - core, 1 - y
    bases = [sum(chunk_counts[:i]) for i in range(len(chunk_counts))]


    def each(act):
        for side in range(2):

            @pl.when(sec == side)
            def _(side=side):
                act(side)

    def row_copies(sources, columns, dst, sems, side):
        del side
        copies, at = [], 0
        for i, src in enumerate(sources):
            copies.append(
                pltpu.make_async_copy(
                    src if columns is None else src.at[:, columns],
                    dst.at[at : at + src.shape[0]],
                    sems.at[i],
                )
            )
            at += src.shape[0]
        return copies

    def start_all(copies):
        for copy in copies:
            copy.start()

    def wait_all(copies):
        for copy in copies:
            copy.wait()

    def left_copies(q, side):
        source = lefts_of[side][LEFT_ORDER[q]]
        return row_copies(source, None, left_stage.at[q % 2], s_left.at[q % 2], side)

    def tall_copies(side):
        return row_copies(lefts_of[side][1], None, tall_stage, s_tall, side)

    def tall_right_copies(side):
        return row_copies(rights_of[side][1], None, tall_right, s_right, side)

    def panel_copies(p, i, slot, side):
        if PRODUCTS[p][1] >= len(rights_of[side]):
            return []
        columns = pl.ds(pl.multiple_of(i * LANES, LANES), LANES)
        return row_copies(
            rights_of[side][PRODUCTS[p][1]], columns, panels.at[slot], s_panel.at[slot], side
        )

    def for_panel(t, act):
        slot = lax.rem(t, PANELS)
        for p in range(len(PRODUCTS)):
            if p != TALL:

                @pl.when((t >= bases[p]) & (t < bases[p] + chunk_counts[p]))
                def _(p=p):
                    each(lambda side: act(p, t - bases[p], slot, side))

    def flip(side, stage, columns, put):
        for at in range(0, rows * token_counts[side], LANES):
            tokens = slice(at, at + LANES)
            put(tokens, stage[tokens, columns].astype(F32).T.astype(BF))

    def build_left(q):
        def act(side):
            wait_all(left_copies(q, side))
            for at in range(0, xt.shape[0], LANES):

                def put(tokens, block, at=at):
                    xt[at : at + LANES, tokens] = block

                flip(side, left_stage.at[q % 2], slice(at, at + LANES), put)
            if q + 2 < len(LEFT_ORDER):
                start_all(left_copies(q + 2, side))

        each(act)

    groups = xt_tall.shape[0] // LANES
    tall_rows = xt_tall.shape[0] // PEERS

    def build_tall(part):
        columns = pl.ds(pl.multiple_of(part * LANES, LANES), LANES)
        targets = LANES // tall_rows

        def act(side):
            def put(tokens, block):
                for k in range(targets):
                    for j in range(tall_rows // 16):
                        to = j * LANES + (part * targets + k) * 16
                        xt_tall[pl.ds(pl.multiple_of(to, 16), 16), tokens] = block[
                            k * tall_rows + j * 16 : k * tall_rows + (j + 1) * 16
                        ]

            flip(side, tall_stage, columns, put)

        each(act)

    def send_core(j):
        slot = lax.rem(j, RING)
        return pltpu.make_async_remote_copy(
            src_ref=ring.at[slot, :, :, other],
            dst_ref=own.at[j],
            send_sem=s_core.at[j],
            recv_sem=r_core.at[j],
            device_id=(sec, by_core),
            device_id_type=MESH,
        )

    def send_y(j):
        return pltpu.make_async_remote_copy(
            src_ref=own.at[j, :, away],
            dst_ref=got_y.at[j],
            send_sem=s_y.at[j],
            recv_sem=r_y.at[j],
            device_id=(sec, by_y),
            device_id_type=MESH,
        )

    def send_right(j, at):
        return pltpu.make_async_remote_copy(
            src_ref=own.at[j, pl.ds(at + 1, NZ - 1 - at), y],
            dst_ref=got_r.at[j, pl.ds(at, NZ - 1 - at)],
            send_sem=s_r.at[j],
            recv_sem=r_r.at[j],
            device_id=(sec, me + 4),
            device_id_type=MESH,
        )

    def send_left(j, at):
        return pltpu.make_async_remote_copy(
            src_ref=own.at[j, pl.ds(0, at), y],
            dst_ref=got_l.at[j, pl.ds(0, at)],
            send_sem=s_l.at[j],
            recv_sem=r_l.at[j],
            device_id=(sec, me - 4),
            device_id_type=MESH,
        )

    def z_first(j):
        return lax.rem(j, ZF_EVERY) == ZF_AT

    def send_along(j, at, right):
        targets = pl.ds(at + 1, NZ - 1 - at) if right else pl.ds(0, at)
        buffer = z_right if right else z_left
        return pltpu.make_async_remote_copy(
            src_ref=own.at[j, targets],
            dst_ref=buffer.at[j // ZF_EVERY, pl.ds(at, NZ - 1 - at) if right else targets],
            send_sem=(s_r if right else s_l).at[j],
            recv_sem=(r_r if right else r_l).at[j],
            device_id=(sec, me + 4 if right else me - 4),
            device_id_type=MESH,
        )

    def send_y_last(j):
        return pltpu.make_async_remote_copy(
            src_ref=own.at[j, z, away],
            dst_ref=got_y.at[j, z],
            send_sem=s_y.at[j],
            recv_sem=r_y.at[j],
            device_id=(sec, by_y),
            device_id_type=MESH,
        )

    def forward_along(j, at, right):
        source = at - 1 if right else at + 1
        if 0 <= source < NZ:
            send_along(j, source, right).wait_recv()
            buffer = z_right if right else z_left
            for t in range(at + 1, NZ) if right else range(at):
                for b in range(NY):
                    add_into(own.at[j, t, b], buffer.at[j // ZF_EVERY, t - 1 if right else t, b])
        send_along(j, at, right).start()

    def turn_to_y(j):
        for at in range(NZ):

            @pl.when(z == at)
            def _(at=at):
                if at == NZ - 1:
                    send_along(j, at - 1, True).wait_recv()
                if at == 0:
                    send_along(j, at + 1, False).wait_recv()
                for b in range(NY):
                    if at > 0:
                        add_into(own.at[j, at, b], z_right.at[j // ZF_EVERY, at - 1, b])
                    if at < NZ - 1:
                        add_into(own.at[j, at, b], z_left.at[j // ZF_EVERY, at, b])

        send_y_last(j).start()

    def add_into(dst, src):
        dst[...] = (dst[...].astype(F32) + src[...].astype(F32)).astype(BF)


    def compute(s):
        slot = lax.rem(s, RING)

        def put_panel(value):
            for t in range(PEERS):
                ring[slot, t // 4, t // 2 % 2, t % 2] = value[t * height : (t + 1) * height]

        for p in range(len(PRODUCTS)):
            left = PRODUCTS[p][0]

            @pl.when((s >= bases[p]) & (s < bases[p] + chunk_counts[p]))
            def _(p=p, left=left):
                if p != TALL:
                    if p == 0 or PRODUCTS[p - 1][0] != left:

                        @pl.when(s == bases[p])
                        def _():
                            build_left(LEFT_ORDER.index(left))

                    where = lax.rem(s, PANELS)

                    def act(side):
                        wait_all(panel_copies(p, s - bases[p], where, side))
                        tokens = rows * token_counts[side]
                        if PRODUCTS[p][1] < len(rights_of[side]):
                            right = panels[where, :tokens, :]
                        else:
                            first = (PRODUCTS[p][1] - 5) * dim + (s - bases[p]) * LANES
                            right = d_packed[:, pl.ds(pl.multiple_of(first, LANES), LANES)]
                        put_panel(mm(xt[:, :tokens], right).astype(BF))

                    each(act)
                else:
                    rows_at = pl.ds(pl.multiple_of((s - bases[p]) * LANES, LANES), LANES)

                    @pl.when(s == bases[p])
                    def _():
                        each(lambda side: wait_all(tall_right_copies(side)))

                    def act(side):
                        tokens = rows * token_counts[side]
                        for k in range(tall_right.shape[1] // LANES):
                            value = mm(
                                xt_tall[rows_at, :tokens],
                                tall_right[:tokens, k * LANES : (k + 1) * LANES],
                            ).astype(BF)
                            for t in range(PEERS):
                                ring[slot, t // 4, t // 2 % 2, t % 2, k * 16 : (k + 1) * 16] = value[
                                    t * 16 : (t + 1) * 16
                                ]

                    each(act)

        @pl.when(s == chunks - 1)
        def _():
            def act(side):
                parts = []
                for group in gain_rows[side]:
                    total_row = dg0[...]
                    if group is not None:
                        total_row = group[0][...]
                        for ref in group[1:]:
                            total_row = total_row + ref[...]
                    parts.append(total_row)
                parts.append(jnp.zeros((LANES - len(parts), dim), F32))
                put_panel(jnp.concatenate(parts, axis=0).T.astype(BF))

            each(act)


    attn_units, block_units, first_block = unit_steps
    tokens_e = token_counts[0]
    per_row = tokens_e // BLOCK
    const_copies = [
        pltpu.make_async_copy(src, dst, s_const.at[i])
        for i, (src, dst) in enumerate(((qx_ref, qx), (kx_ref, kx), (wa_ref, wa)))
    ]
    lse_copies = [
        pltpu.make_async_copy(ref, lse.at[r], s_lse.at[r]) for r, ref in enumerate(lse_of)
    ]

    def row_pieces(refs_of, r):
        found, at = [], 0
        for ref in refs_of:
            if r * tokens_e <= at < (r + 1) * tokens_e:
                found.append((ref, at - r * tokens_e))
            at += ref.shape[0]
        return found

    def attn_loads(u, act):
        slot, p = lax.rem(u, 2), lax.rem(u, HEADS // 2)
        for r in range(rows):

            @pl.when(u // (HEADS // 2) == r)
            def _(r=r):
                at = lambda first: pl.ds(pl.multiple_of(first + p * PAIR, PAIR), PAIR)
                sources = [packed_of[r].at[:, at(k * dim)] for k in range(3)]
                sources.append(o_of[r].at[:, at(0)])
                copies = [
                    pltpu.make_async_copy(src, att.at[slot, k], s_att.at[slot, k])
                    for k, src in enumerate(sources)
                ]
                for ref, begin in row_pieces(do_of, r):
                    copies.append(
                        pltpu.make_async_copy(
                            ref.at[:, at(0)],
                            att.at[slot, 4, begin : begin + ref.shape[0]],
                            s_att.at[slot, len(copies)],
                        )
                    )
                act(copies)

    def attn_unit(u):
        slot, p, r = lax.rem(u, 2), lax.rem(u, HEADS // 2), u // (HEADS // 2)
        attn_loads(u, wait_all)
        q, k, v, o, do = [att[slot, i] for i in range(5)]
        grads = pair_backward(q, k, v, qx[r], kx[r], o, do, lse[r, p], False)
        where = pl.ds(pl.multiple_of(r * tokens_e, tokens_e), tokens_e)
        for i, value in enumerate(grads):
            at = pl.ds(pl.multiple_of(i * dim + p * PAIR, PAIR), PAIR)
            d_packed[where, at] = value.astype(BF)

    def block_loads(v, act):
        slot = lax.rem(v, 2)
        where = pl.ds(pl.multiple_of(lax.rem(v, per_row) * BLOCK, BLOCK), BLOCK)
        for r in range(rows):

            @pl.when(v // per_row == r)
            def _(r=r):
                act([pltpu.make_async_copy(x_ref.at[r, where], x_stage.at[slot], s_block.at[slot, 0])])

            for ref, begin in row_pieces(de1_of, r):
                for at in range(0, ref.shape[0], BLOCK):

                    @pl.when(v == (r * tokens_e + begin + at) // BLOCK)
                    def _(ref=ref, at=at):
                        act(
                            [
                                pltpu.make_async_copy(
                                    ref.at[at : at + BLOCK], grad_stage.at[slot], s_block.at[slot, 1]
                                )
                            ]
                        )

    def block_store(v):
        slot = lax.rem(v, 2)
        where = pl.ds(pl.multiple_of(lax.rem(v, per_row) * BLOCK, BLOCK), BLOCK)
        return pltpu.make_async_copy(
            dx_stage.at[slot], o_results.at[v // per_row, where], s_out.at[slot]
        )

    def block_unit(v):
        slot = lax.rem(v, 2)
        block_loads(v, wait_all)

        @pl.when(v == 0)
        def _():
            const_copies[2].wait()
            dg0[...] = jnp.zeros_like(dg0)

        @pl.when(v >= 2)
        def _():
            block_store(v - 2).wait()

        where = pl.ds(pl.multiple_of(v * BLOCK, BLOCK), BLOCK)
        dn = None
        for i in range(3):
            part = mm(d_packed[where, i * dim : (i + 1) * dim], wa[:, i * dim : (i + 1) * dim], NT)
            dn = part if dn is None else dn + part
        back, gain_part = norm_back(x_stage[slot].astype(F32), g0_ref[...], dn)
        dg0[...] += gain_part
        dx_stage[slot] = grad_stage[slot] + back
        block_store(v).start()

    def dec_results(store):
        half = token_counts[1]
        parts = [
            (ref, stage.at[r], o_results.at[r, k * half : (k + 1) * half], s_dec.at[k, r])
            for k, (group, stage) in enumerate(((out_of, grad_stage), (dx_of, dx_stage)))
            for r, ref in enumerate(group)
        ]
        return [
            pltpu.make_async_copy(held, dst, sem) if store else pltpu.make_async_copy(src, held, sem)
            for src, held, dst, sem in parts
        ]

    def side_work(s):
        @pl.when(s == 0)
        def _():
            start_all(lse_copies)
            start_all(const_copies)
            for v in range(2):
                block_loads(jnp.int32(v), start_all)

        u = s // 2

        @pl.when((lax.rem(s, 2) == 0) & (u < attn_units))
        def _():
            attn_loads(u, start_all)

        @pl.when((lax.rem(s, 2) == 0) & (u >= 1) & (u <= attn_units))
        def _():
            @pl.when(u == 1)
            def _():
                wait_all(lse_copies)
                wait_all(const_copies[:2])

            attn_unit(u - 1)

        v = (s - first_block) // 2

        @pl.when((lax.rem(s, 2) == 0) & (s >= first_block) & (v < block_units))
        def _():
            block_unit(v)

            @pl.when(v + 2 < block_units)
            def _():
                block_loads(v + 2, start_all)


    def open_first(side):
        start_all(left_copies(0, side))
        for t in range(AHEAD):
            start_all(panel_copies(0, t, t % PANELS, side))

    each(open_first)

    barrier = pltpu.get_barrier_semaphore()

    def greet(peer):
        pl.semaphore_signal(barrier, inc=1, device_id=(sec, peer), device_id_type=MESH)

    greet(by_core)
    greet(by_y)

    @pl.when(z > 0)
    def _():
        greet(me - 4)

    @pl.when(z < NZ - 1)
    def _():
        greet(me + 4)

    @pl.when((z > 0) & (z < NZ - 1))
    def _():
        pl.semaphore_wait(barrier, 4)

    @pl.when((z == 0) | (z == NZ - 1))
    def _():
        pl.semaphore_wait(barrier, 3)


    @pl.when(sec == 1)
    def _():
        start_all(dec_results(False))

    def step(s, carry):
        @pl.when(s + AHEAD < chunks - 1)
        def _():
            for_panel(
                s + AHEAD,
                lambda p, i, slot, side: start_all(panel_copies(p, i, slot, side)),
            )

        @pl.when((s >= RING) & (s < chunks))
        def _():
            send_core(s - RING).wait_send()

        @pl.when(s < chunks)
        def _():
            compute(s)
            send_core(s).start()

        @pl.when(sec == 0)
        def _():
            side_work(s)

        @pl.when((sec == 1) & (s == RING))
        def _():
            wait_all(dec_results(False))
            start_all(dec_results(True))

        @pl.when(s == 1)
        def _():
            each(lambda side: start_all(tall_copies(side)))

        @pl.when(s == 4)
        def _():
            each(lambda side: wait_all(tall_copies(side)))
            each(lambda side: start_all(left_copies(1, side)))
            each(lambda side: start_all(tall_right_copies(side)))

        @pl.when((s >= 4) & (s < 4 + groups))
        def _():
            build_tall(s - 4)

        j_c = s - C_LAG

        @pl.when((j_c >= 0) & (j_c < chunks))
        def _():
            send_core(j_c).wait_recv()
            slot = lax.rem(j_c, RING)
            for a in range(NZ):
                for b in range(NY):
                    add_into(own.at[j_c, a, b], ring.at[slot, a, b, core])

            @pl.when(jnp.logical_not(z_first(j_c)))
            def _():
                send_y(j_c).start()

        j_y = s - Y_LAG

        @pl.when((j_y >= 0) & (j_y < chunks) & jnp.logical_not(z_first(j_y)))
        def _():
            send_y(j_y).wait_recv()
            for t in range(NZ):
                add_into(own.at[j_y, t, y], got_y.at[j_y, t])

        for at in range(NZ - 1):
            j_r = s - Y_LAG - HOP * at

            @pl.when((z == at) & (j_r >= 0) & (j_r < chunks) & jnp.logical_not(z_first(j_r)))
            def _(at=at, j_r=j_r):
                if at > 0:
                    send_right(j_r, at - 1).wait_recv()
                    for t in range(at + 1, NZ):
                        add_into(own.at[j_r, t, y], got_r.at[j_r, t - 1])
                send_right(j_r, at).start()

        for at in range(1, NZ):
            j_l = s - Y_LAG - HOP * (NZ - 1 - at)

            @pl.when((z == at) & (j_l >= 0) & (j_l < chunks) & jnp.logical_not(z_first(j_l)))
            def _(at=at, j_l=j_l):
                if at < NZ - 1:
                    send_left(j_l, at + 1).wait_recv()
                    for t in range(at):
                        add_into(own.at[j_l, t, y], got_l.at[j_l, t])
                send_left(j_l, at).start()

        for at in range(NZ):
            for right, hop in ((True, at), (False, NZ - 1 - at)):
                if hop < NZ - 1:
                    j_z = s - C_LAG - HOP * hop

                    @pl.when((z == at) & (j_z >= 0) & (j_z < chunks) & z_first(j_z))
                    def _(at=at, j_z=j_z, right=right):
                        forward_along(j_z, at, right)

        j_t = s - ZF_LAG

        @pl.when((j_t >= 0) & (j_t < chunks) & z_first(j_t))
        def _():
            turn_to_y(j_t)

        return carry

    lax.fori_loop(0, chunks + Y_LAG + HOP * (NZ - 1), step, 0)


    def finish(j):
        @pl.when(j >= chunks - RING)
        def _():
            send_core(j).wait_send()

        @pl.when(z_first(j))
        def _():
            send_y_last(j).wait()
            for at in range(NZ):

                @pl.when(z == at)
                def _(at=at):
                    if at < NZ - 1:
                        send_along(j, at, True).wait_send()
                    if at > 0:
                        send_along(j, at, False).wait_send()

        @pl.when(jnp.logical_not(z_first(j)))
        def _():
            finish_y_first(j)

    def finish_y_first(j):
        @pl.when(z == NZ - 1)
        def _():
            send_right(j, NZ - 2).wait_recv()

        @pl.when(z == 0)
        def _():
            send_left(j, 1).wait_recv()

        send_y(j).wait_send()
        for at in range(NZ):

            @pl.when(z == at)
            def _(at=at):
                if at < NZ - 1:
                    send_right(j, at).wait_send()
                if at > 0:
                    send_left(j, at).wait_send()

    def total(j, part):
        mine = own[j, z, y, part].astype(F32)
        right = got_r[j, jnp.maximum(z - 1, 0), part].astype(F32)
        left = got_l[j, jnp.minimum(z, NZ - 2), part].astype(F32)
        across = got_y[j, z, part].astype(F32)
        along = jnp.where(z > 0, right, 0.0) + jnp.where(z < NZ - 1, left, 0.0)
        return mine + jnp.where(z_first(j), across, along)

    def close(out, base, count, column):
        def panel(i, carry):
            finish(base + i)
            at = pl.ds(pl.multiple_of(column + i * LANES, LANES), LANES)
            out[:, at] = total(base + i, pl.ds(0, height))
            return carry

        lax.fori_loop(0, count, panel, 0)

    close(o_fi, bases[0], chunk_counts[0], 0)

    def tall_out(i, carry):
        finish(bases[TALL] + i)
        at = pl.ds(pl.multiple_of(i * 16, 16), 16)
        for k in range(tall_right.shape[1] // LANES):
            o_fo[at, k * LANES : (k + 1) * LANES] = total(bases[TALL] + i, pl.ds(k * 16, 16))
        return carry

    lax.fori_loop(0, chunk_counts[TALL], tall_out, 0)
    close(o_cross, bases[2], chunk_counts[2], 0)
    close(o_cross, bases[3], chunk_counts[3], dim)
    close(o_out, bases[4], chunk_counts[4], 0)
    for k in range(3):
        close(o_in, bases[5 + k], chunk_counts[5 + k], k * dim)
    close(o_gain, chunks - 1, 1, 0)

    @pl.when(sec == 0)
    def _():
        for v in range(max(0, block_units - 2), block_units):
            block_store(jnp.int32(v)).wait()

    @pl.when(sec == 1)
    def _():
        wait_all(dec_results(True))


def grad_sum(sides, kept, decoded, gain_rows, shared):
    (enc_lefts, enc_rights), (dec_lefts, dec_rights) = sides
    x_in, qx, kx, wa, g0 = shared
    rows = x_in.shape[0]
    token_counts = (enc_lefts[5][0].shape[0], dec_lefts[5][0].shape[0])
    tokens = rows * max(token_counts)
    groups = enc_lefts + enc_rights + dec_lefts + dec_rights + kept + decoded
    group_sizes = tuple(len(g) for g in groups + gain_rows[0] + gain_rows[1])
    most = max(group_sizes)
    dim, tall = dec_lefts[0][0].shape[1], dec_lefts[TALL][0].shape[1]
    height = dim // PEERS
    chunk_counts = tuple(
        dec_lefts[a][0].shape[1] * dec_rights[b][0].shape[1] // (dim * LANES) for a, b in PRODUCTS
    )
    chunks = sum(chunk_counts) + 1
    attn_units, block_units = rows * HEADS // 2, rows * token_counts[0] // BLOCK
    unit_steps = (attn_units, block_units, 2 * attn_units + 2)
    flat = lambda groups: [v for group in groups for v in group]
    moved = flat(groups)
    gains = flat(gain_rows[0] + gain_rows[1])
    half = (chunks, NZ, NY, height, LANES)
    fourth = (chunks, NZ, height, LANES)
    width = lambda *which: sum(dec_rights[i][0].shape[1] for i in which)
    out_shape = [
        jax.ShapeDtypeStruct(s, F32)
        for s in (
            (height, width(5, 6, 7)),
            (height, width(4)),
            (height, width(0)),
            (height, width(2, 3)),
            (height, LANES),
            (tall // PEERS, width(1)),
            x_in.shape,
        )
    ]
    hbm, vmem = pl.BlockSpec(memory_space=pl.ANY), pl.BlockSpec(memory_space=pltpu.VMEM)
    dma = pltpu.SemaphoreType.DMA
    return pl.pallas_call(
        functools.partial(
            grad_sum_kernel, rows, group_sizes, token_counts, chunk_counts, unit_steps
        ),
        in_specs=[hbm] * len(moved) + [vmem] * len(gains) + [hbm] * 4 + [vmem],
        out_specs=[vmem] * 6 + [hbm],
        out_shape=out_shape,
        scratch_shapes=[
            pltpu.VMEM((dim, tokens), BF),
            pltpu.VMEM((tall, tokens), BF),
            pltpu.VMEM((2, tokens, dim), BF),
            pltpu.VMEM((tokens, tall), BF),
            pltpu.VMEM((tokens, width(1)), BF),
            pltpu.VMEM((PANELS, tokens, LANES), BF),
            pltpu.VMEM((RING, NZ, NY, NC, height, LANES), BF),
            pltpu.VMEM(half, BF),
            pltpu.VMEM(fourth, BF),
            pltpu.VMEM((chunks, NZ - 1) + fourth[2:], BF),
            pltpu.VMEM((chunks, NZ - 1) + fourth[2:], BF),
            pltpu.VMEM((-(-chunks // ZF_EVERY), NZ - 1) + half[2:], BF),
            pltpu.VMEM((-(-chunks // ZF_EVERY), NZ - 1) + half[2:], BF),
            dma((2, most)),
            dma((most,)),
            dma((most,)),
            dma((PANELS, most)),
        ]
        + [dma((chunks,))] * 8
        + [
            pltpu.VMEM((rows * token_counts[0], 3 * dim), BF),
            pltpu.VMEM(wa.shape, BF),
            pltpu.VMEM((2, 5, token_counts[0], PAIR), BF),
            pltpu.VMEM(qx.shape, BF),
            pltpu.VMEM(kx.shape, BF),
            pltpu.VMEM((rows,) + kept[3][0].shape, F32),
            pltpu.VMEM((2, BLOCK, dim), BF),
            pltpu.VMEM((max(2, rows), BLOCK, dim), F32),
            pltpu.VMEM((max(2, rows), BLOCK, dim), F32),
            pltpu.VMEM((1, dim), F32),
            dma((2, 4 + most)),
            dma((3,)),
            dma((rows,)),
            dma((2, 2)),
            dma((2,)),
            dma((2, rows)),
        ],
        compiler_params=pltpu.CompilerParams(
            collective_id=1, has_side_effects=True, vmem_limit_bytes=SUM_VMEM
        ),
    )(*moved, *gains, x_in, qx, kx, wa, g0)


def hand_over_kernel(rows, *refs):
    count = (len(refs) - 3) // 3
    gain_ref, sources, gain_out = refs[0], refs[1 : 1 + count], refs[1 + count]
    targets, held = refs[2 + count : 2 + 2 * count], refs[2 + 2 * count : 2 + 3 * count]
    gain, sems = refs[2 + 3 * count], refs[3 + 3 * count]
    moves = []
    for src, keep, dst in zip(sources, held, targets):
        for part in range(rows) if len(src.shape) == 3 else [slice(None)]:
            i = len(moves)
            load = pltpu.make_async_copy(src.at[part], keep.at[part], sems.at[0, i])
            load.start()
            moves.append((load, keep.at[part], dst.at[0].at[part], sems.at[1, i]))
    load_gain = pltpu.make_async_copy(gain_ref, gain, sems.at[0, len(moves)])
    load_gain.start()
    stores = []
    for load, keep, dst, sem in moves:
        load.wait()
        stores.append(pltpu.make_async_copy(keep, dst, sem))
        stores[-1].start()
    load_gain.wait()
    gain_out[0] = gain[...].T[: gain_out.shape[1]]
    for store in stores:
        store.wait()


def hand_over(gain, gain_rows, arrays):
    hbm, vmem = pl.BlockSpec(memory_space=pl.ANY), pl.BlockSpec(memory_space=pltpu.VMEM)
    rows = max(a.shape[0] for a in arrays if a.ndim == 3)
    return pl.pallas_call(
        functools.partial(hand_over_kernel, rows),
        in_specs=[hbm] * (1 + len(arrays)),
        out_specs=[vmem] + [hbm] * len(arrays),
        out_shape=[jax.ShapeDtypeStruct((1, gain_rows, gain.shape[0]), F32)]
        + [jax.ShapeDtypeStruct((1,) + a.shape, F32) for a in arrays],
        scratch_shapes=[pltpu.VMEM(a.shape, F32) for a in arrays]
        + [
            pltpu.VMEM(gain.shape, F32),
            pltpu.SemaphoreType.DMA((2, len(arrays) + rows)),
        ],
        compiler_params=pltpu.CompilerParams(vmem_limit_bytes=SUM_VMEM),
    )(gain, *arrays)


def plain_sum(on_decoder, sides, gain_terms):
    def terms(lefts, rights):
        parts = [
            mm(jnp.concatenate(lefts[i], 0), jnp.concatenate(rights[j], 0), TN).astype(BF)
            for i, j in PRODUCTS
        ]
        return [
            jnp.concatenate(parts[5:8], 1),
            parts[4],
            parts[0],
            jnp.concatenate(parts[2:4], 1),
            parts[1],
        ]

    pieces = lax.cond(on_decoder, lambda: terms(*sides[1]), lambda: terms(*sides[0]))
    pieces.insert(4, gain_terms)
    return [
        lax.psum_scatter(piece, "rows", scatter_dimension=0, tiled=True).astype(F32)
        for piece in pieces
    ]


def low_half(rows):
    return lax.broadcasted_iota(jnp.int32, (rows, PAIR), 1) < HEAD


def masked_scores(q, k, qx, kx, head, causal):
    lo_q, lo_k = low_half(q.shape[0]), low_half(k.shape[0])
    if head == 0:
        qh, kh = jnp.where(lo_q, q, qx), jnp.where(lo_k, k, kx)
    else:
        qh, kh = jnp.where(lo_q, qx, q), jnp.where(lo_k, kx, k)
    s = mm(kh, qh, NT)
    if causal:
        key_at = lax.broadcasted_iota(jnp.int32, s.shape, 0)
        query_at = lax.broadcasted_iota(jnp.int32, s.shape, 1)
        s = jnp.where(key_at <= query_at, s, NEGATIVE)
    return s


def pair_backward(q, k, v, qx, kx, o, do, lse, causal):
    kt = k.astype(F32).T.astype(BF)
    spread = (do.astype(F32) * o.astype(F32)).T
    low_q, low_k = low_half(q.shape[0]), low_half(k.shape[0])
    zero_q, zero_k = jnp.zeros_like(q), jnp.zeros_like(k)
    dqs, grads = [], []

    def begin(head):
        s = mm(pick(head, low_k, k, kx), pick(head, low_q, q, qx), NT)
        return causal_only(s) if causal else s, mm(pick(head, low_k, v, zero_k), do, NT)

    def end(head, values):
        s, dp = values
        half = slice(head * HEAD, (head + 1) * HEAD)
        p = jnp.exp2(s * (SCALE * LOG2E) - lse[head : head + 1])
        ds = (p * (dp - jnp.sum(spread[half], axis=0, keepdims=True))).astype(BF)
        dqs.append(mm(kt[half], ds))
        grads.append(
            (mm(ds, pick(head, low_q, q, zero_q)), mm(p.astype(BF), pick(head, low_q, do, zero_q)))
        )

    in_order(range(2), begin, end)
    (dk0, dv0), (dk1, dv1) = grads
    return jnp.concatenate(dqs, axis=0).T * SCALE, (dk0 + dk1) * SCALE, dv0 + dv1


def attn_bwd_kernel(
    q_ref, k_ref, v_ref, qx_ref, kx_ref, o_ref, do_ref, lse_ref, dq_ref, dk_ref, dv_ref, *, causal
):
    dq, dk, dv = pair_backward(
        q_ref[...], k_ref[...], v_ref[...], qx_ref[0], kx_ref[0], o_ref[...], do_ref[...],
        lse_ref[0], causal,
    )
    dq_ref[...] = dq.astype(BF)
    dk_ref[...] = dk.astype(BF)
    dv_ref[...] = dv.astype(BF)


def column_block(length, first):
    return pl.BlockSpec((length, PAIR), lambda p: (0, first + p))


def mask_block(length, row):
    return pl.BlockSpec((1, length, PAIR), lambda p: (row, 0, 0))


def pair_block(count_q):
    return pl.BlockSpec((1, 2, count_q), lambda p: (p, 0, 0))


def params(**more):
    return pltpu.CompilerParams(vmem_limit_bytes=VMEM_LIMIT, **more)


def attention_backward(q_in, k_in, v_in, qx, kx, row, firsts, mixed, grad_mixed, lse, causal):
    count_q, count_k, pairs = q_in.shape[0], k_in.shape[0], HEADS // 2
    width = HEADS * HEAD
    return pl.pallas_call(
        functools.partial(attn_bwd_kernel, causal=causal),
        grid=(pairs,),
        in_specs=[
            column_block(count_q, firsts[0]),
            column_block(count_k, firsts[1]),
            column_block(count_k, firsts[2]),
            mask_block(count_q, row),
            mask_block(count_k, row),
            column_block(count_q, 0),
            column_block(count_q, 0),
            pair_block(count_q),
        ],
        out_specs=[
            column_block(count_q, 0),
            column_block(count_k, 0),
            column_block(count_k, 0),
        ],
        out_shape=[
            jax.ShapeDtypeStruct((count_q, width), BF),
            jax.ShapeDtypeStruct((count_k, width), BF),
            jax.ShapeDtypeStruct((count_k, width), BF),
        ],
        compiler_params=params(),
    )(q_in, k_in, v_in, qx, kx, mixed, grad_mixed, lse)


BLOCK = 256
SLICE = 512


def inverse_rms(v):
    return lax.rsqrt(jnp.mean(v * v, -1, keepdims=True) + EPSILON)


def norm(v, gain):
    return (v * inverse_rms(v) * gain).astype(BF)


def norm_back(v, gain, grad):
    inv = inverse_rms(v)
    scaled = grad * gain
    along = jnp.mean(scaled * v, -1, keepdims=True)
    return (
        inv * scaled - v * (inv * inv * inv * along),
        jnp.sum(grad * v * inv, 0, keepdims=True),
    )


def gelu(x):
    return 0.5 * x * (1.0 + jnp.tanh(GELU_C * (x + GELU_A * x * x * x)))


def gelu_parts(x):
    square = x * x
    t = jnp.tanh(GELU_C * x * (1.0 + GELU_A * square))
    half = 0.5 * (1.0 + t)
    slope = half + 0.5 * x * (1.0 - t * t) * (GELU_C * (1.0 + 3.0 * GELU_A * square))
    return x * half, slope


class Fetch:
    def __init__(self, sources, held, sems):
        self.copies = [
            pltpu.make_async_copy(src, dst, sems.at[i])
            for i, (src, dst) in enumerate(zip(sources, held))
        ]
        self.held = held
        self.first = pl.program_id(0) == 0

        @pl.when(self.first)
        def _():
            for copy in self.copies:
                copy.start()

    def __getitem__(self, i):
        @pl.when(self.first)
        def _():
            self.copies[i].wait()

        return self.held[i]


def add_gain(ref, part):
    @pl.when(pl.program_id(0) == 0)
    def _():
        ref[...] = part

    @pl.when(pl.program_id(0) > 0)
    def _():
        ref[...] += part


def block_call(kernel, steps, ins, weights, outs, gain_outs=0):
    specs, arrays = [], []
    for array, row, first in ins:
        columns = array.shape[-1]
        if row is None:
            specs.append(pl.BlockSpec((BLOCK, columns), lambda i, f=first: (f + i, 0)))
        else:
            specs.append(
                pl.BlockSpec((None, BLOCK, columns), lambda i, r=row, f=first: (r, f + i, 0))
            )
        arrays.append(array)
    gains = [w for w in weights if w.dtype == F32]
    mats = [w for w in weights if w.dtype != F32]
    specs += [pl.BlockSpec((1, g.shape[1]), lambda i: (0, 0)) for g in gains]
    specs += [pl.BlockSpec(memory_space=pl.ANY)] * len(mats)
    dim = gains[0].shape[1]
    count = len(mats)

    def run(*refs):
        held, sems = refs[-1 - count : -1], refs[-1]
        at = len(arrays) + len(gains)
        fetch = Fetch(refs[at : at + count], held, sems)
        kernel(refs[: len(arrays)], [g[...] for g in refs[len(arrays) : at]], fetch, refs[at + count : -1 - count])

    return pl.pallas_call(
        run,
        grid=(steps,),
        in_specs=specs,
        out_specs=[pl.BlockSpec((BLOCK, c), lambda i: (i, 0)) for c, _ in outs]
        + [pl.BlockSpec((1, dim), lambda i: (0, 0))] * gain_outs,
        out_shape=[jax.ShapeDtypeStruct((steps * BLOCK, c), t) for c, t in outs]
        + [jax.ShapeDtypeStruct((1, dim), F32)] * gain_outs,
        scratch_shapes=[pltpu.VMEM(m.shape, m.dtype) for m in mats]
        + [pltpu.SemaphoreType.DMA((count,))],
        compiler_params=params(),
    )(*arrays, *gains, *mats)


def project_kernel(ins, gains, w, outs):
    (x,), (g0,), (n_ref, packed_ref) = ins, gains, outs
    n = norm(x[...].astype(F32), g0)
    n_ref[...] = n
    wa = w[0]
    dim = x.shape[1]
    for at in range(0, wa.shape[1], dim):
        packed_ref[:, at : at + dim] = mm(n, wa[:, at : at + dim]).astype(BF)


class FeedForward:
    def __init__(self, move, wf_hbm, wd_hbm, wf, wd):
        self.wf, self.wd, self.half = wf, wd, wd.shape[0]
        self.copies, self.move = {}, move
        self.sources = wf_hbm, wd_hbm

    def load(self):
        wf_hbm, wd_hbm = self.sources
        for at in range(0, self.half, SLICE):
            self.copies[at] = [
                self.move.copy(wd_hbm.at[at : at + SLICE], self.wd.at[at : at + SLICE])
            ] + [
                self.move.copy(wf_hbm.at[:, first : first + SLICE], self.wf.at[:, first : first + SLICE])
                for first in (at, self.half + at)
            ]

    def ready(self, at):
        for made in self.copies.pop(at, []):
            made.wait()

    def slices(self):
        return range(0, self.half, SLICE)

    def parts(self, at):
        self.ready(at)
        up = slice(self.half + at, self.half + at + SLICE)
        return self.wf[:, at : at + SLICE], self.wf[:, up], self.wd[at : at + SLICE, :]


def ffn_up(m, ffn, acc, u_ref, act_ref):
    half = ffn.half

    def begin(at):
        gate_w, up_w, _ = ffn.parts(at)
        return mm(m, gate_w), mm(m, up_w)

    total = [acc]

    def end(at, values):
        gate, up = values
        u_ref[:, at : at + SLICE] = gate.astype(BF)
        u_ref[:, half + at : half + at + SLICE] = up.astype(BF)
        act = (gelu(gate) * up).astype(BF)
        if act_ref is not None:
            act_ref[:, at : at + SLICE] = act
        total[0] = total[0] + mm(act, ffn.wd[at : at + SLICE, :])

    in_order(ffn.slices(), begin, end)
    return total[0]


def ffn_down(branch, ffn, u_ref, du_ref, act_ref):
    half = ffn.half
    total = []

    def begin(at):
        return mm(branch, ffn.parts(at)[2], NT)

    def end(at, d_act):
        gate_w, up_w, _ = ffn.parts(at)
        gate = u_ref[:, at : at + SLICE].astype(F32)
        up = u_ref[:, half + at : half + at + SLICE].astype(F32)
        value, slope = gelu_parts(gate)
        if act_ref is not None:
            act_ref[:, at : at + SLICE] = (value * up).astype(BF)
        d_gate = (d_act * up * slope).astype(BF)
        d_up = (d_act * value).astype(BF)
        du_ref[:, at : at + SLICE] = d_gate
        du_ref[:, half + at : half + at + SLICE] = d_up
        part = mm(d_gate, gate_w, NT) + mm(d_up, up_w, NT)
        total[:] = [part if not total else total[0] + part]

    in_order(ffn.slices(), begin, end)
    return total[0]


def dec_query_kernel(ins, gains, w, outs):
    (o, x), (g1,), (d1_ref, c_ref, cq_ref) = ins, gains, outs
    d1 = x[...].astype(F32) + mm(o[...], w[0][...])
    d1_ref[...] = d1
    c = norm(d1, g1)
    c_ref[...] = c
    cq_ref[...] = mm(c, w[1][:, : c.shape[1]]).astype(BF)


def dec_ffn_kernel(row, x_hbm, oc_hbm, d1_hbm, g2, wc_hbm, wf_hbm, wd_hbm, *refs):
    outs, results, held = refs[:9], refs[9:18], refs[18:]
    doc, out, dd2_v, m_v, act, du, branch, dg2, cot = results
    oc, d1, u, proj, wf, wd, sems = held
    move = Mover(sems)
    tokens, width = oc.shape
    got = [
        move.copy(a, b)
        for a, b in ((oc_hbm, oc), (wc_hbm.at[:, width:], proj), (d1_hbm, d1))
    ]
    ffn = FeedForward(move, wf_hbm, wd_hbm, wf, wd)
    ffn.load()
    got_cot = move.copy(x_hbm.at[row, tokens:], cot)
    for made in got:
        made.wait()
    d2 = d1[...] + mm(oc[...], proj[...], NT)
    m = norm(d2, g2[...])
    m_v[...] = m
    out[...] = ffn_up(m, ffn, d2, u, act)
    for i in (3, 1, 4):
        move.store(results[i], outs[i])
    got_cot.wait()
    move.store(cot, outs[8])
    dm = ffn_down(cot[...], ffn, u, du, None)
    back, dg2[...] = norm_back(d2, g2[...], dm)
    dd2 = cot[...].astype(F32) + back
    branch[...] = dd2.astype(BF)
    doc[...] = mm(branch[...], proj[...]).astype(BF)
    dd2_v[...] = dd2
    for i in (0, 2, 5, 6, 7):
        move.store(results[i], outs[i])
    move.drain()


def enc_back_kernel(blocks, dk_hbm, dv_hbm, e1_hbm, e2_hbm, u_hbm, g1, g2, wc_hbm, wd_hbm, wf_hbm, wo_hbm, *refs):
    outs, results, held = refs[:10], refs[10:20], refs[20:]
    mem, fb_v, m_v, act, du, de1_v, ab_v, do, dg1, dg2 = results
    dk, dv, e1_in, e2_in, u, wc, wd, wf, wo, sems = held
    move = Mover(sems)
    width = dk.shape[1]
    here = [slice(i * BLOCK, (i + 1) * BLOCK) for i in range(len(blocks))]
    there = [slice(i * BLOCK, (i + 1) * BLOCK) for i in blocks]

    def load(i, pairs):
        return [move.copy(src.at[there[i]], dst.at[here[i]]) for src, dst in pairs]

    early = ((dk_hbm, dk), (dv_hbm, dv), (e2_hbm, e2_in))
    late = ((u_hbm, u), (e1_hbm, e1_in))
    got_early, got_late = [load(0, early)], []
    got_early[0].append(move.copy(wc_hbm, wc))
    ffn = FeedForward(move, wf_hbm, wd_hbm, wf, wd)
    got_late.append(load(0, late))
    ffn.load()
    got_late[0].append(move.copy(wo_hbm, wo))
    for i in range(1, len(blocks)):
        got_early.append(load(i, early))
        got_late.append(load(i, late))
    for i, b in enumerate(here):
        for made in got_early[i]:
            made.wait()
        dmem = mm(dk[b], wc[:, :width], NT) + mm(dv[b], wc[:, width:], NT)
        mem[b] = norm(e2_in[b], g1[...])
        de2, gain1 = norm_back(e2_in[b], g1[...], dmem)
        fb = de2.astype(BF)
        fb_v[b] = fb
        for made in got_late[i]:
            made.wait()
        m_v[b] = norm(e1_in[b], g2[...])
        dm = ffn_down(fb, ffn, u.at[b], du.at[b], act.at[b])
        back, gain2 = norm_back(e1_in[b], g2[...], dm)
        de1 = de2 + back
        de1_v[b] = de1
        ab = de1.astype(BF)
        ab_v[b] = ab
        do[b] = mm(ab, wo[...], NT).astype(BF)
        for k in range(8):
            move.store(results[k].at[b], outs[k].at[b])
        dg1[...] = gain1 if i == 0 else dg1[...] + gain1
        dg2[...] = gain2 if i == 0 else dg2[...] + gain2
    move.store(dg1, outs[8])
    move.store(dg2, outs[9])
    move.drain()


def dec_back_kernel(ins, gains, w, outs):
    (dcq, d1_in, dd2), (g1,), (dd1_ref, ab_ref, do_ref, dg1_ref) = ins, gains, outs
    d1 = d1_in[...]
    dc = mm(dcq[...], w[0][:, : dcq.shape[1]], NT)
    back, dg1 = norm_back(d1, g1, dc)
    dd1 = dd2[...] + back
    dd1_ref[...] = dd1
    ab = dd1.astype(BF)
    ab_ref[...] = ab
    do_ref[...] = mm(ab, w[1][...], NT).astype(BF)
    add_gain(dg1_ref, dg1)


def input_grad_kernel(ins, gains, w, outs):
    (dq, dk, dv, x, grad), (g0,), (dx_ref, dg0_ref) = ins, gains, outs
    wa = w[0]
    width = dq.shape[1]
    dn = (
        mm(dq[...], wa[:, :width], NT)
        + mm(dk[...], wa[:, width : 2 * width], NT)
        + mm(dv[...], wa[:, 2 * width :], NT)
    )
    back, dg0 = norm_back(x[...].astype(F32), g0, dn)
    dx_ref[...] = grad[...] + back
    add_gain(dg0_ref, dg0)


class Mover:
    def __init__(self, sems):
        self.sems, self.used, self.stores = sems, 0, []

    def copy(self, src, dst):
        made = pltpu.make_async_copy(src, dst, self.sems.at[self.used])
        self.used += 1
        made.start()
        return made

    def store(self, src, dst):
        self.stores.append(self.copy(src, dst))

    def drain(self):
        for made in self.stores:
            made.wait()


def pair_columns(first, p):
    return slice(first + p * PAIR, first + (p + 1) * PAIR)


def pick(head, low, a, b):
    return jnp.where(low, a, b) if head % 2 == 0 else jnp.where(low, b, a)


def in_order(items, begin, end, lead=1):
    waiting = []
    for item in items:
        waiting.append((item, begin(item)))
        if len(waiting) > lead:
            end(*waiting.pop(0))
    while waiting:
        end(*waiting.pop(0))


def attend(q_ref, kv_ref, firsts, qx, kx, o_ref, lse_ref, causal):
    count_q, count_k = qx.shape[0], kx.shape[0]
    low_q, low_k = low_half(count_q), low_half(count_k)
    ones = jnp.ones((8, count_k), BF)
    values, outs = {}, {}

    def begin(head):
        q = q_ref[:, pair_columns(firsts[0], head // 2)]
        k = kv_ref[:, pair_columns(firsts[1], head // 2)]
        s = mm(pick(head, low_k, k, kx), pick(head, low_q, q, qx), NT)
        return causal_only(s) if causal else s

    def end(head, s):
        p = head // 2
        if head % 2 == 0:
            values[p] = kv_ref[:, pair_columns(firsts[2], p)].astype(F32).T.astype(BF)
        vt = values[p][(head % 2) * HEAD : (head % 2 + 1) * HEAD]
        top = jnp.max(s, axis=0, keepdims=True)
        e = jnp.exp2((s - top) * (SCALE * LOG2E)).astype(BF)
        mixed = mm(jnp.concatenate([vt, ones], axis=0), e)
        total = mixed[HEAD : HEAD + 1]
        outs[head] = mixed[:HEAD] * (1.0 / total)
        lse_ref[p, head % 2 : head % 2 + 1, :] = top * (SCALE * LOG2E) + jnp.log2(total)
        if head % 2 == 1:
            both = jnp.concatenate([outs.pop(head - 1), outs.pop(head)], axis=0)
            o_ref[:, pair_columns(0, p)] = both.T.astype(BF)

    in_order(range(HEADS), begin, end)


def causal_only(s):
    key_at = lax.broadcasted_iota(jnp.int32, s.shape, 0)
    query_at = lax.broadcasted_iota(jnp.int32, s.shape, 1)
    return jnp.where(key_at <= query_at, s, NEGATIVE)


def attend_kernel(firsts, row, causal, same, *refs):
    if same:
        q_ref, (qx_ref, kx_ref, o_ref, lse_ref) = refs[0], refs[1:]
        kv_ref = q_ref
    else:
        q_ref, kv_ref, qx_ref, kx_ref, o_ref, lse_ref = refs
    attend(q_ref, kv_ref, firsts, qx_ref[row], kx_ref[row], o_ref, lse_ref, causal)


def attention_forward(q_in, kv_in, qx, kx, row, firsts, causal):
    count_q = q_in.shape[0]
    ins = [q_in] if kv_in is None else [q_in, kv_in]
    vmem = pl.BlockSpec(memory_space=pltpu.VMEM)
    return pl.pallas_call(
        functools.partial(attend_kernel, firsts, row, causal, kv_in is None),
        in_specs=[vmem] * (len(ins) + 2),
        out_specs=[vmem] * 2,
        out_shape=[
            jax.ShapeDtypeStruct((count_q, HEADS * HEAD), BF),
            jax.ShapeDtypeStruct((HEADS // 2, 2, count_q), F32),
        ],
        compiler_params=params(),
    )(*ins, qx, kx)


def enc_attend_kernel(row, x_hbm, qx_hbm, kx_hbm, g0, wa_hbm, *refs):
    outs, (n_v, packed_v, o_v, lse_v, x, qx, kx, wa, sems) = refs[:4], refs[4:]
    move = Mover(sems)
    got_x = move.copy(x_hbm.at[row], x)
    thirds = [slice(at, at + x.shape[1]) for at in range(0, wa.shape[1], x.shape[1])]
    got_wa = [move.copy(wa_hbm.at[:, t], wa.at[:, t]) for t in thirds]
    got_masks = move.copy(qx_hbm.at[row], qx), move.copy(kx_hbm.at[row], kx)
    tokens, dim = x.shape
    got_x.wait()
    blocks = [slice(at, at + BLOCK) for at in range(0, tokens, BLOCK)]
    for b in blocks:
        n_v[b] = norm(x[b].astype(F32), g0[...])
    move.store(n_v, outs[0])
    for t, made in zip(thirds, got_wa):
        made.wait()
        for b in blocks:
            packed_v[b, t] = mm(n_v[b], wa[:, t]).astype(BF)
    move.store(packed_v, outs[1])
    for made in got_masks:
        made.wait()
    attend(packed_v, packed_v, (0, dim, 2 * dim), qx[...], kx[...], o_v, lse_v, False)
    move.store(o_v, outs[2])
    move.store(lse_v, outs[3])
    move.drain()


def enc_rest_kernel(row, x_hbm, o_hbm, g1, g2, wo_hbm, wf_hbm, wd_hbm, wc_hbm, *refs):
    outs, (e1_v, u_v, e2_v, sent_v, x, o, wo, wf, wd, wc, sems) = refs[:4], refs[4:]
    move = Mover(sems)
    got = [move.copy(a, b) for a, b in ((x_hbm.at[row], x), (o_hbm, o), (wo_hbm, wo))]
    ffn = FeedForward(move, wf_hbm, wd_hbm, wf, wd)
    ffn.load()
    got_wc = [move.copy(wc_hbm, wc)]
    for made in got:
        made.wait()
    blocks = [slice(at, at + BLOCK) for at in range(0, x.shape[0], BLOCK)]
    for b in blocks:
        e1_v[b] = x[b].astype(F32) + mm(o[b], wo[...])
        move.store(e1_v.at[b], outs[0].at[b])
    for b in blocks:
        e1 = e1_v[b]
        e2 = ffn_up(norm(e1, g2[...]), ffn, e1, u_v.at[b], None)
        e2_v[b] = e2
        while got_wc:
            got_wc.pop().wait()
        sent_v[b] = mm(norm(e2, g1[...]), wc[...]).astype(BF)
        for src, dst in ((u_v, outs[1]), (e2_v, outs[2]), (sent_v, outs[3])):
            move.store(src.at[b], dst.at[b])
    move.drain()


HBM = pl.BlockSpec(memory_space=pl.ANY)
VMEM = pl.BlockSpec(memory_space=pltpu.VMEM)


def moved_call(kernel, ins, specs, outs, held, copies):
    return list(
        pl.pallas_call(
            kernel,
            in_specs=specs,
            out_specs=[HBM] * len(outs),
            out_shape=[jax.ShapeDtypeStruct(s, t) for s, t in outs],
            scratch_shapes=[pltpu.VMEM(s, t) for s, t in outs + held]
            + [pltpu.SemaphoreType.DMA((copies,))],
            compiler_params=params(),
        )(*ins)
    )


def enc_attend(row, x_in, qx, kx, g0, wa):
    tokens, dim = x_in.shape[1:]
    width = wa.shape[1] // 3
    kept = [
        ((tokens, dim), BF),
        ((tokens, wa.shape[1]), BF),
        ((tokens, width), BF),
        ((HEADS // 2, 2, tokens), F32),
    ]
    held = [(x_in.shape[1:], BF), (qx.shape[1:], BF), (kx.shape[1:], BF), (wa.shape, BF)]
    return moved_call(
        functools.partial(enc_attend_kernel, row),
        (x_in, qx, kx, g0, wa),
        [HBM] * 3 + [VMEM] + [HBM],
        kept,
        held,
        10,
    )


def enc_rest(row, x_in, o, g1, g2, wo, wf, wd, wc):
    tokens, dim = x_in.shape[1:]
    kept = [
        ((tokens, dim), F32),
        ((tokens, wf.shape[1]), BF),
        ((tokens, dim), F32),
        ((tokens, wc.shape[1]), BF),
    ]
    held = [(x_in.shape[1:], BF), (o.shape, BF)] + [(w.shape, BF) for w in (wo, wf, wd, wc)]
    return moved_call(
        functools.partial(enc_rest_kernel, row),
        (x_in, o, g1, g2, wo, wf, wd, wc),
        [HBM] * 2 + [VMEM] * 2 + [HBM] * 4,
        kept,
        held,
        4 + 3 * (wd.shape[0] // SLICE) + 4 * (tokens // BLOCK),
    )


def nothing_kernel(*refs):
    pass


def unwritten(shapes):
    return pl.pallas_call(
        nothing_kernel,
        out_specs=[pl.BlockSpec(memory_space=pl.ANY)] * len(shapes),
        out_shape=[jax.ShapeDtypeStruct(s.shape, s.dtype) for s in shapes],
    )()


def by_section(on_decoder, encoder, decoder):
    enc_shapes = jax.eval_shape(encoder) if encoder else []
    dec_shapes = jax.eval_shape(decoder) if decoder else []
    none = lambda: []
    encoder, decoder = encoder or none, decoder or none
    pool = lambda shapes: list(unwritten(shapes)) if shapes else []
    both = lax.cond(
        on_decoder,
        lambda: pool(enc_shapes) + list(decoder()),
        lambda: list(encoder()) + pool(dec_shapes),
    )
    return both[: len(enc_shapes)], both[len(enc_shapes) :]


def mask_kernel(*refs):
    for lengths_ref, (member_ref, other_ref) in ((refs[0], refs[2:4]), (refs[1], refs[4:6])):
        rows, span, lanes = member_ref.shape
        position = lax.broadcasted_iota(jnp.int32, (span, lanes), 0)
        lane = lax.rem(lax.broadcasted_iota(jnp.int32, (span, lanes), 1), HEAD)
        docs = lengths_ref.shape[1]
        for r in range(rows):
            seg, end = jnp.zeros((span, lanes), jnp.int32), jnp.int32(0)
            for j in range(docs):
                end = end + lengths_ref[r, j]
                seg = seg + jnp.where(position >= end, 1, 0)
            hit = lane == seg
            member_ref[r] = jnp.where(hit, 1.0, 0.0).astype(BF)
            other_ref[r] = jnp.where(hit | (lane >= docs), 0.0, NEGATIVE).astype(BF)


def mask_operands(enc_lengths, dec_lengths, spans):
    smem = pl.BlockSpec(memory_space=pltpu.SMEM)
    vmem = pl.BlockSpec(memory_space=pltpu.VMEM)
    return pl.pallas_call(
        mask_kernel,
        in_specs=[smem] * 2,
        out_specs=[vmem] * 4,
        out_shape=[
            jax.ShapeDtypeStruct((enc_lengths.shape[0], span, PAIR), BF)
            for span in spans
            for _ in range(2)
        ],
        compiler_params=params(),
    )(enc_lengths, dec_lengths)


def shift(x, by):
    pairs = [(0, 1)] if by > 0 else [(1, 0)]
    return lax.ppermute(x, "section", pairs)


def body(
    section_input, enc_lengths, dec_lengths, attn_in, attn_out, ffn_in, ffn_out, cross_weight, gains
):
    wa, wo, wf, wd, wc = attn_in[0], attn_out[0], ffn_in[0], ffn_out[0], cross_weight[0]
    g0, g1, g2 = gains[0, 0:1], gains[0, 1:2], gains[0, 2:3]
    x_in = section_input[0]
    rows, le, dim = x_in.shape
    ld = le // 2
    width = wo.shape[0]
    enc_qx, enc_kx, dec_qx, dec_kx = mask_operands(enc_lengths, dec_lengths, (le, ld))
    on_decoder = lax.axis_index("section") == 1
    steps_e, steps_d = le // BLOCK, ld // BLOCK
    columns = width // PAIR
    own = (0, columns, 2 * columns)
    across = (0, 0, columns)
    inner = wf.shape[1]

    def project(r, steps):
        return list(
            block_call(project_kernel, steps, [(x_in, r, 0)], [g0, wa], [(dim, BF), (3 * width, BF)])
        )

    def dec_first(r):
        n, packed = project(r, steps_d)
        o, lse = attention_forward(packed, None, dec_qx, dec_kx, r, (0, width, 2 * width), True)
        d1, c, cq = block_call(
            dec_query_kernel,
            steps_d,
            [(o, None, 0), (x_in, r, 0)],
            [g1, wo, wc],
            [(dim, F32), (dim, BF), (width, BF)],
        )
        return [n, packed, o, lse, d1, c, cq]

    def cross(r, cq, sent):
        return list(attention_forward(cq, sent, dec_qx, enc_kx, r, (0, 0, width), False))

    feeds = 3 * (wd.shape[0] // SLICE)

    def dec_ffn(r, oc, d1):
        row = lambda columns, kind: ((ld, columns), kind)
        return moved_call(
            functools.partial(dec_ffn_kernel, r),
            (x_in, oc, d1, g2, wc, wf, wd),
            [HBM] * 3 + [VMEM] + [HBM] * 3,
            [row(width, BF), row(dim, F32), row(dim, F32), row(dim, BF), row(wd.shape[0], BF)]
            + [row(inner, BF), row(dim, BF), ((1, dim), F32), row(dim, BF)],
            [row(width, BF), row(dim, F32), row(inner, BF), ((dim, width), BF)]
            + [(wf.shape, BF), (wd.shape, BF)],
            feeds + 4 + 9,
        )

    def cross_back(r, cq, sent, oc, doc, lse):
        return list(
            attention_backward(cq, sent, sent, dec_qx, enc_kx, r, across, oc, doc, lse, False)
        )

    def enc_back(dk, dv, e1, e2, u, blocks):
        row = lambda columns, kind: ((len(blocks) * BLOCK, columns), kind)
        return moved_call(
            functools.partial(enc_back_kernel, blocks),
            (dk, dv, e1, e2, u, g1, g2, wc, wd, wf, wo),
            [HBM] * 5 + [VMEM] * 2 + [HBM] * 4,
            [row(dim, BF)] * 3
            + [row(wd.shape[0], BF), row(inner, BF), row(dim, F32), row(dim, BF), row(width, BF)]
            + [((1, dim), F32)] * 2,
            [row(width, BF)] * 2
            + [row(dim, F32)] * 2
            + [row(inner, BF)]
            + [(w.shape, BF) for w in (wc, wd, wf, wo)],
            feeds + 2 + 5 * len(blocks) + 8 * len(blocks) + 2,
        )

    def self_back(r, steps, masks, causal, packed, o, lse, do, grad):
        dq, dk, dv = attention_backward(
            packed, packed, packed, *masks, r, own, o, do, lse, causal
        )
        dx, dg0 = block_call(
            input_grad_kernel,
            steps,
            [(dq, None, 0), (dk, None, 0), (dv, None, 0), (x_in, r, 0), (grad, None, 0)],
            [g0, wa],
            [(dim, F32)],
            1,
        )
        return [dq, dk, dv, dx, dg0]

    def dec_back(dcq, d1, dd2):
        return list(
            block_call(
                dec_back_kernel,
                steps_d,
                [(dcq, None, 0), (d1, None, 0), (dd2, None, 0)],
                [g1, wc, wo],
                [(dim, F32), (dim, BF), (width, BF)],
                1,
            )
        )

    every = range(rows)
    plain = lax.axis_size("rows") != PEERS
    state = []

    def run(encoder, decoder, *ready):
        held = on_decoder
        if state:
            held, state[0][1], *_ = lax.optimization_barrier((on_decoder, state[0][1]) + ready)
        out = by_section(held, encoder, decoder)
        state[:] = [out[0] or out[1]]
        return out

    def slots():
        return [None] * rows

    first, rest, dfirst, cqs, crossed, ocs = slots(), slots(), slots(), slots(), slots(), slots()
    mids, docs_in, cross_b, dcqs, back, last, dlast = (slots() for _ in range(7))

    def begin_cross(r, beside=None):
        crossed[r], out = run(lambda: cross(r, cqs[r], rest[r][3]), beside)
        ocs[r] = shift(crossed[r][0], 1)
        return out

    def dec_mid(r):
        return lambda: dec_ffn(r, ocs[r], dfirst[r][4])

    def keep_mid(r, out):
        mids[r] = out
        docs_in[r] = shift(out[0], -1)

    def dec_last(r):
        p = dec_back(dcqs[r], dfirst[r][4], mids[r][2])
        n, packed, o, lse = dfirst[r][:4]
        return p + self_back(r, steps_d, (dec_qx, dec_kx), True, packed, o, lse, p[2], p[0])

    def enc_last(r):
        return self_back(
            r, steps_e, (enc_qx, enc_kx), False, *first[r][1:4],
            jnp.concatenate(backs(r, 7), 0), jnp.concatenate(backs(r, 5), 0),
        )

    def enc_first(r):
        return lambda: enc_attend(r, x_in, enc_qx, enc_kx, g0, wa)

    def enc_then(r):
        return lambda: enc_rest(r, x_in, first[r][2], g1, g2, wo, wf, wd, wc)

    first[0], dfirst[0] = run(enc_first(0), lambda: dec_first(0))
    cqs[0] = shift(dfirst[0][6], -1)
    rest[0], more = run(enc_then(0), lambda: [v for r in every[1:] for v in dec_first(r)])
    begin_cross(0)
    for r in every[1:]:
        dfirst[r] = more[7 * (r - 1) : 7 * r]
        cqs[r] = shift(dfirst[r][6], -1)
    for r in every[1:]:
        first[r], _ = run(enc_first(r), None)
        rest[r], out = run(enc_then(r), dec_mid(r - 1), ocs[r - 1])
        keep_mid(r - 1, out)
        begin_cross(r)
    def backs(r, i):
        return [part[i] for part in back[r]]

    def enc_backs(r, blocks):
        return lambda: enc_back(
            cross_b[r][1], cross_b[r][2], rest[r][0], rest[r][2], rest[r][1], blocks
        )

    for r in every:
        cross_b[r], _ = run(
            lambda: cross_back(r, cqs[r], rest[r][3], crossed[r][0], docs_in[r], crossed[r][1]),
            None,
        )
        if r == 0 and steps_e > 1:
            part, out = run(enc_backs(0, (0,)), dec_mid(rows - 1))
            keep_mid(rows - 1, out)
            dcqs[0] = shift(cross_b[0][0], 1)
            others, _ = run(enc_backs(0, tuple(range(1, steps_e))), None)
            back[0] = [part, others]
        else:
            dcqs[r] = shift(cross_b[r][0], 1)
            out = run(enc_backs(r, tuple(range(steps_e))), dec_mid(rows - 1) if r == 0 else None)
            back[r] = [out[0]]
            if r == 0:
                keep_mid(rows - 1, out[1])
        last[r], dlast[r] = run((lambda: enc_last(r)) if plain else None, lambda: dec_last(r))

    def over_rows(lists):
        pieces = lambda v: v if isinstance(v, list) else [v]
        return [[p for v in group for p in pieces(v)] for group in zip(*lists)]

    enc_side = (
        over_rows(
            [backs(r, 2), backs(r, 3), backs(r, 0), backs(r, 0), first[r][2], first[r][0]]
            for r in every
        ),
        over_rows(
            [backs(r, 4), backs(r, 1), cross_b[r][1], cross_b[r][2], backs(r, 6)] + last[r][0:3]
            for r in every
        ),
    )
    dec_side = (
        over_rows(
            [mids[r][3], mids[r][4], dfirst[r][5], mids[r][6], dfirst[r][2], dfirst[r][0]]
            for r in every
        ),
        over_rows(
            [mids[r][5], mids[r][8], dcqs[r], ocs[r], dlast[r][1]] + dlast[r][4:7] for r in every
        ),
    )
    if not plain:
        kept = over_rows(
            [first[r][1], first[r][2], backs(r, 7), first[r][3], backs(r, 5)] for r in every
        )
        decoded = over_rows([mids[r][1], dlast[r][7]] for r in every)
        gain_rows = (
            over_rows([backs(r, 8), backs(r, 9)] for r in every),
            over_rows([dlast[r][8], dlast[r][3], mids[r][7]] for r in every),
        )
        s_in, s_out, s_fi, s_cross, s_gain, s_fo, results = grad_sum(
            (enc_side, dec_side), kept, decoded, gain_rows, (x_in, enc_qx, enc_kx, wa, g0)
        )
        o_gain, *outs = hand_over(
            s_gain, gains.shape[1], [results, s_in, s_out, s_fi, s_fo, s_cross]
        )
        return tuple(outs) + (o_gain,)

    def enc_parts():
        gain_rows = [sum(v) for v in zip(*[[last[r][4], sum(backs(r, 8)), sum(backs(r, 9))] for r in every])]
        return [jnp.concatenate(gain_rows, 0), jnp.stack([last[r][3] for r in every])]

    def dec_parts():
        gain_rows = [sum(v) for v in zip(*[[dlast[r][8], dlast[r][3], mids[r][7]] for r in every])]
        both = [jnp.concatenate([mids[r][1], dlast[r][7]], 0) for r in every]
        return [jnp.concatenate(gain_rows, 0), jnp.stack(both)]

    gain_grads, results = lax.cond(on_decoder, dec_parts, enc_parts)
    gain_terms = jnp.pad(gain_grads.T, ((0, 0), (0, LANES - gain_grads.shape[0]))).astype(BF)

    s_in, s_out, s_fi, s_cross, s_gain, s_fo = plain_sum(on_decoder, (enc_side, dec_side), gain_terms)
    return (
        results[None],
        s_in[None],
        s_out[None],
        s_fi[None],
        s_fo[None],
        s_cross[None],
        s_gain[:, : gain_grads.shape[0]].T[None],
    )


def solution(mesh):
    placed = (
        P("section", "rows", None, None),
        P("rows", None),
        P("rows", None),
    ) + (P("section", None, None),) * 6
    return jax.shard_map(
        body,
        mesh=mesh,
        in_specs=placed,
        out_specs=(
            P("section", "rows", None, None),
            P("section", "rows", None),
            P("section", "rows", None),
            P("section", "rows", None),
            P("section", "rows", None),
            P("section", "rows", None),
            P("section", None, "rows"),
        ),
        check_vma=False,
    )
```

```python
import functools

import jax
import jax.numpy as jnp
from jax import lax
from jax.experimental import pallas as pl
from jax.experimental.pallas import tpu as pltpu
from jax.sharding import PartitionSpec as P

HEADS = 12
HEAD = 64
PAIR = 128
EPSILON = 1e-06
SCALE = 0.125
LOG2E = 1.4426950408889634
NEGATIVE = -1e30
GELU_C = 0.7978845608028654
GELU_A = 0.044715

BF = jnp.bfloat16
F32 = jnp.float32
NT = (((1,), (1,)), ((), ()))
NN = (((1,), (0,)), ((), ()))
TN = (((0,), (0,)), ((), ()))


def mm(a, b, dims=NN):
    return lax.dot_general(a, b, dims, preferred_element_type=F32)


MESH = pl.DeviceIdType.MESH
LANES = 256
VMEM_LIMIT = 56 * 1024 * 1024
SUM_VMEM = 60 * 1024 * 1024

NZ, NY, NC = 4, 2, 2
PEERS = NZ * NY * NC
C_LAG = 2
Y_LAG = C_LAG + 4
HOP = 3
ZF_EVERY, ZF_AT = 6, 3
ZF_LAG = C_LAG + HOP * (NZ - 1)
RING = 6
AHEAD = 3
PANELS = 4

TALL = 1
LEFT_ORDER = (0, 2, 3, 4, 5)
PRODUCTS = ((0, 0), (1, 1), (2, 2), (3, 3), (4, 4), (5, 5), (5, 6), (5, 7))


def grad_sum_kernel(rows, group_sizes, token_counts, chunk_counts, unit_steps, *refs):
    remaining = list(refs)
    sizes = list(group_sizes)

    def take(groups):
        return [[remaining.pop(0) for _ in range(sizes.pop(0))] for _ in range(groups)]

    def take_one():
        return remaining.pop(0)

    lefts_of, rights_of = [], []
    for side in range(2):
        lefts_of.append(take(6))
        rights_of.append(take(5 if side == 0 else 8))
    packed_of, o_of, do_of, lse_of, de1_of = take(5)
    out_of, dx_of = take(2)
    gain_rows = [[None] + take(2), take(3)]
    x_ref, qx_ref, kx_ref, wa_ref, g0_ref = [take_one() for _ in range(5)]
    o_in, o_out, o_fi, o_cross, o_gain, o_fo, o_results = [take_one() for _ in range(7)]
    (
        xt, xt_tall, left_stage, tall_stage, tall_right, panels, ring,
        own, got_y, got_r, got_l, z_right, z_left,
        s_left, s_tall, s_right, s_panel,
        s_core, r_core, s_y, r_y, s_r, r_r, s_l, r_l,
        d_packed, wa, att, qx, kx, lse, x_stage, grad_stage, dx_stage, dg0,
        s_att, s_const, s_lse, s_block, s_out, s_dec,
    ) = remaining
    chunks, height, dim = own.shape[0], own.shape[3], xt.shape[0]
    sec, me = lax.axis_index("section"), lax.axis_index("rows")
    core, y, z = lax.rem(me, 2), lax.rem(me // 2, 2), me // 4
    by_core, by_y = me + 1 - 2 * core, me + 2 - 4 * y
    other, away = 1 - core, 1 - y
    bases = [sum(chunk_counts[:i]) for i in range(len(chunk_counts))]


    def each(act):
        for side in range(2):

            @pl.when(sec == side)
            def _(side=side):
                act(side)

    def row_copies(sources, columns, dst, sems, side):
        del side
        copies, at = [], 0
        for i, src in enumerate(sources):
            copies.append(
                pltpu.make_async_copy(
                    src if columns is None else src.at[:, columns],
                    dst.at[at : at + src.shape[0]],
                    sems.at[i],
                )
            )
            at += src.shape[0]
        return copies

    def start_all(copies):
        for copy in copies:
            copy.start()

    def wait_all(copies):
        for copy in copies:
            copy.wait()

    def left_copies(q, side):
        source = lefts_of[side][LEFT_ORDER[q]]
        return row_copies(source, None, left_stage.at[q % 2], s_left.at[q % 2], side)

    def tall_copies(side):
        return row_copies(lefts_of[side][1], None, tall_stage, s_tall, side)

    def tall_right_copies(side):
        return row_copies(rights_of[side][1], None, tall_right, s_right, side)

    def panel_copies(p, i, slot, side):
        if PRODUCTS[p][1] >= len(rights_of[side]):
            return []
        columns = pl.ds(pl.multiple_of(i * LANES, LANES), LANES)
        return row_copies(
            rights_of[side][PRODUCTS[p][1]], columns, panels.at[slot], s_panel.at[slot], side
        )

    def for_panel(t, act):
        slot = lax.rem(t, PANELS)
        for p in range(len(PRODUCTS)):
            if p != TALL:

                @pl.when((t >= bases[p]) & (t < bases[p] + chunk_counts[p]))
                def _(p=p):
                    each(lambda side: act(p, t - bases[p], slot, side))

    def flip(side, stage, columns, put):
        for at in range(0, rows * token_counts[side], LANES):
            tokens = slice(at, at + LANES)
            put(tokens, stage[tokens, columns].astype(F32).T.astype(BF))

    def build_left(q):
        def act(side):
            wait_all(left_copies(q, side))
            for at in range(0, xt.shape[0], LANES):

                def put(tokens, block, at=at):
                    xt[at : at + LANES, tokens] = block

                flip(side, left_stage.at[q % 2], slice(at, at + LANES), put)
            if q + 2 < len(LEFT_ORDER):
                start_all(left_copies(q + 2, side))

        each(act)

    groups = xt_tall.shape[0] // LANES
    tall_rows = xt_tall.shape[0] // PEERS

    def build_tall(part):
        columns = pl.ds(pl.multiple_of(part * LANES, LANES), LANES)
        targets = LANES // tall_rows

        def act(side):
            def put(tokens, block):
                for k in range(targets):
                    for j in range(tall_rows // 16):
                        to = j * LANES + (part * targets + k) * 16
                        xt_tall[pl.ds(pl.multiple_of(to, 16), 16), tokens] = block[
                            k * tall_rows + j * 16 : k * tall_rows + (j + 1) * 16
                        ]

            flip(side, tall_stage, columns, put)

        each(act)

    def send_core(j):
        slot = lax.rem(j, RING)
        return pltpu.make_async_remote_copy(
            src_ref=ring.at[slot, :, :, other],
            dst_ref=own.at[j],
            send_sem=s_core.at[j],
            recv_sem=r_core.at[j],
            device_id=(sec, by_core),
            device_id_type=MESH,
        )

    def send_y(j):
        return pltpu.make_async_remote_copy(
            src_ref=own.at[j, :, away],
            dst_ref=got_y.at[j],
            send_sem=s_y.at[j],
            recv_sem=r_y.at[j],
            device_id=(sec, by_y),
            device_id_type=MESH,
        )

    def send_right(j, at):
        return pltpu.make_async_remote_copy(
            src_ref=own.at[j, pl.ds(at + 1, NZ - 1 - at), y],
            dst_ref=got_r.at[j, pl.ds(at, NZ - 1 - at)],
            send_sem=s_r.at[j],
            recv_sem=r_r.at[j],
            device_id=(sec, me + 4),
            device_id_type=MESH,
        )

    def send_left(j, at):
        return pltpu.make_async_remote_copy(
            src_ref=own.at[j, pl.ds(0, at), y],
            dst_ref=got_l.at[j, pl.ds(0, at)],
            send_sem=s_l.at[j],
            recv_sem=r_l.at[j],
            device_id=(sec, me - 4),
            device_id_type=MESH,
        )

    def z_first(j):
        return lax.rem(j, ZF_EVERY) == ZF_AT

    def send_along(j, at, right):
        targets = pl.ds(at + 1, NZ - 1 - at) if right else pl.ds(0, at)
        buffer = z_right if right else z_left
        return pltpu.make_async_remote_copy(
            src_ref=own.at[j, targets],
            dst_ref=buffer.at[j // ZF_EVERY, pl.ds(at, NZ - 1 - at) if right else targets],
            send_sem=(s_r if right else s_l).at[j],
            recv_sem=(r_r if right else r_l).at[j],
            device_id=(sec, me + 4 if right else me - 4),
            device_id_type=MESH,
        )

    def send_y_last(j):
        return pltpu.make_async_remote_copy(
            src_ref=own.at[j, z, away],
            dst_ref=got_y.at[j, z],
            send_sem=s_y.at[j],
            recv_sem=r_y.at[j],
            device_id=(sec, by_y),
            device_id_type=MESH,
        )

    def forward_along(j, at, right):
        source = at - 1 if right else at + 1
        if 0 <= source < NZ:
            send_along(j, source, right).wait_recv()
            buffer = z_right if right else z_left
            for t in range(at + 1, NZ) if right else range(at):
                for b in range(NY):
                    add_into(own.at[j, t, b], buffer.at[j // ZF_EVERY, t - 1 if right else t, b])
        send_along(j, at, right).start()

    def turn_to_y(j):
        for at in range(NZ):

            @pl.when(z == at)
            def _(at=at):
                if at == NZ - 1:
                    send_along(j, at - 1, True).wait_recv()
                if at == 0:
                    send_along(j, at + 1, False).wait_recv()
                for b in range(NY):
                    if at > 0:
                        add_into(own.at[j, at, b], z_right.at[j // ZF_EVERY, at - 1, b])
                    if at < NZ - 1:
                        add_into(own.at[j, at, b], z_left.at[j // ZF_EVERY, at, b])

        send_y_last(j).start()

    def add_into(dst, src):
        dst[...] = (dst[...].astype(F32) + src[...].astype(F32)).astype(BF)


    def compute(s):
        slot = lax.rem(s, RING)

        def put_panel(value):
            for t in range(PEERS):
                ring[slot, t // 4, t // 2 % 2, t % 2] = value[t * height : (t + 1) * height]

        for p in range(len(PRODUCTS)):
            left = PRODUCTS[p][0]

            @pl.when((s >= bases[p]) & (s < bases[p] + chunk_counts[p]))
            def _(p=p, left=left):
                if p != TALL:
                    if p == 0 or PRODUCTS[p - 1][0] != left:

                        @pl.when(s == bases[p])
                        def _():
                            build_left(LEFT_ORDER.index(left))

                    where = lax.rem(s, PANELS)

                    def act(side):
                        wait_all(panel_copies(p, s - bases[p], where, side))
                        tokens = rows * token_counts[side]
                        if PRODUCTS[p][1] < len(rights_of[side]):
                            right = panels[where, :tokens, :]
                        else:
                            first = (PRODUCTS[p][1] - 5) * dim + (s - bases[p]) * LANES
                            right = d_packed[:, pl.ds(pl.multiple_of(first, LANES), LANES)]
                        put_panel(mm(xt[:, :tokens], right).astype(BF))

                    each(act)
                else:
                    rows_at = pl.ds(pl.multiple_of((s - bases[p]) * LANES, LANES), LANES)

                    @pl.when(s == bases[p])
                    def _():
                        each(lambda side: wait_all(tall_right_copies(side)))

                    def act(side):
                        tokens = rows * token_counts[side]
                        for k in range(tall_right.shape[1] // LANES):
                            value = mm(
                                xt_tall[rows_at, :tokens],
                                tall_right[:tokens, k * LANES : (k + 1) * LANES],
                            ).astype(BF)
                            for t in range(PEERS):
                                ring[slot, t // 4, t // 2 % 2, t % 2, k * 16 : (k + 1) * 16] = value[
                                    t * 16 : (t + 1) * 16
                                ]

                    each(act)

        @pl.when(s == chunks - 1)
        def _():
            def act(side):
                parts = []
                for group in gain_rows[side]:
                    total_row = dg0[...]
                    if group is not None:
                        total_row = group[0][...]
                        for ref in group[1:]:
                            total_row = total_row + ref[...]
                    parts.append(total_row)
                parts.append(jnp.zeros((LANES - len(parts), dim), F32))
                put_panel(jnp.concatenate(parts, axis=0).T.astype(BF))

            each(act)


    attn_units, block_units, first_block = unit_steps
    tokens_e = token_counts[0]
    per_row = tokens_e // BLOCK
    const_copies = [
        pltpu.make_async_copy(src, dst, s_const.at[i])
        for i, (src, dst) in enumerate(((qx_ref, qx), (kx_ref, kx), (wa_ref, wa)))
    ]
    lse_copies = [
        pltpu.make_async_copy(ref, lse.at[r], s_lse.at[r]) for r, ref in enumerate(lse_of)
    ]

    def row_pieces(refs_of, r):
        found, at = [], 0
        for ref in refs_of:
            if r * tokens_e <= at < (r + 1) * tokens_e:
                found.append((ref, at - r * tokens_e))
            at += ref.shape[0]
        return found

    def attn_loads(u, act):
        slot, p = lax.rem(u, 2), lax.rem(u, HEADS // 2)
        for r in range(rows):

            @pl.when(u // (HEADS // 2) == r)
            def _(r=r):
                at = lambda first: pl.ds(pl.multiple_of(first + p * PAIR, PAIR), PAIR)
                sources = [packed_of[r].at[:, at(k * dim)] for k in range(3)]
                sources.append(o_of[r].at[:, at(0)])
                copies = [
                    pltpu.make_async_copy(src, att.at[slot, k], s_att.at[slot, k])
                    for k, src in enumerate(sources)
                ]
                for ref, begin in row_pieces(do_of, r):
                    copies.append(
                        pltpu.make_async_copy(
                            ref.at[:, at(0)],
                            att.at[slot, 4, begin : begin + ref.shape[0]],
                            s_att.at[slot, len(copies)],
                        )
                    )
                act(copies)

    def attn_unit(u):
        slot, p, r = lax.rem(u, 2), lax.rem(u, HEADS // 2), u // (HEADS // 2)
        attn_loads(u, wait_all)
        q, k, v, o, do = [att[slot, i] for i in range(5)]
        grads = pair_backward(q, k, v, qx[r], kx[r], o, do, lse[r, p], False)
        where = pl.ds(pl.multiple_of(r * tokens_e, tokens_e), tokens_e)
        for i, value in enumerate(grads):
            at = pl.ds(pl.multiple_of(i * dim + p * PAIR, PAIR), PAIR)
            d_packed[where, at] = value.astype(BF)

    def block_loads(v, act):
        slot = lax.rem(v, 2)
        where = pl.ds(pl.multiple_of(lax.rem(v, per_row) * BLOCK, BLOCK), BLOCK)
        for r in range(rows):

            @pl.when(v // per_row == r)
            def _(r=r):
                act([pltpu.make_async_copy(x_ref.at[r, where], x_stage.at[slot], s_block.at[slot, 0])])

            for ref, begin in row_pieces(de1_of, r):
                for at in range(0, ref.shape[0], BLOCK):

                    @pl.when(v == (r * tokens_e + begin + at) // BLOCK)
                    def _(ref=ref, at=at):
                        act(
                            [
                                pltpu.make_async_copy(
                                    ref.at[at : at + BLOCK], grad_stage.at[slot], s_block.at[slot, 1]
                                )
                            ]
                        )

    def block_store(v):
        slot = lax.rem(v, 2)
        where = pl.ds(pl.multiple_of(lax.rem(v, per_row) * BLOCK, BLOCK), BLOCK)
        return pltpu.make_async_copy(
            dx_stage.at[slot], o_results.at[v // per_row, where], s_out.at[slot]
        )

    def block_unit(v):
        slot = lax.rem(v, 2)
        block_loads(v, wait_all)

        @pl.when(v == 0)
        def _():
            const_copies[2].wait()
            dg0[...] = jnp.zeros_like(dg0)

        @pl.when(v >= 2)
        def _():
            block_store(v - 2).wait()

        where = pl.ds(pl.multiple_of(v * BLOCK, BLOCK), BLOCK)
        dn = None
        for i in range(3):
            part = mm(d_packed[where, i * dim : (i + 1) * dim], wa[:, i * dim : (i + 1) * dim], NT)
            dn = part if dn is None else dn + part
        back, gain_part = norm_back(x_stage[slot].astype(F32), g0_ref[...], dn)
        dg0[...] += gain_part
        dx_stage[slot] = grad_stage[slot] + back
        block_store(v).start()

    def dec_results(store):
        half = token_counts[1]
        parts = [
            (ref, stage.at[r], o_results.at[r, k * half : (k + 1) * half], s_dec.at[k, r])
            for k, (group, stage) in enumerate(((out_of, grad_stage), (dx_of, dx_stage)))
            for r, ref in enumerate(group)
        ]
        return [
            pltpu.make_async_copy(held, dst, sem) if store else pltpu.make_async_copy(src, held, sem)
            for src, held, dst, sem in parts
        ]

    def side_work(s):
        @pl.when(s == 0)
        def _():
            start_all(lse_copies)
            start_all(const_copies)
            for v in range(2):
                block_loads(jnp.int32(v), start_all)

        u = s // 2

        @pl.when((lax.rem(s, 2) == 0) & (u < attn_units))
        def _():
            attn_loads(u, start_all)

        @pl.when((lax.rem(s, 2) == 0) & (u >= 1) & (u <= attn_units))
        def _():
            @pl.when(u == 1)
            def _():
                wait_all(lse_copies)
                wait_all(const_copies[:2])

            attn_unit(u - 1)

        v = (s - first_block) // 2

        @pl.when((lax.rem(s, 2) == 0) & (s >= first_block) & (v < block_units))
        def _():
            block_unit(v)

            @pl.when(v + 2 < block_units)
            def _():
                block_loads(v + 2, start_all)


    def open_first(side):
        start_all(left_copies(0, side))
        for t in range(AHEAD):
            start_all(panel_copies(0, t, t % PANELS, side))

    each(open_first)

    barrier = pltpu.get_barrier_semaphore()

    def greet(peer):
        pl.semaphore_signal(barrier, inc=1, device_id=(sec, peer), device_id_type=MESH)

    greet(by_core)
    greet(by_y)

    @pl.when(z > 0)
    def _():
        greet(me - 4)

    @pl.when(z < NZ - 1)
    def _():
        greet(me + 4)

    @pl.when((z > 0) & (z < NZ - 1))
    def _():
        pl.semaphore_wait(barrier, 4)

    @pl.when((z == 0) | (z == NZ - 1))
    def _():
        pl.semaphore_wait(barrier, 3)


    @pl.when(sec == 1)
    def _():
        start_all(dec_results(False))

    def step(s, carry):
        @pl.when(s + AHEAD < chunks - 1)
        def _():
            for_panel(
                s + AHEAD,
                lambda p, i, slot, side: start_all(panel_copies(p, i, slot, side)),
            )

        @pl.when((s >= RING) & (s < chunks))
        def _():
            send_core(s - RING).wait_send()

        @pl.when(s < chunks)
        def _():
            compute(s)
            send_core(s).start()

        @pl.when(sec == 0)
        def _():
            side_work(s)

        @pl.when((sec == 1) & (s == RING))
        def _():
            wait_all(dec_results(False))
            start_all(dec_results(True))

        @pl.when(s == 1)
        def _():
            each(lambda side: start_all(tall_copies(side)))

        @pl.when(s == 4)
        def _():
            each(lambda side: wait_all(tall_copies(side)))
            each(lambda side: start_all(left_copies(1, side)))
            each(lambda side: start_all(tall_right_copies(side)))

        @pl.when((s >= 4) & (s < 4 + groups))
        def _():
            build_tall(s - 4)

        j_c = s - C_LAG

        @pl.when((j_c >= 0) & (j_c < chunks))
        def _():
            send_core(j_c).wait_recv()
            slot = lax.rem(j_c, RING)
            for a in range(NZ):
                for b in range(NY):
                    add_into(own.at[j_c, a, b], ring.at[slot, a, b, core])

            @pl.when(jnp.logical_not(z_first(j_c)))
            def _():
                send_y(j_c).start()

        j_y = s - Y_LAG

        @pl.when((j_y >= 0) & (j_y < chunks) & jnp.logical_not(z_first(j_y)))
        def _():
            send_y(j_y).wait_recv()
            for t in range(NZ):
                add_into(own.at[j_y, t, y], got_y.at[j_y, t])

        for at in range(NZ - 1):
            j_r = s - Y_LAG - HOP * at

            @pl.when((z == at) & (j_r >= 0) & (j_r < chunks) & jnp.logical_not(z_first(j_r)))
            def _(at=at, j_r=j_r):
                if at > 0:
                    send_right(j_r, at - 1).wait_recv()
                    for t in range(at + 1, NZ):
                        add_into(own.at[j_r, t, y], got_r.at[j_r, t - 1])
                send_right(j_r, at).start()

        for at in range(1, NZ):
            j_l = s - Y_LAG - HOP * (NZ - 1 - at)

            @pl.when((z == at) & (j_l >= 0) & (j_l < chunks) & jnp.logical_not(z_first(j_l)))
            def _(at=at, j_l=j_l):
                if at < NZ - 1:
                    send_left(j_l, at + 1).wait_recv()
                    for t in range(at):
                        add_into(own.at[j_l, t, y], got_l.at[j_l, t])
                send_left(j_l, at).start()

        for at in range(NZ):
            for right, hop in ((True, at), (False, NZ - 1 - at)):
                if hop < NZ - 1:
                    j_z = s - C_LAG - HOP * hop

                    @pl.when((z == at) & (j_z >= 0) & (j_z < chunks) & z_first(j_z))
                    def _(at=at, j_z=j_z, right=right):
                        forward_along(j_z, at, right)

        j_t = s - ZF_LAG

        @pl.when((j_t >= 0) & (j_t < chunks) & z_first(j_t))
        def _():
            turn_to_y(j_t)

        return carry

    lax.fori_loop(0, chunks + Y_LAG + HOP * (NZ - 1), step, 0)


    def finish(j):
        @pl.when(j >= chunks - RING)
        def _():
            send_core(j).wait_send()

        @pl.when(z_first(j))
        def _():
            send_y_last(j).wait()
            for at in range(NZ):

                @pl.when(z == at)
                def _(at=at):
                    if at < NZ - 1:
                        send_along(j, at, True).wait_send()
                    if at > 0:
                        send_along(j, at, False).wait_send()

        @pl.when(jnp.logical_not(z_first(j)))
        def _():
            finish_y_first(j)

    def finish_y_first(j):
        @pl.when(z == NZ - 1)
        def _():
            send_right(j, NZ - 2).wait_recv()

        @pl.when(z == 0)
        def _():
            send_left(j, 1).wait_recv()

        send_y(j).wait_send()
        for at in range(NZ):

            @pl.when(z == at)
            def _(at=at):
                if at < NZ - 1:
                    send_right(j, at).wait_send()
                if at > 0:
                    send_left(j, at).wait_send()

    def total(j, part):
        mine = own[j, z, y, part].astype(F32)
        right = got_r[j, jnp.maximum(z - 1, 0), part].astype(F32)
        left = got_l[j, jnp.minimum(z, NZ - 2), part].astype(F32)
        across = got_y[j, z, part].astype(F32)
        along = jnp.where(z > 0, right, 0.0) + jnp.where(z < NZ - 1, left, 0.0)
        return mine + jnp.where(z_first(j), across, along)

    def close(out, base, count, column):
        def panel(i, carry):
            finish(base + i)
            at = pl.ds(pl.multiple_of(column + i * LANES, LANES), LANES)
            out[:, at] = total(base + i, pl.ds(0, height))
            return carry

        lax.fori_loop(0, count, panel, 0)

    close(o_fi, bases[0], chunk_counts[0], 0)

    def tall_out(i, carry):
        finish(bases[TALL] + i)
        at = pl.ds(pl.multiple_of(i * 16, 16), 16)
        for k in range(tall_right.shape[1] // LANES):
            o_fo[at, k * LANES : (k + 1) * LANES] = total(bases[TALL] + i, pl.ds(k * 16, 16))
        return carry

    lax.fori_loop(0, chunk_counts[TALL], tall_out, 0)
    close(o_cross, bases[2], chunk_counts[2], 0)
    close(o_cross, bases[3], chunk_counts[3], dim)
    close(o_out, bases[4], chunk_counts[4], 0)
    for k in range(3):
        close(o_in, bases[5 + k], chunk_counts[5 + k], k * dim)
    close(o_gain, chunks - 1, 1, 0)

    @pl.when(sec == 0)
    def _():
        for v in range(max(0, block_units - 2), block_units):
            block_store(jnp.int32(v)).wait()

    @pl.when(sec == 1)
    def _():
        wait_all(dec_results(True))


def grad_sum(sides, kept, decoded, gain_rows, shared):
    (enc_lefts, enc_rights), (dec_lefts, dec_rights) = sides
    x_in, qx, kx, wa, g0 = shared
    rows = x_in.shape[0]
    token_counts = (enc_lefts[5][0].shape[0], dec_lefts[5][0].shape[0])
    tokens = rows * max(token_counts)
    groups = enc_lefts + enc_rights + dec_lefts + dec_rights + kept + decoded
    group_sizes = tuple(len(g) for g in groups + gain_rows[0] + gain_rows[1])
    most = max(group_sizes)
    dim, tall = dec_lefts[0][0].shape[1], dec_lefts[TALL][0].shape[1]
    height = dim // PEERS
    chunk_counts = tuple(
        dec_lefts[a][0].shape[1] * dec_rights[b][0].shape[1] // (dim * LANES) for a, b in PRODUCTS
    )
    chunks = sum(chunk_counts) + 1
    attn_units, block_units = rows * HEADS // 2, rows * token_counts[0] // BLOCK
    unit_steps = (attn_units, block_units, 2 * attn_units + 2)
    flat = lambda groups: [v for group in groups for v in group]
    moved = flat(groups)
    gains = flat(gain_rows[0] + gain_rows[1])
    half = (chunks, NZ, NY, height, LANES)
    fourth = (chunks, NZ, height, LANES)
    width = lambda *which: sum(dec_rights[i][0].shape[1] for i in which)
    out_shape = [
        jax.ShapeDtypeStruct(s, F32)
        for s in (
            (height, width(5, 6, 7)),
            (height, width(4)),
            (height, width(0)),
            (height, width(2, 3)),
            (height, LANES),
            (tall // PEERS, width(1)),
            x_in.shape,
        )
    ]
    hbm, vmem = pl.BlockSpec(memory_space=pl.ANY), pl.BlockSpec(memory_space=pltpu.VMEM)
    dma = pltpu.SemaphoreType.DMA
    return pl.pallas_call(
        functools.partial(
            grad_sum_kernel, rows, group_sizes, token_counts, chunk_counts, unit_steps
        ),
        in_specs=[hbm] * len(moved) + [vmem] * len(gains) + [hbm] * 4 + [vmem],
        out_specs=[vmem] * 6 + [hbm],
        out_shape=out_shape,
        scratch_shapes=[
            pltpu.VMEM((dim, tokens), BF),
            pltpu.VMEM((tall, tokens), BF),
            pltpu.VMEM((2, tokens, dim), BF),
            pltpu.VMEM((tokens, tall), BF),
            pltpu.VMEM((tokens, width(1)), BF),
            pltpu.VMEM((PANELS, tokens, LANES), BF),
            pltpu.VMEM((RING, NZ, NY, NC, height, LANES), BF),
            pltpu.VMEM(half, BF),
            pltpu.VMEM(fourth, BF),
            pltpu.VMEM((chunks, NZ - 1) + fourth[2:], BF),
            pltpu.VMEM((chunks, NZ - 1) + fourth[2:], BF),
            pltpu.VMEM((-(-chunks // ZF_EVERY), NZ - 1) + half[2:], BF),
            pltpu.VMEM((-(-chunks // ZF_EVERY), NZ - 1) + half[2:], BF),
            dma((2, most)),
            dma((most,)),
            dma((most,)),
            dma((PANELS, most)),
        ]
        + [dma((chunks,))] * 8
        + [
            pltpu.VMEM((rows * token_counts[0], 3 * dim), BF),
            pltpu.VMEM(wa.shape, BF),
            pltpu.VMEM((2, 5, token_counts[0], PAIR), BF),
            pltpu.VMEM(qx.shape, BF),
            pltpu.VMEM(kx.shape, BF),
            pltpu.VMEM((rows,) + kept[3][0].shape, F32),
            pltpu.VMEM((2, BLOCK, dim), BF),
            pltpu.VMEM((max(2, rows), BLOCK, dim), F32),
            pltpu.VMEM((max(2, rows), BLOCK, dim), F32),
            pltpu.VMEM((1, dim), F32),
            dma((2, 4 + most)),
            dma((3,)),
            dma((rows,)),
            dma((2, 2)),
            dma((2,)),
            dma((2, rows)),
        ],
        compiler_params=pltpu.CompilerParams(
            collective_id=1, has_side_effects=True, vmem_limit_bytes=SUM_VMEM
        ),
    )(*moved, *gains, x_in, qx, kx, wa, g0)


def hand_over_kernel(rows, *refs):
    count = (len(refs) - 3) // 3
    gain_ref, sources, gain_out = refs[0], refs[1 : 1 + count], refs[1 + count]
    targets, held = refs[2 + count : 2 + 2 * count], refs[2 + 2 * count : 2 + 3 * count]
    gain, sems = refs[2 + 3 * count], refs[3 + 3 * count]
    moves = []
    for src, keep, dst in zip(sources, held, targets):
        for part in range(rows) if len(src.shape) == 3 else [slice(None)]:
            i = len(moves)
            load = pltpu.make_async_copy(src.at[part], keep.at[part], sems.at[0, i])
            load.start()
            moves.append((load, keep.at[part], dst.at[0].at[part], sems.at[1, i]))
    load_gain = pltpu.make_async_copy(gain_ref, gain, sems.at[0, len(moves)])
    load_gain.start()
    stores = []
    for load, keep, dst, sem in moves:
        load.wait()
        stores.append(pltpu.make_async_copy(keep, dst, sem))
        stores[-1].start()
    load_gain.wait()
    gain_out[0] = gain[...].T[: gain_out.shape[1]]
    for store in stores:
        store.wait()


def hand_over(gain, gain_rows, arrays):
    hbm, vmem = pl.BlockSpec(memory_space=pl.ANY), pl.BlockSpec(memory_space=pltpu.VMEM)
    rows = max(a.shape[0] for a in arrays if a.ndim == 3)
    return pl.pallas_call(
        functools.partial(hand_over_kernel, rows),
        in_specs=[hbm] * (1 + len(arrays)),
        out_specs=[vmem] + [hbm] * len(arrays),
        out_shape=[jax.ShapeDtypeStruct((1, gain_rows, gain.shape[0]), F32)]
        + [jax.ShapeDtypeStruct((1,) + a.shape, F32) for a in arrays],
        scratch_shapes=[pltpu.VMEM(a.shape, F32) for a in arrays]
        + [
            pltpu.VMEM(gain.shape, F32),
            pltpu.SemaphoreType.DMA((2, len(arrays) + rows)),
        ],
        compiler_params=pltpu.CompilerParams(vmem_limit_bytes=SUM_VMEM),
    )(gain, *arrays)


def plain_sum(on_decoder, sides, gain_terms):
    def terms(lefts, rights):
        parts = [
            mm(jnp.concatenate(lefts[i], 0), jnp.concatenate(rights[j], 0), TN).astype(BF)
            for i, j in PRODUCTS
        ]
        return [
            jnp.concatenate(parts[5:8], 1),
            parts[4],
            parts[0],
            jnp.concatenate(parts[2:4], 1),
            parts[1],
        ]

    pieces = lax.cond(on_decoder, lambda: terms(*sides[1]), lambda: terms(*sides[0]))
    pieces.insert(4, gain_terms)
    return [
        lax.psum_scatter(piece, "rows", scatter_dimension=0, tiled=True).astype(F32)
        for piece in pieces
    ]


def low_half(rows):
    return lax.broadcasted_iota(jnp.int32, (rows, PAIR), 1) < HEAD


def masked_scores(q, k, qx, kx, head, causal):
    lo_q, lo_k = low_half(q.shape[0]), low_half(k.shape[0])
    if head == 0:
        qh, kh = jnp.where(lo_q, q, qx), jnp.where(lo_k, k, kx)
    else:
        qh, kh = jnp.where(lo_q, qx, q), jnp.where(lo_k, kx, k)
    s = mm(kh, qh, NT)
    if causal:
        key_at = lax.broadcasted_iota(jnp.int32, s.shape, 0)
        query_at = lax.broadcasted_iota(jnp.int32, s.shape, 1)
        s = jnp.where(key_at <= query_at, s, NEGATIVE)
    return s


def pair_backward(q, k, v, qx, kx, o, do, lse, causal):
    kt = k.astype(F32).T.astype(BF)
    spread = (do.astype(F32) * o.astype(F32)).T
    low_q, low_k = low_half(q.shape[0]), low_half(k.shape[0])
    zero_q, zero_k = jnp.zeros_like(q), jnp.zeros_like(k)
    dqs, grads = [], []

    def begin(head):
        s = mm(pick(head, low_k, k, kx), pick(head, low_q, q, qx), NT)
        return causal_only(s) if causal else s, mm(pick(head, low_k, v, zero_k), do, NT)

    def end(head, values):
        s, dp = values
        half = slice(head * HEAD, (head + 1) * HEAD)
        p = jnp.exp2(s * (SCALE * LOG2E) - lse[head : head + 1])
        ds = (p * (dp - jnp.sum(spread[half], axis=0, keepdims=True))).astype(BF)
        dqs.append(mm(kt[half], ds))
        grads.append(
            (mm(ds, pick(head, low_q, q, zero_q)), mm(p.astype(BF), pick(head, low_q, do, zero_q)))
        )

    in_order(range(2), begin, end)
    (dk0, dv0), (dk1, dv1) = grads
    return jnp.concatenate(dqs, axis=0).T * SCALE, (dk0 + dk1) * SCALE, dv0 + dv1


def attn_bwd_kernel(
    q_ref, k_ref, v_ref, qx_ref, kx_ref, o_ref, do_ref, lse_ref, dq_ref, dk_ref, dv_ref, *, causal
):
    dq, dk, dv = pair_backward(
        q_ref[...], k_ref[...], v_ref[...], qx_ref[0], kx_ref[0], o_ref[...], do_ref[...],
        lse_ref[0], causal,
    )
    dq_ref[...] = dq.astype(BF)
    dk_ref[...] = dk.astype(BF)
    dv_ref[...] = dv.astype(BF)


def column_block(length, first):
    return pl.BlockSpec((length, PAIR), lambda p: (0, first + p))


def mask_block(length, row):
    return pl.BlockSpec((1, length, PAIR), lambda p: (row, 0, 0))


def pair_block(count_q):
    return pl.BlockSpec((1, 2, count_q), lambda p: (p, 0, 0))


def params(**more):
    return pltpu.CompilerParams(vmem_limit_bytes=VMEM_LIMIT, **more)


def attention_backward(q_in, k_in, v_in, qx, kx, row, firsts, mixed, grad_mixed, lse, causal):
    count_q, count_k, pairs = q_in.shape[0], k_in.shape[0], HEADS // 2
    width = HEADS * HEAD
    return pl.pallas_call(
        functools.partial(attn_bwd_kernel, causal=causal),
        grid=(pairs,),
        in_specs=[
            column_block(count_q, firsts[0]),
            column_block(count_k, firsts[1]),
            column_block(count_k, firsts[2]),
            mask_block(count_q, row),
            mask_block(count_k, row),
            column_block(count_q, 0),
            column_block(count_q, 0),
            pair_block(count_q),
        ],
        out_specs=[
            column_block(count_q, 0),
            column_block(count_k, 0),
            column_block(count_k, 0),
        ],
        out_shape=[
            jax.ShapeDtypeStruct((count_q, width), BF),
            jax.ShapeDtypeStruct((count_k, width), BF),
            jax.ShapeDtypeStruct((count_k, width), BF),
        ],
        compiler_params=params(),
    )(q_in, k_in, v_in, qx, kx, mixed, grad_mixed, lse)


BLOCK = 256
SLICE = 512


def inverse_rms(v):
    return lax.rsqrt(jnp.mean(v * v, -1, keepdims=True) + EPSILON)


def norm(v, gain):
    return (v * inverse_rms(v) * gain).astype(BF)


def norm_back(v, gain, grad):
    inv = inverse_rms(v)
    scaled = grad * gain
    along = jnp.mean(scaled * v, -1, keepdims=True)
    return (
        inv * scaled - v * (inv * inv * inv * along),
        jnp.sum(grad * v * inv, 0, keepdims=True),
    )


def gelu(x):
    return 0.5 * x * (1.0 + jnp.tanh(GELU_C * (x + GELU_A * x * x * x)))


def gelu_parts(x):
    square = x * x
    t = jnp.tanh(GELU_C * x * (1.0 + GELU_A * square))
    half = 0.5 * (1.0 + t)
    slope = half + 0.5 * x * (1.0 - t * t) * (GELU_C * (1.0 + 3.0 * GELU_A * square))
    return x * half, slope


class Fetch:
    def __init__(self, sources, held, sems):
        self.copies = [
            pltpu.make_async_copy(src, dst, sems.at[i])
            for i, (src, dst) in enumerate(zip(sources, held))
        ]
        self.held = held
        self.first = pl.program_id(0) == 0

        @pl.when(self.first)
        def _():
            for copy in self.copies:
                copy.start()

    def __getitem__(self, i):
        @pl.when(self.first)
        def _():
            self.copies[i].wait()

        return self.held[i]


def add_gain(ref, part):
    @pl.when(pl.program_id(0) == 0)
    def _():
        ref[...] = part

    @pl.when(pl.program_id(0) > 0)
    def _():
        ref[...] += part


def block_call(kernel, steps, ins, weights, outs, gain_outs=0):
    specs, arrays = [], []
    for array, row, first in ins:
        columns = array.shape[-1]
        if row is None:
            specs.append(pl.BlockSpec((BLOCK, columns), lambda i, f=first: (f + i, 0)))
        else:
            specs.append(
                pl.BlockSpec((None, BLOCK, columns), lambda i, r=row, f=first: (r, f + i, 0))
            )
        arrays.append(array)
    gains = [w for w in weights if w.dtype == F32]
    mats = [w for w in weights if w.dtype != F32]
    specs += [pl.BlockSpec((1, g.shape[1]), lambda i: (0, 0)) for g in gains]
    specs += [pl.BlockSpec(memory_space=pl.ANY)] * len(mats)
    dim = gains[0].shape[1]
    count = len(mats)

    def run(*refs):
        held, sems = refs[-1 - count : -1], refs[-1]
        at = len(arrays) + len(gains)
        fetch = Fetch(refs[at : at + count], held, sems)
        kernel(refs[: len(arrays)], [g[...] for g in refs[len(arrays) : at]], fetch, refs[at + count : -1 - count])

    return pl.pallas_call(
        run,
        grid=(steps,),
        in_specs=specs,
        out_specs=[pl.BlockSpec((BLOCK, c), lambda i: (i, 0)) for c, _ in outs]
        + [pl.BlockSpec((1, dim), lambda i: (0, 0))] * gain_outs,
        out_shape=[jax.ShapeDtypeStruct((steps * BLOCK, c), t) for c, t in outs]
        + [jax.ShapeDtypeStruct((1, dim), F32)] * gain_outs,
        scratch_shapes=[pltpu.VMEM(m.shape, m.dtype) for m in mats]
        + [pltpu.SemaphoreType.DMA((count,))],
        compiler_params=params(),
    )(*arrays, *gains, *mats)


def project_kernel(ins, gains, w, outs):
    (x,), (g0,), (n_ref, packed_ref) = ins, gains, outs
    n = norm(x[...].astype(F32), g0)
    n_ref[...] = n
    wa = w[0]
    dim = x.shape[1]
    for at in range(0, wa.shape[1], dim):
        packed_ref[:, at : at + dim] = mm(n, wa[:, at : at + dim]).astype(BF)


class FeedForward:
    def __init__(self, move, wf_hbm, wd_hbm, wf, wd):
        self.wf, self.wd, self.half = wf, wd, wd.shape[0]
        self.copies, self.move, self.first = {}, move, None
        self.sources = wf_hbm, wd_hbm

    def load(self):
        wf_hbm, wd_hbm = self.sources
        for at in range(0, self.half, SLICE):
            self.copies[at] = [
                self.move.copy(wd_hbm.at[at : at + SLICE], self.wd.at[at : at + SLICE])
            ] + [
                self.move.copy(wf_hbm.at[:, first : first + SLICE], self.wf.at[:, first : first + SLICE])
                for first in (at, self.half + at)
            ]

    def ready(self, at):
        waits = self.copies.pop(at, [])
        if self.first is None:
            for made in waits:
                made.wait()
        elif waits:

            @pl.when(self.first)
            def _():
                for made in waits:
                    made.wait()

    def slices(self):
        return range(0, self.half, SLICE)

    def parts(self, at):
        self.ready(at)
        up = slice(self.half + at, self.half + at + SLICE)
        return self.wf[:, at : at + SLICE], self.wf[:, up], self.wd[at : at + SLICE, :]


def ffn_up(m, ffn, acc, u_ref, act_ref):
    half = ffn.half

    def begin(at):
        gate_w, up_w, _ = ffn.parts(at)
        return mm(m, gate_w), mm(m, up_w)

    total = [acc]

    def end(at, values):
        gate, up = values
        u_ref[:, at : at + SLICE] = gate.astype(BF)
        u_ref[:, half + at : half + at + SLICE] = up.astype(BF)
        act = (gelu(gate) * up).astype(BF)
        if act_ref is not None:
            act_ref[:, at : at + SLICE] = act
        total[0] = total[0] + mm(act, ffn.wd[at : at + SLICE, :])

    in_order(ffn.slices(), begin, end)
    return total[0]


def ffn_down(branch, ffn, u_ref, du_ref, act_ref):
    half = ffn.half
    total = []

    def begin(at):
        return mm(branch, ffn.parts(at)[2], NT)

    def end(at, d_act):
        gate_w, up_w, _ = ffn.parts(at)
        gate = u_ref[:, at : at + SLICE].astype(F32)
        up = u_ref[:, half + at : half + at + SLICE].astype(F32)
        value, slope = gelu_parts(gate)
        if act_ref is not None:
            act_ref[:, at : at + SLICE] = (value * up).astype(BF)
        d_gate = (d_act * up * slope).astype(BF)
        d_up = (d_act * value).astype(BF)
        du_ref[:, at : at + SLICE] = d_gate
        du_ref[:, half + at : half + at + SLICE] = d_up
        part = mm(d_gate, gate_w, NT) + mm(d_up, up_w, NT)
        total[:] = [part if not total else total[0] + part]

    in_order(ffn.slices(), begin, end)
    return total[0]


def dec_query_kernel(ins, gains, w, outs):
    (o, x), (g1,), (d1_ref, c_ref, cq_ref) = ins, gains, outs
    d1 = x[...].astype(F32) + mm(o[...], w[0][...])
    d1_ref[...] = d1
    c = norm(d1, g1)
    c_ref[...] = c
    cq_ref[...] = mm(c, w[1][:, : c.shape[1]]).astype(BF)


def dec_ffn_kernel(row, x_hbm, oc_hbm, d1_hbm, g2, wc_hbm, wf_hbm, wd_hbm, *refs):
    outs, results, held = refs[:9], refs[9:18], refs[18:]
    doc, out, dd2_v, m_v, act, du, branch, dg2, cot = results
    oc, d1, u, proj, wf, wd, sems = held
    move = Mover(sems)
    tokens, width = oc.shape
    got = [
        move.copy(a, b)
        for a, b in ((oc_hbm, oc), (wc_hbm.at[:, width:], proj), (d1_hbm, d1))
    ]
    ffn = FeedForward(move, wf_hbm, wd_hbm, wf, wd)
    ffn.load()
    got_cot = move.copy(x_hbm.at[row, tokens:], cot)
    for made in got:
        made.wait()
    d2 = d1[...] + mm(oc[...], proj[...], NT)
    m = norm(d2, g2[...])
    m_v[...] = m
    out[...] = ffn_up(m, ffn, d2, u, act)
    for i in (3, 1, 4):
        move.store(results[i], outs[i])
    got_cot.wait()
    move.store(cot, outs[8])
    dm = ffn_down(cot[...], ffn, u, du, None)
    back, dg2[...] = norm_back(d2, g2[...], dm)
    dd2 = cot[...].astype(F32) + back
    branch[...] = dd2.astype(BF)
    doc[...] = mm(branch[...], proj[...]).astype(BF)
    dd2_v[...] = dd2
    for i in (0, 2, 5, 6, 7):
        move.store(results[i], outs[i])
    move.drain()


def enc_back_kernel(blocks, dk_hbm, dv_hbm, e1_hbm, e2_hbm, u_hbm, g1, g2, wc_hbm, wd_hbm, wf_hbm, wo_hbm, *refs):
    outs, results, held = refs[:10], refs[10:20], refs[20:]
    mem, fb_v, m_v, act, du, de1_v, ab_v, do, dg1, dg2 = results
    dk, dv, e1_in, e2_in, u, wc, wd, wf, wo, sems = held
    move = Mover(sems)
    width = dk.shape[1]
    here = [slice(i * BLOCK, (i + 1) * BLOCK) for i in range(len(blocks))]
    there = [slice(i * BLOCK, (i + 1) * BLOCK) for i in blocks]

    def load(i, pairs):
        return [move.copy(src.at[there[i]], dst.at[here[i]]) for src, dst in pairs]

    early = ((dk_hbm, dk), (dv_hbm, dv), (e2_hbm, e2_in))
    late = ((u_hbm, u), (e1_hbm, e1_in))
    got_early, got_late = [load(0, early)], []
    got_early[0].append(move.copy(wc_hbm, wc))
    ffn = FeedForward(move, wf_hbm, wd_hbm, wf, wd)
    got_late.append(load(0, late))
    ffn.load()
    got_late[0].append(move.copy(wo_hbm, wo))
    for i in range(1, len(blocks)):
        got_early.append(load(i, early))
        got_late.append(load(i, late))
    for i, b in enumerate(here):
        for made in got_early[i]:
            made.wait()
        dmem = mm(dk[b], wc[:, :width], NT) + mm(dv[b], wc[:, width:], NT)
        mem[b] = norm(e2_in[b], g1[...])
        de2, gain1 = norm_back(e2_in[b], g1[...], dmem)
        fb = de2.astype(BF)
        fb_v[b] = fb
        for made in got_late[i]:
            made.wait()
        m_v[b] = norm(e1_in[b], g2[...])
        dm = ffn_down(fb, ffn, u.at[b], du.at[b], act.at[b])
        back, gain2 = norm_back(e1_in[b], g2[...], dm)
        de1 = de2 + back
        de1_v[b] = de1
        ab = de1.astype(BF)
        ab_v[b] = ab
        do[b] = mm(ab, wo[...], NT).astype(BF)
        for k in range(8):
            move.store(results[k].at[b], outs[k].at[b])
        dg1[...] = gain1 if i == 0 else dg1[...] + gain1
        dg2[...] = gain2 if i == 0 else dg2[...] + gain2
    move.store(dg1, outs[8])
    move.store(dg2, outs[9])
    move.drain()


def dec_back_kernel(ins, gains, w, outs):
    (dcq, d1_in, dd2), (g1,), (dd1_ref, ab_ref, do_ref, dg1_ref) = ins, gains, outs
    d1 = d1_in[...]
    dc = mm(dcq[...], w[0][:, : dcq.shape[1]], NT)
    back, dg1 = norm_back(d1, g1, dc)
    dd1 = dd2[...] + back
    dd1_ref[...] = dd1
    ab = dd1.astype(BF)
    ab_ref[...] = ab
    do_ref[...] = mm(ab, w[1][...], NT).astype(BF)
    add_gain(dg1_ref, dg1)


def input_grad_kernel(ins, gains, w, outs):
    (dq, dk, dv, x, grad), (g0,), (dx_ref, dg0_ref) = ins, gains, outs
    wa = w[0]
    width = dq.shape[1]
    dn = (
        mm(dq[...], wa[:, :width], NT)
        + mm(dk[...], wa[:, width : 2 * width], NT)
        + mm(dv[...], wa[:, 2 * width :], NT)
    )
    back, dg0 = norm_back(x[...].astype(F32), g0, dn)
    dx_ref[...] = grad[...] + back
    add_gain(dg0_ref, dg0)


class Mover:
    def __init__(self, sems):
        self.sems, self.used, self.stores = sems, 0, []

    def copy(self, src, dst):
        made = pltpu.make_async_copy(src, dst, self.sems.at[self.used])
        self.used += 1
        made.start()
        return made

    def store(self, src, dst):
        self.stores.append(self.copy(src, dst))

    def drain(self):
        for made in self.stores:
            made.wait()


def pair_columns(first, p):
    return slice(first + p * PAIR, first + (p + 1) * PAIR)


def pick(head, low, a, b):
    return jnp.where(low, a, b) if head % 2 == 0 else jnp.where(low, b, a)


def in_order(items, begin, end, lead=1):
    waiting = []
    for item in items:
        waiting.append((item, begin(item)))
        if len(waiting) > lead:
            end(*waiting.pop(0))
    while waiting:
        end(*waiting.pop(0))


def attend(q_ref, kv_ref, firsts, qx, kx, o_ref, lse_ref, causal):
    count_q, count_k = qx.shape[0], kx.shape[0]
    low_q, low_k = low_half(count_q), low_half(count_k)
    ones = jnp.ones((8, count_k), BF)
    values, outs = {}, {}

    def begin(head):
        q = q_ref[:, pair_columns(firsts[0], head // 2)]
        k = kv_ref[:, pair_columns(firsts[1], head // 2)]
        s = mm(pick(head, low_k, k, kx), pick(head, low_q, q, qx), NT)
        return causal_only(s) if causal else s

    def end(head, s):
        p = head // 2
        if head % 2 == 0:
            values[p] = kv_ref[:, pair_columns(firsts[2], p)].astype(F32).T.astype(BF)
        vt = values[p][(head % 2) * HEAD : (head % 2 + 1) * HEAD]
        top = jnp.max(s, axis=0, keepdims=True)
        e = jnp.exp2((s - top) * (SCALE * LOG2E)).astype(BF)
        mixed = mm(jnp.concatenate([vt, ones], axis=0), e)
        total = mixed[HEAD : HEAD + 1]
        outs[head] = mixed[:HEAD] * (1.0 / total)
        lse_ref[p, head % 2 : head % 2 + 1, :] = top * (SCALE * LOG2E) + jnp.log2(total)
        if head % 2 == 1:
            both = jnp.concatenate([outs.pop(head - 1), outs.pop(head)], axis=0)
            o_ref[:, pair_columns(0, p)] = both.T.astype(BF)

    in_order(range(HEADS), begin, end)


def causal_only(s):
    key_at = lax.broadcasted_iota(jnp.int32, s.shape, 0)
    query_at = lax.broadcasted_iota(jnp.int32, s.shape, 1)
    return jnp.where(key_at <= query_at, s, NEGATIVE)


def attend_kernel(firsts, row, causal, same, *refs):
    if same:
        q_ref, (qx_ref, kx_ref, o_ref, lse_ref) = refs[0], refs[1:]
        kv_ref = q_ref
    else:
        q_ref, kv_ref, qx_ref, kx_ref, o_ref, lse_ref = refs
    attend(q_ref, kv_ref, firsts, qx_ref[row], kx_ref[row], o_ref, lse_ref, causal)


def attention_forward(q_in, kv_in, qx, kx, row, firsts, causal):
    count_q = q_in.shape[0]
    ins = [q_in] if kv_in is None else [q_in, kv_in]
    vmem = pl.BlockSpec(memory_space=pltpu.VMEM)
    return pl.pallas_call(
        functools.partial(attend_kernel, firsts, row, causal, kv_in is None),
        in_specs=[vmem] * (len(ins) + 2),
        out_specs=[vmem] * 2,
        out_shape=[
            jax.ShapeDtypeStruct((count_q, HEADS * HEAD), BF),
            jax.ShapeDtypeStruct((HEADS // 2, 2, count_q), F32),
        ],
        compiler_params=params(),
    )(*ins, qx, kx)


def enc_attend_kernel(row, x_hbm, qx_hbm, kx_hbm, g0, wa_hbm, *refs):
    outs, (n_v, packed_v, o_v, lse_v, x, qx, kx, wa, sems) = refs[:4], refs[4:]
    move = Mover(sems)
    got_x = move.copy(x_hbm.at[row], x)
    thirds = [slice(at, at + x.shape[1]) for at in range(0, wa.shape[1], x.shape[1])]
    got_wa = [move.copy(wa_hbm.at[:, t], wa.at[:, t]) for t in thirds]
    got_masks = move.copy(qx_hbm.at[row], qx), move.copy(kx_hbm.at[row], kx)
    tokens, dim = x.shape
    got_x.wait()
    blocks = [slice(at, at + BLOCK) for at in range(0, tokens, BLOCK)]
    for b in blocks:
        n_v[b] = norm(x[b].astype(F32), g0[...])
    move.store(n_v, outs[0])
    for t, made in zip(thirds, got_wa):
        made.wait()
        for b in blocks:
            packed_v[b, t] = mm(n_v[b], wa[:, t]).astype(BF)
    move.store(packed_v, outs[1])
    for made in got_masks:
        made.wait()
    attend(packed_v, packed_v, (0, dim, 2 * dim), qx[...], kx[...], o_v, lse_v, False)
    move.store(o_v, outs[2])
    move.store(lse_v, outs[3])
    move.drain()


def enc_rest_kernel(row, x_hbm, o_hbm, g1, g2, wo_hbm, wf_hbm, wd_hbm, wc_hbm, *refs):
    outs, (e1_v, u_v, e2_v, sent_v, x, o, wo, wf, wd, wc, sems) = refs[:4], refs[4:]
    move = Mover(sems)
    got = [move.copy(a, b) for a, b in ((x_hbm.at[row], x), (o_hbm, o), (wo_hbm, wo))]
    ffn = FeedForward(move, wf_hbm, wd_hbm, wf, wd)
    ffn.load()
    got_wc = [move.copy(wc_hbm, wc)]
    for made in got:
        made.wait()
    blocks = [slice(at, at + BLOCK) for at in range(0, x.shape[0], BLOCK)]
    for b in blocks:
        e1_v[b] = x[b].astype(F32) + mm(o[b], wo[...])
        move.store(e1_v.at[b], outs[0].at[b])
    results = ((u_v, outs[1]), (e2_v, outs[2]), (sent_v, outs[3]))

    def stores(i):
        b = pl.ds(pl.multiple_of(i * BLOCK, BLOCK), BLOCK)
        return [
            pltpu.make_async_copy(src.at[b], dst.at[b], sems.at[move.used + len(blocks) * k + i])
            for k, (src, dst) in enumerate(results)
        ]

    def block(i, carry):
        b = pl.ds(pl.multiple_of(i * BLOCK, BLOCK), BLOCK)
        ffn.first = i == 0
        e1 = e1_v[b]
        e2 = ffn_up(norm(e1, g2[...]), ffn, e1, u_v.at[b], None)
        e2_v[b] = e2

        @pl.when(i == 0)
        def _():
            got_wc[0].wait()

        sent_v[b] = mm(norm(e2, g1[...]), wc[...]).astype(BF)
        for copy in stores(i):
            copy.start()
        return carry

    lax.fori_loop(0, len(blocks), block, 0)
    for i in range(len(blocks)):
        for copy in stores(i):
            copy.wait()
    move.drain()


HBM = pl.BlockSpec(memory_space=pl.ANY)
VMEM = pl.BlockSpec(memory_space=pltpu.VMEM)


def moved_call(kernel, ins, specs, outs, held, copies):
    return list(
        pl.pallas_call(
            kernel,
            in_specs=specs,
            out_specs=[HBM] * len(outs),
            out_shape=[jax.ShapeDtypeStruct(s, t) for s, t in outs],
            scratch_shapes=[pltpu.VMEM(s, t) for s, t in outs + held]
            + [pltpu.SemaphoreType.DMA((copies,))],
            compiler_params=params(),
        )(*ins)
    )


def enc_attend(row, x_in, qx, kx, g0, wa):
    tokens, dim = x_in.shape[1:]
    width = wa.shape[1] // 3
    kept = [
        ((tokens, dim), BF),
        ((tokens, wa.shape[1]), BF),
        ((tokens, width), BF),
        ((HEADS // 2, 2, tokens), F32),
    ]
    held = [(x_in.shape[1:], BF), (qx.shape[1:], BF), (kx.shape[1:], BF), (wa.shape, BF)]
    return moved_call(
        functools.partial(enc_attend_kernel, row),
        (x_in, qx, kx, g0, wa),
        [HBM] * 3 + [VMEM] + [HBM],
        kept,
        held,
        10,
    )


def enc_rest(row, x_in, o, g1, g2, wo, wf, wd, wc):
    tokens, dim = x_in.shape[1:]
    kept = [
        ((tokens, dim), F32),
        ((tokens, wf.shape[1]), BF),
        ((tokens, dim), F32),
        ((tokens, wc.shape[1]), BF),
    ]
    held = [(x_in.shape[1:], BF), (o.shape, BF)] + [(w.shape, BF) for w in (wo, wf, wd, wc)]
    return moved_call(
        functools.partial(enc_rest_kernel, row),
        (x_in, o, g1, g2, wo, wf, wd, wc),
        [HBM] * 2 + [VMEM] * 2 + [HBM] * 4,
        kept,
        held,
        4 + 3 * (wd.shape[0] // SLICE) + 4 * (tokens // BLOCK),
    )


def nothing_kernel(*refs):
    pass


def unwritten(shapes):
    return pl.pallas_call(
        nothing_kernel,
        out_specs=[pl.BlockSpec(memory_space=pl.ANY)] * len(shapes),
        out_shape=[jax.ShapeDtypeStruct(s.shape, s.dtype) for s in shapes],
    )()


def by_section(on_decoder, encoder, decoder):
    enc_shapes = jax.eval_shape(encoder) if encoder else []
    dec_shapes = jax.eval_shape(decoder) if decoder else []
    none = lambda: []
    encoder, decoder = encoder or none, decoder or none
    pool = lambda shapes: list(unwritten(shapes)) if shapes else []
    both = lax.cond(
        on_decoder,
        lambda: pool(enc_shapes) + list(decoder()),
        lambda: list(encoder()) + pool(dec_shapes),
    )
    return both[: len(enc_shapes)], both[len(enc_shapes) :]


def mask_kernel(*refs):
    for lengths_ref, (member_ref, other_ref) in ((refs[0], refs[2:4]), (refs[1], refs[4:6])):
        rows, span, lanes = member_ref.shape
        position = lax.broadcasted_iota(jnp.int32, (span, lanes), 0)
        lane = lax.rem(lax.broadcasted_iota(jnp.int32, (span, lanes), 1), HEAD)
        docs = lengths_ref.shape[1]
        for r in range(rows):
            seg, end = jnp.zeros((span, lanes), jnp.int32), jnp.int32(0)
            for j in range(docs):
                end = end + lengths_ref[r, j]
                seg = seg + jnp.where(position >= end, 1, 0)
            hit = lane == seg
            member_ref[r] = jnp.where(hit, 1.0, 0.0).astype(BF)
            other_ref[r] = jnp.where(hit | (lane >= docs), 0.0, NEGATIVE).astype(BF)


def mask_operands(enc_lengths, dec_lengths, spans):
    smem = pl.BlockSpec(memory_space=pltpu.SMEM)
    vmem = pl.BlockSpec(memory_space=pltpu.VMEM)
    return pl.pallas_call(
        mask_kernel,
        in_specs=[smem] * 2,
        out_specs=[vmem] * 4,
        out_shape=[
            jax.ShapeDtypeStruct((enc_lengths.shape[0], span, PAIR), BF)
            for span in spans
            for _ in range(2)
        ],
        compiler_params=params(),
    )(enc_lengths, dec_lengths)


def shift(x, by):
    pairs = [(0, 1)] if by > 0 else [(1, 0)]
    return lax.ppermute(x, "section", pairs)


def body(
    section_input, enc_lengths, dec_lengths, attn_in, attn_out, ffn_in, ffn_out, cross_weight, gains
):
    wa, wo, wf, wd, wc = attn_in[0], attn_out[0], ffn_in[0], ffn_out[0], cross_weight[0]
    g0, g1, g2 = gains[0, 0:1], gains[0, 1:2], gains[0, 2:3]
    x_in = section_input[0]
    rows, le, dim = x_in.shape
    ld = le // 2
    width = wo.shape[0]
    enc_qx, enc_kx, dec_qx, dec_kx = mask_operands(enc_lengths, dec_lengths, (le, ld))
    on_decoder = lax.axis_index("section") == 1
    steps_e, steps_d = le // BLOCK, ld // BLOCK
    columns = width // PAIR
    own = (0, columns, 2 * columns)
    across = (0, 0, columns)
    inner = wf.shape[1]

    def project(r, steps):
        return list(
            block_call(project_kernel, steps, [(x_in, r, 0)], [g0, wa], [(dim, BF), (3 * width, BF)])
        )

    def dec_first(r):
        n, packed = project(r, steps_d)
        o, lse = attention_forward(packed, None, dec_qx, dec_kx, r, (0, width, 2 * width), True)
        d1, c, cq = block_call(
            dec_query_kernel,
            steps_d,
            [(o, None, 0), (x_in, r, 0)],
            [g1, wo, wc],
            [(dim, F32), (dim, BF), (width, BF)],
        )
        return [n, packed, o, lse, d1, c, cq]

    def cross(r, cq, sent):
        return list(attention_forward(cq, sent, dec_qx, enc_kx, r, (0, 0, width), False))

    feeds = 3 * (wd.shape[0] // SLICE)

    def dec_ffn(r, oc, d1):
        row = lambda columns, kind: ((ld, columns), kind)
        return moved_call(
            functools.partial(dec_ffn_kernel, r),
            (x_in, oc, d1, g2, wc, wf, wd),
            [HBM] * 3 + [VMEM] + [HBM] * 3,
            [row(width, BF), row(dim, F32), row(dim, F32), row(dim, BF), row(wd.shape[0], BF)]
            + [row(inner, BF), row(dim, BF), ((1, dim), F32), row(dim, BF)],
            [row(width, BF), row(dim, F32), row(inner, BF), ((dim, width), BF)]
            + [(wf.shape, BF), (wd.shape, BF)],
            feeds + 4 + 9,
        )

    def cross_back(r, cq, sent, oc, doc, lse):
        return list(
            attention_backward(cq, sent, sent, dec_qx, enc_kx, r, across, oc, doc, lse, False)
        )

    def enc_back(dk, dv, e1, e2, u, blocks):
        row = lambda columns, kind: ((len(blocks) * BLOCK, columns), kind)
        return moved_call(
            functools.partial(enc_back_kernel, blocks),
            (dk, dv, e1, e2, u, g1, g2, wc, wd, wf, wo),
            [HBM] * 5 + [VMEM] * 2 + [HBM] * 4,
            [row(dim, BF)] * 3
            + [row(wd.shape[0], BF), row(inner, BF), row(dim, F32), row(dim, BF), row(width, BF)]
            + [((1, dim), F32)] * 2,
            [row(width, BF)] * 2
            + [row(dim, F32)] * 2
            + [row(inner, BF)]
            + [(w.shape, BF) for w in (wc, wd, wf, wo)],
            feeds + 2 + 5 * len(blocks) + 8 * len(blocks) + 2,
        )

    def self_back(r, steps, masks, causal, packed, o, lse, do, grad):
        dq, dk, dv = attention_backward(
            packed, packed, packed, *masks, r, own, o, do, lse, causal
        )
        dx, dg0 = block_call(
            input_grad_kernel,
            steps,
            [(dq, None, 0), (dk, None, 0), (dv, None, 0), (x_in, r, 0), (grad, None, 0)],
            [g0, wa],
            [(dim, F32)],
            1,
        )
        return [dq, dk, dv, dx, dg0]

    def dec_back(dcq, d1, dd2):
        return list(
            block_call(
                dec_back_kernel,
                steps_d,
                [(dcq, None, 0), (d1, None, 0), (dd2, None, 0)],
                [g1, wc, wo],
                [(dim, F32), (dim, BF), (width, BF)],
                1,
            )
        )

    every = range(rows)
    plain = lax.axis_size("rows") != PEERS
    state = []

    def run(encoder, decoder, *ready):
        held = on_decoder
        if state:
            held, state[0][1], *_ = lax.optimization_barrier((on_decoder, state[0][1]) + ready)
        out = by_section(held, encoder, decoder)
        state[:] = [out[0] or out[1]]
        return out

    def slots():
        return [None] * rows

    first, rest, dfirst, cqs, crossed, ocs = slots(), slots(), slots(), slots(), slots(), slots()
    mids, docs_in, cross_b, dcqs, back, last, dlast = (slots() for _ in range(7))

    def begin_cross(r, beside=None):
        crossed[r], out = run(lambda: cross(r, cqs[r], rest[r][3]), beside)
        ocs[r] = shift(crossed[r][0], 1)
        return out

    def dec_mid(r):
        return lambda: dec_ffn(r, ocs[r], dfirst[r][4])

    def keep_mid(r, out):
        mids[r] = out
        docs_in[r] = shift(out[0], -1)

    def dec_last(r):
        p = dec_back(dcqs[r], dfirst[r][4], mids[r][2])
        n, packed, o, lse = dfirst[r][:4]
        return p + self_back(r, steps_d, (dec_qx, dec_kx), True, packed, o, lse, p[2], p[0])

    def enc_last(r):
        return self_back(
            r, steps_e, (enc_qx, enc_kx), False, *first[r][1:4],
            jnp.concatenate(backs(r, 7), 0), jnp.concatenate(backs(r, 5), 0),
        )

    def enc_first(r):
        return lambda: enc_attend(r, x_in, enc_qx, enc_kx, g0, wa)

    def enc_then(r):
        return lambda: enc_rest(r, x_in, first[r][2], g1, g2, wo, wf, wd, wc)

    first[0], dfirst[0] = run(enc_first(0), lambda: dec_first(0))
    cqs[0] = shift(dfirst[0][6], -1)
    rest[0], more = run(enc_then(0), lambda: [v for r in every[1:] for v in dec_first(r)])
    begin_cross(0)
    for r in every[1:]:
        dfirst[r] = more[7 * (r - 1) : 7 * r]
        cqs[r] = shift(dfirst[r][6], -1)
    for r in every[1:]:
        first[r], _ = run(enc_first(r), None)
        rest[r], out = run(enc_then(r), dec_mid(r - 1), ocs[r - 1])
        keep_mid(r - 1, out)
        begin_cross(r)
    def backs(r, i):
        return [part[i] for part in back[r]]

    def enc_backs(r, blocks):
        return lambda: enc_back(
            cross_b[r][1], cross_b[r][2], rest[r][0], rest[r][2], rest[r][1], blocks
        )

    for r in every:
        cross_b[r], _ = run(
            lambda: cross_back(r, cqs[r], rest[r][3], crossed[r][0], docs_in[r], crossed[r][1]),
            None,
        )
        if r == 0 and steps_e > 1:
            part, out = run(enc_backs(0, (0,)), dec_mid(rows - 1))
            keep_mid(rows - 1, out)
            dcqs[0] = shift(cross_b[0][0], 1)
            others, _ = run(enc_backs(0, tuple(range(1, steps_e))), None)
            back[0] = [part, others]
        else:
            dcqs[r] = shift(cross_b[r][0], 1)
            out = run(enc_backs(r, tuple(range(steps_e))), dec_mid(rows - 1) if r == 0 else None)
            back[r] = [out[0]]
            if r == 0:
                keep_mid(rows - 1, out[1])
        last[r], dlast[r] = run((lambda: enc_last(r)) if plain else None, lambda: dec_last(r))

    def over_rows(lists):
        pieces = lambda v: v if isinstance(v, list) else [v]
        return [[p for v in group for p in pieces(v)] for group in zip(*lists)]

    enc_side = (
        over_rows(
            [backs(r, 2), backs(r, 3), backs(r, 0), backs(r, 0), first[r][2], first[r][0]]
            for r in every
        ),
        over_rows(
            [backs(r, 4), backs(r, 1), cross_b[r][1], cross_b[r][2], backs(r, 6)] + last[r][0:3]
            for r in every
        ),
    )
    dec_side = (
        over_rows(
            [mids[r][3], mids[r][4], dfirst[r][5], mids[r][6], dfirst[r][2], dfirst[r][0]]
            for r in every
        ),
        over_rows(
            [mids[r][5], mids[r][8], dcqs[r], ocs[r], dlast[r][1]] + dlast[r][4:7] for r in every
        ),
    )
    if not plain:
        kept = over_rows(
            [first[r][1], first[r][2], backs(r, 7), first[r][3], backs(r, 5)] for r in every
        )
        decoded = over_rows([mids[r][1], dlast[r][7]] for r in every)
        gain_rows = (
            over_rows([backs(r, 8), backs(r, 9)] for r in every),
            over_rows([dlast[r][8], dlast[r][3], mids[r][7]] for r in every),
        )
        s_in, s_out, s_fi, s_cross, s_gain, s_fo, results = grad_sum(
            (enc_side, dec_side), kept, decoded, gain_rows, (x_in, enc_qx, enc_kx, wa, g0)
        )
        o_gain, *outs = hand_over(
            s_gain, gains.shape[1], [results, s_in, s_out, s_fi, s_fo, s_cross]
        )
        return tuple(outs) + (o_gain,)

    def enc_parts():
        gain_rows = [sum(v) for v in zip(*[[last[r][4], sum(backs(r, 8)), sum(backs(r, 9))] for r in every])]
        return [jnp.concatenate(gain_rows, 0), jnp.stack([last[r][3] for r in every])]

    def dec_parts():
        gain_rows = [sum(v) for v in zip(*[[dlast[r][8], dlast[r][3], mids[r][7]] for r in every])]
        both = [jnp.concatenate([mids[r][1], dlast[r][7]], 0) for r in every]
        return [jnp.concatenate(gain_rows, 0), jnp.stack(both)]

    gain_grads, results = lax.cond(on_decoder, dec_parts, enc_parts)
    gain_terms = jnp.pad(gain_grads.T, ((0, 0), (0, LANES - gain_grads.shape[0]))).astype(BF)

    s_in, s_out, s_fi, s_cross, s_gain, s_fo = plain_sum(on_decoder, (enc_side, dec_side), gain_terms)
    return (
        results[None],
        s_in[None],
        s_out[None],
        s_fi[None],
        s_fo[None],
        s_cross[None],
        s_gain[:, : gain_grads.shape[0]].T[None],
    )


def solution(mesh):
    placed = (
        P("section", "rows", None, None),
        P("rows", None),
        P("rows", None),
    ) + (P("section", None, None),) * 6
    return jax.shard_map(
        body,
        mesh=mesh,
        in_specs=placed,
        out_specs=(
            P("section", "rows", None, None),
            P("section", "rows", None),
            P("section", "rows", None),
            P("section", "rows", None),
            P("section", "rows", None),
            P("section", "rows", None),
            P("section", None, "rows"),
        ),
        check_vma=False,
    )
```

```python
import functools

import jax
import jax.numpy as jnp
from jax import lax
from jax.experimental import pallas as pl
from jax.experimental.pallas import tpu as pltpu
from jax.sharding import PartitionSpec as P

HEADS = 12
HEAD = 64
PAIR = 128
EPSILON = 1e-06
SCALE = 0.125
LOG2E = 1.4426950408889634
NEGATIVE = -1e30
GELU_C = 0.7978845608028654
GELU_A = 0.044715

BF = jnp.bfloat16
F32 = jnp.float32
NT = (((1,), (1,)), ((), ()))
NN = (((1,), (0,)), ((), ()))
TN = (((0,), (0,)), ((), ()))


def mm(a, b, dims=NN):
    return lax.dot_general(a, b, dims, preferred_element_type=F32)


MESH = pl.DeviceIdType.MESH
LANES = 256
VMEM_LIMIT = 56 * 1024 * 1024
SUM_VMEM = 60 * 1024 * 1024

NZ, NY, NC = 4, 2, 2
PEERS = NZ * NY * NC
C_LAG = 2
Y_LAG = C_LAG + 4
HOP = 3
ZF_EVERY, ZF_AT = 6, 3
ZF_LAG = C_LAG + HOP * (NZ - 1)
RING = 6
AHEAD = 3
PANELS = 4

TALL = 1
LEFT_ORDER = (0, 2, 3, 4, 5)
PRODUCTS = ((0, 0), (1, 1), (2, 2), (3, 3), (4, 4), (5, 5), (5, 6), (5, 7))


def grad_sum_kernel(rows, group_sizes, token_counts, chunk_counts, unit_steps, *refs):
    remaining = list(refs)
    sizes = list(group_sizes)

    def take(groups):
        return [[remaining.pop(0) for _ in range(sizes.pop(0))] for _ in range(groups)]

    def take_one():
        return remaining.pop(0)

    lefts_of, rights_of = [], []
    for side in range(2):
        lefts_of.append(take(6))
        rights_of.append(take(5 if side == 0 else 8))
    packed_of, o_of, do_of, lse_of, de1_of = take(5)
    out_of, dx_of = take(2)
    gain_rows = [[None] + take(2), take(3)]
    x_ref, qx_ref, kx_ref, wa_ref, g0_ref = [take_one() for _ in range(5)]
    o_in, o_out, o_fi, o_cross, o_gain, o_fo, o_results = [take_one() for _ in range(7)]
    (
        xt, xt_tall, left_stage, tall_stage, tall_right, panels, ring,
        own, got_y, got_r, got_l, z_right, z_left,
        s_left, s_tall, s_right, s_panel,
        s_core, r_core, s_y, r_y, s_r, r_r, s_l, r_l,
        d_packed, wa, att, qx, kx, lse, x_stage, grad_stage, dx_stage, dg0,
        s_att, s_const, s_lse, s_block, s_out, s_dec,
    ) = remaining
    chunks, height, dim = own.shape[0], own.shape[3], xt.shape[0]
    sec, me = lax.axis_index("section"), lax.axis_index("rows")
    core, y, z = lax.rem(me, 2), lax.rem(me // 2, 2), me // 4
    by_core, by_y = me + 1 - 2 * core, me + 2 - 4 * y
    other, away = 1 - core, 1 - y
    bases = [sum(chunk_counts[:i]) for i in range(len(chunk_counts))]


    def each(act):
        for side in range(2):

            @pl.when(sec == side)
            def _(side=side):
                act(side)

    def row_copies(sources, columns, dst, sems, side):
        del side
        copies, at = [], 0
        for i, src in enumerate(sources):
            copies.append(
                pltpu.make_async_copy(
                    src if columns is None else src.at[:, columns],
                    dst.at[at : at + src.shape[0]],
                    sems.at[i],
                )
            )
            at += src.shape[0]
        return copies

    def start_all(copies):
        for copy in copies:
            copy.start()

    def wait_all(copies):
        for copy in copies:
            copy.wait()

    def left_copies(q, side):
        source = lefts_of[side][LEFT_ORDER[q]]
        return row_copies(source, None, left_stage.at[q % 2], s_left.at[q % 2], side)

    def tall_copies(side):
        return row_copies(lefts_of[side][1], None, tall_stage, s_tall, side)

    def tall_right_copies(side):
        return row_copies(rights_of[side][1], None, tall_right, s_right, side)

    def panel_copies(p, i, slot, side):
        if PRODUCTS[p][1] >= len(rights_of[side]):
            return []
        columns = pl.ds(pl.multiple_of(i * LANES, LANES), LANES)
        return row_copies(
            rights_of[side][PRODUCTS[p][1]], columns, panels.at[slot], s_panel.at[slot], side
        )

    def for_panel(t, act):
        slot = lax.rem(t, PANELS)
        for p in range(len(PRODUCTS)):
            if p != TALL:

                @pl.when((t >= bases[p]) & (t < bases[p] + chunk_counts[p]))
                def _(p=p):
                    each(lambda side: act(p, t - bases[p], slot, side))

    def flip(side, stage, columns, put):
        for at in range(0, rows * token_counts[side], LANES):
            tokens = slice(at, at + LANES)
            put(tokens, stage[tokens, columns].astype(F32).T.astype(BF))

    def held_already(q, side):
        return side == 0 and (LEFT_ORDER[q - 1], LEFT_ORDER[q]) == (2, 3)

    def build_left(q):
        def act(side):
            if not held_already(q, side):
                wait_all(left_copies(q, side))
                for at in range(0, xt.shape[0], LANES):

                    def put(tokens, block, at=at):
                        xt[at : at + LANES, tokens] = block

                    flip(side, left_stage.at[q % 2], slice(at, at + LANES), put)
            if q + 2 < len(LEFT_ORDER) and not held_already(q + 2, side):
                start_all(left_copies(q + 2, side))

        each(act)

    groups = xt_tall.shape[0] // LANES
    tall_rows = xt_tall.shape[0] // PEERS

    def build_tall(part):
        columns = pl.ds(pl.multiple_of(part * LANES, LANES), LANES)
        targets = LANES // tall_rows

        def act(side):
            def put(tokens, block):
                for k in range(targets):
                    for j in range(tall_rows // 16):
                        to = j * LANES + (part * targets + k) * 16
                        xt_tall[pl.ds(pl.multiple_of(to, 16), 16), tokens] = block[
                            k * tall_rows + j * 16 : k * tall_rows + (j + 1) * 16
                        ]

            flip(side, tall_stage, columns, put)

        each(act)

    def send_core(j):
        slot = lax.rem(j, RING)
        return pltpu.make_async_remote_copy(
            src_ref=ring.at[slot, :, :, other],
            dst_ref=own.at[j],
            send_sem=s_core.at[j],
            recv_sem=r_core.at[j],
            device_id=(sec, by_core),
            device_id_type=MESH,
        )

    def send_y(j):
        return pltpu.make_async_remote_copy(
            src_ref=own.at[j, :, away],
            dst_ref=got_y.at[j],
            send_sem=s_y.at[j],
            recv_sem=r_y.at[j],
            device_id=(sec, by_y),
            device_id_type=MESH,
        )

    def send_right(j, at):
        return pltpu.make_async_remote_copy(
            src_ref=own.at[j, pl.ds(at + 1, NZ - 1 - at), y],
            dst_ref=got_r.at[j, pl.ds(at, NZ - 1 - at)],
            send_sem=s_r.at[j],
            recv_sem=r_r.at[j],
            device_id=(sec, me + 4),
            device_id_type=MESH,
        )

    def send_left(j, at):
        return pltpu.make_async_remote_copy(
            src_ref=own.at[j, pl.ds(0, at), y],
            dst_ref=got_l.at[j, pl.ds(0, at)],
            send_sem=s_l.at[j],
            recv_sem=r_l.at[j],
            device_id=(sec, me - 4),
            device_id_type=MESH,
        )

    def z_first(j):
        return lax.rem(j, ZF_EVERY) == ZF_AT

    def send_along(j, at, right):
        targets = pl.ds(at + 1, NZ - 1 - at) if right else pl.ds(0, at)
        buffer = z_right if right else z_left
        return pltpu.make_async_remote_copy(
            src_ref=own.at[j, targets],
            dst_ref=buffer.at[j // ZF_EVERY, pl.ds(at, NZ - 1 - at) if right else targets],
            send_sem=(s_r if right else s_l).at[j],
            recv_sem=(r_r if right else r_l).at[j],
            device_id=(sec, me + 4 if right else me - 4),
            device_id_type=MESH,
        )

    def send_y_last(j):
        return pltpu.make_async_remote_copy(
            src_ref=own.at[j, z, away],
            dst_ref=got_y.at[j, z],
            send_sem=s_y.at[j],
            recv_sem=r_y.at[j],
            device_id=(sec, by_y),
            device_id_type=MESH,
        )

    def forward_along(j, at, right):
        source = at - 1 if right else at + 1
        if 0 <= source < NZ:
            send_along(j, source, right).wait_recv()
            buffer = z_right if right else z_left
            for t in range(at + 1, NZ) if right else range(at):
                for b in range(NY):
                    add_into(own.at[j, t, b], buffer.at[j // ZF_EVERY, t - 1 if right else t, b])
        send_along(j, at, right).start()

    def turn_to_y(j):
        for at in range(NZ):

            @pl.when(z == at)
            def _(at=at):
                if at == NZ - 1:
                    send_along(j, at - 1, True).wait_recv()
                if at == 0:
                    send_along(j, at + 1, False).wait_recv()
                for b in range(NY):
                    if at > 0:
                        add_into(own.at[j, at, b], z_right.at[j // ZF_EVERY, at - 1, b])
                    if at < NZ - 1:
                        add_into(own.at[j, at, b], z_left.at[j // ZF_EVERY, at, b])

        send_y_last(j).start()

    def add_into(dst, src):
        dst[...] = (dst[...].astype(F32) + src[...].astype(F32)).astype(BF)


    def compute(s):
        slot = lax.rem(s, RING)

        def put_panel(value):
            for t in range(PEERS):
                ring[slot, t // 4, t // 2 % 2, t % 2] = value[t * height : (t + 1) * height]

        for p in range(len(PRODUCTS)):
            left = PRODUCTS[p][0]

            @pl.when((s >= bases[p]) & (s < bases[p] + chunk_counts[p]))
            def _(p=p, left=left):
                if p != TALL:
                    if p == 0 or PRODUCTS[p - 1][0] != left:

                        @pl.when(s == bases[p])
                        def _():
                            build_left(LEFT_ORDER.index(left))

                    where = lax.rem(s, PANELS)

                    def act(side):
                        wait_all(panel_copies(p, s - bases[p], where, side))
                        tokens = rows * token_counts[side]
                        if PRODUCTS[p][1] < len(rights_of[side]):
                            right = panels[where, :tokens, :]
                        else:
                            first = (PRODUCTS[p][1] - 5) * dim + (s - bases[p]) * LANES
                            right = d_packed[:, pl.ds(pl.multiple_of(first, LANES), LANES)]
                        put_panel(mm(xt[:, :tokens], right).astype(BF))

                    each(act)
                else:
                    rows_at = pl.ds(pl.multiple_of((s - bases[p]) * LANES, LANES), LANES)

                    @pl.when(s == bases[p])
                    def _():
                        each(lambda side: wait_all(tall_right_copies(side)))

                    def act(side):
                        tokens = rows * token_counts[side]
                        for k in range(tall_right.shape[1] // LANES):
                            value = mm(
                                xt_tall[rows_at, :tokens],
                                tall_right[:tokens, k * LANES : (k + 1) * LANES],
                            ).astype(BF)
                            for t in range(PEERS):
                                ring[slot, t // 4, t // 2 % 2, t % 2, k * 16 : (k + 1) * 16] = value[
                                    t * 16 : (t + 1) * 16
                                ]

                    each(act)

        @pl.when(s == chunks - 1)
        def _():
            def act(side):
                parts = []
                for group in gain_rows[side]:
                    total_row = dg0[...]
                    if group is not None:
                        total_row = group[0][...]
                        for ref in group[1:]:
                            total_row = total_row + ref[...]
                    parts.append(total_row)
                parts.append(jnp.zeros((LANES - len(parts), dim), F32))
                put_panel(jnp.concatenate(parts, axis=0).T.astype(BF))

            each(act)


    attn_units, block_units, first_block = unit_steps
    tokens_e = token_counts[0]
    per_row = tokens_e // BLOCK
    const_copies = [
        pltpu.make_async_copy(src, dst, s_const.at[i])
        for i, (src, dst) in enumerate(((qx_ref, qx), (kx_ref, kx), (wa_ref, wa)))
    ]
    lse_copies = [
        pltpu.make_async_copy(ref, lse.at[r], s_lse.at[r]) for r, ref in enumerate(lse_of)
    ]

    def row_pieces(refs_of, r):
        found, at = [], 0
        for ref in refs_of:
            if r * tokens_e <= at < (r + 1) * tokens_e:
                found.append((ref, at - r * tokens_e))
            at += ref.shape[0]
        return found

    def attn_loads(u, act):
        slot, p = lax.rem(u, 2), lax.rem(u, HEADS // 2)
        for r in range(rows):

            @pl.when(u // (HEADS // 2) == r)
            def _(r=r):
                at = lambda first: pl.ds(pl.multiple_of(first + p * PAIR, PAIR), PAIR)
                sources = [packed_of[r].at[:, at(k * dim)] for k in range(3)]
                sources.append(o_of[r].at[:, at(0)])
                copies = [
                    pltpu.make_async_copy(src, att.at[slot, k], s_att.at[slot, k])
                    for k, src in enumerate(sources)
                ]
                for ref, begin in row_pieces(do_of, r):
                    copies.append(
                        pltpu.make_async_copy(
                            ref.at[:, at(0)],
                            att.at[slot, 4, begin : begin + ref.shape[0]],
                            s_att.at[slot, len(copies)],
                        )
                    )
                act(copies)

    def attn_unit(u):
        slot, p, r = lax.rem(u, 2), lax.rem(u, HEADS // 2), u // (HEADS // 2)
        attn_loads(u, wait_all)
        q, k, v, o, do = [att[slot, i] for i in range(5)]
        grads = pair_backward(q, k, v, qx[r], kx[r], o, do, lse[r, p], False)
        where = pl.ds(pl.multiple_of(r * tokens_e, tokens_e), tokens_e)
        for i, value in enumerate(grads):
            at = pl.ds(pl.multiple_of(i * dim + p * PAIR, PAIR), PAIR)
            d_packed[where, at] = value.astype(BF)

    def block_loads(v, act):
        slot = lax.rem(v, 2)
        where = pl.ds(pl.multiple_of(lax.rem(v, per_row) * BLOCK, BLOCK), BLOCK)
        for r in range(rows):

            @pl.when(v // per_row == r)
            def _(r=r):
                act([pltpu.make_async_copy(x_ref.at[r, where], x_stage.at[slot], s_block.at[slot, 0])])

            for ref, begin in row_pieces(de1_of, r):
                for at in range(0, ref.shape[0], BLOCK):

                    @pl.when(v == (r * tokens_e + begin + at) // BLOCK)
                    def _(ref=ref, at=at):
                        act(
                            [
                                pltpu.make_async_copy(
                                    ref.at[at : at + BLOCK], grad_stage.at[slot], s_block.at[slot, 1]
                                )
                            ]
                        )

    def block_store(v):
        slot = lax.rem(v, 2)
        where = pl.ds(pl.multiple_of(lax.rem(v, per_row) * BLOCK, BLOCK), BLOCK)
        return pltpu.make_async_copy(
            dx_stage.at[slot], o_results.at[v // per_row, where], s_out.at[slot]
        )

    def block_unit(v):
        slot = lax.rem(v, 2)
        block_loads(v, wait_all)

        @pl.when(v == 0)
        def _():
            const_copies[2].wait()
            dg0[...] = jnp.zeros_like(dg0)

        @pl.when(v >= 2)
        def _():
            block_store(v - 2).wait()

        where = pl.ds(pl.multiple_of(v * BLOCK, BLOCK), BLOCK)
        dn = None
        for i in range(3):
            part = mm(d_packed[where, i * dim : (i + 1) * dim], wa[:, i * dim : (i + 1) * dim], NT)
            dn = part if dn is None else dn + part
        back, gain_part = norm_back(x_stage[slot].astype(F32), g0_ref[...], dn)
        dg0[...] += gain_part
        dx_stage[slot] = grad_stage[slot] + back
        block_store(v).start()

    def dec_results(store):
        half = token_counts[1]
        parts = [
            (ref, stage.at[r], o_results.at[r, k * half : (k + 1) * half], s_dec.at[k, r])
            for k, (group, stage) in enumerate(((out_of, grad_stage), (dx_of, dx_stage)))
            for r, ref in enumerate(group)
        ]
        return [
            pltpu.make_async_copy(held, dst, sem) if store else pltpu.make_async_copy(src, held, sem)
            for src, held, dst, sem in parts
        ]

    def side_work(s):
        @pl.when(s == 0)
        def _():
            start_all(lse_copies)
            start_all(const_copies)
            for v in range(2):
                block_loads(jnp.int32(v), start_all)

        u = s // 2

        @pl.when((lax.rem(s, 2) == 0) & (u < attn_units))
        def _():
            attn_loads(u, start_all)

        @pl.when((lax.rem(s, 2) == 0) & (u >= 1) & (u <= attn_units))
        def _():
            @pl.when(u == 1)
            def _():
                wait_all(lse_copies)
                wait_all(const_copies[:2])

            attn_unit(u - 1)

        v = (s - first_block) // 2

        @pl.when((lax.rem(s, 2) == 0) & (s >= first_block) & (v < block_units))
        def _():
            block_unit(v)

            @pl.when(v + 2 < block_units)
            def _():
                block_loads(v + 2, start_all)


    def open_first(side):
        start_all(left_copies(0, side))
        for t in range(AHEAD):
            start_all(panel_copies(0, t, t % PANELS, side))

    each(open_first)

    barrier = pltpu.get_barrier_semaphore()

    def greet(peer):
        pl.semaphore_signal(barrier, inc=1, device_id=(sec, peer), device_id_type=MESH)

    greet(by_core)
    greet(by_y)

    @pl.when(z > 0)
    def _():
        greet(me - 4)

    @pl.when(z < NZ - 1)
    def _():
        greet(me + 4)

    @pl.when((z > 0) & (z < NZ - 1))
    def _():
        pl.semaphore_wait(barrier, 4)

    @pl.when((z == 0) | (z == NZ - 1))
    def _():
        pl.semaphore_wait(barrier, 3)


    @pl.when(sec == 1)
    def _():
        start_all(dec_results(False))

    def step(s, carry):
        @pl.when(s + AHEAD < chunks - 1)
        def _():
            for_panel(
                s + AHEAD,
                lambda p, i, slot, side: start_all(panel_copies(p, i, slot, side)),
            )

        @pl.when((s >= RING) & (s < chunks))
        def _():
            send_core(s - RING).wait_send()

        @pl.when(s < chunks)
        def _():
            compute(s)
            send_core(s).start()

        @pl.when(sec == 0)
        def _():
            side_work(s)

        @pl.when((sec == 1) & (s == RING))
        def _():
            wait_all(dec_results(False))
            start_all(dec_results(True))

        @pl.when(s == 1)
        def _():
            each(lambda side: start_all(tall_copies(side)))

        @pl.when(s == 4)
        def _():
            each(lambda side: wait_all(tall_copies(side)))
            each(lambda side: start_all(left_copies(1, side)))
            each(lambda side: start_all(tall_right_copies(side)))

        @pl.when((s >= 4) & (s < 4 + groups))
        def _():
            build_tall(s - 4)

        j_c = s - C_LAG

        @pl.when((j_c >= 0) & (j_c < chunks))
        def _():
            send_core(j_c).wait_recv()
            slot = lax.rem(j_c, RING)
            for a in range(NZ):
                for b in range(NY):
                    add_into(own.at[j_c, a, b], ring.at[slot, a, b, core])

            @pl.when(jnp.logical_not(z_first(j_c)))
            def _():
                send_y(j_c).start()

        j_y = s - Y_LAG

        @pl.when((j_y >= 0) & (j_y < chunks) & jnp.logical_not(z_first(j_y)))
        def _():
            send_y(j_y).wait_recv()
            for t in range(NZ):
                add_into(own.at[j_y, t, y], got_y.at[j_y, t])

        for at in range(NZ - 1):
            j_r = s - Y_LAG - HOP * at

            @pl.when((z == at) & (j_r >= 0) & (j_r < chunks) & jnp.logical_not(z_first(j_r)))
            def _(at=at, j_r=j_r):
                if at > 0:
                    send_right(j_r, at - 1).wait_recv()
                    for t in range(at + 1, NZ):
                        add_into(own.at[j_r, t, y], got_r.at[j_r, t - 1])
                send_right(j_r, at).start()

        for at in range(1, NZ):
            j_l = s - Y_LAG - HOP * (NZ - 1 - at)

            @pl.when((z == at) & (j_l >= 0) & (j_l < chunks) & jnp.logical_not(z_first(j_l)))
            def _(at=at, j_l=j_l):
                if at < NZ - 1:
                    send_left(j_l, at + 1).wait_recv()
                    for t in range(at):
                        add_into(own.at[j_l, t, y], got_l.at[j_l, t])
                send_left(j_l, at).start()

        for at in range(NZ):
            for right, hop in ((True, at), (False, NZ - 1 - at)):
                if hop < NZ - 1:
                    j_z = s - C_LAG - HOP * hop

                    @pl.when((z == at) & (j_z >= 0) & (j_z < chunks) & z_first(j_z))
                    def _(at=at, j_z=j_z, right=right):
                        forward_along(j_z, at, right)

        j_t = s - ZF_LAG

        @pl.when((j_t >= 0) & (j_t < chunks) & z_first(j_t))
        def _():
            turn_to_y(j_t)

        return carry

    lax.fori_loop(0, chunks + Y_LAG + HOP * (NZ - 1), step, 0)


    def finish(j):
        @pl.when(j >= chunks - RING)
        def _():
            send_core(j).wait_send()

        @pl.when(z_first(j))
        def _():
            send_y_last(j).wait()
            for at in range(NZ):

                @pl.when(z == at)
                def _(at=at):
                    if at < NZ - 1:
                        send_along(j, at, True).wait_send()
                    if at > 0:
                        send_along(j, at, False).wait_send()

        @pl.when(jnp.logical_not(z_first(j)))
        def _():
            finish_y_first(j)

    def finish_y_first(j):
        @pl.when(z == NZ - 1)
        def _():
            send_right(j, NZ - 2).wait_recv()

        @pl.when(z == 0)
        def _():
            send_left(j, 1).wait_recv()

        send_y(j).wait_send()
        for at in range(NZ):

            @pl.when(z == at)
            def _(at=at):
                if at < NZ - 1:
                    send_right(j, at).wait_send()
                if at > 0:
                    send_left(j, at).wait_send()

    def total(j, part):
        mine = own[j, z, y, part].astype(F32)
        right = got_r[j, jnp.maximum(z - 1, 0), part].astype(F32)
        left = got_l[j, jnp.minimum(z, NZ - 2), part].astype(F32)
        across = got_y[j, z, part].astype(F32)
        along = jnp.where(z > 0, right, 0.0) + jnp.where(z < NZ - 1, left, 0.0)
        return mine + jnp.where(z_first(j), across, along)

    def close(out, base, count, column):
        def panel(i, carry):
            finish(base + i)
            at = pl.ds(pl.multiple_of(column + i * LANES, LANES), LANES)
            out[:, at] = total(base + i, pl.ds(0, height))
            return carry

        lax.fori_loop(0, count, panel, 0)

    close(o_fi, bases[0], chunk_counts[0], 0)

    def tall_out(i, carry):
        finish(bases[TALL] + i)
        at = pl.ds(pl.multiple_of(i * 16, 16), 16)
        for k in range(tall_right.shape[1] // LANES):
            o_fo[at, k * LANES : (k + 1) * LANES] = total(bases[TALL] + i, pl.ds(k * 16, 16))
        return carry

    lax.fori_loop(0, chunk_counts[TALL], tall_out, 0)
    close(o_cross, bases[2], chunk_counts[2], 0)
    close(o_cross, bases[3], chunk_counts[3], dim)
    close(o_out, bases[4], chunk_counts[4], 0)
    for k in range(3):
        close(o_in, bases[5 + k], chunk_counts[5 + k], k * dim)
    close(o_gain, chunks - 1, 1, 0)

    @pl.when(sec == 0)
    def _():
        for v in range(max(0, block_units - 2), block_units):
            block_store(jnp.int32(v)).wait()

    @pl.when(sec == 1)
    def _():
        wait_all(dec_results(True))


def grad_sum(sides, kept, decoded, gain_rows, shared):
    (enc_lefts, enc_rights), (dec_lefts, dec_rights) = sides
    x_in, qx, kx, wa, g0 = shared
    rows = x_in.shape[0]
    token_counts = (enc_lefts[5][0].shape[0], dec_lefts[5][0].shape[0])
    tokens = rows * max(token_counts)
    groups = enc_lefts + enc_rights + dec_lefts + dec_rights + kept + decoded
    group_sizes = tuple(len(g) for g in groups + gain_rows[0] + gain_rows[1])
    most = max(group_sizes)
    dim, tall = dec_lefts[0][0].shape[1], dec_lefts[TALL][0].shape[1]
    height = dim // PEERS
    chunk_counts = tuple(
        dec_lefts[a][0].shape[1] * dec_rights[b][0].shape[1] // (dim * LANES) for a, b in PRODUCTS
    )
    chunks = sum(chunk_counts) + 1
    attn_units, block_units = rows * HEADS // 2, rows * token_counts[0] // BLOCK
    unit_steps = (attn_units, block_units, 2 * attn_units + 2)
    flat = lambda groups: [v for group in groups for v in group]
    moved = flat(groups)
    gains = flat(gain_rows[0] + gain_rows[1])
    half = (chunks, NZ, NY, height, LANES)
    fourth = (chunks, NZ, height, LANES)
    width = lambda *which: sum(dec_rights[i][0].shape[1] for i in which)
    out_shape = [
        jax.ShapeDtypeStruct(s, F32)
        for s in (
            (height, width(5, 6, 7)),
            (height, width(4)),
            (height, width(0)),
            (height, width(2, 3)),
            (height, LANES),
            (tall // PEERS, width(1)),
            x_in.shape,
        )
    ]
    hbm, vmem = pl.BlockSpec(memory_space=pl.ANY), pl.BlockSpec(memory_space=pltpu.VMEM)
    dma = pltpu.SemaphoreType.DMA
    return pl.pallas_call(
        functools.partial(
            grad_sum_kernel, rows, group_sizes, token_counts, chunk_counts, unit_steps
        ),
        in_specs=[hbm] * len(moved) + [vmem] * len(gains) + [hbm] * 4 + [vmem],
        out_specs=[vmem] * 6 + [hbm],
        out_shape=out_shape,
        scratch_shapes=[
            pltpu.VMEM((dim, tokens), BF),
            pltpu.VMEM((tall, tokens), BF),
            pltpu.VMEM((2, tokens, dim), BF),
            pltpu.VMEM((tokens, tall), BF),
            pltpu.VMEM((tokens, width(1)), BF),
            pltpu.VMEM((PANELS, tokens, LANES), BF),
            pltpu.VMEM((RING, NZ, NY, NC, height, LANES), BF),
            pltpu.VMEM(half, BF),
            pltpu.VMEM(fourth, BF),
            pltpu.VMEM((chunks, NZ - 1) + fourth[2:], BF),
            pltpu.VMEM((chunks, NZ - 1) + fourth[2:], BF),
            pltpu.VMEM((-(-chunks // ZF_EVERY), NZ - 1) + half[2:], BF),
            pltpu.VMEM((-(-chunks // ZF_EVERY), NZ - 1) + half[2:], BF),
            dma((2, most)),
            dma((most,)),
            dma((most,)),
            dma((PANELS, most)),
        ]
        + [dma((chunks,))] * 8
        + [
            pltpu.VMEM((rows * token_counts[0], 3 * dim), BF),
            pltpu.VMEM(wa.shape, BF),
            pltpu.VMEM((2, 5, token_counts[0], PAIR), BF),
            pltpu.VMEM(qx.shape, BF),
            pltpu.VMEM(kx.shape, BF),
            pltpu.VMEM((rows,) + kept[3][0].shape, F32),
            pltpu.VMEM((2, BLOCK, dim), BF),
            pltpu.VMEM((max(2, rows), BLOCK, dim), F32),
            pltpu.VMEM((max(2, rows), BLOCK, dim), F32),
            pltpu.VMEM((1, dim), F32),
            dma((2, 4 + most)),
            dma((3,)),
            dma((rows,)),
            dma((2, 2)),
            dma((2,)),
            dma((2, rows)),
        ],
        compiler_params=pltpu.CompilerParams(
            collective_id=1, has_side_effects=True, vmem_limit_bytes=SUM_VMEM
        ),
    )(*moved, *gains, x_in, qx, kx, wa, g0)


def hand_over_kernel(rows, *refs):
    count = (len(refs) - 3) // 3
    gain_ref, sources, gain_out = refs[0], refs[1 : 1 + count], refs[1 + count]
    targets, held = refs[2 + count : 2 + 2 * count], refs[2 + 2 * count : 2 + 3 * count]
    gain, sems = refs[2 + 3 * count], refs[3 + 3 * count]
    moves = []
    for src, keep, dst in zip(sources, held, targets):
        for part in range(rows) if len(src.shape) == 3 else [slice(None)]:
            i = len(moves)
            load = pltpu.make_async_copy(src.at[part], keep.at[part], sems.at[0, i])
            load.start()
            moves.append((load, keep.at[part], dst.at[0].at[part], sems.at[1, i]))
    load_gain = pltpu.make_async_copy(gain_ref, gain, sems.at[0, len(moves)])
    load_gain.start()
    stores = []
    for load, keep, dst, sem in moves:
        load.wait()
        stores.append(pltpu.make_async_copy(keep, dst, sem))
        stores[-1].start()
    load_gain.wait()
    gain_out[0] = gain[...].T[: gain_out.shape[1]]
    for store in stores:
        store.wait()


def hand_over(gain, gain_rows, arrays):
    hbm, vmem = pl.BlockSpec(memory_space=pl.ANY), pl.BlockSpec(memory_space=pltpu.VMEM)
    rows = max(a.shape[0] for a in arrays if a.ndim == 3)
    return pl.pallas_call(
        functools.partial(hand_over_kernel, rows),
        in_specs=[hbm] * (1 + len(arrays)),
        out_specs=[vmem] + [hbm] * len(arrays),
        out_shape=[jax.ShapeDtypeStruct((1, gain_rows, gain.shape[0]), F32)]
        + [jax.ShapeDtypeStruct((1,) + a.shape, F32) for a in arrays],
        scratch_shapes=[pltpu.VMEM(a.shape, F32) for a in arrays]
        + [
            pltpu.VMEM(gain.shape, F32),
            pltpu.SemaphoreType.DMA((2, len(arrays) + rows)),
        ],
        compiler_params=pltpu.CompilerParams(vmem_limit_bytes=SUM_VMEM),
    )(gain, *arrays)


def plain_sum(on_decoder, sides, gain_terms):
    def terms(lefts, rights):
        parts = [
            mm(jnp.concatenate(lefts[i], 0), jnp.concatenate(rights[j], 0), TN).astype(BF)
            for i, j in PRODUCTS
        ]
        return [
            jnp.concatenate(parts[5:8], 1),
            parts[4],
            parts[0],
            jnp.concatenate(parts[2:4], 1),
            parts[1],
        ]

    pieces = lax.cond(on_decoder, lambda: terms(*sides[1]), lambda: terms(*sides[0]))
    pieces.insert(4, gain_terms)
    return [
        lax.psum_scatter(piece, "rows", scatter_dimension=0, tiled=True).astype(F32)
        for piece in pieces
    ]


def low_half(rows):
    return lax.broadcasted_iota(jnp.int32, (rows, PAIR), 1) < HEAD


def masked_scores(q, k, qx, kx, head, causal):
    lo_q, lo_k = low_half(q.shape[0]), low_half(k.shape[0])
    if head == 0:
        qh, kh = jnp.where(lo_q, q, qx), jnp.where(lo_k, k, kx)
    else:
        qh, kh = jnp.where(lo_q, qx, q), jnp.where(lo_k, kx, k)
    s = mm(kh, qh, NT)
    if causal:
        key_at = lax.broadcasted_iota(jnp.int32, s.shape, 0)
        query_at = lax.broadcasted_iota(jnp.int32, s.shape, 1)
        s = jnp.where(key_at <= query_at, s, NEGATIVE)
    return s


def pair_backward(q, k, v, qx, kx, o, do, lse, causal):
    kt = k.astype(F32).T.astype(BF)
    spread = (do.astype(F32) * o.astype(F32)).T
    low_q, low_k = low_half(q.shape[0]), low_half(k.shape[0])
    zero_q, zero_k = jnp.zeros_like(q), jnp.zeros_like(k)
    dqs, grads = [], []

    def begin(head):
        s = mm(pick(head, low_k, k, kx), pick(head, low_q, q, qx), NT)
        return causal_only(s) if causal else s, mm(pick(head, low_k, v, zero_k), do, NT)

    def end(head, values):
        s, dp = values
        half = slice(head * HEAD, (head + 1) * HEAD)
        p = jnp.exp2(s * (SCALE * LOG2E) - lse[head : head + 1])
        ds = (p * (dp - jnp.sum(spread[half], axis=0, keepdims=True))).astype(BF)
        dqs.append(mm(kt[half], ds))
        grads.append(
            (mm(ds, pick(head, low_q, q, zero_q)), mm(p.astype(BF), pick(head, low_q, do, zero_q)))
        )

    in_order(range(2), begin, end)
    (dk0, dv0), (dk1, dv1) = grads
    return jnp.concatenate(dqs, axis=0).T * SCALE, (dk0 + dk1) * SCALE, dv0 + dv1


def attn_bwd_kernel(
    q_ref, k_ref, v_ref, qx_ref, kx_ref, o_ref, do_ref, lse_ref, dq_ref, dk_ref, dv_ref, *, causal
):
    dq, dk, dv = pair_backward(
        q_ref[...], k_ref[...], v_ref[...], qx_ref[0], kx_ref[0], o_ref[...], do_ref[...],
        lse_ref[0], causal,
    )
    dq_ref[...] = dq.astype(BF)
    dk_ref[...] = dk.astype(BF)
    dv_ref[...] = dv.astype(BF)


def column_block(length, first):
    return pl.BlockSpec((length, PAIR), lambda p: (0, first + p))


def mask_block(length, row):
    return pl.BlockSpec((1, length, PAIR), lambda p: (row, 0, 0))


def pair_block(count_q):
    return pl.BlockSpec((1, 2, count_q), lambda p: (p, 0, 0))


def params(**more):
    return pltpu.CompilerParams(vmem_limit_bytes=VMEM_LIMIT, **more)


def attention_backward(q_in, k_in, v_in, qx, kx, row, firsts, mixed, grad_mixed, lse, causal):
    count_q, count_k, pairs = q_in.shape[0], k_in.shape[0], HEADS // 2
    width = HEADS * HEAD
    return pl.pallas_call(
        functools.partial(attn_bwd_kernel, causal=causal),
        grid=(pairs,),
        in_specs=[
            column_block(count_q, firsts[0]),
            column_block(count_k, firsts[1]),
            column_block(count_k, firsts[2]),
            mask_block(count_q, row),
            mask_block(count_k, row),
            column_block(count_q, 0),
            column_block(count_q, 0),
            pair_block(count_q),
        ],
        out_specs=[
            column_block(count_q, 0),
            column_block(count_k, 0),
            column_block(count_k, 0),
        ],
        out_shape=[
            jax.ShapeDtypeStruct((count_q, width), BF),
            jax.ShapeDtypeStruct((count_k, width), BF),
            jax.ShapeDtypeStruct((count_k, width), BF),
        ],
        compiler_params=params(),
    )(q_in, k_in, v_in, qx, kx, mixed, grad_mixed, lse)


BLOCK = 256
SLICE = 256


def inverse_rms(v):
    return lax.rsqrt(jnp.mean(v * v, -1, keepdims=True) + EPSILON)


def norm(v, gain):
    return (v * inverse_rms(v) * gain).astype(BF)


def norm_back(v, gain, grad):
    inv = inverse_rms(v)
    scaled = grad * gain
    along = jnp.mean(scaled * v, -1, keepdims=True)
    return (
        inv * scaled - v * (inv * inv * inv * along),
        jnp.sum(grad * v * inv, 0, keepdims=True),
    )


def gelu(x):
    return 0.5 * x * (1.0 + jnp.tanh(GELU_C * (x + GELU_A * x * x * x)))


def gelu_parts(x):
    square = x * x
    t = jnp.tanh(GELU_C * x * (1.0 + GELU_A * square))
    half = 0.5 * (1.0 + t)
    slope = half + 0.5 * x * (1.0 - t * t) * (GELU_C * (1.0 + 3.0 * GELU_A * square))
    return x * half, slope


class Fetch:
    def __init__(self, sources, held, sems):
        self.copies = [
            pltpu.make_async_copy(src, dst, sems.at[i])
            for i, (src, dst) in enumerate(zip(sources, held))
        ]
        self.held = held
        self.first = pl.program_id(0) == 0

        @pl.when(self.first)
        def _():
            for copy in self.copies:
                copy.start()

    def __getitem__(self, i):
        @pl.when(self.first)
        def _():
            self.copies[i].wait()

        return self.held[i]


def add_gain(ref, part):
    @pl.when(pl.program_id(0) == 0)
    def _():
        ref[...] = part

    @pl.when(pl.program_id(0) > 0)
    def _():
        ref[...] += part


def block_call(kernel, steps, ins, weights, outs, gain_outs=0):
    specs, arrays = [], []
    for array, row, first in ins:
        columns = array.shape[-1]
        if row is None:
            specs.append(pl.BlockSpec((BLOCK, columns), lambda i, f=first: (f + i, 0)))
        else:
            specs.append(
                pl.BlockSpec((None, BLOCK, columns), lambda i, r=row, f=first: (r, f + i, 0))
            )
        arrays.append(array)
    gains = [w for w in weights if w.dtype == F32]
    mats = [w for w in weights if w.dtype != F32]
    specs += [pl.BlockSpec((1, g.shape[1]), lambda i: (0, 0)) for g in gains]
    specs += [pl.BlockSpec(memory_space=pl.ANY)] * len(mats)
    dim = gains[0].shape[1]
    count = len(mats)

    def run(*refs):
        held, sems = refs[-1 - count : -1], refs[-1]
        at = len(arrays) + len(gains)
        fetch = Fetch(refs[at : at + count], held, sems)
        kernel(refs[: len(arrays)], [g[...] for g in refs[len(arrays) : at]], fetch, refs[at + count : -1 - count])

    return pl.pallas_call(
        run,
        grid=(steps,),
        in_specs=specs,
        out_specs=[pl.BlockSpec((BLOCK, c), lambda i: (i, 0)) for c, _ in outs]
        + [pl.BlockSpec((1, dim), lambda i: (0, 0))] * gain_outs,
        out_shape=[jax.ShapeDtypeStruct((steps * BLOCK, c), t) for c, t in outs]
        + [jax.ShapeDtypeStruct((1, dim), F32)] * gain_outs,
        scratch_shapes=[pltpu.VMEM(m.shape, m.dtype) for m in mats]
        + [pltpu.SemaphoreType.DMA((count,))],
        compiler_params=params(),
    )(*arrays, *gains, *mats)


def project_kernel(ins, gains, w, outs):
    (x,), (g0,), (n_ref, packed_ref) = ins, gains, outs
    n = norm(x[...].astype(F32), g0)
    n_ref[...] = n
    wa = w[0]
    dim = x.shape[1]
    for at in range(0, wa.shape[1], dim):
        packed_ref[:, at : at + dim] = mm(n, wa[:, at : at + dim]).astype(BF)


class FeedForward:
    def __init__(self, move, wf_hbm, wd_hbm, wf, wd):
        self.wf, self.wd, self.half = wf, wd, wd.shape[0]
        self.copies, self.move, self.first = {}, move, None
        self.sources = wf_hbm, wd_hbm

    def load(self):
        wf_hbm, wd_hbm = self.sources
        for at in range(0, self.half, SLICE):
            self.copies[at] = [
                self.move.copy(wd_hbm.at[at : at + SLICE], self.wd.at[at : at + SLICE])
            ] + [
                self.move.copy(wf_hbm.at[:, first : first + SLICE], self.wf.at[:, first : first + SLICE])
                for first in (at, self.half + at)
            ]

    def ready(self, at):
        waits = self.copies.pop(at, [])
        if self.first is None:
            for made in waits:
                made.wait()
        elif waits:

            @pl.when(self.first)
            def _():
                for made in waits:
                    made.wait()

    def slices(self):
        return range(0, self.half, SLICE)

    def parts(self, at):
        self.ready(at)
        up = slice(self.half + at, self.half + at + SLICE)
        return self.wf[:, at : at + SLICE], self.wf[:, up], self.wd[at : at + SLICE, :]


def ffn_up(m, ffn, acc, u_ref, act_ref):
    half = ffn.half

    def begin(at):
        gate_w, up_w, _ = ffn.parts(at)
        return mm(m, gate_w), mm(m, up_w)

    total = [acc]

    def end(at, values):
        gate, up = values
        u_ref[:, at : at + SLICE] = gate.astype(BF)
        u_ref[:, half + at : half + at + SLICE] = up.astype(BF)
        act = (gelu(gate) * up).astype(BF)
        if act_ref is not None:
            act_ref[:, at : at + SLICE] = act
        total[0] = total[0] + mm(act, ffn.wd[at : at + SLICE, :])

    in_order(ffn.slices(), begin, end)
    return total[0]


def ffn_down(branch, ffn, u_ref, du_ref, act_ref):
    half = ffn.half
    total = []

    def begin(at):
        return mm(branch, ffn.parts(at)[2], NT)

    def end(at, d_act):
        gate_w, up_w, _ = ffn.parts(at)
        gate = u_ref[:, at : at + SLICE].astype(F32)
        up = u_ref[:, half + at : half + at + SLICE].astype(F32)
        value, slope = gelu_parts(gate)
        if act_ref is not None:
            act_ref[:, at : at + SLICE] = (value * up).astype(BF)
        d_gate = (d_act * up * slope).astype(BF)
        d_up = (d_act * value).astype(BF)
        du_ref[:, at : at + SLICE] = d_gate
        du_ref[:, half + at : half + at + SLICE] = d_up
        part = mm(d_gate, gate_w, NT) + mm(d_up, up_w, NT)
        total[:] = [part if not total else total[0] + part]

    in_order(ffn.slices(), begin, end)
    return total[0]


def dec_query_kernel(ins, gains, w, outs):
    (o, x), (g1,), (d1_ref, c_ref, cq_ref) = ins, gains, outs
    d1 = x[...].astype(F32) + mm(o[...], w[0][...])
    d1_ref[...] = d1
    c = norm(d1, g1)
    c_ref[...] = c
    cq_ref[...] = mm(c, w[1][:, : c.shape[1]]).astype(BF)


def dec_ffn_kernel(row, x_hbm, oc_hbm, d1_hbm, g2, wc_hbm, wf_hbm, wd_hbm, *refs):
    outs, results, held = refs[:9], refs[9:18], refs[18:]
    doc, out, dd2_v, m_v, act, du, branch, dg2, cot = results
    oc, d1, u, proj, wf, wd, sems = held
    move = Mover(sems)
    tokens, width = oc.shape
    got = [
        move.copy(a, b)
        for a, b in ((oc_hbm, oc), (wc_hbm.at[:, width:], proj), (d1_hbm, d1))
    ]
    ffn = FeedForward(move, wf_hbm, wd_hbm, wf, wd)
    ffn.load()
    got_cot = move.copy(x_hbm.at[row, tokens:], cot)
    for made in got:
        made.wait()
    d2 = d1[...] + mm(oc[...], proj[...], NT)
    m = norm(d2, g2[...])
    m_v[...] = m
    out[...] = ffn_up(m, ffn, d2, u, act)
    for i in (3, 1, 4):
        move.store(results[i], outs[i])
    got_cot.wait()
    move.store(cot, outs[8])
    dm = ffn_down(cot[...], ffn, u, du, None)
    back, dg2[...] = norm_back(d2, g2[...], dm)
    dd2 = cot[...].astype(F32) + back
    branch[...] = dd2.astype(BF)
    doc[...] = mm(branch[...], proj[...]).astype(BF)
    dd2_v[...] = dd2
    for i in (0, 2, 5, 6, 7):
        move.store(results[i], outs[i])
    move.drain()


def enc_back_kernel(blocks, dk_hbm, dv_hbm, e1_hbm, e2_hbm, u_hbm, g1, g2, wc_hbm, wd_hbm, wf_hbm, wo_hbm, *refs):
    outs, results, held = refs[:10], refs[10:20], refs[20:]
    mem, fb_v, m_v, act, du, de1_v, ab_v, do, dg1, dg2 = results
    dk, dv, e1_in, e2_in, u, wc, wd, wf, wo, sems = held
    move = Mover(sems)
    width = dk.shape[1]
    here = [slice(i * BLOCK, (i + 1) * BLOCK) for i in range(len(blocks))]
    there = [slice(i * BLOCK, (i + 1) * BLOCK) for i in blocks]

    def load(i, pairs):
        return [move.copy(src.at[there[i]], dst.at[here[i]]) for src, dst in pairs]

    early = ((dk_hbm, dk), (dv_hbm, dv), (e2_hbm, e2_in))
    late = ((u_hbm, u), (e1_hbm, e1_in))
    got_early, got_late = [load(0, early)], []
    got_early[0].append(move.copy(wc_hbm, wc))
    ffn = FeedForward(move, wf_hbm, wd_hbm, wf, wd)
    got_late.append(load(0, late))
    ffn.load()
    got_late[0].append(move.copy(wo_hbm, wo))
    for i in range(1, len(blocks)):
        got_early.append(load(i, early))
        got_late.append(load(i, late))
    for i, b in enumerate(here):
        for made in got_early[i]:
            made.wait()
        dmem = mm(dk[b], wc[:, :width], NT) + mm(dv[b], wc[:, width:], NT)
        mem[b] = norm(e2_in[b], g1[...])
        de2, gain1 = norm_back(e2_in[b], g1[...], dmem)
        fb = de2.astype(BF)
        fb_v[b] = fb
        for made in got_late[i]:
            made.wait()
        m_v[b] = norm(e1_in[b], g2[...])
        dm = ffn_down(fb, ffn, u.at[b], du.at[b], act.at[b])
        back, gain2 = norm_back(e1_in[b], g2[...], dm)
        de1 = de2 + back
        de1_v[b] = de1
        ab = de1.astype(BF)
        ab_v[b] = ab
        do[b] = mm(ab, wo[...], NT).astype(BF)
        for k in range(8):
            move.store(results[k].at[b], outs[k].at[b])
        dg1[...] = gain1 if i == 0 else dg1[...] + gain1
        dg2[...] = gain2 if i == 0 else dg2[...] + gain2
    move.store(dg1, outs[8])
    move.store(dg2, outs[9])
    move.drain()


def dec_back_kernel(ins, gains, w, outs):
    (dcq, d1_in, dd2), (g1,), (dd1_ref, ab_ref, do_ref, dg1_ref) = ins, gains, outs
    d1 = d1_in[...]
    dc = mm(dcq[...], w[0][:, : dcq.shape[1]], NT)
    back, dg1 = norm_back(d1, g1, dc)
    dd1 = dd2[...] + back
    dd1_ref[...] = dd1
    ab = dd1.astype(BF)
    ab_ref[...] = ab
    do_ref[...] = mm(ab, w[1][...], NT).astype(BF)
    add_gain(dg1_ref, dg1)


def input_grad_kernel(ins, gains, w, outs):
    (dq, dk, dv, x, grad), (g0,), (dx_ref, dg0_ref) = ins, gains, outs
    wa = w[0]
    width = dq.shape[1]
    dn = (
        mm(dq[...], wa[:, :width], NT)
        + mm(dk[...], wa[:, width : 2 * width], NT)
        + mm(dv[...], wa[:, 2 * width :], NT)
    )
    back, dg0 = norm_back(x[...].astype(F32), g0, dn)
    dx_ref[...] = grad[...] + back
    add_gain(dg0_ref, dg0)


class Mover:
    def __init__(self, sems):
        self.sems, self.used, self.stores = sems, 0, []

    def copy(self, src, dst):
        made = pltpu.make_async_copy(src, dst, self.sems.at[self.used])
        self.used += 1
        made.start()
        return made

    def store(self, src, dst):
        self.stores.append(self.copy(src, dst))

    def drain(self):
        for made in self.stores:
            made.wait()


def pair_columns(first, p):
    return slice(first + p * PAIR, first + (p + 1) * PAIR)


def pick(head, low, a, b):
    return jnp.where(low, a, b) if head % 2 == 0 else jnp.where(low, b, a)


def in_order(items, begin, end, lead=1):
    waiting = []
    for item in items:
        waiting.append((item, begin(item)))
        if len(waiting) > lead:
            end(*waiting.pop(0))
    while waiting:
        end(*waiting.pop(0))


def attend(q_ref, kv_ref, firsts, qx, kx, o_ref, lse_ref, causal):
    count_q, count_k = qx.shape[0], kx.shape[0]
    low_q, low_k = low_half(count_q), low_half(count_k)
    ones = jnp.ones((8, count_k), BF)
    values, outs = {}, {}

    def begin(head):
        q = q_ref[:, pair_columns(firsts[0], head // 2)]
        k = kv_ref[:, pair_columns(firsts[1], head // 2)]
        s = mm(pick(head, low_k, k, kx), pick(head, low_q, q, qx), NT)
        return causal_only(s) if causal else s

    def end(head, s):
        p = head // 2
        if head % 2 == 0:
            values[p] = kv_ref[:, pair_columns(firsts[2], p)].astype(F32).T.astype(BF)
        vt = values[p][(head % 2) * HEAD : (head % 2 + 1) * HEAD]
        top = jnp.max(s, axis=0, keepdims=True)
        e = jnp.exp2((s - top) * (SCALE * LOG2E)).astype(BF)
        mixed = mm(jnp.concatenate([vt, ones], axis=0), e)
        total = mixed[HEAD : HEAD + 1]
        outs[head] = mixed[:HEAD] * (1.0 / total)
        lse_ref[p, head % 2 : head % 2 + 1, :] = top * (SCALE * LOG2E) + jnp.log2(total)
        if head % 2 == 1:
            both = jnp.concatenate([outs.pop(head - 1), outs.pop(head)], axis=0)
            o_ref[:, pair_columns(0, p)] = both.T.astype(BF)

    in_order(range(HEADS), begin, end)


def causal_only(s):
    key_at = lax.broadcasted_iota(jnp.int32, s.shape, 0)
    query_at = lax.broadcasted_iota(jnp.int32, s.shape, 1)
    return jnp.where(key_at <= query_at, s, NEGATIVE)


def attend_kernel(firsts, row, causal, same, *refs):
    if same:
        q_ref, (qx_ref, kx_ref, o_ref, lse_ref) = refs[0], refs[1:]
        kv_ref = q_ref
    else:
        q_ref, kv_ref, qx_ref, kx_ref, o_ref, lse_ref = refs
    attend(q_ref, kv_ref, firsts, qx_ref[row], kx_ref[row], o_ref, lse_ref, causal)


def attention_forward(q_in, kv_in, qx, kx, row, firsts, causal):
    count_q = q_in.shape[0]
    ins = [q_in] if kv_in is None else [q_in, kv_in]
    vmem = pl.BlockSpec(memory_space=pltpu.VMEM)
    return pl.pallas_call(
        functools.partial(attend_kernel, firsts, row, causal, kv_in is None),
        in_specs=[vmem] * (len(ins) + 2),
        out_specs=[vmem] * 2,
        out_shape=[
            jax.ShapeDtypeStruct((count_q, HEADS * HEAD), BF),
            jax.ShapeDtypeStruct((HEADS // 2, 2, count_q), F32),
        ],
        compiler_params=params(),
    )(*ins, qx, kx)


def enc_attend_kernel(row, x_hbm, qx_hbm, kx_hbm, g0, wa_hbm, *refs):
    outs, (n_v, packed_v, o_v, lse_v, x, qx, kx, wa, sems) = refs[:4], refs[4:]
    move = Mover(sems)
    got_x = move.copy(x_hbm.at[row], x)
    thirds = [slice(at, at + x.shape[1]) for at in range(0, wa.shape[1], x.shape[1])]
    got_wa = [move.copy(wa_hbm.at[:, t], wa.at[:, t]) for t in thirds]
    got_masks = move.copy(qx_hbm.at[row], qx), move.copy(kx_hbm.at[row], kx)
    tokens, dim = x.shape
    got_x.wait()
    blocks = [slice(at, at + BLOCK) for at in range(0, tokens, BLOCK)]
    for b in blocks:
        n_v[b] = norm(x[b].astype(F32), g0[...])
    move.store(n_v, outs[0])
    for t, made in zip(thirds, got_wa):
        made.wait()
        for b in blocks:
            packed_v[b, t] = mm(n_v[b], wa[:, t]).astype(BF)
    move.store(packed_v, outs[1])
    for made in got_masks:
        made.wait()
    attend(packed_v, packed_v, (0, dim, 2 * dim), qx[...], kx[...], o_v, lse_v, False)
    move.store(o_v, outs[2])
    move.store(lse_v, outs[3])
    move.drain()


def enc_rest_kernel(row, x_hbm, o_hbm, g1, g2, wo_hbm, wf_hbm, wd_hbm, wc_hbm, *refs):
    outs, (e1_v, u_v, e2_v, sent_v, x, o, wo, wf, wd, wc, sems) = refs[:4], refs[4:]
    move = Mover(sems)
    got = [move.copy(a, b) for a, b in ((x_hbm.at[row], x), (o_hbm, o), (wo_hbm, wo))]
    ffn = FeedForward(move, wf_hbm, wd_hbm, wf, wd)
    ffn.load()
    got_wc = [move.copy(wc_hbm, wc)]
    for made in got:
        made.wait()
    blocks = [slice(at, at + BLOCK) for at in range(0, x.shape[0], BLOCK)]
    for b in blocks:
        e1_v[b] = x[b].astype(F32) + mm(o[b], wo[...])
        move.store(e1_v.at[b], outs[0].at[b])
    results = ((u_v, outs[1]), (e2_v, outs[2]), (sent_v, outs[3]))

    def stores(i):
        b = pl.ds(pl.multiple_of(i * BLOCK, BLOCK), BLOCK)
        return [
            pltpu.make_async_copy(src.at[b], dst.at[b], sems.at[move.used + len(blocks) * k + i])
            for k, (src, dst) in enumerate(results)
        ]

    def block(i, carry):
        b = pl.ds(pl.multiple_of(i * BLOCK, BLOCK), BLOCK)
        ffn.first = i == 0
        e1 = e1_v[b]
        e2 = ffn_up(norm(e1, g2[...]), ffn, e1, u_v.at[b], None)
        e2_v[b] = e2

        @pl.when(i == 0)
        def _():
            got_wc[0].wait()

        sent_v[b] = mm(norm(e2, g1[...]), wc[...]).astype(BF)
        for copy in stores(i):
            copy.start()
        return carry

    lax.fori_loop(0, len(blocks), block, 0)
    for i in range(len(blocks)):
        for copy in stores(i):
            copy.wait()
    move.drain()


HBM = pl.BlockSpec(memory_space=pl.ANY)
VMEM = pl.BlockSpec(memory_space=pltpu.VMEM)


def moved_call(kernel, ins, specs, outs, held, copies):
    return list(
        pl.pallas_call(
            kernel,
            in_specs=specs,
            out_specs=[HBM] * len(outs),
            out_shape=[jax.ShapeDtypeStruct(s, t) for s, t in outs],
            scratch_shapes=[pltpu.VMEM(s, t) for s, t in outs + held]
            + [pltpu.SemaphoreType.DMA((copies,))],
            compiler_params=params(),
        )(*ins)
    )


def enc_attend(row, x_in, qx, kx, g0, wa):
    tokens, dim = x_in.shape[1:]
    width = wa.shape[1] // 3
    kept = [
        ((tokens, dim), BF),
        ((tokens, wa.shape[1]), BF),
        ((tokens, width), BF),
        ((HEADS // 2, 2, tokens), F32),
    ]
    held = [(x_in.shape[1:], BF), (qx.shape[1:], BF), (kx.shape[1:], BF), (wa.shape, BF)]
    return moved_call(
        functools.partial(enc_attend_kernel, row),
        (x_in, qx, kx, g0, wa),
        [HBM] * 3 + [VMEM] + [HBM],
        kept,
        held,
        10,
    )


def enc_rest(row, x_in, o, g1, g2, wo, wf, wd, wc):
    tokens, dim = x_in.shape[1:]
    kept = [
        ((tokens, dim), F32),
        ((tokens, wf.shape[1]), BF),
        ((tokens, dim), F32),
        ((tokens, wc.shape[1]), BF),
    ]
    held = [(x_in.shape[1:], BF), (o.shape, BF)] + [(w.shape, BF) for w in (wo, wf, wd, wc)]
    return moved_call(
        functools.partial(enc_rest_kernel, row),
        (x_in, o, g1, g2, wo, wf, wd, wc),
        [HBM] * 2 + [VMEM] * 2 + [HBM] * 4,
        kept,
        held,
        4 + 3 * (wd.shape[0] // SLICE) + 4 * (tokens // BLOCK),
    )


def nothing_kernel(*refs):
    pass


def unwritten(shapes):
    return pl.pallas_call(
        nothing_kernel,
        out_specs=[pl.BlockSpec(memory_space=pl.ANY)] * len(shapes),
        out_shape=[jax.ShapeDtypeStruct(s.shape, s.dtype) for s in shapes],
    )()


def by_section(on_decoder, encoder, decoder):
    enc_shapes = jax.eval_shape(encoder) if encoder else []
    dec_shapes = jax.eval_shape(decoder) if decoder else []
    none = lambda: []
    encoder, decoder = encoder or none, decoder or none
    pool = lambda shapes: list(unwritten(shapes)) if shapes else []
    both = lax.cond(
        on_decoder,
        lambda: pool(enc_shapes) + list(decoder()),
        lambda: list(encoder()) + pool(dec_shapes),
    )
    return both[: len(enc_shapes)], both[len(enc_shapes) :]


def mask_kernel(*refs):
    for lengths_ref, (member_ref, other_ref) in ((refs[0], refs[2:4]), (refs[1], refs[4:6])):
        rows, span, lanes = member_ref.shape
        position = lax.broadcasted_iota(jnp.int32, (span, lanes), 0)
        lane = lax.rem(lax.broadcasted_iota(jnp.int32, (span, lanes), 1), HEAD)
        docs = lengths_ref.shape[1]
        for r in range(rows):
            seg, end = jnp.zeros((span, lanes), jnp.int32), jnp.int32(0)
            for j in range(docs):
                end = end + lengths_ref[r, j]
                seg = seg + jnp.where(position >= end, 1, 0)
            hit = lane == seg
            member_ref[r] = jnp.where(hit, 1.0, 0.0).astype(BF)
            other_ref[r] = jnp.where(hit | (lane >= docs), 0.0, NEGATIVE).astype(BF)


def mask_operands(enc_lengths, dec_lengths, spans):
    smem = pl.BlockSpec(memory_space=pltpu.SMEM)
    vmem = pl.BlockSpec(memory_space=pltpu.VMEM)
    return pl.pallas_call(
        mask_kernel,
        in_specs=[smem] * 2,
        out_specs=[vmem] * 4,
        out_shape=[
            jax.ShapeDtypeStruct((enc_lengths.shape[0], span, PAIR), BF)
            for span in spans
            for _ in range(2)
        ],
        compiler_params=params(),
    )(enc_lengths, dec_lengths)


def shift(x, by):
    pairs = [(0, 1)] if by > 0 else [(1, 0)]
    return lax.ppermute(x, "section", pairs)


def body(
    section_input, enc_lengths, dec_lengths, attn_in, attn_out, ffn_in, ffn_out, cross_weight, gains
):
    wa, wo, wf, wd, wc = attn_in[0], attn_out[0], ffn_in[0], ffn_out[0], cross_weight[0]
    g0, g1, g2 = gains[0, 0:1], gains[0, 1:2], gains[0, 2:3]
    x_in = section_input[0]
    rows, le, dim = x_in.shape
    ld = le // 2
    width = wo.shape[0]
    enc_qx, enc_kx, dec_qx, dec_kx = mask_operands(enc_lengths, dec_lengths, (le, ld))
    on_decoder = lax.axis_index("section") == 1
    steps_e, steps_d = le // BLOCK, ld // BLOCK
    columns = width // PAIR
    own = (0, columns, 2 * columns)
    across = (0, 0, columns)
    inner = wf.shape[1]

    def project(r, steps):
        return list(
            block_call(project_kernel, steps, [(x_in, r, 0)], [g0, wa], [(dim, BF), (3 * width, BF)])
        )

    def dec_first(r):
        n, packed = project(r, steps_d)
        o, lse = attention_forward(packed, None, dec_qx, dec_kx, r, (0, width, 2 * width), True)
        d1, c, cq = block_call(
            dec_query_kernel,
            steps_d,
            [(o, None, 0), (x_in, r, 0)],
            [g1, wo, wc],
            [(dim, F32), (dim, BF), (width, BF)],
        )
        return [n, packed, o, lse, d1, c, cq]

    def cross(r, cq, sent):
        return list(attention_forward(cq, sent, dec_qx, enc_kx, r, (0, 0, width), False))

    feeds = 3 * (wd.shape[0] // SLICE)

    def dec_ffn(r, oc, d1):
        row = lambda columns, kind: ((ld, columns), kind)
        return moved_call(
            functools.partial(dec_ffn_kernel, r),
            (x_in, oc, d1, g2, wc, wf, wd),
            [HBM] * 3 + [VMEM] + [HBM] * 3,
            [row(width, BF), row(dim, F32), row(dim, F32), row(dim, BF), row(wd.shape[0], BF)]
            + [row(inner, BF), row(dim, BF), ((1, dim), F32), row(dim, BF)],
            [row(width, BF), row(dim, F32), row(inner, BF), ((dim, width), BF)]
            + [(wf.shape, BF), (wd.shape, BF)],
            feeds + 4 + 9,
        )

    def cross_back(r, cq, sent, oc, doc, lse):
        return list(
            attention_backward(cq, sent, sent, dec_qx, enc_kx, r, across, oc, doc, lse, False)
        )

    def enc_back(dk, dv, e1, e2, u, blocks):
        row = lambda columns, kind: ((len(blocks) * BLOCK, columns), kind)
        return moved_call(
            functools.partial(enc_back_kernel, blocks),
            (dk, dv, e1, e2, u, g1, g2, wc, wd, wf, wo),
            [HBM] * 5 + [VMEM] * 2 + [HBM] * 4,
            [row(dim, BF)] * 3
            + [row(wd.shape[0], BF), row(inner, BF), row(dim, F32), row(dim, BF), row(width, BF)]
            + [((1, dim), F32)] * 2,
            [row(width, BF)] * 2
            + [row(dim, F32)] * 2
            + [row(inner, BF)]
            + [(w.shape, BF) for w in (wc, wd, wf, wo)],
            feeds + 2 + 5 * len(blocks) + 8 * len(blocks) + 2,
        )

    def self_back(r, steps, masks, causal, packed, o, lse, do, grad):
        dq, dk, dv = attention_backward(
            packed, packed, packed, *masks, r, own, o, do, lse, causal
        )
        dx, dg0 = block_call(
            input_grad_kernel,
            steps,
            [(dq, None, 0), (dk, None, 0), (dv, None, 0), (x_in, r, 0), (grad, None, 0)],
            [g0, wa],
            [(dim, F32)],
            1,
        )
        return [dq, dk, dv, dx, dg0]

    def dec_back(dcq, d1, dd2):
        return list(
            block_call(
                dec_back_kernel,
                steps_d,
                [(dcq, None, 0), (d1, None, 0), (dd2, None, 0)],
                [g1, wc, wo],
                [(dim, F32), (dim, BF), (width, BF)],
                1,
            )
        )

    every = range(rows)
    plain = lax.axis_size("rows") != PEERS
    state = []

    def run(encoder, decoder, *ready):
        held = on_decoder
        if state:
            held, state[0][1], *_ = lax.optimization_barrier((on_decoder, state[0][1]) + ready)
        out = by_section(held, encoder, decoder)
        state[:] = [out[0] or out[1]]
        return out

    def slots():
        return [None] * rows

    first, rest, dfirst, cqs, crossed, ocs = slots(), slots(), slots(), slots(), slots(), slots()
    mids, docs_in, cross_b, dcqs, back, last, dlast = (slots() for _ in range(7))

    def begin_cross(r, beside=None):
        crossed[r], out = run(lambda: cross(r, cqs[r], rest[r][3]), beside)
        ocs[r] = shift(crossed[r][0], 1)
        return out

    def dec_mid(r):
        return lambda: dec_ffn(r, ocs[r], dfirst[r][4])

    def keep_mid(r, out):
        mids[r] = out
        docs_in[r] = shift(out[0], -1)

    def dec_last(r):
        p = dec_back(dcqs[r], dfirst[r][4], mids[r][2])
        n, packed, o, lse = dfirst[r][:4]
        return p + self_back(r, steps_d, (dec_qx, dec_kx), True, packed, o, lse, p[2], p[0])

    def enc_last(r):
        return self_back(
            r, steps_e, (enc_qx, enc_kx), False, *first[r][1:4],
            jnp.concatenate(backs(r, 7), 0), jnp.concatenate(backs(r, 5), 0),
        )

    def enc_first(r):
        return lambda: enc_attend(r, x_in, enc_qx, enc_kx, g0, wa)

    def enc_then(r):
        return lambda: enc_rest(r, x_in, first[r][2], g1, g2, wo, wf, wd, wc)

    first[0], dfirst[0] = run(enc_first(0), lambda: dec_first(0))
    cqs[0] = shift(dfirst[0][6], -1)
    rest[0], more = run(enc_then(0), lambda: [v for r in every[1:] for v in dec_first(r)])
    begin_cross(0)
    for r in every[1:]:
        dfirst[r] = more[7 * (r - 1) : 7 * r]
        cqs[r] = shift(dfirst[r][6], -1)
    for r in every[1:]:
        first[r], _ = run(enc_first(r), None)
        rest[r], out = run(enc_then(r), dec_mid(r - 1), ocs[r - 1])
        keep_mid(r - 1, out)
        begin_cross(r)
    def backs(r, i):
        return [part[i] for part in back[r]]

    def enc_backs(r, blocks):
        return lambda: enc_back(
            cross_b[r][1], cross_b[r][2], rest[r][0], rest[r][2], rest[r][1], blocks
        )

    for r in every:
        cross_b[r], _ = run(
            lambda: cross_back(r, cqs[r], rest[r][3], crossed[r][0], docs_in[r], crossed[r][1]),
            None,
        )
        if r == 0 and steps_e > 1:
            part, out = run(enc_backs(0, (0,)), dec_mid(rows - 1))
            keep_mid(rows - 1, out)
            dcqs[0] = shift(cross_b[0][0], 1)
            others, _ = run(enc_backs(0, tuple(range(1, steps_e))), None)
            back[0] = [part, others]
        else:
            dcqs[r] = shift(cross_b[r][0], 1)
            out = run(enc_backs(r, tuple(range(steps_e))), dec_mid(rows - 1) if r == 0 else None)
            back[r] = [out[0]]
            if r == 0:
                keep_mid(rows - 1, out[1])
        last[r], dlast[r] = run((lambda: enc_last(r)) if plain else None, lambda: dec_last(r))

    def over_rows(lists):
        pieces = lambda v: v if isinstance(v, list) else [v]
        return [[p for v in group for p in pieces(v)] for group in zip(*lists)]

    enc_side = (
        over_rows(
            [backs(r, 2), backs(r, 3), backs(r, 0), backs(r, 0), first[r][2], first[r][0]]
            for r in every
        ),
        over_rows(
            [backs(r, 4), backs(r, 1), cross_b[r][1], cross_b[r][2], backs(r, 6)] + last[r][0:3]
            for r in every
        ),
    )
    dec_side = (
        over_rows(
            [mids[r][3], mids[r][4], dfirst[r][5], mids[r][6], dfirst[r][2], dfirst[r][0]]
            for r in every
        ),
        over_rows(
            [mids[r][5], mids[r][8], dcqs[r], ocs[r], dlast[r][1]] + dlast[r][4:7] for r in every
        ),
    )
    if not plain:
        kept = over_rows(
            [first[r][1], first[r][2], backs(r, 7), first[r][3], backs(r, 5)] for r in every
        )
        decoded = over_rows([mids[r][1], dlast[r][7]] for r in every)
        gain_rows = (
            over_rows([backs(r, 8), backs(r, 9)] for r in every),
            over_rows([dlast[r][8], dlast[r][3], mids[r][7]] for r in every),
        )
        s_in, s_out, s_fi, s_cross, s_gain, s_fo, results = grad_sum(
            (enc_side, dec_side), kept, decoded, gain_rows, (x_in, enc_qx, enc_kx, wa, g0)
        )
        o_gain, *outs = hand_over(
            s_gain, gains.shape[1], [results, s_in, s_out, s_fi, s_fo, s_cross]
        )
        return tuple(outs) + (o_gain,)

    def enc_parts():
        gain_rows = [sum(v) for v in zip(*[[last[r][4], sum(backs(r, 8)), sum(backs(r, 9))] for r in every])]
        return [jnp.concatenate(gain_rows, 0), jnp.stack([last[r][3] for r in every])]

    def dec_parts():
        gain_rows = [sum(v) for v in zip(*[[dlast[r][8], dlast[r][3], mids[r][7]] for r in every])]
        both = [jnp.concatenate([mids[r][1], dlast[r][7]], 0) for r in every]
        return [jnp.concatenate(gain_rows, 0), jnp.stack(both)]

    gain_grads, results = lax.cond(on_decoder, dec_parts, enc_parts)
    gain_terms = jnp.pad(gain_grads.T, ((0, 0), (0, LANES - gain_grads.shape[0]))).astype(BF)

    s_in, s_out, s_fi, s_cross, s_gain, s_fo = plain_sum(on_decoder, (enc_side, dec_side), gain_terms)
    return (
        results[None],
        s_in[None],
        s_out[None],
        s_fi[None],
        s_fo[None],
        s_cross[None],
        s_gain[:, : gain_grads.shape[0]].T[None],
    )


def solution(mesh):
    placed = (
        P("section", "rows", None, None),
        P("rows", None),
        P("rows", None),
    ) + (P("section", None, None),) * 6
    return jax.shard_map(
        body,
        mesh=mesh,
        in_specs=placed,
        out_specs=(
            P("section", "rows", None, None),
            P("section", "rows", None),
            P("section", "rows", None),
            P("section", "rows", None),
            P("section", "rows", None),
            P("section", "rows", None),
            P("section", None, "rows"),
        ),
        check_vma=False,
    )
```
